32 devices in a mesh: dp: 4 (over x, core), ctx: 8 (over z, y).
Axes of the slice: x: 2, y: 2, z: 4, core: 2. Of those that a mesh axis runs over, the one named last changes fastest.
Arguments:
- layer_input: bfloat16 [4096, 1536], P(('dp', 'ctx')), may hold values from -6 to 6
- cotangent: bfloat16 [4096, 1536], P(('dp', 'ctx')), may hold values from -6 to 6
- seq_lengths: int32 [4, 3], P('dp'), may hold values from 1 to 1022, as said below
- gains: float32 [2, 1536], replicated, may hold values from 0.5 to 1.5
- head_bias: float32 [2, 24], replicated, may hold values from -2 to 10
- w_query: bfloat16 [1536, 1536], P(('dp', 'ctx')), may hold values from -0.15625 to 0.15625
- w_key: bfloat16 [1536, 1536], P(('dp', 'ctx')), may hold values from -0.15625 to 0.15625
- w_value: bfloat16 [1536, 1536], P(('dp', 'ctx')), may hold values from -0.15625 to 0.15625
- w_gate: bfloat16 [1536, 1536], P(('dp', 'ctx')), may hold values from -0.15625 to 0.15625
- w_out: bfloat16 [1536, 1536], P(('dp', 'ctx')), may hold values from -0.625 to 0.625
- w_heads: bfloat16 [1536, 48], P(('dp', 'ctx')), may hold values from -0.15625 to 0.15625
- w_ff_gate: bfloat16 [1536, 4096], P(('dp', 'ctx')), may hold values from -0.15625 to 0.15625
- w_ff_up: bfloat16 [1536, 4096], P(('dp', 'ctx')), may hold values from -0.15625 to 0.15625
- w_ff_down: bfloat16 [4096, 1536], P(('dp', 'ctx')), may hold values from -0.09375 to 0.09375
Outputs:
- layer_output: bfloat16 [4096, 1536], P(('dp', 'ctx'))
- grad_x: float32 [4096, 1536], P(('dp', 'ctx'))
- grad_gains: float32 [2, 1536], replicated
- grad_head_bias: float32 [2, 24], replicated
- grad_w_query: float32 [1536, 1536], P(('dp', 'ctx'))
- grad_w_key: float32 [1536, 1536], P(('dp', 'ctx'))
- grad_w_value: float32 [1536, 1536], P(('dp', 'ctx'))
- grad_w_gate: float32 [1536, 1536], P(('dp', 'ctx'))
- grad_w_out: float32 [1536, 1536], P(('dp', 'ctx'))
- grad_w_heads: float32 [1536, 48], P(('dp', 'ctx'))
- grad_w_ff_gate: float32 [1536, 4096], P(('dp', 'ctx'))
- grad_w_ff_up: float32 [1536, 4096], P(('dp', 'ctx'))
- grad_w_ff_down: float32 [4096, 1536], P(('dp', 'ctx'))
The draws below stay inside these ranges and needn't reach their ends.
Inputs may be any that keep to these rules, and one draw needn't show every extreme that they name: `seq_lengths`: row g holds the lengths of the three sequences packed in order into group g of 1024 tokens; the first and the last are shorter than 128, the middle one takes the rest.
All inputs are finite; a program needn't handle non-finite values.
Results may differ from the reference program's by a relative error of at most 0.014.
Values may be sent and summed in bfloat16 or wider, within the bound.
A program may use at most 320 MiB of HBM per device.

```python
import jax
import jax.numpy as jnp
from jax import lax

D = 1536
H = 24
HD = 64
FF = 4096
TOK_DEV = 128
GROUP = 1024
TOKENS = 4096
N_DP = 4
N_CTX = 8


def draw_seq_lengths(key, part):
    key = jax.random.fold_in(key, 23)
    key_head, key_tail, key_pick = jax.random.split(key, 3)
    head = jax.random.randint(key_head, (N_DP, 1), 1, TOK_DEV)
    tail = jax.random.randint(key_tail, (N_DP, 1), 1, TOK_DEV)
    picked = jax.random.randint(key_pick, (), 0, N_DP)
    chosen = (jnp.arange(N_DP, dtype=jnp.int32) == picked)[:, None]
    head = jnp.where(chosen, 1, head)
    tail = jnp.where(chosen, 1, tail)
    middle = TOK_DEV * N_CTX - head - tail
    return jnp.concatenate([head, middle, tail], axis=1).astype(jnp.int32)


def draw_head_bias(key, part):
    key = jax.random.fold_in(key, 11)
    key_forget, key_shift = jax.random.split(key)
    slowest = jnp.log(jnp.float32(GROUP) / 1.2)
    fastest = jnp.log(jnp.float32(40.0))
    forget = fastest + jax.random.uniform(key_forget, (H,), jnp.float32, 0.0, 1.0) * (slowest - fastest)
    shift = jax.random.uniform(key_shift, (H,), jnp.float32, -2.0, 2.0)
    return jnp.stack([forget, shift]).astype(jnp.float32)


def block_levels(key, extent, cuts, smallest, high):
    level, own = 1.0, jax.random.fold_in(key, 6)
    for axis_at, blocks in cuts:
        heights = jnp.exp(jax.random.uniform(jax.random.fold_in(own, axis_at), (blocks,), jnp.float32, smallest / len(cuts), high / len(cuts)))
        level = level * jnp.repeat(heights, extent[axis_at] // blocks).reshape([-1 if axis == axis_at else 1 for axis in range(len(extent))])
    return level


def normal_values(stream_key, extent, width, limit, cuts=(), kind=jnp.bfloat16):
    loudness = block_levels(stream_key, extent, cuts, -0.22, 0.18) if cuts else 1.0
    values = jax.random.normal(stream_key, extent, jnp.float32) * width * loudness
    return jnp.minimum(jnp.maximum(values, -limit), limit).astype(kind)


def setup_inputs(seed: int = 0) -> dict:
    arg_keys = jax.random.split(jax.random.key(seed), 15)
    return {
        "layer_input": normal_values(arg_keys[0], (TOKENS, D), 1.0, 6.0, ((0, 32),)),
        "cotangent": normal_values(arg_keys[1], (TOKENS, D), 1.0, 6.0, ((0, 32),)),
        "seq_lengths": draw_seq_lengths(jax.random.fold_in(arg_keys[14], 71), 0),
        "gains": jnp.clip(1.0 + 0.1 * jax.random.normal(arg_keys[3], (2, D), jnp.float32), 0.5, 1.5),
        "head_bias": draw_head_bias(jax.random.fold_in(arg_keys[14], 71), 0),
        "w_query": normal_values(arg_keys[5], (D, D), D ** -0.5, 0.15625, ((0, 32),)),
        "w_key": normal_values(arg_keys[6], (D, D), D ** -0.5, 0.15625, ((0, 32),)),
        "w_value": normal_values(arg_keys[7], (D, D), D ** -0.5, 0.15625, ((0, 32),)),
        "w_gate": normal_values(arg_keys[8], (D, D), D ** -0.5, 0.15625, ((0, 32),)),
        "w_out": normal_values(arg_keys[9], (D, D), (D // 16) ** -0.5, 0.625, ((0, 32),)),
        "w_heads": normal_values(arg_keys[10], (D, 2 * H), D ** -0.5, 0.15625, ((0, 32),)),
        "w_ff_gate": normal_values(arg_keys[11], (D, FF), D ** -0.5, 0.15625, ((0, 32),)),
        "w_ff_up": normal_values(arg_keys[12], (D, FF), D ** -0.5, 0.15625, ((0, 32),)),
        "w_ff_down": normal_values(arg_keys[13], (FF, D), FF ** -0.5, 0.09375, ((0, 32),)),
    }


EPS = 1e-06
HIGH = lax.Precision.HIGHEST

@jax.custom_vjp
def low(v):
    return lax.optimization_barrier(v.astype(jnp.bfloat16)).astype(jnp.float32)

@jax.custom_vjp
def low_back(v):
    return v

def low_keep(v):
    return (low(v), None)

def low_pass(kept, grad):
    return (grad,)

def back_keep(v):
    return (v, None)

def back_low(kept, grad):
    return (low(grad),)
low.defvjp(low_keep, low_pass)
low_back.defvjp(back_keep, back_low)

def norm_rows(value, gain):
    return value * lax.rsqrt(lax.optimization_barrier(jnp.mean(value * value, axis=-1, keepdims=True)) + EPS) * gain

def norm_heads(value):
    count = value.shape[0]
    split = value.reshape(count, H, HD)
    split = split * lax.rsqrt(lax.optimization_barrier(jnp.mean(split * split, axis=-1, keepdims=True)) + EPS)
    return split.reshape(count, D)

def attend_group(q_group, k_group, v_group, decay, seg_row):
    block = min(512, GROUP)
    count = GROUP // block
    positions = jnp.arange(GROUP, dtype=jnp.int32)
    keys4 = k_group.reshape(GROUP, H, HD)
    values4 = v_group.reshape(GROUP, H, HD)

    def one_block(pieces):
        q_part, f_part, s_part, p_part = pieces
        q4 = q_part.reshape(block, H, HD)
        scores = jnp.einsum('bhd,ghd->hbg', q4, keys4, precision=HIGH) * HD ** (-0.5)
        scores = scores + f_part.T[:, :, None] - decay.T[:, None, :]
        scores = low_back(scores)
        allowed = (s_part[:, None] == seg_row[None, :]) & (positions[None, :] <= p_part[:, None])
        scores = jnp.where(allowed[None], scores, -1e+30)
        top = lax.optimization_barrier(jnp.max(scores, axis=-1, keepdims=True))
        expd = jnp.exp(scores - top)
        probs = expd / lax.optimization_barrier(jnp.sum(expd, axis=-1, keepdims=True))
        mixed = jnp.einsum('hbg,ghd->bhd', low(probs), values4, precision=HIGH)
        return mixed.reshape(block, D)
    pieces = (q_group.reshape(count, block, D), decay.reshape(count, block, H), seg_row.reshape(count, block), positions.reshape(count, block))
    return lax.map(jax.checkpoint(one_block), pieces).reshape(GROUP, D)

def forward(layer_in, gains, head_bias, w_query, w_key, w_value, w_gate, w_out, w_heads, w_ff_gate, w_ff_up, w_ff_down, seg, start):
    h_one = low(norm_rows(layer_in, gains[0]))
    query = low_back(jnp.dot(h_one, w_query, precision=HIGH))
    key_raw = low_back(jnp.dot(h_one, w_key, precision=HIGH))
    value_raw = low_back(jnp.dot(h_one, w_value, precision=HIGH))
    gate_raw = low_back(jnp.dot(h_one, w_gate, precision=HIGH))
    head_raw = low_back(jnp.dot(h_one, w_heads, precision=HIGH))
    log_forget = jax.nn.log_sigmoid(head_raw[:, :H] + head_bias[0])
    mix = jnp.repeat(jax.nn.sigmoid(head_raw[:, H:] + head_bias[1]), HD, axis=1)
    keep = (1 - start).astype(jnp.float32)[:, None]
    zero_row = jnp.zeros((1, D), jnp.float32)
    key_prev = jnp.concatenate([zero_row, key_raw[:-1]], 0) * keep
    value_prev = jnp.concatenate([zero_row, value_raw[:-1]], 0) * keep
    key_mix = mix * key_prev + (1.0 - mix) * key_raw
    value_mix = mix * value_prev + (1.0 - mix) * value_raw
    q_low = low(norm_heads(query))
    k_low = low(norm_heads(key_mix))
    v_low = low(value_mix)
    decay = jnp.cumsum(log_forget.reshape(N_DP, GROUP, H), axis=1)

    def per_group(parts):
        return attend_group(parts[0], parts[1], parts[2], parts[3], parts[4])
    attn = lax.map(per_group, (q_low.reshape(N_DP, GROUP, D), k_low.reshape(N_DP, GROUP, D), v_low.reshape(N_DP, GROUP, D), decay, seg.reshape(N_DP, GROUP)))
    attn = low_back(attn.reshape(TOKENS, D))
    branch_in = low(jax.nn.sigmoid(gate_raw) * attn)
    mid = layer_in + low_back(jnp.dot(branch_in, w_out, precision=HIGH))
    h_two = low(norm_rows(mid, gains[1]))
    ff_gate = low_back(jnp.dot(h_two, w_ff_gate, precision=HIGH))
    ff_up = low_back(jnp.dot(h_two, w_ff_up, precision=HIGH))
    hidden = low(ff_gate * jax.nn.sigmoid(ff_gate) * ff_up)
    return mid + jnp.dot(hidden, w_ff_down, precision=HIGH)

def reference(layer_input, cotangent, seq_lengths, gains, head_bias, w_query, w_key, w_value, w_gate, w_out, w_heads, w_ff_gate, w_ff_up, w_ff_down):
    positions = jnp.arange(GROUP, dtype=jnp.int32)[None, :]
    first = seq_lengths[:, 0:1]
    second = first + seq_lengths[:, 1:2]
    seg = ((positions >= first).astype(jnp.int32) + (positions >= second).astype(jnp.int32)).reshape(TOKENS)
    start = ((positions == 0) | (positions == first) | (positions == second)).astype(jnp.int32).reshape(TOKENS)
    weights = (w_query, w_key, w_value, w_gate, w_out, w_heads, w_ff_gate, w_ff_up, w_ff_down)
    weights = tuple((weight.astype(jnp.float32) for weight in weights))

    def run(input_value, gain_value, bias_value, *weight_values):
        return forward(input_value, gain_value, bias_value, *weight_values, seg, start)
    result, pull = jax.vjp(run, layer_input.astype(jnp.float32), gains, head_bias, *weights)
    grads = pull(cotangent.astype(jnp.float32))
    return (result.astype(jnp.bfloat16), grads[0], grads[1], grads[2], grads[3], grads[4], grads[5], grads[6], grads[7], grads[8], grads[9], grads[10], grads[11])
```

```python
import jax
import jax.numpy as jnp
import numpy as np
from jax import lax
from jax.sharding import Mesh
from jax.sharding import PartitionSpec as P

EPS = 1e-06


def passed_along(array, axis, by):
    size = lax.axis_size(axis)
    pairs = [(i, i + by) for i in range(size) if 0 <= i + by < size]
    return lax.ppermute(array, axis, pairs)


def entering(part, axis, combine, identity, reverse):
    count = lax.axis_size(axis)
    place = lax.axis_index(axis)
    ahead = count - 1 - place if reverse else place
    gathered = lax.all_gather(part, axis)
    state = jnp.zeros_like(part) + jnp.asarray(identity, part.dtype)

    def one(step, state):
        source = count - 1 - step if reverse else step
        return combine(state, lax.dynamic_index_in_dim(gathered, source, 0, False))

    return lax.fori_loop(0, ahead, one, state)


def fetch_attention(w_query, w_key, w_value, w_gate, w_out, w_heads):
    return (
        lax.all_gather(w_query, ("dp", "ctx"), axis=0, tiled=True),
        lax.all_gather(w_key, ("dp", "ctx"), axis=0, tiled=True),
        lax.all_gather(w_value, ("dp", "ctx"), axis=0, tiled=True),
        lax.all_gather(w_gate, ("dp", "ctx"), axis=0, tiled=True),
        lax.all_gather(w_out, ("dp", "ctx"), axis=0, tiled=True),
        lax.all_gather(w_heads, ("dp", "ctx"), axis=0, tiled=True),
    )


def fetch_feed(w_ff_gate, w_ff_up, w_ff_down):
    return (
        lax.all_gather(w_ff_gate, ("dp", "ctx"), axis=0, tiled=True),
        lax.all_gather(w_ff_up, ("dp", "ctx"), axis=0, tiled=True),
        lax.all_gather(w_ff_down, ("dp", "ctx"), axis=0, tiled=True),
    )


def add_arrays(earlier, later):
    return earlier + later


def norm_back(grad, normed, inverse):
    return inverse * (grad - normed * jnp.mean(grad * normed, axis=-1, keepdims=True))


def project(left, right):
    return jnp.dot(left, right, preferred_element_type=jnp.float32)


def weight_grad(left, right):
    return jnp.einsum("ra,rb->ab", left, right, preferred_element_type=jnp.float32)


def input_grad(grad, weight):
    return jnp.einsum("rb,ab->ra", grad, weight, preferred_element_type=jnp.float32)


def shards(
    layer_input,
    cotangent,
    seq_lengths,
    gains,
    head_bias,
    w_query,
    w_key,
    w_value,
    w_gate,
    w_out,
    w_heads,
    w_ff_gate,
    w_ff_up,
    w_ff_down,
):
    rows, width = layer_input.shape
    heads = head_bias.shape[1]
    head_dim = width // heads
    spans = lax.axis_size("ctx")
    group = rows * spans
    scale = head_dim ** (-0.5)
    here = lax.axis_index("ctx")
    local_pos = here * rows + jnp.arange(rows, dtype=jnp.int32)
    key_pos = jnp.arange(group, dtype=jnp.int32)
    first = seq_lengths[0, 0]
    second = first + seq_lengths[0, 1]
    local_seg = (local_pos >= first).astype(jnp.int32) + (local_pos >= second).astype(jnp.int32)
    key_seg = (key_pos >= first).astype(jnp.int32) + (key_pos >= second).astype(jnp.int32)
    starts = (local_pos == 0) | (local_pos == first) | (local_pos == second)
    keep = (1 - starts.astype(jnp.int32)).astype(jnp.float32)[:, None]
    allowed = (local_seg[:, None] == key_seg[None, :]) & (key_pos[None, :] <= local_pos[:, None])
    x_full = layer_input.astype(jnp.float32)
    inv_one = lax.rsqrt(jnp.mean(x_full * x_full, axis=-1, keepdims=True) + EPS)
    normed_one = x_full * inv_one
    h_one = (normed_one * gains[0]).astype(jnp.bfloat16)
    full_query, full_key, full_value, full_gate, full_out, full_heads = fetch_attention(
        w_query, w_key, w_value, w_gate, w_out, w_heads
    )
    query = project(h_one, full_query)
    key_raw = project(h_one, full_key)
    value_raw = project(h_one, full_value)
    gate_raw = project(h_one, full_gate)
    head_raw = project(h_one, full_heads)
    forget_logit = head_raw[:, :heads] + head_bias[0]
    shift_logit = head_raw[:, heads:] + head_bias[1]
    log_forget = jax.nn.log_sigmoid(forget_logit)
    mix_small = jax.nn.sigmoid(shift_logit)
    mix = jnp.repeat(mix_small, head_dim, axis=1)
    prev_row = passed_along(h_one[rows - 1 :], "ctx", 1)
    key_prev = jnp.concatenate([project(prev_row, full_key), key_raw[:-1]], 0) * keep
    value_prev = jnp.concatenate([project(prev_row, full_value), value_raw[:-1]], 0) * keep
    key_mix = mix * key_prev + (1.0 - mix) * key_raw
    value_mix = mix * value_prev + (1.0 - mix) * value_raw
    query4 = query.reshape(rows, heads, head_dim)
    query_inv = lax.rsqrt(jnp.mean(query4 * query4, axis=-1, keepdims=True) + EPS)
    query_norm = query4 * query_inv
    key4 = key_mix.reshape(rows, heads, head_dim)
    key_inv = lax.rsqrt(jnp.mean(key4 * key4, axis=-1, keepdims=True) + EPS)
    key_norm = key4 * key_inv
    q_low = query_norm.astype(jnp.bfloat16)
    k_low = key_norm.reshape(rows, width).astype(jnp.bfloat16)
    v_low = value_mix.astype(jnp.bfloat16)
    local_cum = jnp.cumsum(log_forget, axis=0)
    offset = entering(
        local_cum[rows - 1], "ctx", add_arrays, jnp.zeros((heads,), jnp.float32), False
    )
    decay = local_cum + offset
    gathered_k, gathered_v, all_decay = (
        lax.all_gather(k_low.astype(jnp.float32), "ctx", axis=0, tiled=True),
        lax.all_gather(v_low.astype(jnp.float32), "ctx", axis=0, tiled=True),
        lax.all_gather(decay, "ctx", axis=0, tiled=True),
    )
    all_keys = gathered_k.astype(jnp.bfloat16).reshape(group, heads, head_dim)
    all_values = gathered_v.astype(jnp.bfloat16).reshape(group, heads, head_dim)

    def scores_of(index, keys_whole, decay_whole):
        q_part = lax.dynamic_slice_in_dim(q_low, index * 4, 4, 1)
        k_part = lax.dynamic_slice_in_dim(keys_whole, index * 4, 4, 1)
        own = lax.dynamic_slice_in_dim(decay, index * 4, 4, 1)
        far = lax.dynamic_slice_in_dim(decay_whole, index * 4, 4, 1)
        raw = jnp.einsum("rhd,ghd->hrg", q_part, k_part, preferred_element_type=jnp.float32) * scale
        raw = raw + own.T[:, :, None] - far.T[:, None, :]
        return (jnp.where(allowed[None], raw, -1e30), q_part, k_part)

    group_count = heads // 4

    def forward_step(index, carry):
        mixed, log_total = carry
        scores, q_part, k_part = scores_of(index, all_keys, all_decay)
        v_part = lax.dynamic_slice_in_dim(all_values, index * 4, 4, 1)
        top = jnp.max(scores, axis=-1, keepdims=True)
        expd = jnp.exp(scores - top)
        total = jnp.sum(expd, axis=-1, keepdims=True)
        probs = (expd / total).astype(jnp.bfloat16)
        part = jnp.einsum("hrg,ghd->rhd", probs, v_part, preferred_element_type=jnp.float32)
        mixed = lax.dynamic_update_slice_in_dim(mixed, part, index * 4, 1)
        log_total = lax.dynamic_update_slice_in_dim(
            log_total, (top + jnp.log(total))[:, :, 0].T, index * 4, 1
        )
        return (mixed, log_total)

    attn4, log_total = lax.fori_loop(
        0,
        group_count,
        forward_step,
        (jnp.zeros((rows, heads, head_dim), jnp.float32), jnp.zeros((rows, heads), jnp.float32)),
    )
    attn = attn4.reshape(rows, width)
    gate_sig = jax.nn.sigmoid(gate_raw)
    branch_in = (gate_sig * attn).astype(jnp.bfloat16)
    mid = x_full + project(branch_in, full_out)
    inv_two = lax.rsqrt(jnp.mean(mid * mid, axis=-1, keepdims=True) + EPS)
    normed_two = mid * inv_two
    h_two = (normed_two * gains[1]).astype(jnp.bfloat16)
    full_ff_gate, full_ff_up, full_ff_down = fetch_feed(w_ff_gate, w_ff_up, w_ff_down)
    ff_gate = project(h_two, full_ff_gate)
    ff_up = project(h_two, full_ff_up)
    ff_sig = jax.nn.sigmoid(ff_gate)
    hidden = (ff_gate * ff_sig * ff_up).astype(jnp.bfloat16)
    result = (mid + project(hidden, full_ff_down)).astype(jnp.bfloat16)
    full_ff_gate, full_ff_up, full_ff_down = fetch_feed(w_ff_gate, w_ff_up, w_ff_down)
    full_query, full_key, full_value, full_gate, full_out, full_heads = fetch_attention(
        w_query, w_key, w_value, w_gate, w_out, w_heads
    )
    grad_out = cotangent.astype(jnp.float32)
    grad_down = weight_grad(hidden, cotangent)
    grad_hidden = input_grad(cotangent, full_ff_down)
    grad_gate_ff = (grad_hidden * ff_up * ff_sig * (1.0 + ff_gate * (1.0 - ff_sig))).astype(
        jnp.bfloat16
    )
    grad_up_ff = (grad_hidden * (ff_gate * ff_sig)).astype(jnp.bfloat16)
    ffn_grads = (
        lax.psum_scatter(
            weight_grad(h_two, grad_gate_ff), ("dp", "ctx"), scatter_dimension=0, tiled=True
        ),
        lax.psum_scatter(
            weight_grad(h_two, grad_up_ff), ("dp", "ctx"), scatter_dimension=0, tiled=True
        ),
        lax.psum_scatter(grad_down, ("dp", "ctx"), scatter_dimension=0, tiled=True),
    )
    grad_h_two = input_grad(grad_gate_ff, full_ff_gate) + input_grad(grad_up_ff, full_ff_up)
    gain_two = jnp.sum(grad_h_two * normed_two, axis=0)
    grad_mid = norm_back(grad_h_two * gains[1], normed_two, inv_two) + grad_out
    grad_branch = grad_mid.astype(jnp.bfloat16)
    grad_wout = weight_grad(branch_in, grad_branch)
    grad_branch_in = input_grad(grad_branch, full_out)
    grad_attn = (grad_branch_in * gate_sig).astype(jnp.bfloat16).reshape(rows, heads, head_dim)
    grad_gate = (grad_branch_in * attn * gate_sig * (1.0 - gate_sig)).astype(jnp.bfloat16)
    gathered_k, gathered_v, all_decay = (
        lax.all_gather(k_low.astype(jnp.float32), "ctx", axis=0, tiled=True),
        lax.all_gather(v_low.astype(jnp.float32), "ctx", axis=0, tiled=True),
        lax.all_gather(decay, "ctx", axis=0, tiled=True),
    )
    all_keys = gathered_k.astype(jnp.bfloat16).reshape(group, heads, head_dim)
    all_values = gathered_v.astype(jnp.bfloat16).reshape(group, heads, head_dim)

    def backward_step(index, carry):
        grad_q, grad_k, grad_v, grad_own, grad_far = carry
        scores, q_part, k_part = scores_of(index, all_keys, all_decay)
        v_part = lax.dynamic_slice_in_dim(all_values, index * 4, 4, 1)
        lse = lax.dynamic_slice_in_dim(log_total, index * 4, 4, 1).T[:, :, None]
        probs = jnp.exp(scores - lse)
        probs_low = probs.astype(jnp.bfloat16)
        grad_part = lax.dynamic_slice_in_dim(grad_attn, index * 4, 4, 1)
        grad_probs = jnp.einsum(
            "rhd,ghd->hrg", grad_part, v_part, preferred_element_type=jnp.float32
        )
        value_term = jnp.einsum(
            "hrg,rhd->ghd", probs_low, grad_part, preferred_element_type=jnp.float32
        )
        grad_scores = (
            probs * (grad_probs - jnp.sum(probs * grad_probs, axis=-1, keepdims=True))
        ).astype(jnp.bfloat16)
        query_term = (
            jnp.einsum("hrg,ghd->rhd", grad_scores, k_part, preferred_element_type=jnp.float32)
            * scale
        )
        key_term = (
            jnp.einsum("hrg,rhd->ghd", grad_scores, q_part, preferred_element_type=jnp.float32)
            * scale
        )
        scores_full = grad_scores.astype(jnp.float32)
        own_term = jnp.sum(scores_full, axis=-1).T
        far_term = -jnp.sum(scores_full, axis=1).T
        grad_q = lax.dynamic_update_slice_in_dim(grad_q, query_term, index * 4, 1)
        grad_k = lax.dynamic_update_slice_in_dim(grad_k, key_term, index * 4, 1)
        grad_v = lax.dynamic_update_slice_in_dim(grad_v, value_term, index * 4, 1)
        grad_own = lax.dynamic_update_slice_in_dim(grad_own, own_term, index * 4, 1)
        grad_far = lax.dynamic_update_slice_in_dim(grad_far, far_term, index * 4, 1)
        return (grad_q, grad_k, grad_v, grad_own, grad_far)

    grad_q, grad_k, grad_v, grad_own, grad_far = lax.fori_loop(
        0,
        group_count,
        backward_step,
        (
            jnp.zeros((rows, heads, head_dim), jnp.float32),
            jnp.zeros((group, heads, head_dim), jnp.float32),
            jnp.zeros((group, heads, head_dim), jnp.float32),
            jnp.zeros((rows, heads), jnp.float32),
            jnp.zeros((group, heads), jnp.float32),
        ),
    )
    grad_k_local, grad_v_local, grad_far_local = (
        lax.psum_scatter(grad_k, "ctx", scatter_dimension=0, tiled=True),
        lax.psum_scatter(grad_v, "ctx", scatter_dimension=0, tiled=True),
        lax.psum_scatter(grad_far, "ctx", scatter_dimension=0, tiled=True),
    )
    grad_decay = grad_own + grad_far_local
    local_rev = jnp.flip(jnp.cumsum(jnp.flip(grad_decay, 0), axis=0), 0)
    later = entering(
        jnp.sum(grad_decay, axis=0), "ctx", add_arrays, jnp.zeros((heads,), jnp.float32), True
    )
    grad_forget_logit = (local_rev + later) * jax.nn.sigmoid(-forget_logit)
    grad_query = norm_back(grad_q, query_norm, query_inv).reshape(rows, width)
    grad_key_mix = norm_back(grad_k_local, key_norm, key_inv).reshape(rows, width)
    grad_value_mix = grad_v_local.reshape(rows, width)
    grad_mix = jnp.sum(
        (grad_key_mix * (key_prev - key_raw) + grad_value_mix * (value_prev - value_raw)).reshape(
            rows, heads, head_dim
        ),
        axis=-1,
    )
    grad_shift_logit = grad_mix * mix_small * (1.0 - mix_small)
    carried_key = grad_key_mix * mix * keep
    carried_value = grad_value_mix * mix * keep
    from_next = passed_along(jnp.concatenate([carried_key[:1], carried_value[:1]], 0), "ctx", -1)
    grad_key_raw = (
        grad_key_mix * (1.0 - mix) + jnp.concatenate([carried_key[1:], from_next[:1]], 0)
    ).astype(jnp.bfloat16)
    grad_value_raw = (
        grad_value_mix * (1.0 - mix) + jnp.concatenate([carried_value[1:], from_next[1:]], 0)
    ).astype(jnp.bfloat16)
    grad_query_low = grad_query.astype(jnp.bfloat16)
    grad_head = jnp.concatenate([grad_forget_logit, grad_shift_logit], axis=1).astype(jnp.bfloat16)
    attn_grads = (
        lax.psum_scatter(
            weight_grad(h_one, grad_query_low), ("dp", "ctx"), scatter_dimension=0, tiled=True
        ),
        lax.psum_scatter(
            weight_grad(h_one, grad_key_raw), ("dp", "ctx"), scatter_dimension=0, tiled=True
        ),
        lax.psum_scatter(
            weight_grad(h_one, grad_value_raw), ("dp", "ctx"), scatter_dimension=0, tiled=True
        ),
        lax.psum_scatter(
            weight_grad(h_one, grad_gate), ("dp", "ctx"), scatter_dimension=0, tiled=True
        ),
        lax.psum_scatter(grad_wout, ("dp", "ctx"), scatter_dimension=0, tiled=True),
        lax.psum_scatter(
            weight_grad(h_one, grad_head), ("dp", "ctx"), scatter_dimension=0, tiled=True
        ),
    )
    grad_h_one = (
        input_grad(grad_query_low, full_query)
        + input_grad(grad_key_raw, full_key)
        + input_grad(grad_value_raw, full_value)
        + input_grad(grad_gate, full_gate)
        + input_grad(grad_head, full_heads)
    )
    gain_one = jnp.sum(grad_h_one * normed_one, axis=0)
    grad_input = norm_back(grad_h_one * gains[0], normed_one, inv_one) + grad_mid
    small = lax.psum(
        (
            jnp.stack([gain_one, gain_two]),
            jnp.stack([jnp.sum(grad_forget_logit, axis=0), jnp.sum(grad_shift_logit, axis=0)]),
        ),
        ("dp", "ctx"),
    )
    return (
        result,
        grad_input,
        small[0],
        small[1],
        attn_grads[0],
        attn_grads[1],
        attn_grads[2],
        attn_grads[3],
        attn_grads[4],
        attn_grads[5],
        ffn_grads[0],
        ffn_grads[1],
        ffn_grads[2],
    )


AXES = ("x", "core", "zh", "zl", "y")
SQUARE = ("core", "zl", "y")
SPREAD = ("x", "zh")
SWAP = [(0, 0), (1, 2), (2, 1), (3, 3)]
HAND_OUT = [
    (
        (((x * 2 + core) * 2 + zh) * 2 + zl) * 2 + y,
        (((zl * 2 + x) * 2 + y) * 2 + core) * 2 + zh,
    )
    for x in range(2)
    for core in range(2)
    for zh in range(2)
    for zl in range(2)
    for y in range(2)
]
HAND_BACK = [(b, a) for a, b in HAND_OUT]


def by_spread(array, axis):
    shape = array.shape
    split = array.reshape(*shape[:axis], 2, 2, 2, -1, *shape[axis + 1 :])
    return jnp.swapaxes(split, axis + 1, axis + 2).reshape(shape)


def spread_gather(part):
    return lax.all_gather(part, SPREAD, axis=0, tiled=True)


def spread_sum(whole):
    return lax.psum_scatter(whole, SPREAD, scatter_dimension=0, tiled=True)


def square_gather(part):
    return lax.all_gather(part, SQUARE, axis=0, tiled=True)


def square_sum(whole):
    return lax.psum_scatter(whole, SQUARE, scatter_dimension=0, tiled=True)


def square_exchange(parts):
    return lax.all_to_all(parts, SQUARE, 0, 0)


def dot(left, right, dims):
    return lax.dot_general(left, right, (dims, ((), ())), preferred_element_type=jnp.float32)


def ab(left, right):
    return dot(left, right, ((1,), (0,)))


def abt(left, right):
    return dot(left, right, ((1,), (1,)))


def atb(left, right):
    return dot(left, right, ((0,), (0,)))


def squares(
    layer_input,
    cotangent,
    seq_lengths,
    gains,
    head_bias,
    w_query,
    w_key,
    w_value,
    w_gate,
    w_out,
    w_heads,
    w_ff_gate,
    w_ff_up,
    w_ff_down,
):
    rows, width = layer_input.shape
    heads = head_bias.shape[1]
    head_dim = width // heads
    ranks = 8
    group = rows * ranks
    mine = heads // ranks
    cols = mine * head_dim
    shard = w_query.shape[0]
    units = w_ff_gate.shape[1] // ranks
    low = jnp.bfloat16
    scale = head_dim ** (-0.5)
    rank = (lax.axis_index("core") * 2 + lax.axis_index("zl")) * 2 + lax.axis_index("y")

    packed = jnp.concatenate([layer_input, cotangent], axis=1)
    packed = lax.ppermute(packed, ("core", "zh"), SWAP)
    x_full = packed[:, :width].astype(jnp.float32)
    cot = packed[:, width:]
    lengths = lax.ppermute(seq_lengths, ("core", "zh"), SWAP)

    head_cols = w_heads.reshape(shard, 2, ranks, mine)
    head_cols = jnp.moveaxis(head_cols, 2, 0).reshape(ranks, shard, 2 * mine)
    head_cols = jnp.pad(head_cols, ((0, 0), (0, 0), (0, 128 - 2 * mine)))
    pack = jnp.concatenate(
        [jnp.moveaxis(w.reshape(shard, ranks, cols), 1, 0) for w in (w_query, w_key, w_value, w_gate)]
        + [head_cols],
        axis=2,
    )
    w_attn = spread_gather(square_exchange(pack).reshape(ranks * shard, -1))
    w_o = spread_gather(lax.ppermute(w_out, AXES, HAND_OUT))

    def feed_cols(w):
        split = w.reshape(shard, 2, 2, 2, 4, -1)
        return split.transpose(2, 4, 0, 1, 3, 5).reshape(ranks, shard, units)

    pack = jnp.concatenate([feed_cols(w_ff_gate), feed_cols(w_ff_up)], axis=2)
    w_gu = spread_gather(square_exchange(pack).reshape(ranks * shard, -1))
    w_d = spread_gather(w_ff_down)

    pos = jnp.arange(group, dtype=jnp.int32)
    first = lengths[0, 0]
    second = first + lengths[0, 1]
    seg = (pos >= first).astype(jnp.int32) + (pos >= second).astype(jnp.int32)
    starts = (pos == 0) | (pos == first) | (pos == second)
    keep = 1.0 - starts.astype(jnp.float32)[:, None]
    allowed = (seg[:, None] == seg[None, :]) & (pos[None, :] <= pos[:, None])
    inv_one = lax.rsqrt(jnp.mean(x_full * x_full, axis=-1, keepdims=True) + EPS)
    normed_one = x_full * inv_one
    h_one = (normed_one * gains[0]).astype(low)
    h_one_all = square_gather(by_spread(h_one, 1))
    proj = ab(h_one_all, w_attn)
    query, key_raw, value_raw, gate_raw = (proj[:, i * cols : (i + 1) * cols] for i in range(4))
    small = proj[:, 4 * cols : 4 * cols + 2 * mine]
    bias = lax.dynamic_slice_in_dim(head_bias, rank * mine, mine, 1)
    forget_logit = small[:, :mine] + bias[0]
    shift_logit = small[:, mine:] + bias[1]
    log_forget = jax.nn.log_sigmoid(forget_logit)
    mix_small = jax.nn.sigmoid(shift_logit)
    mix = jnp.repeat(mix_small, head_dim, axis=1)
    zero_row = jnp.zeros((1, cols), jnp.float32)
    key_prev = jnp.concatenate([zero_row, key_raw[:-1]], 0) * keep
    value_prev = jnp.concatenate([zero_row, value_raw[:-1]], 0) * keep
    key_mix = mix * key_prev + (1.0 - mix) * key_raw
    value_mix = mix * value_prev + (1.0 - mix) * value_raw
    query3 = query.reshape(group, mine, head_dim)
    query_inv = lax.rsqrt(jnp.mean(query3 * query3, axis=-1, keepdims=True) + EPS)
    query_norm = query3 * query_inv
    key3 = key_mix.reshape(group, mine, head_dim)
    key_inv = lax.rsqrt(jnp.mean(key3 * key3, axis=-1, keepdims=True) + EPS)
    key_norm = key3 * key_inv
    q_low, k_low = query_norm.astype(low), key_norm.astype(low)
    v_low = value_mix.astype(low).reshape(group, mine, head_dim)
    decay = jnp.cumsum(log_forget, axis=0)
    scores = jnp.einsum("ihd,jhd->hij", q_low, k_low, preferred_element_type=jnp.float32) * scale
    scores = scores + decay.T[:, :, None] - decay.T[:, None, :]
    scores = jnp.where(allowed[None], scores, -1e30)
    probs = jax.nn.softmax(scores, axis=-1)
    probs_low = probs.astype(low)
    attn = jnp.einsum("hij,jhd->ihd", probs_low, v_low, preferred_element_type=jnp.float32)
    attn = attn.reshape(group, cols)
    gate_sig = jax.nn.sigmoid(gate_raw)
    branch_in = (gate_sig * attn).astype(low)
    mid = x_full + square_sum(ab(branch_in, w_o).astype(low)).astype(jnp.float32)
    inv_two = lax.rsqrt(jnp.mean(mid * mid, axis=-1, keepdims=True) + EPS)
    normed_two = mid * inv_two
    h_two = (normed_two * gains[1]).astype(low)
    h_two_all = square_gather(by_spread(h_two, 1))
    cot_all = square_gather(cot)
    gate_up = ab(h_two_all, w_gu)
    ff_gate, ff_up = gate_up[:, :units], gate_up[:, units:]
    ff_sig = jax.nn.sigmoid(ff_gate)
    hidden = (ff_gate * ff_sig * ff_up).astype(low)
    result = (mid + square_sum(ab(hidden, w_d).astype(low)).astype(jnp.float32)).astype(low)
    result = lax.ppermute(result, ("core", "zh"), SWAP)

    grad_hidden = abt(cot_all, w_d)
    grad_down = spread_sum(atb(hidden, cot_all).astype(low)).astype(jnp.float32)
    grad_gate_up = jnp.concatenate(
        [
            (grad_hidden * ff_up * ff_sig * (1.0 + ff_gate * (1.0 - ff_sig))).astype(low),
            (grad_hidden * (ff_gate * ff_sig)).astype(low),
        ],
        axis=1,
    )
    grad_gu = square_exchange(
        spread_sum(atb(h_two_all, grad_gate_up).astype(low)).reshape(ranks, shard, -1)
    )
    grad_h_two = by_spread(square_sum(abt(grad_gate_up, w_gu).astype(low)).astype(jnp.float32), 1)
    gain_two = jnp.sum(grad_h_two * normed_two, axis=0)
    grad_mid = norm_back(grad_h_two * gains[1], normed_two, inv_two) + cot.astype(jnp.float32)
    grad_branch = square_gather(grad_mid.astype(low))
    grad_wout = lax.ppermute(
        spread_sum(atb(branch_in, grad_branch).astype(low)), AXES, HAND_BACK
    ).astype(jnp.float32)
    grad_branch_in = abt(grad_branch, w_o)
    grad_attn = (grad_branch_in * gate_sig).astype(low).reshape(group, mine, head_dim)
    grad_gate = (grad_branch_in * attn * gate_sig * (1.0 - gate_sig)).astype(low)

    grad_probs = jnp.einsum("ihd,jhd->hij", grad_attn, v_low, preferred_element_type=jnp.float32)
    grad_v = jnp.einsum("hij,ihd->jhd", probs_low, grad_attn, preferred_element_type=jnp.float32)
    grad_scores = (
        probs * (grad_probs - jnp.sum(probs * grad_probs, axis=-1, keepdims=True))
    ).astype(low)
    grad_q = jnp.einsum("hij,jhd->ihd", grad_scores, k_low, preferred_element_type=jnp.float32)
    grad_k = jnp.einsum("hij,ihd->jhd", grad_scores, q_low, preferred_element_type=jnp.float32)
    full = grad_scores.astype(jnp.float32)
    grad_decay = jnp.sum(full, axis=2).T - jnp.sum(full, axis=1).T
    total = jnp.sum(grad_decay, axis=0, keepdims=True)
    later = total - jnp.cumsum(grad_decay, axis=0) + grad_decay
    grad_forget_logit = later * jax.nn.sigmoid(-forget_logit)
    grad_query = norm_back(grad_q * scale, query_norm, query_inv).reshape(group, cols)
    grad_key_mix = norm_back(grad_k * scale, key_norm, key_inv).reshape(group, cols)
    grad_value_mix = grad_v.reshape(group, cols)
    grad_mix = jnp.sum(
        (grad_key_mix * (key_prev - key_raw) + grad_value_mix * (value_prev - value_raw)).reshape(
            group, mine, head_dim
        ),
        axis=-1,
    )
    grad_shift_logit = grad_mix * mix_small * (1.0 - mix_small)
    carried_key = grad_key_mix * mix * keep
    carried_value = grad_value_mix * mix * keep
    grad_key_raw = grad_key_mix * (1.0 - mix) + jnp.concatenate([carried_key[1:], zero_row], 0)
    grad_value_raw = grad_value_mix * (1.0 - mix) + jnp.concatenate(
        [carried_value[1:], zero_row], 0
    )
    grad_small = jnp.concatenate([grad_forget_logit, grad_shift_logit], axis=1)
    grad_proj = jnp.concatenate(
        [
            grad_query.astype(low),
            grad_key_raw.astype(low),
            grad_value_raw.astype(low),
            grad_gate,
            jnp.pad(grad_small, ((0, 0), (0, 128 - 2 * mine))).astype(low),
        ],
        axis=1,
    )
    grad_attn_w = square_exchange(
        spread_sum(atb(h_one_all, grad_proj).astype(low)).reshape(ranks, shard, -1)
    )
    grad_h_one = by_spread(square_sum(abt(grad_proj, w_attn).astype(low)).astype(jnp.float32), 1)
    gain_one = jnp.sum(grad_h_one * normed_one, axis=0)
    grad_input = norm_back(grad_h_one * gains[0], normed_one, inv_one) + grad_mid
    grad_input = lax.ppermute(grad_input.astype(low), ("core", "zh"), SWAP).astype(jnp.float32)
    bias_sums = jnp.sum(grad_small, axis=0).reshape(2, mine)
    bias_sums = lax.dynamic_update_slice_in_dim(
        jnp.zeros((2, heads), jnp.float32), bias_sums, rank * mine, 1
    )
    small = lax.psum((jnp.stack([gain_one, gain_two]), bias_sums), AXES)

    def attn_cols(i):
        part = grad_attn_w[:, :, i * cols : (i + 1) * cols]
        return jnp.moveaxis(part, 0, 1).reshape(shard, width).astype(jnp.float32)

    head_part = grad_attn_w[:, :, 4 * cols : 4 * cols + 2 * mine].reshape(ranks, shard, 2, mine)
    head_part = head_part.transpose(1, 2, 0, 3).reshape(shard, 2 * heads).astype(jnp.float32)

    def feed_back(part):
        split = part.reshape(2, 4, shard, 2, 2, -1)
        return split.transpose(2, 3, 0, 4, 1, 5).reshape(shard, -1).astype(jnp.float32)

    return (
        result,
        grad_input,
        small[0],
        small[1],
        attn_cols(0),
        attn_cols(1),
        attn_cols(2),
        attn_cols(3),
        grad_wout,
        head_part,
        feed_back(grad_gu[:, :, :units]),
        feed_back(grad_gu[:, :, units:]),
        grad_down,
    )


def solution(mesh):
    if mesh.shape["dp"] == 4 and mesh.shape["ctx"] == 8:
        body, axes, group = squares, AXES, ("x", "core")
        mesh = Mesh(np.reshape(mesh.devices, (2, 2, 2, 2, 2)), AXES)
    else:
        body, axes, group = shards, ("dp", "ctx"), "dp"
    cut = P(axes, None)
    return jax.shard_map(
        body,
        mesh=mesh,
        in_specs=(cut, cut, P(group, None), P(), P()) + (cut,) * 9,
        out_specs=(cut, cut, P(), P()) + (cut,) * 9,
        check_vma=False,
    )
```

```python
import jax
import jax.numpy as jnp
import numpy as np
from jax import lax
from jax.experimental import pallas as pl
from jax.experimental.pallas import tpu as pltpu
from jax.sharding import Mesh
from jax.sharding import PartitionSpec as P

EPS = 1e-06


def passed_along(array, axis, by):
    size = lax.axis_size(axis)
    pairs = [(i, i + by) for i in range(size) if 0 <= i + by < size]
    return lax.ppermute(array, axis, pairs)


def entering(part, axis, combine, identity, reverse):
    count = lax.axis_size(axis)
    place = lax.axis_index(axis)
    ahead = count - 1 - place if reverse else place
    gathered = lax.all_gather(part, axis)
    state = jnp.zeros_like(part) + jnp.asarray(identity, part.dtype)

    def one(step, state):
        source = count - 1 - step if reverse else step
        return combine(state, lax.dynamic_index_in_dim(gathered, source, 0, False))

    return lax.fori_loop(0, ahead, one, state)


def fetch_attention(w_query, w_key, w_value, w_gate, w_out, w_heads):
    return (
        lax.all_gather(w_query, ("dp", "ctx"), axis=0, tiled=True),
        lax.all_gather(w_key, ("dp", "ctx"), axis=0, tiled=True),
        lax.all_gather(w_value, ("dp", "ctx"), axis=0, tiled=True),
        lax.all_gather(w_gate, ("dp", "ctx"), axis=0, tiled=True),
        lax.all_gather(w_out, ("dp", "ctx"), axis=0, tiled=True),
        lax.all_gather(w_heads, ("dp", "ctx"), axis=0, tiled=True),
    )


def fetch_feed(w_ff_gate, w_ff_up, w_ff_down):
    return (
        lax.all_gather(w_ff_gate, ("dp", "ctx"), axis=0, tiled=True),
        lax.all_gather(w_ff_up, ("dp", "ctx"), axis=0, tiled=True),
        lax.all_gather(w_ff_down, ("dp", "ctx"), axis=0, tiled=True),
    )


def add_arrays(earlier, later):
    return earlier + later


def norm_back(grad, normed, inverse):
    return inverse * (grad - normed * jnp.mean(grad * normed, axis=-1, keepdims=True))


def project(left, right):
    return jnp.dot(left, right, preferred_element_type=jnp.float32)


def weight_grad(left, right):
    return jnp.einsum("ra,rb->ab", left, right, preferred_element_type=jnp.float32)


def input_grad(grad, weight):
    return jnp.einsum("rb,ab->ra", grad, weight, preferred_element_type=jnp.float32)


def shards(
    layer_input,
    cotangent,
    seq_lengths,
    gains,
    head_bias,
    w_query,
    w_key,
    w_value,
    w_gate,
    w_out,
    w_heads,
    w_ff_gate,
    w_ff_up,
    w_ff_down,
):
    rows, width = layer_input.shape
    heads = head_bias.shape[1]
    head_dim = width // heads
    spans = lax.axis_size("ctx")
    group = rows * spans
    scale = head_dim ** (-0.5)
    here = lax.axis_index("ctx")
    local_pos = here * rows + jnp.arange(rows, dtype=jnp.int32)
    key_pos = jnp.arange(group, dtype=jnp.int32)
    first = seq_lengths[0, 0]
    second = first + seq_lengths[0, 1]
    local_seg = (local_pos >= first).astype(jnp.int32) + (local_pos >= second).astype(jnp.int32)
    key_seg = (key_pos >= first).astype(jnp.int32) + (key_pos >= second).astype(jnp.int32)
    starts = (local_pos == 0) | (local_pos == first) | (local_pos == second)
    keep = (1 - starts.astype(jnp.int32)).astype(jnp.float32)[:, None]
    allowed = (local_seg[:, None] == key_seg[None, :]) & (key_pos[None, :] <= local_pos[:, None])
    x_full = layer_input.astype(jnp.float32)
    inv_one = lax.rsqrt(jnp.mean(x_full * x_full, axis=-1, keepdims=True) + EPS)
    normed_one = x_full * inv_one
    h_one = (normed_one * gains[0]).astype(jnp.bfloat16)
    full_query, full_key, full_value, full_gate, full_out, full_heads = fetch_attention(
        w_query, w_key, w_value, w_gate, w_out, w_heads
    )
    query = project(h_one, full_query)
    key_raw = project(h_one, full_key)
    value_raw = project(h_one, full_value)
    gate_raw = project(h_one, full_gate)
    head_raw = project(h_one, full_heads)
    forget_logit = head_raw[:, :heads] + head_bias[0]
    shift_logit = head_raw[:, heads:] + head_bias[1]
    log_forget = jax.nn.log_sigmoid(forget_logit)
    mix_small = jax.nn.sigmoid(shift_logit)
    mix = jnp.repeat(mix_small, head_dim, axis=1)
    prev_row = passed_along(h_one[rows - 1 :], "ctx", 1)
    key_prev = jnp.concatenate([project(prev_row, full_key), key_raw[:-1]], 0) * keep
    value_prev = jnp.concatenate([project(prev_row, full_value), value_raw[:-1]], 0) * keep
    key_mix = mix * key_prev + (1.0 - mix) * key_raw
    value_mix = mix * value_prev + (1.0 - mix) * value_raw
    query4 = query.reshape(rows, heads, head_dim)
    query_inv = lax.rsqrt(jnp.mean(query4 * query4, axis=-1, keepdims=True) + EPS)
    query_norm = query4 * query_inv
    key4 = key_mix.reshape(rows, heads, head_dim)
    key_inv = lax.rsqrt(jnp.mean(key4 * key4, axis=-1, keepdims=True) + EPS)
    key_norm = key4 * key_inv
    q_low = query_norm.astype(jnp.bfloat16)
    k_low = key_norm.reshape(rows, width).astype(jnp.bfloat16)
    v_low = value_mix.astype(jnp.bfloat16)
    local_cum = jnp.cumsum(log_forget, axis=0)
    offset = entering(
        local_cum[rows - 1], "ctx", add_arrays, jnp.zeros((heads,), jnp.float32), False
    )
    decay = local_cum + offset
    gathered_k, gathered_v, all_decay = (
        lax.all_gather(k_low.astype(jnp.float32), "ctx", axis=0, tiled=True),
        lax.all_gather(v_low.astype(jnp.float32), "ctx", axis=0, tiled=True),
        lax.all_gather(decay, "ctx", axis=0, tiled=True),
    )
    all_keys = gathered_k.astype(jnp.bfloat16).reshape(group, heads, head_dim)
    all_values = gathered_v.astype(jnp.bfloat16).reshape(group, heads, head_dim)

    def scores_of(index, keys_whole, decay_whole):
        q_part = lax.dynamic_slice_in_dim(q_low, index * 4, 4, 1)
        k_part = lax.dynamic_slice_in_dim(keys_whole, index * 4, 4, 1)
        own = lax.dynamic_slice_in_dim(decay, index * 4, 4, 1)
        far = lax.dynamic_slice_in_dim(decay_whole, index * 4, 4, 1)
        raw = jnp.einsum("rhd,ghd->hrg", q_part, k_part, preferred_element_type=jnp.float32) * scale
        raw = raw + own.T[:, :, None] - far.T[:, None, :]
        return (jnp.where(allowed[None], raw, -1e30), q_part, k_part)

    group_count = heads // 4

    def forward_step(index, carry):
        mixed, log_total = carry
        scores, q_part, k_part = scores_of(index, all_keys, all_decay)
        v_part = lax.dynamic_slice_in_dim(all_values, index * 4, 4, 1)
        top = jnp.max(scores, axis=-1, keepdims=True)
        expd = jnp.exp(scores - top)
        total = jnp.sum(expd, axis=-1, keepdims=True)
        probs = (expd / total).astype(jnp.bfloat16)
        part = jnp.einsum("hrg,ghd->rhd", probs, v_part, preferred_element_type=jnp.float32)
        mixed = lax.dynamic_update_slice_in_dim(mixed, part, index * 4, 1)
        log_total = lax.dynamic_update_slice_in_dim(
            log_total, (top + jnp.log(total))[:, :, 0].T, index * 4, 1
        )
        return (mixed, log_total)

    attn4, log_total = lax.fori_loop(
        0,
        group_count,
        forward_step,
        (jnp.zeros((rows, heads, head_dim), jnp.float32), jnp.zeros((rows, heads), jnp.float32)),
    )
    attn = attn4.reshape(rows, width)
    gate_sig = jax.nn.sigmoid(gate_raw)
    branch_in = (gate_sig * attn).astype(jnp.bfloat16)
    mid = x_full + project(branch_in, full_out)
    inv_two = lax.rsqrt(jnp.mean(mid * mid, axis=-1, keepdims=True) + EPS)
    normed_two = mid * inv_two
    h_two = (normed_two * gains[1]).astype(jnp.bfloat16)
    full_ff_gate, full_ff_up, full_ff_down = fetch_feed(w_ff_gate, w_ff_up, w_ff_down)
    ff_gate = project(h_two, full_ff_gate)
    ff_up = project(h_two, full_ff_up)
    ff_sig = jax.nn.sigmoid(ff_gate)
    hidden = (ff_gate * ff_sig * ff_up).astype(jnp.bfloat16)
    result = (mid + project(hidden, full_ff_down)).astype(jnp.bfloat16)
    full_ff_gate, full_ff_up, full_ff_down = fetch_feed(w_ff_gate, w_ff_up, w_ff_down)
    full_query, full_key, full_value, full_gate, full_out, full_heads = fetch_attention(
        w_query, w_key, w_value, w_gate, w_out, w_heads
    )
    grad_out = cotangent.astype(jnp.float32)
    grad_down = weight_grad(hidden, cotangent)
    grad_hidden = input_grad(cotangent, full_ff_down)
    grad_gate_ff = (grad_hidden * ff_up * ff_sig * (1.0 + ff_gate * (1.0 - ff_sig))).astype(
        jnp.bfloat16
    )
    grad_up_ff = (grad_hidden * (ff_gate * ff_sig)).astype(jnp.bfloat16)
    ffn_grads = (
        lax.psum_scatter(
            weight_grad(h_two, grad_gate_ff), ("dp", "ctx"), scatter_dimension=0, tiled=True
        ),
        lax.psum_scatter(
            weight_grad(h_two, grad_up_ff), ("dp", "ctx"), scatter_dimension=0, tiled=True
        ),
        lax.psum_scatter(grad_down, ("dp", "ctx"), scatter_dimension=0, tiled=True),
    )
    grad_h_two = input_grad(grad_gate_ff, full_ff_gate) + input_grad(grad_up_ff, full_ff_up)
    gain_two = jnp.sum(grad_h_two * normed_two, axis=0)
    grad_mid = norm_back(grad_h_two * gains[1], normed_two, inv_two) + grad_out
    grad_branch = grad_mid.astype(jnp.bfloat16)
    grad_wout = weight_grad(branch_in, grad_branch)
    grad_branch_in = input_grad(grad_branch, full_out)
    grad_attn = (grad_branch_in * gate_sig).astype(jnp.bfloat16).reshape(rows, heads, head_dim)
    grad_gate = (grad_branch_in * attn * gate_sig * (1.0 - gate_sig)).astype(jnp.bfloat16)
    gathered_k, gathered_v, all_decay = (
        lax.all_gather(k_low.astype(jnp.float32), "ctx", axis=0, tiled=True),
        lax.all_gather(v_low.astype(jnp.float32), "ctx", axis=0, tiled=True),
        lax.all_gather(decay, "ctx", axis=0, tiled=True),
    )
    all_keys = gathered_k.astype(jnp.bfloat16).reshape(group, heads, head_dim)
    all_values = gathered_v.astype(jnp.bfloat16).reshape(group, heads, head_dim)

    def backward_step(index, carry):
        grad_q, grad_k, grad_v, grad_own, grad_far = carry
        scores, q_part, k_part = scores_of(index, all_keys, all_decay)
        v_part = lax.dynamic_slice_in_dim(all_values, index * 4, 4, 1)
        lse = lax.dynamic_slice_in_dim(log_total, index * 4, 4, 1).T[:, :, None]
        probs = jnp.exp(scores - lse)
        probs_low = probs.astype(jnp.bfloat16)
        grad_part = lax.dynamic_slice_in_dim(grad_attn, index * 4, 4, 1)
        grad_probs = jnp.einsum(
            "rhd,ghd->hrg", grad_part, v_part, preferred_element_type=jnp.float32
        )
        value_term = jnp.einsum(
            "hrg,rhd->ghd", probs_low, grad_part, preferred_element_type=jnp.float32
        )
        grad_scores = (
            probs * (grad_probs - jnp.sum(probs * grad_probs, axis=-1, keepdims=True))
        ).astype(jnp.bfloat16)
        query_term = (
            jnp.einsum("hrg,ghd->rhd", grad_scores, k_part, preferred_element_type=jnp.float32)
            * scale
        )
        key_term = (
            jnp.einsum("hrg,rhd->ghd", grad_scores, q_part, preferred_element_type=jnp.float32)
            * scale
        )
        scores_full = grad_scores.astype(jnp.float32)
        own_term = jnp.sum(scores_full, axis=-1).T
        far_term = -jnp.sum(scores_full, axis=1).T
        grad_q = lax.dynamic_update_slice_in_dim(grad_q, query_term, index * 4, 1)
        grad_k = lax.dynamic_update_slice_in_dim(grad_k, key_term, index * 4, 1)
        grad_v = lax.dynamic_update_slice_in_dim(grad_v, value_term, index * 4, 1)
        grad_own = lax.dynamic_update_slice_in_dim(grad_own, own_term, index * 4, 1)
        grad_far = lax.dynamic_update_slice_in_dim(grad_far, far_term, index * 4, 1)
        return (grad_q, grad_k, grad_v, grad_own, grad_far)

    grad_q, grad_k, grad_v, grad_own, grad_far = lax.fori_loop(
        0,
        group_count,
        backward_step,
        (
            jnp.zeros((rows, heads, head_dim), jnp.float32),
            jnp.zeros((group, heads, head_dim), jnp.float32),
            jnp.zeros((group, heads, head_dim), jnp.float32),
            jnp.zeros((rows, heads), jnp.float32),
            jnp.zeros((group, heads), jnp.float32),
        ),
    )
    grad_k_local, grad_v_local, grad_far_local = (
        lax.psum_scatter(grad_k, "ctx", scatter_dimension=0, tiled=True),
        lax.psum_scatter(grad_v, "ctx", scatter_dimension=0, tiled=True),
        lax.psum_scatter(grad_far, "ctx", scatter_dimension=0, tiled=True),
    )
    grad_decay = grad_own + grad_far_local
    local_rev = jnp.flip(jnp.cumsum(jnp.flip(grad_decay, 0), axis=0), 0)
    later = entering(
        jnp.sum(grad_decay, axis=0), "ctx", add_arrays, jnp.zeros((heads,), jnp.float32), True
    )
    grad_forget_logit = (local_rev + later) * jax.nn.sigmoid(-forget_logit)
    grad_query = norm_back(grad_q, query_norm, query_inv).reshape(rows, width)
    grad_key_mix = norm_back(grad_k_local, key_norm, key_inv).reshape(rows, width)
    grad_value_mix = grad_v_local.reshape(rows, width)
    grad_mix = jnp.sum(
        (grad_key_mix * (key_prev - key_raw) + grad_value_mix * (value_prev - value_raw)).reshape(
            rows, heads, head_dim
        ),
        axis=-1,
    )
    grad_shift_logit = grad_mix * mix_small * (1.0 - mix_small)
    carried_key = grad_key_mix * mix * keep
    carried_value = grad_value_mix * mix * keep
    from_next = passed_along(jnp.concatenate([carried_key[:1], carried_value[:1]], 0), "ctx", -1)
    grad_key_raw = (
        grad_key_mix * (1.0 - mix) + jnp.concatenate([carried_key[1:], from_next[:1]], 0)
    ).astype(jnp.bfloat16)
    grad_value_raw = (
        grad_value_mix * (1.0 - mix) + jnp.concatenate([carried_value[1:], from_next[1:]], 0)
    ).astype(jnp.bfloat16)
    grad_query_low = grad_query.astype(jnp.bfloat16)
    grad_head = jnp.concatenate([grad_forget_logit, grad_shift_logit], axis=1).astype(jnp.bfloat16)
    attn_grads = (
        lax.psum_scatter(
            weight_grad(h_one, grad_query_low), ("dp", "ctx"), scatter_dimension=0, tiled=True
        ),
        lax.psum_scatter(
            weight_grad(h_one, grad_key_raw), ("dp", "ctx"), scatter_dimension=0, tiled=True
        ),
        lax.psum_scatter(
            weight_grad(h_one, grad_value_raw), ("dp", "ctx"), scatter_dimension=0, tiled=True
        ),
        lax.psum_scatter(
            weight_grad(h_one, grad_gate), ("dp", "ctx"), scatter_dimension=0, tiled=True
        ),
        lax.psum_scatter(grad_wout, ("dp", "ctx"), scatter_dimension=0, tiled=True),
        lax.psum_scatter(
            weight_grad(h_one, grad_head), ("dp", "ctx"), scatter_dimension=0, tiled=True
        ),
    )
    grad_h_one = (
        input_grad(grad_query_low, full_query)
        + input_grad(grad_key_raw, full_key)
        + input_grad(grad_value_raw, full_value)
        + input_grad(grad_gate, full_gate)
        + input_grad(grad_head, full_heads)
    )
    gain_one = jnp.sum(grad_h_one * normed_one, axis=0)
    grad_input = norm_back(grad_h_one * gains[0], normed_one, inv_one) + grad_mid
    small = lax.psum(
        (
            jnp.stack([gain_one, gain_two]),
            jnp.stack([jnp.sum(grad_forget_logit, axis=0), jnp.sum(grad_shift_logit, axis=0)]),
        ),
        ("dp", "ctx"),
    )
    return (
        result,
        grad_input,
        small[0],
        small[1],
        attn_grads[0],
        attn_grads[1],
        attn_grads[2],
        attn_grads[3],
        attn_grads[4],
        attn_grads[5],
        ffn_grads[0],
        ffn_grads[1],
        ffn_grads[2],
    )


AXES = ("x", "core", "zh", "zl", "y")
SQUARE = ("core", "zl", "y")
SPREAD = ("x", "zh")
SWAP = [(0, 0), (1, 2), (2, 1), (3, 3)]

def by_spread(array, axis):
    shape = array.shape
    split = array.reshape(*shape[:axis], 2, 2, 2, -1, *shape[axis + 1 :])
    return jnp.swapaxes(split, axis + 1, axis + 2).reshape(shape)


def spread_gather(part):
    return lax.all_gather(part, SPREAD, axis=0, tiled=True)


def spread_sum(whole):
    return lax.psum_scatter(whole, SPREAD, scatter_dimension=0, tiled=True)


def square_gather(part):
    return lax.all_gather(part, SQUARE, axis=0, tiled=True)


def square_sum(whole):
    return lax.psum_scatter(whole, SQUARE, scatter_dimension=0, tiled=True)


def square_exchange(parts):
    return lax.all_to_all(parts, SQUARE, 0, 0)


def dot(left, right, dims):
    return lax.dot_general(left, right, (dims, ((), ())), preferred_element_type=jnp.float32)


def ab(left, right):
    return dot(left, right, ((1,), (0,)))


def abt(left, right):
    return dot(left, right, ((1,), (1,)))


def atb(left, right):
    return dot(left, right, ((0,), (0,)))


MESH = pl.DeviceIdType.MESH


class Net:
    def __init__(self, send, recv):
        self.send, self.recv, self.count, self.open = send, recv, 0, []
        self.at = {name: lax.axis_index(name) for name in AXES}

    def flip(self, names):
        return {name: 1 - self.at[name] for name in names}

    def greet(self):
        barrier = pltpu.get_barrier_semaphore()
        for names in PARTNERS:
            pl.semaphore_signal(barrier, 1, device_id=self.flip(names), device_id_type=MESH)
        moved = self.at["core"] != self.at["zh"]

        @pl.when(moved)
        def _():
            other = self.flip(("core", "zh"))
            pl.semaphore_signal(barrier, 1, device_id=other, device_id_type=MESH)
            pl.semaphore_wait(barrier, len(PARTNERS) + 1)

        @pl.when(jnp.logical_not(moved))
        def _():
            pl.semaphore_wait(barrier, len(PARTNERS))

    def copy(self, source, target, names):
        i = self.count
        self.count += 1
        return pltpu.make_async_remote_copy(
            source,
            target,
            self.send.at[i],
            self.recv.at[i],
            device_id=self.flip(names),
            device_id_type=MESH,
        )

    def push(self, source, target, names):
        made = self.copy(source, target, names)
        made.start()
        self.open.append(made)
        return made

    def drain(self):
        for made in self.open:
            made.wait_send()


PARTNERS = (
    ("y",),
    ("zl",),
    ("zl", "y"),
    ("core",),
    ("core", "y"),
    ("core", "zl"),
    ("core", "zl", "y"),
    ("x",),
    ("zh",),
)


def rank_of(at):
    return (at["core"] * 2 + at["zl"]) * 2 + at["y"]


def flipped(at, names):
    return {name: 1 - at[name] if name in names else at[name] for name in at}


class Gather:
    def __init__(self, net, ref, rows):
        self.net, self.ref, self.rows = net, ref, rows

    def part(self, names, half=None):
        start = rank_of(flipped(self.net.at, names)) * self.rows
        size = self.rows
        if half is not None:
            size = self.rows // 2
            start = start + half * size
        return self.ref.at[pl.ds(pl.multiple_of(start, size), size)]

    def send(self, block, half, to):
        part = self.part(block, half)
        return self.net.push(part, part, to)

    def first(self):
        self.y0 = self.send((), 0, ("y",))
        self.z1 = self.send((), 1, ("zl",))
        self.y1 = self.send((), 1, ("y",))
        self.z0 = self.send((), 0, ("zl",))
        self.cores = [self.send((), None, ("core",))]

    def second(self):
        self.y0.wait_recv()
        self.d0 = self.send(("y",), 0, ("zl",))
        self.z1.wait_recv()
        self.d1 = self.send(("zl",), 1, ("y",))
        self.y1.wait_recv()
        self.cores.append(self.send(("y",), None, ("core",)))
        self.z0.wait_recv()
        self.cores.append(self.send(("zl",), None, ("core",)))

    def third(self):
        self.d0.wait_recv()
        self.d1.wait_recv()
        self.cores.append(self.send(("zl", "y"), None, ("core",)))

    def done(self):
        for made in self.cores:
            made.wait_recv()


class Spread:
    def __init__(self, net, ref, pieces):
        self.net, self.ref, self.pieces = net, ref, pieces
        self.size = ref.shape[1] // pieces
        self.unit = net.at["x"] * 2 + net.at["zh"]
        self.from_zh = net.at["x"] * 2 + 1 - net.at["zh"]

    def send(self, unit, piece, to):
        part = self.ref.at[unit, pl.ds(piece * self.size, self.size)]
        return self.net.push(part, part, to)

    def first(self):
        self.along, self.across = [], []
        for piece in range(self.pieces):
            self.along.append(self.send(self.unit, piece, ("zh",)))
            self.across.append(self.send(self.unit, piece, ("x",)))

    def second(self):
        self.corner = []
        for piece in range(self.pieces):
            self.along[piece].wait_recv()
            self.corner.append(self.send(self.from_zh, piece, ("x",)))

    def wait_across(self):
        for made in self.across:
            made.wait_recv()

    def wait_corner(self):
        for made in self.corner:
            made.wait_recv()


def exchange(net, source, target):
    rank = rank_of(net.at)
    target[rank] = source[rank]
    made = []
    for names in PARTNERS[:7]:
        to = rank_of(flipped(net.at, names))
        made.append(net.push(source.at[to], target.at[rank], names))
    return made


def swap_chunks(value):
    size = value.shape[1] // 8
    order = (0, 2, 1, 3, 4, 6, 5, 7)
    return jnp.concatenate([value[:, i * size : (i + 1) * size] for i in order], axis=1)


def normed(value):
    inverse = lax.rsqrt(jnp.mean(value * value, axis=-1, keepdims=True) + EPS)
    return value * inverse, inverse


def kernel_a(
    x_ref, lens_ref, gains_ref, pack_ref, pack_gu_ref,
    xs_ref, lens_out, h_ref, w_ref, proj_ref, gu_ref,
    send, recv, sems,
):
    net = Net(send, recv)
    rows = x_ref.shape[0]
    rank = rank_of(net.at)
    net.greet()
    moved = net.at["core"] != net.at["zh"]
    swap = [net.copy(x_ref, xs_ref, ("core", "zh")), net.copy(lens_ref, lens_out, ("core", "zh"))]
    stay = [pltpu.make_async_copy(x_ref, xs_ref, sems.at[0]), pltpu.make_async_copy(lens_ref, lens_out, sems.at[1])]

    @pl.when(moved)
    def _():
        for made in swap:
            made.start()

    @pl.when(jnp.logical_not(moved))
    def _():
        for made in stay:
            made.start()

    spread = Spread(net, w_ref, 4)
    unit = spread.unit
    packs = exchange(net, pack_ref, w_ref.at[unit])

    @pl.when(moved)
    def _():
        for made in swap:
            made.wait()

    @pl.when(jnp.logical_not(moved))
    def _():
        for made in stay:
            made.wait()

    value, _inverse = normed(xs_ref[...].astype(jnp.float32))
    h_ref[pl.ds(pl.multiple_of(rank * rows, rows), rows)] = swap_chunks(
        (value * gains_ref[0:1, :]).astype(jnp.bfloat16)
    )
    gather = Gather(net, h_ref, rows)
    gather.first()
    for made in packs:
        made.wait_recv()
    spread.first()
    gather.second()
    gather.third()
    feed = exchange(net, pack_gu_ref, gu_ref)
    depth = pack_ref.shape[0] * pack_ref.shape[1]
    tall = 2 * rows

    def multiply(which, fresh):
        def one(i, _):
            at = pl.ds(pl.multiple_of(i * tall, tall), tall)
            left = h_ref[at, pl.ds(pl.multiple_of(which * depth, 128), depth)]
            part = ab(left, w_ref[which].reshape(depth, -1))
            if fresh:
                proj_ref[at, :] = part
            else:
                proj_ref[at, :] += part
            return 0

        lax.fori_loop(0, h_ref.shape[0] // tall, one, 0)

    gather.done()
    multiply(unit, True)
    spread.second()
    spread.wait_across()
    multiply((1 - net.at["x"]) * 2 + net.at["zh"], False)
    multiply(spread.from_zh, False)
    for made in feed:
        made.wait_recv()
    spread.wait_corner()
    multiply((1 - net.at["x"]) * 2 + 1 - net.at["zh"], False)
    net.drain()


def whole(shape, dtype):
    return jax.ShapeDtypeStruct(shape, dtype)


def vmem(count):
    return [pl.BlockSpec(memory_space=pltpu.VMEM)] * count


def call(kernel, number, outs, args, copies, scratch=(), local=2, cost=None):
    return pl.pallas_call(
        kernel,
        out_shape=outs,
        in_specs=vmem(len(args)),
        out_specs=vmem(len(outs)),
        scratch_shapes=[
            *scratch,
            pltpu.SemaphoreType.DMA((copies,)),
            pltpu.SemaphoreType.DMA((copies,)),
            pltpu.SemaphoreType.DMA((local,)),
        ],
        compiler_params=pltpu.CompilerParams(
            collective_id=number, has_side_effects=True, vmem_limit_bytes=60 * 2**20
        ),
    )(*args)


def squares(
    layer_input,
    cotangent,
    seq_lengths,
    gains,
    head_bias,
    w_query,
    w_key,
    w_value,
    w_gate,
    w_out,
    w_heads,
    w_ff_gate,
    w_ff_up,
    w_ff_down,
):
    rows, width = layer_input.shape
    heads = head_bias.shape[1]
    head_dim = width // heads
    ranks = 8
    group = rows * ranks
    mine = heads // ranks
    cols = mine * head_dim
    shard = w_query.shape[0]
    units = w_ff_gate.shape[1] // ranks
    low = jnp.bfloat16
    scale = head_dim ** (-0.5)
    slice_at = (lax.axis_index("zl") * 2 + lax.axis_index("core")) * 2 + lax.axis_index("y")

    cot = lax.ppermute(cotangent, ("core", "zh"), SWAP)

    def by_rank(w):
        split = w.reshape(shard, 2, 2, 2, -1)
        return split.transpose(2, 1, 3, 0, 4).reshape(ranks, shard, -1)

    head_cols = jnp.concatenate(
        [by_rank(w_heads[:, :heads]), by_rank(w_heads[:, heads:])], axis=2
    )
    head_cols = jnp.pad(head_cols, ((0, 0), (0, 0), (0, 128 - 2 * mine)))
    pack = jnp.concatenate(
        [by_rank(w) for w in (w_query, w_key, w_value, w_gate)] + [head_cols], axis=2
    )
    w_o = spread_gather(w_out).reshape(2, 2, shard, width)
    w_o = w_o.reshape(4, shard, width)
    w_o = lax.all_to_all(w_o, ("zl", "y"), 0, 0).reshape(cols, width)

    def feed_cols(w):
        split = w.reshape(shard, 2, 2, 2, 4, -1)
        return split.transpose(2, 4, 0, 1, 3, 5).reshape(ranks, shard, units)

    pack_gu = jnp.concatenate([feed_cols(w_ff_gate), feed_cols(w_ff_up)], axis=2)
    lens = jnp.pad(seq_lengths, ((0, 7), (0, 125)))
    packed, lengths, h_one_all, w_attn, proj, gu_own = call(
        kernel_a,
        1,
        (
            whole(layer_input.shape, low),
            whole(lens.shape, lens.dtype),
            whole((group, width), low),
            whole((4, *pack.shape), low),
            whole((group, pack.shape[2]), jnp.float32),
            whole(pack_gu.shape, low),
        ),
        (layer_input, lens, gains, pack, pack_gu),
        40,
    )
    w_attn = w_attn.reshape(width, -1)
    x_full = packed.astype(jnp.float32)
    w_gu = spread_gather(gu_own.reshape(ranks * shard, -1))
    w_d = spread_gather(w_ff_down)

    pos = jnp.arange(group, dtype=jnp.int32)
    first = lengths[0, 0]
    second = first + lengths[0, 1]
    seg = (pos >= first).astype(jnp.int32) + (pos >= second).astype(jnp.int32)
    starts = (pos == 0) | (pos == first) | (pos == second)
    keep = 1.0 - starts.astype(jnp.float32)[:, None]
    allowed = (seg[:, None] == seg[None, :]) & (pos[None, :] <= pos[:, None])
    inv_one = lax.rsqrt(jnp.mean(x_full * x_full, axis=-1, keepdims=True) + EPS)
    normed_one = x_full * inv_one
    query, key_raw, value_raw, gate_raw = (proj[:, i * cols : (i + 1) * cols] for i in range(4))
    small = proj[:, 4 * cols : 4 * cols + 2 * mine]
    bias = lax.dynamic_slice_in_dim(head_bias, slice_at * mine, mine, 1)
    forget_logit = small[:, :mine] + bias[0]
    shift_logit = small[:, mine:] + bias[1]
    log_forget = jax.nn.log_sigmoid(forget_logit)
    mix_small = jax.nn.sigmoid(shift_logit)
    mix = jnp.repeat(mix_small, head_dim, axis=1)
    zero_row = jnp.zeros((1, cols), jnp.float32)
    key_prev = jnp.concatenate([zero_row, key_raw[:-1]], 0) * keep
    value_prev = jnp.concatenate([zero_row, value_raw[:-1]], 0) * keep
    key_mix = mix * key_prev + (1.0 - mix) * key_raw
    value_mix = mix * value_prev + (1.0 - mix) * value_raw
    query3 = query.reshape(group, mine, head_dim)
    query_inv = lax.rsqrt(jnp.mean(query3 * query3, axis=-1, keepdims=True) + EPS)
    query_norm = query3 * query_inv
    key3 = key_mix.reshape(group, mine, head_dim)
    key_inv = lax.rsqrt(jnp.mean(key3 * key3, axis=-1, keepdims=True) + EPS)
    key_norm = key3 * key_inv
    q_low, k_low = query_norm.astype(low), key_norm.astype(low)
    v_low = value_mix.astype(low).reshape(group, mine, head_dim)
    decay = jnp.cumsum(log_forget, axis=0)
    scores = jnp.einsum("ihd,jhd->hij", q_low, k_low, preferred_element_type=jnp.float32) * scale
    scores = scores + decay.T[:, :, None] - decay.T[:, None, :]
    scores = jnp.where(allowed[None], scores, -1e30)
    probs = jax.nn.softmax(scores, axis=-1)
    probs_low = probs.astype(low)
    attn = jnp.einsum("hij,jhd->ihd", probs_low, v_low, preferred_element_type=jnp.float32)
    attn = attn.reshape(group, cols)
    gate_sig = jax.nn.sigmoid(gate_raw)
    branch_in = (gate_sig * attn).astype(low)
    mid = x_full + square_sum(ab(branch_in, w_o).astype(low)).astype(jnp.float32)
    inv_two = lax.rsqrt(jnp.mean(mid * mid, axis=-1, keepdims=True) + EPS)
    normed_two = mid * inv_two
    h_two = (normed_two * gains[1]).astype(low)
    h_two_all = square_gather(by_spread(h_two, 1))
    cot_all = square_gather(cot)
    gate_up = ab(h_two_all, w_gu)
    ff_gate, ff_up = gate_up[:, :units], gate_up[:, units:]
    ff_sig = jax.nn.sigmoid(ff_gate)
    hidden = (ff_gate * ff_sig * ff_up).astype(low)
    result = (mid + square_sum(ab(hidden, w_d).astype(low)).astype(jnp.float32)).astype(low)
    result = lax.ppermute(result, ("core", "zh"), SWAP)

    grad_hidden = abt(cot_all, w_d)
    grad_down = spread_sum(atb(hidden, cot_all).astype(low)).astype(jnp.float32)
    grad_gate_up = jnp.concatenate(
        [
            (grad_hidden * ff_up * ff_sig * (1.0 + ff_gate * (1.0 - ff_sig))).astype(low),
            (grad_hidden * (ff_gate * ff_sig)).astype(low),
        ],
        axis=1,
    )
    grad_gu = square_exchange(
        spread_sum(atb(h_two_all, grad_gate_up).astype(low)).reshape(ranks, shard, -1)
    )
    grad_h_two = by_spread(square_sum(abt(grad_gate_up, w_gu).astype(low)).astype(jnp.float32), 1)
    gain_two = jnp.sum(grad_h_two * normed_two, axis=0)
    grad_mid = norm_back(grad_h_two * gains[1], normed_two, inv_two) + cot.astype(jnp.float32)
    grad_branch = square_gather(grad_mid.astype(low))
    grad_wout = atb(branch_in, grad_branch).astype(low).reshape(4, shard, width)
    grad_wout = lax.all_to_all(grad_wout, ("zl", "y"), 0, 0).reshape(cols, width)
    grad_wout = spread_sum(grad_wout).astype(jnp.float32)
    grad_branch_in = abt(grad_branch, w_o)
    grad_attn = (grad_branch_in * gate_sig).astype(low).reshape(group, mine, head_dim)
    grad_gate = (grad_branch_in * attn * gate_sig * (1.0 - gate_sig)).astype(low)

    grad_probs = jnp.einsum("ihd,jhd->hij", grad_attn, v_low, preferred_element_type=jnp.float32)
    grad_v = jnp.einsum("hij,ihd->jhd", probs_low, grad_attn, preferred_element_type=jnp.float32)
    grad_scores = (
        probs * (grad_probs - jnp.sum(probs * grad_probs, axis=-1, keepdims=True))
    ).astype(low)
    grad_q = jnp.einsum("hij,jhd->ihd", grad_scores, k_low, preferred_element_type=jnp.float32)
    grad_k = jnp.einsum("hij,ihd->jhd", grad_scores, q_low, preferred_element_type=jnp.float32)
    full = grad_scores.astype(jnp.float32)
    grad_decay = jnp.sum(full, axis=2).T - jnp.sum(full, axis=1).T
    total = jnp.sum(grad_decay, axis=0, keepdims=True)
    later = total - jnp.cumsum(grad_decay, axis=0) + grad_decay
    grad_forget_logit = later * jax.nn.sigmoid(-forget_logit)
    grad_query = norm_back(grad_q * scale, query_norm, query_inv).reshape(group, cols)
    grad_key_mix = norm_back(grad_k * scale, key_norm, key_inv).reshape(group, cols)
    grad_value_mix = grad_v.reshape(group, cols)
    grad_mix = jnp.sum(
        (grad_key_mix * (key_prev - key_raw) + grad_value_mix * (value_prev - value_raw)).reshape(
            group, mine, head_dim
        ),
        axis=-1,
    )
    grad_shift_logit = grad_mix * mix_small * (1.0 - mix_small)
    carried_key = grad_key_mix * mix * keep
    carried_value = grad_value_mix * mix * keep
    grad_key_raw = grad_key_mix * (1.0 - mix) + jnp.concatenate([carried_key[1:], zero_row], 0)
    grad_value_raw = grad_value_mix * (1.0 - mix) + jnp.concatenate(
        [carried_value[1:], zero_row], 0
    )
    grad_small = jnp.concatenate([grad_forget_logit, grad_shift_logit], axis=1)
    grad_proj = jnp.concatenate(
        [
            grad_query.astype(low),
            grad_key_raw.astype(low),
            grad_value_raw.astype(low),
            grad_gate,
            jnp.pad(grad_small, ((0, 0), (0, 128 - 2 * mine))).astype(low),
        ],
        axis=1,
    )
    grad_attn_w = square_exchange(
        spread_sum(atb(h_one_all, grad_proj).astype(low)).reshape(ranks, shard, -1)
    )
    grad_h_one = by_spread(square_sum(abt(grad_proj, w_attn).astype(low)).astype(jnp.float32), 1)
    gain_one = jnp.sum(grad_h_one * normed_one, axis=0)
    grad_input = norm_back(grad_h_one * gains[0], normed_one, inv_one) + grad_mid
    grad_input = lax.ppermute(grad_input.astype(low), ("core", "zh"), SWAP).astype(jnp.float32)
    bias_sums = jnp.sum(grad_small, axis=0).reshape(2, mine)
    bias_sums = lax.dynamic_update_slice_in_dim(
        jnp.zeros((2, heads), jnp.float32), bias_sums, slice_at * mine, 1
    )
    small = lax.psum((jnp.stack([gain_one, gain_two]), bias_sums), AXES)

    def from_ranks(part):
        split = part.reshape(2, 2, 2, shard, -1).transpose(3, 1, 0, 2, 4)
        return split.reshape(shard, -1).astype(jnp.float32)

    def attn_cols(i):
        return from_ranks(grad_attn_w[:, :, i * cols : (i + 1) * cols])

    head_part = grad_attn_w[:, :, 4 * cols : 4 * cols + 2 * mine]
    head_part = jnp.concatenate(
        [from_ranks(head_part[:, :, :mine]), from_ranks(head_part[:, :, mine:])], axis=1
    )

    def feed_back(part):
        split = part.reshape(2, 4, shard, 2, 2, -1)
        return split.transpose(2, 3, 0, 4, 1, 5).reshape(shard, -1).astype(jnp.float32)

    return (
        result,
        grad_input,
        small[0],
        small[1],
        attn_cols(0),
        attn_cols(1),
        attn_cols(2),
        attn_cols(3),
        grad_wout,
        head_part,
        feed_back(grad_gu[:, :, :units]),
        feed_back(grad_gu[:, :, units:]),
        grad_down,
    )


def solution(mesh):
    if mesh.shape["dp"] == 4 and mesh.shape["ctx"] == 8:
        body, axes, group = squares, AXES, ("x", "core")
        mesh = Mesh(np.reshape(mesh.devices, (2, 2, 2, 2, 2)), AXES)
    else:
        body, axes, group = shards, ("dp", "ctx"), "dp"
    cut = P(axes, None)
    return jax.shard_map(
        body,
        mesh=mesh,
        in_specs=(cut, cut, P(group, None), P(), P()) + (cut,) * 9,
        out_specs=(cut, cut, P(), P()) + (cut,) * 9,
        check_vma=False,
    )
```

```python
import jax
import jax.numpy as jnp
import numpy as np
from jax import lax
from jax.experimental import pallas as pl
from jax.experimental.pallas import tpu as pltpu
from jax.sharding import Mesh
from jax.sharding import PartitionSpec as P

EPS = 1e-06


def passed_along(array, axis, by):
    size = lax.axis_size(axis)
    pairs = [(i, i + by) for i in range(size) if 0 <= i + by < size]
    return lax.ppermute(array, axis, pairs)


def entering(part, axis, combine, identity, reverse):
    count = lax.axis_size(axis)
    place = lax.axis_index(axis)
    ahead = count - 1 - place if reverse else place
    gathered = lax.all_gather(part, axis)
    state = jnp.zeros_like(part) + jnp.asarray(identity, part.dtype)

    def one(step, state):
        source = count - 1 - step if reverse else step
        return combine(state, lax.dynamic_index_in_dim(gathered, source, 0, False))

    return lax.fori_loop(0, ahead, one, state)


def fetch_attention(w_query, w_key, w_value, w_gate, w_out, w_heads):
    return (
        lax.all_gather(w_query, ("dp", "ctx"), axis=0, tiled=True),
        lax.all_gather(w_key, ("dp", "ctx"), axis=0, tiled=True),
        lax.all_gather(w_value, ("dp", "ctx"), axis=0, tiled=True),
        lax.all_gather(w_gate, ("dp", "ctx"), axis=0, tiled=True),
        lax.all_gather(w_out, ("dp", "ctx"), axis=0, tiled=True),
        lax.all_gather(w_heads, ("dp", "ctx"), axis=0, tiled=True),
    )


def fetch_feed(w_ff_gate, w_ff_up, w_ff_down):
    return (
        lax.all_gather(w_ff_gate, ("dp", "ctx"), axis=0, tiled=True),
        lax.all_gather(w_ff_up, ("dp", "ctx"), axis=0, tiled=True),
        lax.all_gather(w_ff_down, ("dp", "ctx"), axis=0, tiled=True),
    )


def add_arrays(earlier, later):
    return earlier + later


def norm_back(grad, normed, inverse):
    return inverse * (grad - normed * jnp.mean(grad * normed, axis=-1, keepdims=True))


def project(left, right):
    return jnp.dot(left, right, preferred_element_type=jnp.float32)


def weight_grad(left, right):
    return jnp.einsum("ra,rb->ab", left, right, preferred_element_type=jnp.float32)


def input_grad(grad, weight):
    return jnp.einsum("rb,ab->ra", grad, weight, preferred_element_type=jnp.float32)


def shards(
    layer_input,
    cotangent,
    seq_lengths,
    gains,
    head_bias,
    w_query,
    w_key,
    w_value,
    w_gate,
    w_out,
    w_heads,
    w_ff_gate,
    w_ff_up,
    w_ff_down,
):
    rows, width = layer_input.shape
    heads = head_bias.shape[1]
    head_dim = width // heads
    spans = lax.axis_size("ctx")
    group = rows * spans
    scale = head_dim ** (-0.5)
    here = lax.axis_index("ctx")
    local_pos = here * rows + jnp.arange(rows, dtype=jnp.int32)
    key_pos = jnp.arange(group, dtype=jnp.int32)
    first = seq_lengths[0, 0]
    second = first + seq_lengths[0, 1]
    local_seg = (local_pos >= first).astype(jnp.int32) + (local_pos >= second).astype(jnp.int32)
    key_seg = (key_pos >= first).astype(jnp.int32) + (key_pos >= second).astype(jnp.int32)
    starts = (local_pos == 0) | (local_pos == first) | (local_pos == second)
    keep = (1 - starts.astype(jnp.int32)).astype(jnp.float32)[:, None]
    allowed = (local_seg[:, None] == key_seg[None, :]) & (key_pos[None, :] <= local_pos[:, None])
    x_full = layer_input.astype(jnp.float32)
    inv_one = lax.rsqrt(jnp.mean(x_full * x_full, axis=-1, keepdims=True) + EPS)
    normed_one = x_full * inv_one
    h_one = (normed_one * gains[0]).astype(jnp.bfloat16)
    full_query, full_key, full_value, full_gate, full_out, full_heads = fetch_attention(
        w_query, w_key, w_value, w_gate, w_out, w_heads
    )
    query = project(h_one, full_query)
    key_raw = project(h_one, full_key)
    value_raw = project(h_one, full_value)
    gate_raw = project(h_one, full_gate)
    head_raw = project(h_one, full_heads)
    forget_logit = head_raw[:, :heads] + head_bias[0]
    shift_logit = head_raw[:, heads:] + head_bias[1]
    log_forget = jax.nn.log_sigmoid(forget_logit)
    mix_small = jax.nn.sigmoid(shift_logit)
    mix = jnp.repeat(mix_small, head_dim, axis=1)
    prev_row = passed_along(h_one[rows - 1 :], "ctx", 1)
    key_prev = jnp.concatenate([project(prev_row, full_key), key_raw[:-1]], 0) * keep
    value_prev = jnp.concatenate([project(prev_row, full_value), value_raw[:-1]], 0) * keep
    key_mix = mix * key_prev + (1.0 - mix) * key_raw
    value_mix = mix * value_prev + (1.0 - mix) * value_raw
    query4 = query.reshape(rows, heads, head_dim)
    query_inv = lax.rsqrt(jnp.mean(query4 * query4, axis=-1, keepdims=True) + EPS)
    query_norm = query4 * query_inv
    key4 = key_mix.reshape(rows, heads, head_dim)
    key_inv = lax.rsqrt(jnp.mean(key4 * key4, axis=-1, keepdims=True) + EPS)
    key_norm = key4 * key_inv
    q_low = query_norm.astype(jnp.bfloat16)
    k_low = key_norm.reshape(rows, width).astype(jnp.bfloat16)
    v_low = value_mix.astype(jnp.bfloat16)
    local_cum = jnp.cumsum(log_forget, axis=0)
    offset = entering(
        local_cum[rows - 1], "ctx", add_arrays, jnp.zeros((heads,), jnp.float32), False
    )
    decay = local_cum + offset
    gathered_k, gathered_v, all_decay = (
        lax.all_gather(k_low.astype(jnp.float32), "ctx", axis=0, tiled=True),
        lax.all_gather(v_low.astype(jnp.float32), "ctx", axis=0, tiled=True),
        lax.all_gather(decay, "ctx", axis=0, tiled=True),
    )
    all_keys = gathered_k.astype(jnp.bfloat16).reshape(group, heads, head_dim)
    all_values = gathered_v.astype(jnp.bfloat16).reshape(group, heads, head_dim)

    def scores_of(index, keys_whole, decay_whole):
        q_part = lax.dynamic_slice_in_dim(q_low, index * 4, 4, 1)
        k_part = lax.dynamic_slice_in_dim(keys_whole, index * 4, 4, 1)
        own = lax.dynamic_slice_in_dim(decay, index * 4, 4, 1)
        far = lax.dynamic_slice_in_dim(decay_whole, index * 4, 4, 1)
        raw = jnp.einsum("rhd,ghd->hrg", q_part, k_part, preferred_element_type=jnp.float32) * scale
        raw = raw + own.T[:, :, None] - far.T[:, None, :]
        return (jnp.where(allowed[None], raw, -1e30), q_part, k_part)

    group_count = heads // 4

    def forward_step(index, carry):
        mixed, log_total = carry
        scores, q_part, k_part = scores_of(index, all_keys, all_decay)
        v_part = lax.dynamic_slice_in_dim(all_values, index * 4, 4, 1)
        top = jnp.max(scores, axis=-1, keepdims=True)
        expd = jnp.exp(scores - top)
        total = jnp.sum(expd, axis=-1, keepdims=True)
        probs = (expd / total).astype(jnp.bfloat16)
        part = jnp.einsum("hrg,ghd->rhd", probs, v_part, preferred_element_type=jnp.float32)
        mixed = lax.dynamic_update_slice_in_dim(mixed, part, index * 4, 1)
        log_total = lax.dynamic_update_slice_in_dim(
            log_total, (top + jnp.log(total))[:, :, 0].T, index * 4, 1
        )
        return (mixed, log_total)

    attn4, log_total = lax.fori_loop(
        0,
        group_count,
        forward_step,
        (jnp.zeros((rows, heads, head_dim), jnp.float32), jnp.zeros((rows, heads), jnp.float32)),
    )
    attn = attn4.reshape(rows, width)
    gate_sig = jax.nn.sigmoid(gate_raw)
    branch_in = (gate_sig * attn).astype(jnp.bfloat16)
    mid = x_full + project(branch_in, full_out)
    inv_two = lax.rsqrt(jnp.mean(mid * mid, axis=-1, keepdims=True) + EPS)
    normed_two = mid * inv_two
    h_two = (normed_two * gains[1]).astype(jnp.bfloat16)
    full_ff_gate, full_ff_up, full_ff_down = fetch_feed(w_ff_gate, w_ff_up, w_ff_down)
    ff_gate = project(h_two, full_ff_gate)
    ff_up = project(h_two, full_ff_up)
    ff_sig = jax.nn.sigmoid(ff_gate)
    hidden = (ff_gate * ff_sig * ff_up).astype(jnp.bfloat16)
    result = (mid + project(hidden, full_ff_down)).astype(jnp.bfloat16)
    full_ff_gate, full_ff_up, full_ff_down = fetch_feed(w_ff_gate, w_ff_up, w_ff_down)
    full_query, full_key, full_value, full_gate, full_out, full_heads = fetch_attention(
        w_query, w_key, w_value, w_gate, w_out, w_heads
    )
    grad_out = cotangent.astype(jnp.float32)
    grad_down = weight_grad(hidden, cotangent)
    grad_hidden = input_grad(cotangent, full_ff_down)
    grad_gate_ff = (grad_hidden * ff_up * ff_sig * (1.0 + ff_gate * (1.0 - ff_sig))).astype(
        jnp.bfloat16
    )
    grad_up_ff = (grad_hidden * (ff_gate * ff_sig)).astype(jnp.bfloat16)
    ffn_grads = (
        lax.psum_scatter(
            weight_grad(h_two, grad_gate_ff), ("dp", "ctx"), scatter_dimension=0, tiled=True
        ),
        lax.psum_scatter(
            weight_grad(h_two, grad_up_ff), ("dp", "ctx"), scatter_dimension=0, tiled=True
        ),
        lax.psum_scatter(grad_down, ("dp", "ctx"), scatter_dimension=0, tiled=True),
    )
    grad_h_two = input_grad(grad_gate_ff, full_ff_gate) + input_grad(grad_up_ff, full_ff_up)
    gain_two = jnp.sum(grad_h_two * normed_two, axis=0)
    grad_mid = norm_back(grad_h_two * gains[1], normed_two, inv_two) + grad_out
    grad_branch = grad_mid.astype(jnp.bfloat16)
    grad_wout = weight_grad(branch_in, grad_branch)
    grad_branch_in = input_grad(grad_branch, full_out)
    grad_attn = (grad_branch_in * gate_sig).astype(jnp.bfloat16).reshape(rows, heads, head_dim)
    grad_gate = (grad_branch_in * attn * gate_sig * (1.0 - gate_sig)).astype(jnp.bfloat16)
    gathered_k, gathered_v, all_decay = (
        lax.all_gather(k_low.astype(jnp.float32), "ctx", axis=0, tiled=True),
        lax.all_gather(v_low.astype(jnp.float32), "ctx", axis=0, tiled=True),
        lax.all_gather(decay, "ctx", axis=0, tiled=True),
    )
    all_keys = gathered_k.astype(jnp.bfloat16).reshape(group, heads, head_dim)
    all_values = gathered_v.astype(jnp.bfloat16).reshape(group, heads, head_dim)

    def backward_step(index, carry):
        grad_q, grad_k, grad_v, grad_own, grad_far = carry
        scores, q_part, k_part = scores_of(index, all_keys, all_decay)
        v_part = lax.dynamic_slice_in_dim(all_values, index * 4, 4, 1)
        lse = lax.dynamic_slice_in_dim(log_total, index * 4, 4, 1).T[:, :, None]
        probs = jnp.exp(scores - lse)
        probs_low = probs.astype(jnp.bfloat16)
        grad_part = lax.dynamic_slice_in_dim(grad_attn, index * 4, 4, 1)
        grad_probs = jnp.einsum(
            "rhd,ghd->hrg", grad_part, v_part, preferred_element_type=jnp.float32
        )
        value_term = jnp.einsum(
            "hrg,rhd->ghd", probs_low, grad_part, preferred_element_type=jnp.float32
        )
        grad_scores = (
            probs * (grad_probs - jnp.sum(probs * grad_probs, axis=-1, keepdims=True))
        ).astype(jnp.bfloat16)
        query_term = (
            jnp.einsum("hrg,ghd->rhd", grad_scores, k_part, preferred_element_type=jnp.float32)
            * scale
        )
        key_term = (
            jnp.einsum("hrg,rhd->ghd", grad_scores, q_part, preferred_element_type=jnp.float32)
            * scale
        )
        scores_full = grad_scores.astype(jnp.float32)
        own_term = jnp.sum(scores_full, axis=-1).T
        far_term = -jnp.sum(scores_full, axis=1).T
        grad_q = lax.dynamic_update_slice_in_dim(grad_q, query_term, index * 4, 1)
        grad_k = lax.dynamic_update_slice_in_dim(grad_k, key_term, index * 4, 1)
        grad_v = lax.dynamic_update_slice_in_dim(grad_v, value_term, index * 4, 1)
        grad_own = lax.dynamic_update_slice_in_dim(grad_own, own_term, index * 4, 1)
        grad_far = lax.dynamic_update_slice_in_dim(grad_far, far_term, index * 4, 1)
        return (grad_q, grad_k, grad_v, grad_own, grad_far)

    grad_q, grad_k, grad_v, grad_own, grad_far = lax.fori_loop(
        0,
        group_count,
        backward_step,
        (
            jnp.zeros((rows, heads, head_dim), jnp.float32),
            jnp.zeros((group, heads, head_dim), jnp.float32),
            jnp.zeros((group, heads, head_dim), jnp.float32),
            jnp.zeros((rows, heads), jnp.float32),
            jnp.zeros((group, heads), jnp.float32),
        ),
    )
    grad_k_local, grad_v_local, grad_far_local = (
        lax.psum_scatter(grad_k, "ctx", scatter_dimension=0, tiled=True),
        lax.psum_scatter(grad_v, "ctx", scatter_dimension=0, tiled=True),
        lax.psum_scatter(grad_far, "ctx", scatter_dimension=0, tiled=True),
    )
    grad_decay = grad_own + grad_far_local
    local_rev = jnp.flip(jnp.cumsum(jnp.flip(grad_decay, 0), axis=0), 0)
    later = entering(
        jnp.sum(grad_decay, axis=0), "ctx", add_arrays, jnp.zeros((heads,), jnp.float32), True
    )
    grad_forget_logit = (local_rev + later) * jax.nn.sigmoid(-forget_logit)
    grad_query = norm_back(grad_q, query_norm, query_inv).reshape(rows, width)
    grad_key_mix = norm_back(grad_k_local, key_norm, key_inv).reshape(rows, width)
    grad_value_mix = grad_v_local.reshape(rows, width)
    grad_mix = jnp.sum(
        (grad_key_mix * (key_prev - key_raw) + grad_value_mix * (value_prev - value_raw)).reshape(
            rows, heads, head_dim
        ),
        axis=-1,
    )
    grad_shift_logit = grad_mix * mix_small * (1.0 - mix_small)
    carried_key = grad_key_mix * mix * keep
    carried_value = grad_value_mix * mix * keep
    from_next = passed_along(jnp.concatenate([carried_key[:1], carried_value[:1]], 0), "ctx", -1)
    grad_key_raw = (
        grad_key_mix * (1.0 - mix) + jnp.concatenate([carried_key[1:], from_next[:1]], 0)
    ).astype(jnp.bfloat16)
    grad_value_raw = (
        grad_value_mix * (1.0 - mix) + jnp.concatenate([carried_value[1:], from_next[1:]], 0)
    ).astype(jnp.bfloat16)
    grad_query_low = grad_query.astype(jnp.bfloat16)
    grad_head = jnp.concatenate([grad_forget_logit, grad_shift_logit], axis=1).astype(jnp.bfloat16)
    attn_grads = (
        lax.psum_scatter(
            weight_grad(h_one, grad_query_low), ("dp", "ctx"), scatter_dimension=0, tiled=True
        ),
        lax.psum_scatter(
            weight_grad(h_one, grad_key_raw), ("dp", "ctx"), scatter_dimension=0, tiled=True
        ),
        lax.psum_scatter(
            weight_grad(h_one, grad_value_raw), ("dp", "ctx"), scatter_dimension=0, tiled=True
        ),
        lax.psum_scatter(
            weight_grad(h_one, grad_gate), ("dp", "ctx"), scatter_dimension=0, tiled=True
        ),
        lax.psum_scatter(grad_wout, ("dp", "ctx"), scatter_dimension=0, tiled=True),
        lax.psum_scatter(
            weight_grad(h_one, grad_head), ("dp", "ctx"), scatter_dimension=0, tiled=True
        ),
    )
    grad_h_one = (
        input_grad(grad_query_low, full_query)
        + input_grad(grad_key_raw, full_key)
        + input_grad(grad_value_raw, full_value)
        + input_grad(grad_gate, full_gate)
        + input_grad(grad_head, full_heads)
    )
    gain_one = jnp.sum(grad_h_one * normed_one, axis=0)
    grad_input = norm_back(grad_h_one * gains[0], normed_one, inv_one) + grad_mid
    small = lax.psum(
        (
            jnp.stack([gain_one, gain_two]),
            jnp.stack([jnp.sum(grad_forget_logit, axis=0), jnp.sum(grad_shift_logit, axis=0)]),
        ),
        ("dp", "ctx"),
    )
    return (
        result,
        grad_input,
        small[0],
        small[1],
        attn_grads[0],
        attn_grads[1],
        attn_grads[2],
        attn_grads[3],
        attn_grads[4],
        attn_grads[5],
        ffn_grads[0],
        ffn_grads[1],
        ffn_grads[2],
    )


AXES = ("x", "core", "zh", "zl", "y")

def dot(left, right, dims):
    return lax.dot_general(left, right, (dims, ((), ())), preferred_element_type=jnp.float32)


def ab(left, right):
    return dot(left, right, ((1,), (0,)))


def abt(left, right):
    return dot(left, right, ((1,), (1,)))


def atb(left, right):
    return dot(left, right, ((0,), (0,)))


MESH = pl.DeviceIdType.MESH


class Net:
    def __init__(self, send, recv):
        self.send, self.recv, self.count, self.open = send, recv, 0, []
        self.at = {name: lax.axis_index(name) for name in AXES}

    def flip(self, names):
        return {name: 1 - self.at[name] for name in names}

    def greet(self):
        barrier = pltpu.get_barrier_semaphore()
        for names in PARTNERS:
            pl.semaphore_signal(barrier, 1, device_id=self.flip(names), device_id_type=MESH)
        moved = self.at["core"] != self.at["zh"]

        @pl.when(moved)
        def _():
            other = self.flip(("core", "zh"))
            pl.semaphore_signal(barrier, 1, device_id=other, device_id_type=MESH)
            pl.semaphore_wait(barrier, len(PARTNERS) + 1)

        @pl.when(jnp.logical_not(moved))
        def _():
            pl.semaphore_wait(barrier, len(PARTNERS))

    def copy(self, source, target, names):
        i = self.count
        self.count += 1
        return pltpu.make_async_remote_copy(
            source,
            target,
            self.send.at[i],
            self.recv.at[i],
            device_id=self.flip(names),
            device_id_type=MESH,
        )

    def push(self, source, target, names):
        made = self.copy(source, target, names)
        made.start()
        self.open.append(made)
        return made

    def left(self, copies):
        for made in copies:
            made.wait_send()
            self.open = [other for other in self.open if other is not made]

    def drain(self):
        for made in self.open:
            made.wait_send()


PARTNERS = (
    ("y",),
    ("zl",),
    ("zl", "y"),
    ("core",),
    ("core", "y"),
    ("core", "zl"),
    ("core", "zl", "y"),
    ("x",),
    ("zh",),
)


def rank_of(at):
    return (at["core"] * 2 + at["zl"]) * 2 + at["y"]


def flipped(at, names):
    return {name: 1 - at[name] if name in names else at[name] for name in at}


def unit_of(at, names):
    at = flipped(at, names)
    return at["zl"] * 2 + at["y"]


class Gather:
    def __init__(self, net, ref, rows):
        self.net, self.ref, self.rows = net, ref, rows

    def part(self, names, half=None):
        start = rank_of(flipped(self.net.at, names)) * self.rows
        size = self.rows
        if half is not None:
            size = self.rows // 2
            start = start + half * size
        return self.ref.at[pl.ds(pl.multiple_of(start, size), size)]

    def send(self, block, half, to):
        part = self.part(block, half)
        return self.net.push(part, part, to)

    def first(self):
        self.y0 = self.send((), 0, ("y",))
        self.z1 = self.send((), 1, ("zl",))
        self.y1 = self.send((), 1, ("y",))
        self.z0 = self.send((), 0, ("zl",))
        self.cores = [self.send((), None, ("core",))]

    def second(self):
        self.y0.wait_recv()
        self.d0 = self.send(("y",), 0, ("zl",))
        self.z1.wait_recv()
        self.d1 = self.send(("zl",), 1, ("y",))
        self.y1.wait_recv()
        self.cores.append(self.send(("y",), None, ("core",)))
        self.z0.wait_recv()
        self.cores.append(self.send(("zl",), None, ("core",)))

    def third(self):
        self.d0.wait_recv()
        self.d1.wait_recv()
        self.cores.append(self.send(("zl", "y"), None, ("core",)))

    def done(self):
        for made in self.cores:
            made.wait_recv()


class Spread:
    def __init__(self, net, ref, pieces):
        self.net, self.ref, self.pieces = net, ref, pieces
        self.size = ref.shape[1] // pieces
        self.unit = net.at["x"] * 2 + net.at["zh"]
        self.from_zh = net.at["x"] * 2 + 1 - net.at["zh"]

    def send(self, unit, piece, to):
        part = self.ref.at[unit, pl.ds(piece * self.size, self.size)]
        return self.net.push(part, part, to)

    def first(self):
        self.along, self.across, self.corner = [], [], []
        for piece in range(self.pieces):
            self.along.append(self.send(self.unit, piece, ("zh",)))
            self.across.append(self.send(self.unit, piece, ("x",)))

    def second_one(self, piece):
        self.along[piece].wait_recv()
        self.corner.append(self.send(self.from_zh, piece, ("x",)))

    def second(self):
        for piece in range(self.pieces):
            self.second_one(piece)

    def wait_across(self):
        for made in self.across:
            made.wait_recv()

    def wait_corner(self):
        for made in self.corner:
            made.wait_recv()


def exchange(net, source, target):
    rank = rank_of(net.at)
    target[rank] = source[rank]
    made = []
    for names in PARTNERS[:7]:
        to = rank_of(flipped(net.at, names))
        made.append(net.push(source.at[to], target.at[rank], names))
    return made


def swap_chunks(value):
    size = value.shape[1] // 8
    order = (0, 2, 1, 3, 4, 6, 5, 7)
    return jnp.concatenate([value[:, i * size : (i + 1) * size] for i in order], axis=1)


def normed(value):
    inverse = lax.rsqrt(jnp.mean(value * value, axis=-1, keepdims=True) + EPS)
    return value * inverse, inverse


def kernel_a(
    x_ref, lens_ref, gains_ref, pack_ref, pack_gu_ref,
    xs_ref, lens_out, h_ref, w_ref, proj_ref, gu_ref,
    send, recv, sems,
):
    net = Net(send, recv)
    rows = x_ref.shape[0]
    rank = rank_of(net.at)
    net.greet()
    moved = move(net, [(x_ref, xs_ref), (lens_ref, lens_out)], sems)
    spread = Spread(net, w_ref, 4)
    unit = spread.unit
    packs = exchange(net, pack_ref, w_ref.at[unit])

    moved()
    value, _inverse = normed(xs_ref[...].astype(jnp.float32))
    h_ref[pl.ds(pl.multiple_of(rank * rows, rows), rows)] = swap_chunks(
        (value * gains_ref[0:1, :]).astype(jnp.bfloat16)
    )
    gather = Gather(net, h_ref, rows)
    gather.first()
    for made in packs:
        made.wait_recv()
    spread.first()
    gather.second()
    gather.third()
    feed = exchange(net, pack_gu_ref, gu_ref)
    depth = pack_ref.shape[0] * pack_ref.shape[1]
    tall = 2 * rows

    def multiply(which, fresh):
        def one(i, _):
            at = pl.ds(pl.multiple_of(i * tall, tall), tall)
            left = h_ref[at, pl.ds(pl.multiple_of(which * depth, 128), depth)]
            part = ab(left, w_ref[which].reshape(depth, -1))
            if fresh:
                proj_ref[at, :] = part
            else:
                proj_ref[at, :] += part
            return 0

        lax.fori_loop(0, h_ref.shape[0] // tall, one, 0)

    gather.done()
    multiply(unit, True)
    spread.second()
    spread.wait_across()
    multiply((1 - net.at["x"]) * 2 + net.at["zh"], False)
    multiply(spread.from_zh, False)
    for made in feed:
        made.wait_recv()
    spread.wait_corner()
    multiply((1 - net.at["x"]) * 2 + 1 - net.at["zh"], False)
    net.drain()


def whole(shape, dtype):
    return jax.ShapeDtypeStruct(shape, dtype)


def vmem(count):
    return [pl.BlockSpec(memory_space=pltpu.VMEM)] * count


def call(kernel, number, outs, args, copies, scratch=(), local=2, far=()):
    return pl.pallas_call(
        kernel,
        out_shape=outs,
        in_specs=[
            pl.BlockSpec(memory_space=pl.ANY if i in far else pltpu.VMEM) for i in range(len(args))
        ],
        out_specs=vmem(len(outs)),
        scratch_shapes=[
            *scratch,
            pltpu.SemaphoreType.DMA((copies,)),
            pltpu.SemaphoreType.DMA((copies,)),
            pltpu.SemaphoreType.DMA((local,)),
        ],
        compiler_params=pltpu.CompilerParams(
            collective_id=number, has_side_effects=True, vmem_limit_bytes=60 * 2**20
        ),
    )(*args)


class Sum:
    def __init__(self, net, part, core, near, corner):
        self.net, self.part, self.core, self.near, self.corner = net, part, core, near, corner
        self.rows = part.shape[1]
        self.half = self.rows // 2
        self.given = {}

    def place(self, names):
        at = flipped(self.net.at, names)
        return at["zl"] * 2 + at["y"]

    def rank(self, names):
        return rank_of(flipped(self.net.at, names))

    def give(self, names):
        block = self.part.at[self.rank(("core", *names))]
        self.given[names] = self.net.push(block, self.core.at[self.place(names)], ("core",))

    def take(self, names):
        self.given[names].wait_recv()
        rank = self.rank(names)
        self.part[rank] = (
            self.part[rank].astype(jnp.float32) + self.core[self.place(names)].astype(jnp.float32)
        ).astype(jnp.bfloat16)

    def rows_of(self, names, half):
        return self.part.at[self.rank(names), pl.ds(half * self.half, self.half)]

    def send_corner(self):
        self.take(("zl", "y"))
        self.c0 = self.net.push(self.rows_of(("zl", "y"), 0), self.corner.at[0], ("y",))
        self.c1 = self.net.push(self.rows_of(("zl", "y"), 1), self.corner.at[1], ("zl",))

    def send_near(self, names, half):
        slot = 0 if names == ("y",) else 1
        to = self.near.at[slot, pl.ds(half * self.half, self.half)]
        return self.net.push(self.rows_of(names, half), to, names)

    def send_zl(self):
        self.take(("zl",))
        self.z1 = self.send_near(("zl",), 1)

    def send_y(self):
        self.take(("y",))
        self.y0 = self.send_near(("y",), 0)

    def add_corner(self, names, half):
        rows = self.rows_of(names, half)
        rows[...] = (
            rows[...].astype(jnp.float32) + self.corner[half].astype(jnp.float32)
        ).astype(jnp.bfloat16)

    def left_cores(self):
        self.net.left(self.given.values())

    def left(self):
        self.net.left((self.c0, self.c1, self.z1, self.y0, self.z0, self.y1))

    def pass_on(self):
        self.c0.wait_recv()
        self.add_corner(("zl",), 0)
        self.z0 = self.send_near(("zl",), 0)
        self.c1.wait_recv()
        self.add_corner(("y",), 1)
        self.y1 = self.send_near(("y",), 1)

    def total(self):
        self.given[()].wait_recv()
        own = self.part[self.rank(())].astype(jnp.float32)
        own = own + self.core[self.place(())].astype(jnp.float32)
        for made in (self.y0, self.z1, self.z0, self.y1):
            made.wait_recv()
        return own + self.near[0].astype(jnp.float32) + self.near[1].astype(jnp.float32)


def sum_scratch(rows, width):
    return [
        pltpu.VMEM((8, rows, width), jnp.bfloat16),
        pltpu.VMEM((4, rows, width), jnp.bfloat16),
        pltpu.VMEM((2, rows, width), jnp.bfloat16),
        pltpu.VMEM((2, rows // 2, width), jnp.bfloat16),
    ]


def move(net, pairs, sems):
    moved = net.at["core"] != net.at["zh"]
    away = [net.copy(source, target, ("core", "zh")) for source, target in pairs]
    stay = [pltpu.make_async_copy(*pair, sems.at[i]) for i, pair in enumerate(pairs)]

    def each(act):
        @pl.when(moved)
        def _():
            for made in away:
                act(made)

        @pl.when(jnp.logical_not(moved))
        def _():
            for made in stay:
                act(made)

    each(lambda made: made.start())
    return lambda: each(lambda made: made.wait())


def lanes(columns, size):
    lane = lax.broadcasted_iota(jnp.int32, (size, 128), 1)
    out = jnp.zeros((size, 128), jnp.float32)
    for i, column in enumerate(columns):
        out = jnp.where(lane == i, column, out)
    return out


def triangle(size, upper):
    row = lax.broadcasted_iota(jnp.int32, (size, size), 0)
    col = lax.broadcasted_iota(jnp.int32, (size, size), 1)
    return jnp.where(row <= col if upper else row >= col, 1.0, 0.0)


def exact(left, right):
    return jnp.dot(
        left, right, precision=lax.Precision.HIGHEST, preferred_element_type=jnp.float32
    )


def spread_lanes(columns, size, wide):
    which = (lax.broadcasted_iota(jnp.int32, (size, wide), 1) // 64) % 3
    return jnp.where(which == 0, columns[0], jnp.where(which == 1, columns[1], columns[2]))


def bounds(lens_ref, first_row, size):
    place = first_row + lax.broadcasted_iota(jnp.int32, (size, 1), 0)
    first = lens_ref[0:1, 0:1]
    second = first + lens_ref[0:1, 1:2]
    low = jnp.where(place >= second, second, jnp.where(place >= first, first, 0))
    return place, low


def head_rows(value, h):
    return value[:, h * 64 : (h + 1) * 64]


def with_one(value, lane_at):
    size = value.shape[0]
    lane = lax.broadcasted_iota(jnp.int32, (size, 64), 1)
    return jnp.concatenate([value, jnp.where(lane == lane_at, 1.0, 0.0)], axis=1)


def mixing(proj_ref, lens_ref, bias_ref, q_ref, k_ref, v_ref, diff_ref, stat_ref, fcol_ref, frow_ref):
    size = 128
    lower = triangle(size, False)

    def one(i, carry):
        last, below = carry
        at = pl.ds(pl.multiple_of(i * size, size), size)
        block = proj_ref[at, :]
        kv = block[:, 384:768]
        logits = block[:, 768:896] + bias_ref[0:1, :]
        logf = jax.nn.log_sigmoid(logits)
        mix = jax.nn.sigmoid(logits)
        place, low = bounds(lens_ref, i * size, size)
        row = lax.broadcasted_iota(jnp.int32, (size, 384), 0)
        prev = jnp.where(row == 0, last, pltpu.roll(kv, 1, 0))
        prev = jnp.where(place == low, 0.0, prev)
        diff = prev - kv
        diff_ref[at, :] = diff
        mixed = kv + spread_lanes([mix[:, 3 + h : 4 + h] for h in range(3)], size, 384) * diff
        decay = exact(lower, logf) + below
        frows = decay.T
        stats = []
        for h in range(3):
            q = head_rows(block, h)
            inv = lax.rsqrt(jnp.mean(q * q, axis=-1, keepdims=True) + EPS)
            stats.append(inv)
            q_ref[h, at, :] = with_one(q * inv * 0.125, 0).astype(jnp.bfloat16)
            fcol_ref[h, at, :] = jnp.broadcast_to(decay[:, h : h + 1], (size, 128))
            frow_ref[h, :, at] = frows[h : h + 1, :]
        for h in range(3):
            k = head_rows(mixed, h)
            inv = lax.rsqrt(jnp.mean(k * k, axis=-1, keepdims=True) + EPS)
            stats.append(inv)
            k_ref[h, at, :] = with_one(k * inv, 1).astype(jnp.bfloat16)
            v_ref[h, at, :] = head_rows(mixed, 3 + h).astype(jnp.bfloat16)
        shut = jax.nn.sigmoid(-logits)
        stats += [shut[:, h : h + 1] for h in range(3)]
        stats += [mix[:, 3 + h : 4 + h] for h in range(3)]
        stat_ref[at, :] = lanes(stats, size)
        return kv[size - 1 :, :], decay[size - 1 :, :]

    lax.fori_loop(
        0,
        proj_ref.shape[0] // size,
        one,
        (jnp.zeros((1, 384), jnp.float32), jnp.zeros((1, 128), jnp.float32)),
    )


def scores(h, at, start, size, keys, q_ref, k_ref, fcol_ref, frow_ref, lens_ref):
    raw = abt(q_ref[h, at, :], k_ref[h, :keys, :])
    own = jnp.concatenate([fcol_ref[h, at, :]] * (keys // 128), axis=1)
    raw = raw + own - frow_ref[h, :, :keys]
    place, low = bounds(lens_ref, start, size)
    col = lax.broadcasted_iota(jnp.int32, (size, keys), 1)
    return jnp.where((col <= place) & (col >= low), jnp.exp(raw), 0.0)


def over_blocks(body, begin, end):
    for part in range(begin, end):

        def one(n, _, part=part):
            body(n // 2, part * 256 + n % 2 * 128, (part + 1) * 256)
            return 0

        lax.fori_loop(0, 6, one, 0)


def kernel_b(
    proj_ref, lens_ref, bias_ref, x_ref, cot_ref, gains_ref, wo_ref, gu_ref, down_ref,
    q_ref, k_ref, v_ref, diff_ref, stat_ref, fcol_ref, frow_ref, gate_ref, attn_ref, a_ref,
    wo_all, gu_all, down_all, mid_ref, h_ref, cot_all,
    spread_o, part, core, near, corner, send, recv, sems,
):
    net = Net(send, recv)
    rank = rank_of(net.at)
    rows = x_ref.shape[0]
    group = proj_ref.shape[0]
    mine = pl.ds(pl.multiple_of(rank * rows, rows), rows)
    net.greet()
    out = Spread(net, spread_o, 1)
    feed = Spread(net, gu_all, 4)
    down = Spread(net, down_all, 2)
    unit = out.unit
    spread_o[unit] = wo_ref[...]
    out.first()
    there = (net.at["zh"] * 2 + net.at["zl"]) * 2 + net.at["y"]
    there = pl.ds(pl.multiple_of(there * rows, rows), rows)
    moved = move(net, [(cot_ref, cot_all.at[there])], sems)
    gu_all[unit] = gu_ref[...]
    down_all[unit] = down_ref[...]
    mixing(proj_ref, lens_ref, bias_ref, q_ref, k_ref, v_ref, diff_ref, stat_ref, fcol_ref, frow_ref)
    feed.first()
    out.second()

    def attend(h, start, keys):
        at = pl.ds(pl.multiple_of(start, 128), 128)
        e = scores(h, at, start, 128, keys, q_ref, k_ref, fcol_ref, frow_ref, lens_ref)
        total = jnp.sum(e, axis=-1, keepdims=True)
        inv = 1.0 / total
        fcol_ref[h, at, :] -= jnp.broadcast_to(jnp.log(total), (128, 128))
        attn_ref[h, at, :] = ab((e * inv).astype(jnp.bfloat16), v_ref[h, :keys, :])

    over_blocks(attend, 0, group // 256)
    out.wait_across()
    out.wait_corner()
    pieces = []
    wo_all[unit_of(net.at, ())] = spread_o[unit_of(net.at, ())]
    for names in (("y",), ("zl",), ("zl", "y")):
        pieces.append(net.push(spread_o.at[unit_of(net.at, names)], wo_all.at[unit_of(net.at, ())], names))
    for h in range(3):
        gate = jax.nn.sigmoid(proj_ref[:, 192 + 64 * h : 256 + 64 * h])
        gate_ref[:, 64 * h : 64 * h + 64] = gate
        a_ref[:, 64 * h : 64 * h + 64] = (gate * attn_ref[h]).astype(jnp.bfloat16)
    for made in pieces:
        made.wait_recv()

    total = Sum(net, part, core, near, corner)

    def project_block(names):
        to = rank_of(flipped(net.at, names))
        left = a_ref[pl.ds(pl.multiple_of(to * rows, rows), rows), :]
        part[to] = ab(left, wo_all[...].reshape(-1, wo_all.shape[2])).astype(jnp.bfloat16)

    for names in (("zl", "y"), ("zl",), ("y",), ()):
        project_block(("core", *names))
        total.give(names)
    project_block(("zl", "y"))
    total.send_corner()
    project_block(("zl",))
    total.send_zl()
    project_block(("y",))
    total.send_y()
    project_block(())
    total.pass_on()
    mid = x_ref[...].astype(jnp.float32) + total.total()
    mid_ref[...] = mid
    value, _inverse = normed(mid)
    h_ref[mine] = swap_chunks((value * gains_ref[1:2, :]).astype(jnp.bfloat16))
    gather = Gather(net, h_ref, rows)
    gather.first()
    feed.second_one(0)
    down.first()
    gather.second()
    gather.third()
    moved()
    other = Gather(net, cot_all, rows)
    other.first()
    feed.second_one(1)
    feed.second_one(2)
    other.second()
    other.third()
    feed.second_one(3)
    down.second()
    gather.done()
    other.done()
    for job in (feed, down):
        job.wait_across()
        job.wait_corner()
    net.drain()


class SpreadSum:
    def __init__(self, net, whole_ref, over_x, over_zh, pieces):
        self.net, self.whole, self.over_x, self.over_zh, self.pieces = net, whole_ref, over_x, over_zh, pieces
        self.size = whole_ref.shape[1] // pieces
        self.x, self.zh = net.at["x"], net.at["zh"]

    def part(self, ref, at, piece):
        return ref.at[at, pl.ds(piece * self.size, self.size)]

    def first(self):
        self.far, self.own, self.last = [], [], []
        for zh, to in ((1 - self.zh, self.far), (self.zh, self.own)):
            for piece in range(self.pieces):
                source = self.part(self.whole, (1 - self.x) * 2 + zh, piece)
                to.append(self.net.push(source, self.part(self.over_x, zh, piece), ("x",)))

    def second(self, piece):
        self.far[piece].wait_recv()
        here = self.part(self.whole, self.x * 2 + 1 - self.zh, piece)
        came = self.part(self.over_x, 1 - self.zh, piece)
        here[...] = (here[...].astype(jnp.float32) + came[...].astype(jnp.float32)).astype(jnp.bfloat16)
        target = self.over_zh.at[pl.ds(piece * self.size, self.size)]
        self.last.append(self.net.push(here, target, ("zh",)))

    def total(self, piece):
        self.own[piece].wait_recv()
        self.last[piece].wait_recv()
        here = self.part(self.whole, self.x * 2 + self.zh, piece)
        came = self.part(self.over_x, self.zh, piece)
        last = self.over_zh.at[pl.ds(piece * self.size, self.size)]
        return (
            here[...].astype(jnp.float32) + came[...].astype(jnp.float32) + last[...].astype(jnp.float32)
        )


def norm_grad(grad, gain, value, inverse):
    scaled = grad * gain
    return (
        inverse * (scaled - value * jnp.mean(scaled * value, axis=-1, keepdims=True)),
        jnp.sum(grad * value, axis=0, keepdims=True),
    )


def kernel_c(
    h_ref, cot_ref, wgu_ref, wd_ref, mid_ref, gains_ref,
    hid_ref, dmid_ref, dao_ref, gain_ref, gdown_ref, ggu_ref,
    dgu_ref, gd_ref, over_x, over_zh, part, core, near, corner, send, recv, sems,
):
    net = Net(send, recv)
    rank = rank_of(net.at)
    rows = mid_ref.shape[0]
    mine = pl.ds(pl.multiple_of(rank * rows, rows), rows)
    wide = hid_ref.shape[1]
    width = mid_ref.shape[1]
    four = 4 * rows
    net.greet()

    def half(which):
        at = pl.ds(pl.multiple_of(which * four, four), four)
        wgu = wgu_ref[...].reshape(width, 2 * wide)
        both = ab(h_ref[at, :], wgu)
        gate, up = both[:, :wide], both[:, wide:]
        sig = jax.nn.sigmoid(gate)
        act = gate * sig
        hid_ref[at, :] = (act * up).astype(jnp.bfloat16)
        grad = abt(cot_ref[at, :], wd_ref[...].reshape(wide, width))
        dgate = grad * up * sig * (1.0 + gate * (1.0 - sig))
        dgu = jnp.concatenate([dgate, grad * act], axis=1).astype(jnp.bfloat16)
        dgu_ref[at, :] = dgu
        back = abt(dgu, wgu).astype(jnp.bfloat16)
        for i in range(4):
            part[which * 4 + i] = back[i * rows : (i + 1) * rows]

    total = Sum(net, part, core, near, corner)
    half(1 - net.at["core"])
    for names in (("zl", "y"), ("zl",), ("y",), ()):
        total.give(names)
    half(net.at["core"])
    total.send_corner()
    total.send_zl()
    total.send_y()
    down = SpreadSum(net, gd_ref, over_x, over_zh, 2)

    def grad_down(k, _):
        left = hid_ref[:, pl.ds(pl.multiple_of(k * rows, rows), rows)]
        gd_ref[k] = atb(left, cot_ref[...]).astype(jnp.bfloat16)
        return 0

    lax.fori_loop(0, 4, grad_down, 0)
    down.first()
    total.pass_on()
    depth = width // 4

    def grad_gu(k, _):
        left = h_ref[:, pl.ds(pl.multiple_of(k * depth, depth), depth)]
        ggu_ref[k] = atb(left, dgu_ref[...]).astype(jnp.bfloat16).reshape(ggu_ref.shape[1:])
        return 0

    lax.fori_loop(0, 4, grad_gu, 0)
    grad = swap_chunks(total.total())
    value, inverse = normed(mid_ref[...])
    back, gain = norm_grad(grad, gains_ref[1:2, :], value, inverse)
    gain_ref[...] = gain
    dmid = cot_ref[mine, :].astype(jnp.float32) + back
    dmid_ref[...] = dmid
    dao_ref[mine] = dmid.astype(jnp.bfloat16)
    gather = Gather(net, dao_ref, rows)
    gather.first()
    down.second(0)
    down.second(1)
    gather.second()
    gather.third()
    for piece in range(2):
        gdown_ref[pl.ds(piece * rows // 2, rows // 2)] = down.total(piece)
    gather.done()
    net.drain()


def spread_scratch(shape):
    return [
        pltpu.VMEM((4, *shape), jnp.bfloat16),
        pltpu.VMEM((2, *shape), jnp.bfloat16),
        pltpu.VMEM(shape, jnp.bfloat16),
    ]


def unmixing(
    lens_ref, q_ref, k_ref, diff_ref, stat_ref, dq_ref, dk_ref, dv_ref, dproj_ref
):
    size = 128
    count = diff_ref.shape[0] // size
    upper = triangle(size, True)

    def one(step, carry):
        after, above, sums = carry
        i = count - 1 - step
        at = pl.ds(pl.multiple_of(i * size, size), size)
        stat = stat_ref[at, :]
        decay, keys, values = [], [], []
        for h in range(3):
            dq, dk = dq_ref[h, at, :], dk_ref[h, at, :]
            decay.append(dq[:, 65:66] - dk[:, 64:65])
            grad = dq[:, :64] * 0.125
            unit = q_ref[h, at, :][:, :64].astype(jnp.float32) * 8.0
            grad = grad - unit * jnp.mean(grad * unit, axis=-1, keepdims=True)
            dproj_ref[at, 64 * h : 64 * h + 64] = (stat[:, h : h + 1] * grad).astype(jnp.bfloat16)
            grad = dk[:, :64]
            unit = k_ref[h, at, :][:, :64].astype(jnp.float32)
            grad = grad - unit * jnp.mean(grad * unit, axis=-1, keepdims=True)
            keys.append(stat[:, 3 + h : 4 + h] * grad)
            values.append(dv_ref[h, at, :])
        both = jnp.concatenate(keys + values, axis=1)
        prod = both * diff_ref[at, :]
        mix = [stat[:, 9 + h : 10 + h] for h in range(3)]
        mixes = spread_lanes(mix, size, 384)
        place, low = bounds(lens_ref, i * size, size)
        carried = jnp.where(place == low, 0.0, both * mixes)
        row = lax.broadcasted_iota(jnp.int32, (size, 384), 0)
        later = jnp.where(row == size - 1, after, pltpu.roll(carried, size - 1, 0))
        dproj_ref[at, 384:768] = (both * (1.0 - mixes) + later).astype(jnp.bfloat16)
        decay = lanes(decay, size)
        suffix = exact(upper, decay) + above
        small = []
        for h in range(3):
            small.append(suffix[:, h : h + 1] * stat[:, 6 + h : 7 + h])
        for h in range(3):
            grad = jnp.sum(head_rows(prod, h) + head_rows(prod, 3 + h), axis=-1, keepdims=True)
            small.append(grad * mix[h] * (1.0 - mix[h]))
        small = lanes(small, size)
        dproj_ref[at, 768:896] = small.astype(jnp.bfloat16)
        above = above + jnp.sum(decay, axis=0, keepdims=True)
        return carried[:1, :], above, sums + jnp.sum(small, axis=0, keepdims=True)

    none = jnp.zeros((1, 128), jnp.float32)
    carry = lax.fori_loop(0, count, one, (jnp.zeros((1, 384), jnp.float32), none, none))
    return carry[2]


def kernel_d(
    dao_ref, wo_ref, a_ref, attn_ref, gate_ref, lens_ref, q_ref, k_ref, v_ref, diff_ref, stat_ref,
    fcol_ref, frow_ref, w_ref, h_ref, dmid_ref, x_ref, gains_ref, gain_two_ref, ggu_ref,
    hid_ref, wd_ref, mid_ref,
    out_ref, gx_ref, gain_ref, bias_ref, ga_ref, go_ref, gu_ref,
    do_ref, dq_ref, dk_ref, dv_ref, dproj_ref,
    gu_x, gu_zh, a_whole, a_x, a_zh, o_raw, o_whole, o_x, o_zh, small, slots, tall, gx_own,
    part, core, near, corner, core2, near2, corner2, send, recv, sems,
):
    net = Net(send, recv)
    rank = rank_of(net.at)
    rows, width = mid_ref.shape
    group = a_ref.shape[0]
    mine = pl.ds(pl.multiple_of(rank * rows, rows), rows)
    fetch = [pltpu.make_async_copy(ref, tall, sems.at[2 + i]) for i, ref in enumerate((dao_ref, h_ref))]
    fetch[0].start()
    net.greet()
    feed = SpreadSum(net, ggu_ref, gu_x, gu_zh, 4)
    attn = SpreadSum(net, a_whole, a_x, a_zh, 4)
    out = SpreadSum(net, o_whole, o_x, o_zh, 1)
    feed.first()

    wo = wo_ref[...].reshape(-1, width)
    fetch[0].wait()
    da = abt(tall[...], wo)
    for h in range(3):
        sig = gate_ref[:, 64 * h : 64 * h + 64]
        grad = da[:, 64 * h : 64 * h + 64] * sig
        do_ref[h] = grad.astype(jnp.bfloat16)
        dproj_ref[:, 192 + 64 * h : 256 + 64 * h] = (grad * attn_ref[h] * (1.0 - sig)).astype(
            jnp.bfloat16
        )
    o_raw[...] = atb(a_ref[...], tall[...]).astype(jnp.bfloat16).reshape(o_raw.shape)
    fetch[1].start()
    here = unit_of(net.at, ())
    o_whole[here] = o_raw[here]
    pieces = []
    for names in (("y",), ("zl",), ("zl", "y")):
        pieces.append(net.push(o_raw.at[unit_of(net.at, names)], o_whole.at[here], names))
    dk_ref[...] = jnp.zeros(dk_ref.shape, jnp.float32)
    dv_ref[...] = jnp.zeros(dv_ref.shape, jnp.float32)

    def attend(h, start, keys):
        at = pl.ds(pl.multiple_of(start, 128), 128)
        p = scores(h, at, start, 128, keys, q_ref, k_ref, fcol_ref, frow_ref, lens_ref)
        do = do_ref[h, at, :]
        dp = abt(do, v_ref[h, :keys, :])
        ds = p * (dp - jnp.sum(p * dp, axis=-1, keepdims=True))
        ds = ds.astype(jnp.bfloat16)
        dq_ref[h, at, :] = ab(ds, k_ref[h, :keys, :])
        dk_ref[h, :keys, :] += atb(ds, q_ref[h, at, :])
        dv_ref[h, :keys, :] += atb(p.astype(jnp.bfloat16), do)

    over_blocks(attend, 0, 3)
    feed.second(0)
    feed.second(1)
    for made in pieces:
        made.wait_recv()
    out.first()
    over_blocks(attend, 3, 4)
    feed.second(2)
    feed.second(3)
    sums = unmixing(lens_ref, q_ref, k_ref, diff_ref, stat_ref, dq_ref, dk_ref, dv_ref, dproj_ref)

    total = Sum(net, part, core, near, corner)
    four = 4 * rows

    def half(which, left_ref, right, multiply, to):
        def one(i, _):
            at = pl.multiple_of(which * four + i * 2 * rows, 2 * rows)
            back = multiply(left_ref[pl.ds(at, 2 * rows), :], right).astype(jnp.bfloat16)
            to[which * 4 + 2 * i] = back[:rows]
            to[which * 4 + 2 * i + 1] = back[rows:]
            return 0

        lax.fori_loop(0, 2, one, 0)

    w = w_ref[...].reshape(width, -1)
    half(1 - net.at["core"], dproj_ref, w, abt, part)
    for names in (("zl", "y"), ("zl",), ("y",), ()):
        total.give(names)
    half(net.at["core"], dproj_ref, w, abt, part)
    total.send_corner()
    total.send_zl()
    total.send_y()
    depth = width // 4

    def grad_attn(k, _):
        left = tall[:, pl.ds(pl.multiple_of(k * depth, depth), depth)]
        a_whole[k] = atb(left, dproj_ref[...]).astype(jnp.bfloat16).reshape(a_whole.shape[1:])
        return 0

    fetch[1].wait()
    lax.fori_loop(0, 4, grad_attn, 0)
    attn.first()
    total.pass_on()
    out.second(0)

    result = Sum(net, part, core2, near2, corner2)
    wd = wd_ref[...].reshape(-1, width)
    total.left_cores()
    half(1 - net.at["core"], hid_ref, wd, ab, part)
    for names in (("zl", "y"), ("zl",), ("y",), ()):
        result.give(names)

    grad = swap_chunks(total.total())
    value, inverse = normed(x_ref[...].astype(jnp.float32))
    back, gain = norm_grad(grad, gains_ref[0:1, :], value, inverse)
    gx_own[...] = (dmid_ref[...] + back).astype(jnp.bfloat16)
    moved_gx = move(net, [(gx_own, gx_ref)], sems)
    total.left()
    half(net.at["core"], hid_ref, wd, ab, part)
    result.send_corner()
    result.send_zl()
    result.send_y()
    small[0] = jnp.concatenate(
        [gain, gain_two_ref[...], jnp.concatenate([sums, jnp.zeros((1, width - 128), jnp.float32)], axis=1)]
        + [jnp.zeros((5, width), jnp.float32)],
        axis=0,
    )
    first = net.push(small.at[0], small.at[1], ("x",))
    for piece in range(4):
        gu_zh[2 * piece : 2 * piece + 2] = feed.total(piece).astype(jnp.bfloat16)
    given = exchange(net, gu_zh, gu_ref)
    go_ref[...] = out.total(0)
    result.pass_on()
    first.wait_recv()
    small[2] = small[0] + small[1]
    second = net.push(small.at[2], small.at[3], ("zh",))
    attn.second(0)
    attn.second(1)
    second.wait_recv()
    slots[rank] = small[2] + small[3]
    shared = [net.push(slots.at[rank], slots.at[rank], names) for names in PARTNERS[:7]]
    part[rank] = (mid_ref[...] + result.total()).astype(jnp.bfloat16)
    moved_out = move(net, [(part.at[rank], out_ref)], sems)
    attn.second(2)
    attn.second(3)
    for made in shared:
        made.wait_recv()
    gain_ref[...] = jnp.sum(slots[:, 0:2, :], axis=0)
    bias_ref[...] = slots[:, 2:3, :128]
    for piece in range(4):
        a_zh[2 * piece : 2 * piece + 2] = attn.total(piece).astype(jnp.bfloat16)
    given += exchange(net, a_zh, ga_ref)
    for made in given:
        made.wait_recv()
    moved_gx()
    moved_out()
    net.drain()


def squares(
    layer_input,
    cotangent,
    seq_lengths,
    gains,
    head_bias,
    w_query,
    w_key,
    w_value,
    w_gate,
    w_out,
    w_heads,
    w_ff_gate,
    w_ff_up,
    w_ff_down,
):
    rows, width = layer_input.shape
    heads = head_bias.shape[1]
    head_dim = width // heads
    ranks = 8
    group = rows * ranks
    mine = heads // ranks
    cols = mine * head_dim
    shard = w_query.shape[0]
    units = w_ff_gate.shape[1] // ranks
    low = jnp.bfloat16
    slice_at = (lax.axis_index("zl") * 2 + lax.axis_index("core")) * 2 + lax.axis_index("y")

    def by_rank(w):
        split = w.reshape(shard, 2, 2, 2, -1)
        return split.transpose(2, 1, 3, 0, 4).reshape(ranks, shard, -1)

    head_cols = jnp.concatenate(
        [by_rank(w_heads[:, :heads]), by_rank(w_heads[:, heads:])], axis=2
    )
    head_cols = jnp.pad(head_cols, ((0, 0), (0, 0), (0, 128 - 2 * mine)))
    pack = jnp.concatenate(
        [by_rank(w) for w in (w_query, w_gate, w_key, w_value)] + [head_cols], axis=2
    )
    def feed_cols(w):
        split = w.reshape(shard, 2, 2, 2, 4, -1)
        return split.transpose(2, 4, 0, 1, 3, 5).reshape(ranks, shard, units)

    pack_gu = jnp.concatenate([feed_cols(w_ff_gate), feed_cols(w_ff_up)], axis=2)
    lens = jnp.pad(seq_lengths, ((0, 7), (0, 125)))
    packed, lengths, h_one_all, w_attn, proj, gu_own = call(
        kernel_a,
        1,
        (
            whole(layer_input.shape, low),
            whole(lens.shape, lens.dtype),
            whole((group, width), low),
            whole((4, *pack.shape), low),
            whole((group, pack.shape[2]), jnp.float32),
            whole(pack_gu.shape, low),
        ),
        (layer_input, lens, gains, pack, pack_gu),
        40,
    )
    bias = lax.dynamic_slice_in_dim(head_bias, slice_at * mine, mine, 1).reshape(1, -1)
    bias = jnp.pad(bias, ((0, 7), (0, 128 - 2 * mine)))
    f32 = jnp.float32
    (
        q_all, k_all, v_all, diff, stat, fcol, frow, gate_sig, attn3, branch_in,
        w_o, w_gu, w_d, mid, h_two_all, cot_all,
    ) = call(
        kernel_b,
        2,
        (
            whole((mine, group, 128), low),
            whole((mine, group, 128), low),
            whole((mine, group, head_dim), low),
            whole((group, 2 * cols), f32),
            whole((group, 128), f32),
            whole((mine, group, 128), f32),
            whole((mine, 1, group), f32),
            whole((group, cols), f32),
            whole((mine, group, head_dim), f32),
            whole((group, cols), low),
            whole((4, shard, width), low),
            whole((4, *pack_gu.shape), low),
            whole((4, *w_ff_down.shape), low),
            whole((rows, width), f32),
            whole((group, width), low),
            whole((group, width), low),
        ),
        (proj, lengths, bias, packed, cotangent, gains, w_out, gu_own, w_ff_down),
        64,
        [pltpu.VMEM((4, shard, width), low), *sum_scratch(rows, width)],
    )
    hidden, grad_mid, grad_branch, gain_two, grad_down, grad_gu = call(
        kernel_c,
        3,
        (
            whole((group, units), low),
            whole((rows, width), f32),
            whole((group, width), low),
            whole((1, width), f32),
            whole((rows, width), f32),
            whole((4, *pack_gu.shape), low),
        ),
        (h_two_all, cot_all, w_gu, w_d, mid, gains),
        48,
        [
            pltpu.VMEM((group, 2 * units), low),
            pltpu.VMEM((4, rows, width), low),
            pltpu.VMEM((2, rows, width), low),
            pltpu.VMEM((rows, width), low),
            *sum_scratch(rows, width),
        ],
    )
    result, grad_input, gain_sums, bias_sums, grad_attn_w, grad_wout, grad_gu = call(
        kernel_d,
        4,
        (
            whole((rows, width), low),
            whole((rows, width), low),
            whole((2, width), f32),
            whole((ranks, 1, 128), f32),
            whole(pack.shape, low),
            whole((shard, width), f32),
            whole(pack_gu.shape, low),
        ),
        (
            grad_branch, w_o, branch_in, attn3, gate_sig, lengths, q_all, k_all, v_all, diff, stat,
            fcol, frow, w_attn, h_one_all, grad_mid, packed, gains, gain_two, grad_gu,
            hidden, w_d, mid,
        ),
        96,
        [
            pltpu.VMEM((mine, group, head_dim), low),
            pltpu.VMEM((mine, group, 128), f32),
            pltpu.VMEM((mine, group, 128), f32),
            pltpu.VMEM((mine, group, head_dim), f32),
            pltpu.VMEM((group, pack.shape[2]), low),
            *spread_scratch(pack_gu.shape)[1:],
            *spread_scratch(pack.shape),
            pltpu.VMEM((4, shard, width), low),
            *spread_scratch((shard, width)),
            pltpu.VMEM((4, 8, width), f32),
            pltpu.VMEM((ranks, 8, width), f32),
            pltpu.VMEM((group, width), low),
            pltpu.VMEM((rows, width), low),
            *sum_scratch(rows, width),
            *sum_scratch(rows, width)[1:],
        ],
        4,
        (0, 14),
    )

    def from_ranks(part):
        split = part.reshape(2, 2, 2, shard, -1).transpose(3, 1, 0, 2, 4)
        return split.reshape(shard, -1).astype(f32)

    def attn_cols(i):
        return from_ranks(grad_attn_w[:, :, i * cols : (i + 1) * cols])

    head_part = grad_attn_w[:, :, 4 * cols : 4 * cols + 2 * mine]
    head_part = jnp.concatenate(
        [from_ranks(head_part[:, :, :mine]), from_ranks(head_part[:, :, mine:])], axis=1
    )
    bias_sums = bias_sums[:, 0, : 2 * mine].reshape(2, 2, 2, 2, mine)
    bias_sums = bias_sums.transpose(3, 1, 0, 2, 4).reshape(2, heads)

    def feed_back(part):
        split = part.reshape(2, 4, shard, 2, 2, -1)
        return split.transpose(2, 3, 0, 4, 1, 5).reshape(shard, -1).astype(f32)

    return (
        result,
        grad_input.astype(f32),
        gain_sums,
        bias_sums,
        attn_cols(0),
        attn_cols(2),
        attn_cols(3),
        attn_cols(1),
        grad_wout,
        head_part,
        feed_back(grad_gu[:, :, :units]),
        feed_back(grad_gu[:, :, units:]),
        grad_down,
    )


def solution(mesh):
    if mesh.shape["dp"] == 4 and mesh.shape["ctx"] == 8:
        body, axes, group = squares, AXES, ("x", "core")
        mesh = Mesh(np.reshape(mesh.devices, (2, 2, 2, 2, 2)), AXES)
    else:
        body, axes, group = shards, ("dp", "ctx"), "dp"
    cut = P(axes, None)
    return jax.shard_map(
        body,
        mesh=mesh,
        in_specs=(cut, cut, P(group, None), P(), P()) + (cut,) * 9,
        out_specs=(cut, cut, P(), P()) + (cut,) * 9,
        check_vma=False,
    )
```

```python
import jax
import jax.numpy as jnp
import numpy as np
from jax import lax
from jax.experimental import pallas as pl
from jax.experimental.pallas import tpu as pltpu
from jax.sharding import Mesh
from jax.sharding import PartitionSpec as P

EPS = 1e-06


def passed_along(array, axis, by):
    size = lax.axis_size(axis)
    pairs = [(i, i + by) for i in range(size) if 0 <= i + by < size]
    return lax.ppermute(array, axis, pairs)


def entering(part, axis, combine, identity, reverse):
    count = lax.axis_size(axis)
    place = lax.axis_index(axis)
    ahead = count - 1 - place if reverse else place
    gathered = lax.all_gather(part, axis)
    state = jnp.zeros_like(part) + jnp.asarray(identity, part.dtype)

    def one(step, state):
        source = count - 1 - step if reverse else step
        return combine(state, lax.dynamic_index_in_dim(gathered, source, 0, False))

    return lax.fori_loop(0, ahead, one, state)


def fetch_attention(w_query, w_key, w_value, w_gate, w_out, w_heads):
    return (
        lax.all_gather(w_query, ("dp", "ctx"), axis=0, tiled=True),
        lax.all_gather(w_key, ("dp", "ctx"), axis=0, tiled=True),
        lax.all_gather(w_value, ("dp", "ctx"), axis=0, tiled=True),
        lax.all_gather(w_gate, ("dp", "ctx"), axis=0, tiled=True),
        lax.all_gather(w_out, ("dp", "ctx"), axis=0, tiled=True),
        lax.all_gather(w_heads, ("dp", "ctx"), axis=0, tiled=True),
    )


def fetch_feed(w_ff_gate, w_ff_up, w_ff_down):
    return (
        lax.all_gather(w_ff_gate, ("dp", "ctx"), axis=0, tiled=True),
        lax.all_gather(w_ff_up, ("dp", "ctx"), axis=0, tiled=True),
        lax.all_gather(w_ff_down, ("dp", "ctx"), axis=0, tiled=True),
    )


def add_arrays(earlier, later):
    return earlier + later


def norm_back(grad, normed, inverse):
    return inverse * (grad - normed * jnp.mean(grad * normed, axis=-1, keepdims=True))


def project(left, right):
    return jnp.dot(left, right, preferred_element_type=jnp.float32)


def weight_grad(left, right):
    return jnp.einsum("ra,rb->ab", left, right, preferred_element_type=jnp.float32)


def input_grad(grad, weight):
    return jnp.einsum("rb,ab->ra", grad, weight, preferred_element_type=jnp.float32)


def shards(
    layer_input,
    cotangent,
    seq_lengths,
    gains,
    head_bias,
    w_query,
    w_key,
    w_value,
    w_gate,
    w_out,
    w_heads,
    w_ff_gate,
    w_ff_up,
    w_ff_down,
):
    rows, width = layer_input.shape
    heads = head_bias.shape[1]
    head_dim = width // heads
    spans = lax.axis_size("ctx")
    group = rows * spans
    scale = head_dim ** (-0.5)
    here = lax.axis_index("ctx")
    local_pos = here * rows + jnp.arange(rows, dtype=jnp.int32)
    key_pos = jnp.arange(group, dtype=jnp.int32)
    first = seq_lengths[0, 0]
    second = first + seq_lengths[0, 1]
    local_seg = (local_pos >= first).astype(jnp.int32) + (local_pos >= second).astype(jnp.int32)
    key_seg = (key_pos >= first).astype(jnp.int32) + (key_pos >= second).astype(jnp.int32)
    starts = (local_pos == 0) | (local_pos == first) | (local_pos == second)
    keep = (1 - starts.astype(jnp.int32)).astype(jnp.float32)[:, None]
    allowed = (local_seg[:, None] == key_seg[None, :]) & (key_pos[None, :] <= local_pos[:, None])
    x_full = layer_input.astype(jnp.float32)
    inv_one = lax.rsqrt(jnp.mean(x_full * x_full, axis=-1, keepdims=True) + EPS)
    normed_one = x_full * inv_one
    h_one = (normed_one * gains[0]).astype(jnp.bfloat16)
    full_query, full_key, full_value, full_gate, full_out, full_heads = fetch_attention(
        w_query, w_key, w_value, w_gate, w_out, w_heads
    )
    query = project(h_one, full_query)
    key_raw = project(h_one, full_key)
    value_raw = project(h_one, full_value)
    gate_raw = project(h_one, full_gate)
    head_raw = project(h_one, full_heads)
    forget_logit = head_raw[:, :heads] + head_bias[0]
    shift_logit = head_raw[:, heads:] + head_bias[1]
    log_forget = jax.nn.log_sigmoid(forget_logit)
    mix_small = jax.nn.sigmoid(shift_logit)
    mix = jnp.repeat(mix_small, head_dim, axis=1)
    prev_row = passed_along(h_one[rows - 1 :], "ctx", 1)
    key_prev = jnp.concatenate([project(prev_row, full_key), key_raw[:-1]], 0) * keep
    value_prev = jnp.concatenate([project(prev_row, full_value), value_raw[:-1]], 0) * keep
    key_mix = mix * key_prev + (1.0 - mix) * key_raw
    value_mix = mix * value_prev + (1.0 - mix) * value_raw
    query4 = query.reshape(rows, heads, head_dim)
    query_inv = lax.rsqrt(jnp.mean(query4 * query4, axis=-1, keepdims=True) + EPS)
    query_norm = query4 * query_inv
    key4 = key_mix.reshape(rows, heads, head_dim)
    key_inv = lax.rsqrt(jnp.mean(key4 * key4, axis=-1, keepdims=True) + EPS)
    key_norm = key4 * key_inv
    q_low = query_norm.astype(jnp.bfloat16)
    k_low = key_norm.reshape(rows, width).astype(jnp.bfloat16)
    v_low = value_mix.astype(jnp.bfloat16)
    local_cum = jnp.cumsum(log_forget, axis=0)
    offset = entering(
        local_cum[rows - 1], "ctx", add_arrays, jnp.zeros((heads,), jnp.float32), False
    )
    decay = local_cum + offset
    gathered_k, gathered_v, all_decay = (
        lax.all_gather(k_low.astype(jnp.float32), "ctx", axis=0, tiled=True),
        lax.all_gather(v_low.astype(jnp.float32), "ctx", axis=0, tiled=True),
        lax.all_gather(decay, "ctx", axis=0, tiled=True),
    )
    all_keys = gathered_k.astype(jnp.bfloat16).reshape(group, heads, head_dim)
    all_values = gathered_v.astype(jnp.bfloat16).reshape(group, heads, head_dim)

    def scores_of(index, keys_whole, decay_whole):
        q_part = lax.dynamic_slice_in_dim(q_low, index * 4, 4, 1)
        k_part = lax.dynamic_slice_in_dim(keys_whole, index * 4, 4, 1)
        own = lax.dynamic_slice_in_dim(decay, index * 4, 4, 1)
        far = lax.dynamic_slice_in_dim(decay_whole, index * 4, 4, 1)
        raw = jnp.einsum("rhd,ghd->hrg", q_part, k_part, preferred_element_type=jnp.float32) * scale
        raw = raw + own.T[:, :, None] - far.T[:, None, :]
        return (jnp.where(allowed[None], raw, -1e30), q_part, k_part)

    group_count = heads // 4

    def forward_step(index, carry):
        mixed, log_total = carry
        scores, q_part, k_part = scores_of(index, all_keys, all_decay)
        v_part = lax.dynamic_slice_in_dim(all_values, index * 4, 4, 1)
        top = jnp.max(scores, axis=-1, keepdims=True)
        expd = jnp.exp(scores - top)
        total = jnp.sum(expd, axis=-1, keepdims=True)
        probs = (expd / total).astype(jnp.bfloat16)
        part = jnp.einsum("hrg,ghd->rhd", probs, v_part, preferred_element_type=jnp.float32)
        mixed = lax.dynamic_update_slice_in_dim(mixed, part, index * 4, 1)
        log_total = lax.dynamic_update_slice_in_dim(
            log_total, (top + jnp.log(total))[:, :, 0].T, index * 4, 1
        )
        return (mixed, log_total)

    attn4, log_total = lax.fori_loop(
        0,
        group_count,
        forward_step,
        (jnp.zeros((rows, heads, head_dim), jnp.float32), jnp.zeros((rows, heads), jnp.float32)),
    )
    attn = attn4.reshape(rows, width)
    gate_sig = jax.nn.sigmoid(gate_raw)
    branch_in = (gate_sig * attn).astype(jnp.bfloat16)
    mid = x_full + project(branch_in, full_out)
    inv_two = lax.rsqrt(jnp.mean(mid * mid, axis=-1, keepdims=True) + EPS)
    normed_two = mid * inv_two
    h_two = (normed_two * gains[1]).astype(jnp.bfloat16)
    full_ff_gate, full_ff_up, full_ff_down = fetch_feed(w_ff_gate, w_ff_up, w_ff_down)
    ff_gate = project(h_two, full_ff_gate)
    ff_up = project(h_two, full_ff_up)
    ff_sig = jax.nn.sigmoid(ff_gate)
    hidden = (ff_gate * ff_sig * ff_up).astype(jnp.bfloat16)
    result = (mid + project(hidden, full_ff_down)).astype(jnp.bfloat16)
    full_ff_gate, full_ff_up, full_ff_down = fetch_feed(w_ff_gate, w_ff_up, w_ff_down)
    full_query, full_key, full_value, full_gate, full_out, full_heads = fetch_attention(
        w_query, w_key, w_value, w_gate, w_out, w_heads
    )
    grad_out = cotangent.astype(jnp.float32)
    grad_down = weight_grad(hidden, cotangent)
    grad_hidden = input_grad(cotangent, full_ff_down)
    grad_gate_ff = (grad_hidden * ff_up * ff_sig * (1.0 + ff_gate * (1.0 - ff_sig))).astype(
        jnp.bfloat16
    )
    grad_up_ff = (grad_hidden * (ff_gate * ff_sig)).astype(jnp.bfloat16)
    ffn_grads = (
        lax.psum_scatter(
            weight_grad(h_two, grad_gate_ff), ("dp", "ctx"), scatter_dimension=0, tiled=True
        ),
        lax.psum_scatter(
            weight_grad(h_two, grad_up_ff), ("dp", "ctx"), scatter_dimension=0, tiled=True
        ),
        lax.psum_scatter(grad_down, ("dp", "ctx"), scatter_dimension=0, tiled=True),
    )
    grad_h_two = input_grad(grad_gate_ff, full_ff_gate) + input_grad(grad_up_ff, full_ff_up)
    gain_two = jnp.sum(grad_h_two * normed_two, axis=0)
    grad_mid = norm_back(grad_h_two * gains[1], normed_two, inv_two) + grad_out
    grad_branch = grad_mid.astype(jnp.bfloat16)
    grad_wout = weight_grad(branch_in, grad_branch)
    grad_branch_in = input_grad(grad_branch, full_out)
    grad_attn = (grad_branch_in * gate_sig).astype(jnp.bfloat16).reshape(rows, heads, head_dim)
    grad_gate = (grad_branch_in * attn * gate_sig * (1.0 - gate_sig)).astype(jnp.bfloat16)
    gathered_k, gathered_v, all_decay = (
        lax.all_gather(k_low.astype(jnp.float32), "ctx", axis=0, tiled=True),
        lax.all_gather(v_low.astype(jnp.float32), "ctx", axis=0, tiled=True),
        lax.all_gather(decay, "ctx", axis=0, tiled=True),
    )
    all_keys = gathered_k.astype(jnp.bfloat16).reshape(group, heads, head_dim)
    all_values = gathered_v.astype(jnp.bfloat16).reshape(group, heads, head_dim)

    def backward_step(index, carry):
        grad_q, grad_k, grad_v, grad_own, grad_far = carry
        scores, q_part, k_part = scores_of(index, all_keys, all_decay)
        v_part = lax.dynamic_slice_in_dim(all_values, index * 4, 4, 1)
        lse = lax.dynamic_slice_in_dim(log_total, index * 4, 4, 1).T[:, :, None]
        probs = jnp.exp(scores - lse)
        probs_low = probs.astype(jnp.bfloat16)
        grad_part = lax.dynamic_slice_in_dim(grad_attn, index * 4, 4, 1)
        grad_probs = jnp.einsum(
            "rhd,ghd->hrg", grad_part, v_part, preferred_element_type=jnp.float32
        )
        value_term = jnp.einsum(
            "hrg,rhd->ghd", probs_low, grad_part, preferred_element_type=jnp.float32
        )
        grad_scores = (
            probs * (grad_probs - jnp.sum(probs * grad_probs, axis=-1, keepdims=True))
        ).astype(jnp.bfloat16)
        query_term = (
            jnp.einsum("hrg,ghd->rhd", grad_scores, k_part, preferred_element_type=jnp.float32)
            * scale
        )
        key_term = (
            jnp.einsum("hrg,rhd->ghd", grad_scores, q_part, preferred_element_type=jnp.float32)
            * scale
        )
        scores_full = grad_scores.astype(jnp.float32)
        own_term = jnp.sum(scores_full, axis=-1).T
        far_term = -jnp.sum(scores_full, axis=1).T
        grad_q = lax.dynamic_update_slice_in_dim(grad_q, query_term, index * 4, 1)
        grad_k = lax.dynamic_update_slice_in_dim(grad_k, key_term, index * 4, 1)
        grad_v = lax.dynamic_update_slice_in_dim(grad_v, value_term, index * 4, 1)
        grad_own = lax.dynamic_update_slice_in_dim(grad_own, own_term, index * 4, 1)
        grad_far = lax.dynamic_update_slice_in_dim(grad_far, far_term, index * 4, 1)
        return (grad_q, grad_k, grad_v, grad_own, grad_far)

    grad_q, grad_k, grad_v, grad_own, grad_far = lax.fori_loop(
        0,
        group_count,
        backward_step,
        (
            jnp.zeros((rows, heads, head_dim), jnp.float32),
            jnp.zeros((group, heads, head_dim), jnp.float32),
            jnp.zeros((group, heads, head_dim), jnp.float32),
            jnp.zeros((rows, heads), jnp.float32),
            jnp.zeros((group, heads), jnp.float32),
        ),
    )
    grad_k_local, grad_v_local, grad_far_local = (
        lax.psum_scatter(grad_k, "ctx", scatter_dimension=0, tiled=True),
        lax.psum_scatter(grad_v, "ctx", scatter_dimension=0, tiled=True),
        lax.psum_scatter(grad_far, "ctx", scatter_dimension=0, tiled=True),
    )
    grad_decay = grad_own + grad_far_local
    local_rev = jnp.flip(jnp.cumsum(jnp.flip(grad_decay, 0), axis=0), 0)
    later = entering(
        jnp.sum(grad_decay, axis=0), "ctx", add_arrays, jnp.zeros((heads,), jnp.float32), True
    )
    grad_forget_logit = (local_rev + later) * jax.nn.sigmoid(-forget_logit)
    grad_query = norm_back(grad_q, query_norm, query_inv).reshape(rows, width)
    grad_key_mix = norm_back(grad_k_local, key_norm, key_inv).reshape(rows, width)
    grad_value_mix = grad_v_local.reshape(rows, width)
    grad_mix = jnp.sum(
        (grad_key_mix * (key_prev - key_raw) + grad_value_mix * (value_prev - value_raw)).reshape(
            rows, heads, head_dim
        ),
        axis=-1,
    )
    grad_shift_logit = grad_mix * mix_small * (1.0 - mix_small)
    carried_key = grad_key_mix * mix * keep
    carried_value = grad_value_mix * mix * keep
    from_next = passed_along(jnp.concatenate([carried_key[:1], carried_value[:1]], 0), "ctx", -1)
    grad_key_raw = (
        grad_key_mix * (1.0 - mix) + jnp.concatenate([carried_key[1:], from_next[:1]], 0)
    ).astype(jnp.bfloat16)
    grad_value_raw = (
        grad_value_mix * (1.0 - mix) + jnp.concatenate([carried_value[1:], from_next[1:]], 0)
    ).astype(jnp.bfloat16)
    grad_query_low = grad_query.astype(jnp.bfloat16)
    grad_head = jnp.concatenate([grad_forget_logit, grad_shift_logit], axis=1).astype(jnp.bfloat16)
    attn_grads = (
        lax.psum_scatter(
            weight_grad(h_one, grad_query_low), ("dp", "ctx"), scatter_dimension=0, tiled=True
        ),
        lax.psum_scatter(
            weight_grad(h_one, grad_key_raw), ("dp", "ctx"), scatter_dimension=0, tiled=True
        ),
        lax.psum_scatter(
            weight_grad(h_one, grad_value_raw), ("dp", "ctx"), scatter_dimension=0, tiled=True
        ),
        lax.psum_scatter(
            weight_grad(h_one, grad_gate), ("dp", "ctx"), scatter_dimension=0, tiled=True
        ),
        lax.psum_scatter(grad_wout, ("dp", "ctx"), scatter_dimension=0, tiled=True),
        lax.psum_scatter(
            weight_grad(h_one, grad_head), ("dp", "ctx"), scatter_dimension=0, tiled=True
        ),
    )
    grad_h_one = (
        input_grad(grad_query_low, full_query)
        + input_grad(grad_key_raw, full_key)
        + input_grad(grad_value_raw, full_value)
        + input_grad(grad_gate, full_gate)
        + input_grad(grad_head, full_heads)
    )
    gain_one = jnp.sum(grad_h_one * normed_one, axis=0)
    grad_input = norm_back(grad_h_one * gains[0], normed_one, inv_one) + grad_mid
    small = lax.psum(
        (
            jnp.stack([gain_one, gain_two]),
            jnp.stack([jnp.sum(grad_forget_logit, axis=0), jnp.sum(grad_shift_logit, axis=0)]),
        ),
        ("dp", "ctx"),
    )
    return (
        result,
        grad_input,
        small[0],
        small[1],
        attn_grads[0],
        attn_grads[1],
        attn_grads[2],
        attn_grads[3],
        attn_grads[4],
        attn_grads[5],
        ffn_grads[0],
        ffn_grads[1],
        ffn_grads[2],
    )


AXES = ("x", "core", "zh", "zl", "y")

def dot(left, right, dims):
    return lax.dot_general(left, right, (dims, ((), ())), preferred_element_type=jnp.float32)


def ab(left, right):
    return dot(left, right, ((1,), (0,)))


def abt(left, right):
    return dot(left, right, ((1,), (1,)))


def atb(left, right):
    return dot(left, right, ((0,), (0,)))


MESH = pl.DeviceIdType.MESH


class Net:
    def __init__(self, send, recv):
        self.send, self.recv, self.count, self.open = send, recv, 0, []
        self.at = {name: lax.axis_index(name) for name in AXES}

    def flip(self, names):
        return {name: 1 - self.at[name] for name in names}

    def greet(self):
        barrier = pltpu.get_barrier_semaphore()
        for names in PARTNERS:
            pl.semaphore_signal(barrier, 1, device_id=self.flip(names), device_id_type=MESH)
        moved = self.at["core"] != self.at["zh"]

        @pl.when(moved)
        def _():
            other = self.flip(("core", "zh"))
            pl.semaphore_signal(barrier, 1, device_id=other, device_id_type=MESH)
            pl.semaphore_wait(barrier, len(PARTNERS) + 1)

        @pl.when(jnp.logical_not(moved))
        def _():
            pl.semaphore_wait(barrier, len(PARTNERS))

    def copy(self, source, target, names):
        i = self.count
        self.count += 1
        return pltpu.make_async_remote_copy(
            source,
            target,
            self.send.at[i],
            self.recv.at[i],
            device_id=self.flip(names),
            device_id_type=MESH,
        )

    def push(self, source, target, names):
        made = self.copy(source, target, names)
        made.start()
        self.open.append(made)
        return made

    def left(self, copies):
        for made in copies:
            made.wait_send()
            self.open = [other for other in self.open if other is not made]

    def drain(self):
        for made in self.open:
            made.wait_send()


PARTNERS = (
    ("y",),
    ("zl",),
    ("zl", "y"),
    ("core",),
    ("core", "y"),
    ("core", "zl"),
    ("core", "zl", "y"),
    ("x",),
    ("zh",),
)


def rank_of(at):
    return (at["core"] * 2 + at["zl"]) * 2 + at["y"]


def flipped(at, names):
    return {name: 1 - at[name] if name in names else at[name] for name in at}


def unit_of(at, names):
    at = flipped(at, names)
    return at["zl"] * 2 + at["y"]


class Gather:
    def __init__(self, net, ref, rows):
        self.net, self.ref, self.rows = net, ref, rows

    def part(self, names, half=None):
        start = rank_of(flipped(self.net.at, names)) * self.rows
        size = self.rows
        if half is not None:
            size = self.rows // 2
            start = start + half * size
        return self.ref.at[pl.ds(pl.multiple_of(start, size), size)]

    def send(self, block, half, to):
        part = self.part(block, half)
        return self.net.push(part, part, to)

    def first(self):
        self.along = [self.send((), half, ("zl",)) for half in range(2)]
        self.near = self.send((), None, ("y",))
        self.cores = [self.send((), None, ("core",))]

    def second(self):
        self.corner = []
        for half in range(2):
            self.along[half].wait_recv()
            self.corner.append(self.send(("zl",), half, ("y",)))
        self.cores.append(self.send(("zl",), None, ("core",)))
        self.near.wait_recv()
        self.cores.append(self.send(("y",), None, ("core",)))

    def third(self):
        for made in self.corner:
            made.wait_recv()
        self.cores.append(self.send(("zl", "y"), None, ("core",)))

    def done(self):
        for made in self.cores:
            made.wait_recv()


class Spread:
    def __init__(self, net, ref, pieces):
        self.net, self.ref, self.pieces = net, ref, pieces
        self.size = ref.shape[1] // pieces
        self.unit = net.at["x"] * 2 + net.at["zh"]
        self.from_zh = net.at["x"] * 2 + 1 - net.at["zh"]

    def send(self, unit, piece, to):
        part = self.ref.at[unit, pl.ds(piece * self.size, self.size)]
        return self.net.push(part, part, to)

    def first(self, ahead):
        self.along, self.across, self.corner = [], [], []
        for piece in range(self.pieces):
            if piece < ahead:
                self.along.append(self.send(self.unit, piece, ("zh",)))
            self.across.append(self.send(self.unit, piece, ("x",)))

    def second(self, piece):
        self.along[piece].wait_recv()
        self.corner.append(self.send(self.from_zh, piece, ("x",)))
        if len(self.along) < self.pieces:
            self.push_next()

    def push_next(self):
        self.along.append(self.send(self.unit, len(self.along), ("zh",)))

    def wait_across(self):
        for made in self.across:
            made.wait_recv()

    def wait_corner(self):
        for made in self.corner:
            made.wait_recv()


def exchange(net, source, target):
    rank = rank_of(net.at)
    target[rank] = source[rank]
    made = []
    for names in PARTNERS[:7]:
        to = rank_of(flipped(net.at, names))
        made.append(net.push(source.at[to], target.at[rank], names))
    return made


def swap_chunks(value):
    size = value.shape[1] // 8
    order = (0, 2, 1, 3, 4, 6, 5, 7)
    return jnp.concatenate([value[:, i * size : (i + 1) * size] for i in order], axis=1)


def normed(value):
    inverse = lax.rsqrt(jnp.mean(value * value, axis=-1, keepdims=True) + EPS)
    return value * inverse, inverse


def slice_of(rank):
    return rank // 2 % 2 * 4 + rank // 4 * 2 + rank % 2


def pack_weights(wide, heads_ref, feeds, pack_ref, pack_gu_ref):
    size = wide[0].shape[1] // 8
    few = heads_ref.shape[1] // 16
    block = feeds[0].shape[1] // 32
    for rank in range(8):
        at = slice_of(rank)
        for i, ref in enumerate(wide):
            pack_ref[rank, :, i * size : (i + 1) * size] = ref[:, at * size : (at + 1) * size]
        pack_ref[rank, :, 4 * size :] = jnp.concatenate(
            [heads_ref[:, (i * 8 + at) * few : (i * 8 + at + 1) * few] for i in range(2)]
            + [jnp.zeros((heads_ref.shape[0], 128 - 2 * few), jnp.bfloat16)],
            axis=1,
        )
        for i, ref in enumerate(feeds):
            for unit in range(4):
                source = unit // 2 * 16 + rank // 4 * 8 + unit % 2 * 4 + rank % 4
                to = (i * 4 + unit) * block
                pack_gu_ref[rank, :, to : to + block] = ref[:, source * block : (source + 1) * block]


def kernel_a(
    x_ref, seq_ref, gains_ref, cot_ref, bias_ref, wq_ref, wg_ref, wk_ref, wv_ref, wh_ref, wfg_ref, wfu_ref,
    xs_ref, lens_out, bias_out, cots_ref, h_ref, w_ref, proj_ref, gu_ref,
    lens_ref, pack_ref, pack_gu_ref, send, recv, sems,
):
    net = Net(send, recv)
    rows = x_ref.shape[0]
    rank = rank_of(net.at)
    lens_ref[...] = jnp.zeros(lens_ref.shape, jnp.int32)
    lens_ref[0:1, 0:3] = seq_ref[...]
    pack_weights((wq_ref, wg_ref, wk_ref, wv_ref), wh_ref, (wfg_ref, wfu_ref), pack_ref, pack_gu_ref)
    few = bias_ref.shape[1] // 8
    bias = jnp.zeros((1, 128), jnp.float32)
    for at in range(8):
        own = jnp.concatenate(
            [bias_ref[i : i + 1, at * few : (at + 1) * few] for i in range(2)]
            + [jnp.zeros((1, 128 - 2 * few), jnp.float32)],
            axis=1,
        )
        bias = jnp.where(slice_of(rank) == at, own, bias)
    bias_out[...] = jnp.broadcast_to(bias, bias_out.shape)
    net.greet()
    moved = move(net, [(x_ref, xs_ref), (lens_ref, lens_out)], sems)
    spread = Spread(net, w_ref, 4)
    unit = spread.unit
    packs = exchange(net, pack_ref, w_ref.at[unit])

    moved()
    value, _inverse = normed(xs_ref[...].astype(jnp.float32))
    h_ref[pl.ds(pl.multiple_of(rank * rows, rows), rows)] = swap_chunks(
        (value * gains_ref[0:1, :]).astype(jnp.bfloat16)
    )
    gather = Gather(net, h_ref, rows)
    gather.first()
    for made in packs:
        made.wait_recv()
    spread.first(4)
    moved_cot = move(net, [(cot_ref, cots_ref)], sems, 2)
    gather.second()
    spread.second(0)
    gather.third()
    spread.second(1)
    feed = exchange(net, pack_gu_ref, gu_ref)
    depth = pack_ref.shape[0] * pack_ref.shape[1]
    tall = 2 * rows

    def multiply(which, fresh):
        def one(i, _):
            at = pl.ds(pl.multiple_of(i * tall, tall), tall)
            left = h_ref[at, pl.ds(pl.multiple_of(which * depth, 128), depth)]
            part = ab(left, w_ref[which].reshape(depth, -1))
            if fresh:
                proj_ref[at, :] = part
            else:
                proj_ref[at, :] += part
            return 0

        lax.fori_loop(0, h_ref.shape[0] // tall, one, 0)

    gather.done()
    multiply(unit, True)
    spread.wait_across()
    multiply((1 - net.at["x"]) * 2 + net.at["zh"], False)
    spread.second(2)
    spread.second(3)
    multiply(spread.from_zh, False)
    for made in feed:
        made.wait_recv()
    spread.wait_corner()
    multiply((1 - net.at["x"]) * 2 + 1 - net.at["zh"], False)
    moved_cot()
    net.drain()


def whole(shape, dtype):
    return jax.ShapeDtypeStruct(shape, dtype)


def vmem(count):
    return [pl.BlockSpec(memory_space=pltpu.VMEM)] * count


def call(kernel, number, outs, args, copies, scratch=(), local=2, far=()):
    return pl.pallas_call(
        kernel,
        out_shape=outs,
        in_specs=[
            pl.BlockSpec(memory_space=pl.ANY if i in far else pltpu.VMEM) for i in range(len(args))
        ],
        out_specs=vmem(len(outs)),
        scratch_shapes=[
            *scratch,
            pltpu.SemaphoreType.DMA((copies,)),
            pltpu.SemaphoreType.DMA((copies,)),
            pltpu.SemaphoreType.DMA((local,)),
        ],
        compiler_params=pltpu.CompilerParams(
            collective_id=number, has_side_effects=True, vmem_limit_bytes=60 * 2**20
        ),
    )(*args)


class Sum:
    def __init__(self, net, part, core, near, corner):
        self.net, self.part, self.core, self.near, self.corner = net, part, core, near, corner
        self.rows = part.shape[1]
        self.half = self.rows // 2
        self.given = {}

    def place(self, names):
        at = flipped(self.net.at, names)
        return at["zl"] * 2 + at["y"]

    def rank(self, names):
        return rank_of(flipped(self.net.at, names))

    def give(self, names):
        block = self.part.at[self.rank(("core", *names))]
        self.given[names] = self.net.push(block, self.core.at[self.place(names)], ("core",))

    def take(self, names):
        self.given[names].wait_recv()
        rank = self.rank(names)
        self.part[rank] = (
            self.part[rank].astype(jnp.float32) + self.core[self.place(names)].astype(jnp.float32)
        ).astype(jnp.bfloat16)

    def rows_of(self, names, half):
        return self.part.at[self.rank(names), pl.ds(half * self.half, self.half)]

    def send_corner(self):
        self.take(("zl", "y"))
        self.by_y = [
            self.net.push(self.rows_of(("zl", "y"), half), self.corner.at[half], ("y",))
            for half in range(2)
        ]

    def send_y(self):
        self.take(("y",))
        self.near_y = self.net.push(self.part.at[self.rank(("y",))], self.near.at[0], ("y",))

    def left_cores(self):
        self.net.left(self.given.values())

    def left(self):
        self.net.left((*self.by_y, self.near_y, *self.near_zl))

    def pass_on(self):
        self.take(("zl",))
        self.near_zl = []
        for half in range(2):
            self.by_y[half].wait_recv()
            rows = self.rows_of(("zl",), half)
            rows[...] = (
                rows[...].astype(jnp.float32) + self.corner[half].astype(jnp.float32)
            ).astype(jnp.bfloat16)
            to = self.near.at[1, pl.ds(half * self.half, self.half)]
            self.near_zl.append(self.net.push(rows, to, ("zl",)))

    def total(self):
        self.given[()].wait_recv()
        own = self.part[self.rank(())].astype(jnp.float32)
        own = own + self.core[self.place(())].astype(jnp.float32)
        for made in (self.near_y, *self.near_zl):
            made.wait_recv()
        return own + self.near[0].astype(jnp.float32) + self.near[1].astype(jnp.float32)


def sum_scratch(rows, width):
    return [
        pltpu.VMEM((8, rows, width), jnp.bfloat16),
        pltpu.VMEM((4, rows, width), jnp.bfloat16),
        pltpu.VMEM((2, rows, width), jnp.bfloat16),
        pltpu.VMEM((2, rows // 2, width), jnp.bfloat16),
    ]


def move(net, pairs, sems, start=0):
    moved = net.at["core"] != net.at["zh"]
    away = [net.copy(source, target, ("core", "zh")) for source, target in pairs]
    stay = [pltpu.make_async_copy(*pair, sems.at[start + i]) for i, pair in enumerate(pairs)]

    def each(act):
        @pl.when(moved)
        def _():
            for made in away:
                act(made)

        @pl.when(jnp.logical_not(moved))
        def _():
            for made in stay:
                act(made)

    each(lambda made: made.start())
    return lambda: each(lambda made: made.wait())


def lanes(columns, size):
    lane = lax.broadcasted_iota(jnp.int32, (size, 128), 1)
    out = jnp.zeros((size, 128), jnp.float32)
    for i, column in enumerate(columns):
        out = jnp.where(lane == i, column, out)
    return out


def triangle(size, upper):
    row = lax.broadcasted_iota(jnp.int32, (size, size), 0)
    col = lax.broadcasted_iota(jnp.int32, (size, size), 1)
    return jnp.where(row <= col if upper else row >= col, 1.0, 0.0)


def exact(left, right):
    return jnp.dot(
        left, right, precision=lax.Precision.HIGHEST, preferred_element_type=jnp.float32
    )


def spread_lanes(columns, size, wide):
    which = (lax.broadcasted_iota(jnp.int32, (size, wide), 1) // 64) % 3
    return jnp.where(which == 0, columns[0], jnp.where(which == 1, columns[1], columns[2]))


def bounds(lens_ref, first_row, size):
    place = first_row + lax.broadcasted_iota(jnp.int32, (size, 1), 0)
    first = lens_ref[0:1, 0:1]
    second = first + lens_ref[0:1, 1:2]
    low = jnp.where(place >= second, second, jnp.where(place >= first, first, 0))
    return place, low


def head_rows(value, h):
    return value[:, h * 64 : (h + 1) * 64]


def with_one(value, lane_at):
    size = value.shape[0]
    lane = lax.broadcasted_iota(jnp.int32, (size, 64), 1)
    return jnp.concatenate([value, jnp.where(lane == lane_at, 1.0, 0.0)], axis=1)


def mixing(proj_ref, lens_ref, bias_ref, q_ref, k_ref, v_ref, diff_ref, stat_ref, fcol_ref, frow_ref):
    size = 128
    lower = triangle(size, False)

    def one(i, carry):
        last, below = carry
        at = pl.ds(pl.multiple_of(i * size, size), size)
        block = proj_ref[at, :]
        kv = block[:, 384:768]
        logits = block[:, 768:896] + bias_ref[0:1, :]
        logf = jax.nn.log_sigmoid(logits)
        mix = jax.nn.sigmoid(logits)
        place, low = bounds(lens_ref, i * size, size)
        row = lax.broadcasted_iota(jnp.int32, (size, 384), 0)
        prev = jnp.where(row == 0, last, pltpu.roll(kv, 1, 0))
        prev = jnp.where(place == low, 0.0, prev)
        diff = prev - kv
        diff_ref[at, :] = diff
        mixed = kv + spread_lanes([mix[:, 3 + h : 4 + h] for h in range(3)], size, 384) * diff
        decay = exact(lower, logf) + below
        frows = decay.T
        stats = []
        for h in range(3):
            q = head_rows(block, h)
            inv = lax.rsqrt(jnp.mean(q * q, axis=-1, keepdims=True) + EPS)
            stats.append(inv)
            q_ref[h, at, :] = with_one(q * inv * 0.125, 0).astype(jnp.bfloat16)
            fcol_ref[h, at, :] = jnp.broadcast_to(decay[:, h : h + 1], (size, 128))
            frow_ref[h, :, at] = frows[h : h + 1, :]
        for h in range(3):
            k = head_rows(mixed, h)
            inv = lax.rsqrt(jnp.mean(k * k, axis=-1, keepdims=True) + EPS)
            stats.append(inv)
            k_ref[h, at, :] = with_one(k * inv, 1).astype(jnp.bfloat16)
            v_ref[h, at, :] = head_rows(mixed, 3 + h).astype(jnp.bfloat16)
        shut = jax.nn.sigmoid(-logits)
        stats += [shut[:, h : h + 1] for h in range(3)]
        stats += [mix[:, 3 + h : 4 + h] for h in range(3)]
        stat_ref[at, :] = lanes(stats, size)
        return kv[size - 1 :, :], decay[size - 1 :, :]

    lax.fori_loop(
        0,
        proj_ref.shape[0] // size,
        one,
        (jnp.zeros((1, 384), jnp.float32), jnp.zeros((1, 128), jnp.float32)),
    )


def scores(h, at, start, size, keys, q_ref, k_ref, fcol_ref, frow_ref, lens_ref):
    raw = abt(q_ref[h, at, :], k_ref[h, :keys, :])
    own = jnp.concatenate([fcol_ref[h, at, :]] * (keys // 128), axis=1)
    raw = raw + own - frow_ref[h, :, :keys]
    place, low = bounds(lens_ref, start, size)
    col = lax.broadcasted_iota(jnp.int32, (size, keys), 1)
    return jnp.where((col <= place) & (col >= low), jnp.exp(raw), 0.0)


def over_blocks(body, begin, end):
    for part in range(begin, end):

        def one(n, _, part=part):
            body(n // 2, part * 256 + n % 2 * 128, (part + 1) * 256)
            return 0

        lax.fori_loop(0, 6, one, 0)


def kernel_b(
    proj_ref, lens_ref, bias_ref, x_ref, cot_ref, gains_ref, wo_ref, gu_ref, down_ref,
    q_ref, k_ref, v_ref, diff_ref, stat_ref, fcol_ref, frow_ref, gate_ref, attn_ref, a_ref,
    wo_all, gu_all, down_all, mid_ref, h_ref, cot_all,
    spread_o, part, core, near, corner, send, recv, sems,
):
    net = Net(send, recv)
    rank = rank_of(net.at)
    rows = x_ref.shape[0]
    group = proj_ref.shape[0]
    mine = pl.ds(pl.multiple_of(rank * rows, rows), rows)
    net.greet()
    out = Spread(net, spread_o, 1)
    feed = Spread(net, gu_all, 4)
    down = Spread(net, down_all, 2)
    unit = out.unit
    spread_o[unit] = wo_ref[...]
    out.first(1)
    cot_all[mine] = cot_ref[...]
    other = Gather(net, cot_all, rows)
    other.first()
    gu_all[unit] = gu_ref[...]
    down_all[unit] = down_ref[...]
    feed.first(1)
    down.first(0)
    mixing(proj_ref, lens_ref, bias_ref, q_ref, k_ref, v_ref, diff_ref, stat_ref, fcol_ref, frow_ref)
    out.second(0)
    other.second()
    feed.second(0)

    def attend(h, start, keys):
        at = pl.ds(pl.multiple_of(start, 128), 128)
        e = scores(h, at, start, 128, keys, q_ref, k_ref, fcol_ref, frow_ref, lens_ref)
        total = jnp.sum(e, axis=-1, keepdims=True)
        inv = 1.0 / total
        fcol_ref[h, at, :] -= jnp.broadcast_to(jnp.log(total), (128, 128))
        attn_ref[h, at, :] = ab((e * inv).astype(jnp.bfloat16), v_ref[h, :keys, :])

    over_blocks(attend, 0, 2)
    other.third()
    feed.second(1)
    over_blocks(attend, 2, group // 256)
    out.wait_across()
    out.wait_corner()
    pieces = []
    wo_all[unit_of(net.at, ())] = spread_o[unit_of(net.at, ())]
    for names in (("y",), ("zl",), ("zl", "y")):
        pieces.append(net.push(spread_o.at[unit_of(net.at, names)], wo_all.at[unit_of(net.at, ())], names))
    feed.second(2)
    for h in range(3):
        gate = jax.nn.sigmoid(proj_ref[:, 192 + 64 * h : 256 + 64 * h])
        gate_ref[:, 64 * h : 64 * h + 64] = gate
        a_ref[:, 64 * h : 64 * h + 64] = (gate * attn_ref[h]).astype(jnp.bfloat16)
    for made in pieces:
        made.wait_recv()

    total = Sum(net, part, core, near, corner)

    def project_block(names):
        to = rank_of(flipped(net.at, names))
        left = a_ref[pl.ds(pl.multiple_of(to * rows, rows), rows), :]
        part[to] = ab(left, wo_all[...].reshape(-1, wo_all.shape[2])).astype(jnp.bfloat16)

    for names in (("zl", "y"), ("zl",), ("y",), ()):
        project_block(("core", *names))
        total.give(names)
    project_block(("zl", "y"))
    total.send_corner()
    project_block(("zl",))
    project_block(("y",))
    total.send_y()
    project_block(())
    total.pass_on()
    feed.second(3)
    down.push_next()
    mid = x_ref[...].astype(jnp.float32) + total.total()
    mid_ref[...] = mid
    value, _inverse = normed(mid)
    h_ref[mine] = swap_chunks((value * gains_ref[1:2, :]).astype(jnp.bfloat16))
    gather = Gather(net, h_ref, rows)
    gather.first()
    down.second(0)
    gather.second()
    gather.third()
    down.second(1)
    gather.done()
    other.done()
    for job in (feed, down):
        job.wait_across()
        job.wait_corner()
    net.drain()


class SpreadSum:
    def __init__(self, net, whole_ref, over_x, over_zh, pieces, relay=None):
        self.relay = relay
        self.net, self.whole, self.over_x, self.over_zh, self.pieces = net, whole_ref, over_x, over_zh, pieces
        self.size = whole_ref.shape[1] // pieces
        self.x, self.zh = net.at["x"], net.at["zh"]
        self.far, self.own, self.last = [], [], []

    def part(self, ref, at, piece):
        return ref.at[at, pl.ds(piece * self.size, self.size)]

    def send(self, zh, target, piece):
        source = self.part(self.whole, (1 - self.x) * 2 + zh, piece)
        return self.net.push(source, target, ("x",))

    def first(self):
        for zh, to in ((1 - self.zh, self.far), (self.zh, self.own)):
            for piece in range(self.pieces):
                to.append(self.send(zh, self.part(self.over_x, zh, piece), piece))

    def pass_far(self):
        for piece in range(self.pieces):
            to = self.over_x.at[pl.ds(piece * self.size, self.size)]
            self.own.append(self.send(self.zh, to, piece))

    def pass_far_on(self, far, begin, end):
        for piece in range(begin, end):
            self.pass_one(piece, far.at[pl.ds(piece * self.size, self.size)])

    def second(self, piece):
        self.far[piece].wait_recv()
        self.pass_one(piece, self.part(self.over_x, 1 - self.zh, piece))

    def pass_one(self, piece, came):
        here = self.part(self.whole, self.x * 2 + 1 - self.zh, piece)
        total = (here[...].astype(jnp.float32) + came[...].astype(jnp.float32)).astype(jnp.bfloat16)
        if self.relay is not None:
            here = self.relay.at[pl.ds(piece * self.size, self.size)]
        here[...] = total
        target = self.over_zh.at[pl.ds(piece * self.size, self.size)]
        self.last.append(self.net.push(here, target, ("zh",)))

    def total(self, piece):
        self.own[piece].wait_recv()
        self.last[piece].wait_recv()
        here = self.part(self.whole, self.x * 2 + self.zh, piece)
        if self.relay is None:
            came = self.part(self.over_x, self.zh, piece)
        else:
            came = self.over_x.at[pl.ds(piece * self.size, self.size)]
        last = self.over_zh.at[pl.ds(piece * self.size, self.size)]
        return (
            here[...].astype(jnp.float32) + came[...].astype(jnp.float32) + last[...].astype(jnp.float32)
        )


def norm_grad(grad, gain, value, inverse):
    scaled = grad * gain
    return (
        inverse * (scaled - value * jnp.mean(scaled * value, axis=-1, keepdims=True)),
        jnp.sum(grad * value, axis=0, keepdims=True),
    )


def kernel_c(
    h_ref, cot_ref, wgu_ref, wd_ref, mid_ref, gains_ref,
    hid_ref, dmid_ref, dao_ref, gain_ref, gdown_ref, ggu_ref, gfar_ref,
    dgu_ref, gd_ref, over_x, over_zh, part, core, near, corner, send, recv, sems,
):
    net = Net(send, recv)
    rank = rank_of(net.at)
    rows = mid_ref.shape[0]
    mine = pl.ds(pl.multiple_of(rank * rows, rows), rows)
    wide = hid_ref.shape[1]
    width = mid_ref.shape[1]
    four = 4 * rows
    net.greet()

    def half(which):
        at = pl.ds(pl.multiple_of(which * four, four), four)
        wgu = wgu_ref[...].reshape(width, 2 * wide)
        both = ab(h_ref[at, :], wgu)
        gate, up = both[:, :wide], both[:, wide:]
        sig = jax.nn.sigmoid(gate)
        act = gate * sig
        hid_ref[at, :] = (act * up).astype(jnp.bfloat16)
        grad = abt(cot_ref[at, :], wd_ref[...].reshape(wide, width))
        dgate = grad * up * sig * (1.0 + gate * (1.0 - sig))
        dgu = jnp.concatenate([dgate, grad * act], axis=1).astype(jnp.bfloat16)
        dgu_ref[at, :] = dgu
        back = abt(dgu, wgu).astype(jnp.bfloat16)
        for i in range(4):
            part[which * 4 + i] = back[i * rows : (i + 1) * rows]

    total = Sum(net, part, core, near, corner)
    half(1 - net.at["core"])
    for names in (("zl", "y"), ("zl",), ("y",), ()):
        total.give(names)
    half(net.at["core"])
    total.send_corner()
    total.send_y()
    down = SpreadSum(net, gd_ref, over_x, over_zh, 2)

    def grad_down(k, _):
        left = hid_ref[:, pl.ds(pl.multiple_of(k * rows, rows), rows)]
        gd_ref[k] = atb(left, cot_ref[...]).astype(jnp.bfloat16)
        return 0

    lax.fori_loop(0, 4, grad_down, 0)
    down.first()
    total.pass_on()
    depth = width // 4

    def grad_gu(k, _):
        left = h_ref[:, pl.ds(pl.multiple_of(k * depth, depth), depth)]
        ggu_ref[k] = atb(left, dgu_ref[...]).astype(jnp.bfloat16).reshape(ggu_ref.shape[1:])
        return 0

    lax.fori_loop(0, 4, grad_gu, 0)
    feed = SpreadSum(net, ggu_ref, None, None, 1)
    far = feed.send(1 - net.at["zh"], gfar_ref, 0)
    grad = swap_chunks(total.total())
    value, inverse = normed(mid_ref[...])
    back, gain = norm_grad(grad, gains_ref[1:2, :], value, inverse)
    gain_ref[...] = gain
    dmid = cot_ref[mine, :].astype(jnp.float32) + back
    dmid_ref[...] = dmid
    dao_ref[mine] = dmid.astype(jnp.bfloat16)
    gather = Gather(net, dao_ref, rows)
    gather.first()
    down.second(0)
    down.second(1)
    gather.second()
    gather.third()
    for piece in range(2):
        gdown_ref[pl.ds(piece * rows // 2, rows // 2)] = down.total(piece)
    gather.done()
    far.wait_recv()
    net.drain()


def spread_scratch(shape):
    return [
        pltpu.VMEM((4, *shape), jnp.bfloat16),
        pltpu.VMEM((2, *shape), jnp.bfloat16),
        pltpu.VMEM(shape, jnp.bfloat16),
    ]


def unmixing(
    lens_ref, q_ref, k_ref, diff_ref, stat_ref, dq_ref, dk_ref, dv_ref, dproj_ref
):
    size = 128
    count = diff_ref.shape[0] // size
    upper = triangle(size, True)

    def one(step, carry):
        after, above, sums = carry
        i = count - 1 - step
        at = pl.ds(pl.multiple_of(i * size, size), size)
        stat = stat_ref[at, :]
        decay, keys, values = [], [], []
        for h in range(3):
            dq, dk = dq_ref[h, at, :], dk_ref[h, at, :]
            decay.append(dq[:, 65:66] - dk[:, 64:65])
            grad = dq[:, :64] * 0.125
            unit = q_ref[h, at, :][:, :64].astype(jnp.float32) * 8.0
            grad = grad - unit * jnp.mean(grad * unit, axis=-1, keepdims=True)
            dproj_ref[at, 64 * h : 64 * h + 64] = (stat[:, h : h + 1] * grad).astype(jnp.bfloat16)
            grad = dk[:, :64]
            unit = k_ref[h, at, :][:, :64].astype(jnp.float32)
            grad = grad - unit * jnp.mean(grad * unit, axis=-1, keepdims=True)
            keys.append(stat[:, 3 + h : 4 + h] * grad)
            values.append(dv_ref[h, at, :])
        both = jnp.concatenate(keys + values, axis=1)
        prod = both * diff_ref[at, :]
        mix = [stat[:, 9 + h : 10 + h] for h in range(3)]
        mixes = spread_lanes(mix, size, 384)
        place, low = bounds(lens_ref, i * size, size)
        carried = jnp.where(place == low, 0.0, both * mixes)
        row = lax.broadcasted_iota(jnp.int32, (size, 384), 0)
        later = jnp.where(row == size - 1, after, pltpu.roll(carried, size - 1, 0))
        dproj_ref[at, 384:768] = (both * (1.0 - mixes) + later).astype(jnp.bfloat16)
        decay = lanes(decay, size)
        suffix = exact(upper, decay) + above
        small = []
        for h in range(3):
            small.append(suffix[:, h : h + 1] * stat[:, 6 + h : 7 + h])
        for h in range(3):
            grad = jnp.sum(head_rows(prod, h) + head_rows(prod, 3 + h), axis=-1, keepdims=True)
            small.append(grad * mix[h] * (1.0 - mix[h]))
        small = lanes(small, size)
        dproj_ref[at, 768:896] = small.astype(jnp.bfloat16)
        above = above + jnp.sum(decay, axis=0, keepdims=True)
        return carried[:1, :], above, sums + jnp.sum(small, axis=0, keepdims=True)

    none = jnp.zeros((1, 128), jnp.float32)
    carry = lax.fori_loop(0, count, one, (jnp.zeros((1, 384), jnp.float32), none, none))
    return carry[2]


def kernel_d(
    dao_ref, wo_ref, a_ref, attn_ref, gate_ref, lens_ref, q_ref, k_ref, v_ref, diff_ref, stat_ref,
    fcol_ref, frow_ref, w_ref, h_ref, dmid_ref, x_ref, gains_ref, gain_two_ref, ggu_ref, gfar_ref,
    hid_ref, wd_ref, mid_ref,
    out_ref, gx_ref, gain_ref, bias_ref, ga_ref, go_ref, gu_ref,
    do_ref, dq_ref, dk_ref, dv_ref, dproj_ref,
    gu_x, gu_zh, a_whole, a_x, a_zh, o_raw, o_whole, o_x, o_zh, small, slots, tall, gx_own, out_own,
    part, core, near, corner, core2, near2, corner2, send, recv, sems,
):
    net = Net(send, recv)
    rank = rank_of(net.at)
    rows, width = mid_ref.shape
    group = a_ref.shape[0]
    mine = pl.ds(pl.multiple_of(rank * rows, rows), rows)
    fetch = [pltpu.make_async_copy(ref, tall, sems.at[2 + i]) for i, ref in enumerate((dao_ref, h_ref))]
    fetch[0].start()
    net.greet()
    feed = SpreadSum(net, ggu_ref, gu_x.at[0], gu_zh, 4, gu_x.at[1])
    attn = SpreadSum(net, a_whole, a_x, a_zh, 4)
    out = SpreadSum(net, o_whole, o_x, o_zh, 1)

    wo = wo_ref[...].reshape(-1, width)
    four = 4 * rows

    def half(which, left_ref, right, multiply, to):
        def one(i, _):
            at = pl.multiple_of(which * four + i * 2 * rows, 2 * rows)
            back = multiply(left_ref[pl.ds(at, 2 * rows), :], right).astype(jnp.bfloat16)
            to[which * 4 + 2 * i] = back[:rows]
            to[which * 4 + 2 * i + 1] = back[rows:]
            return 0

        lax.fori_loop(0, 2, one, 0)

    result = Sum(net, part, core2, near2, corner2)
    wd = wd_ref[...].reshape(-1, width)
    feed.pass_far()
    feed.pass_far_on(gfar_ref, 0, 2)
    half(1 - net.at["core"], hid_ref, wd, ab, part)
    for names in (("zl", "y"), ("zl",), ("y",), ()):
        result.give(names)
    half(net.at["core"], hid_ref, wd, ab, part)
    fetch[0].wait()
    da = abt(tall[...], wo)
    for h in range(3):
        sig = gate_ref[:, 64 * h : 64 * h + 64]
        grad = da[:, 64 * h : 64 * h + 64] * sig
        do_ref[h] = grad.astype(jnp.bfloat16)
        dproj_ref[:, 192 + 64 * h : 256 + 64 * h] = (grad * attn_ref[h] * (1.0 - sig)).astype(
            jnp.bfloat16
        )
    o_raw[...] = atb(a_ref[...], tall[...]).astype(jnp.bfloat16).reshape(o_raw.shape)
    fetch[1].start()
    here = unit_of(net.at, ())
    o_whole[here] = o_raw[here]
    pieces = []
    for names in (("y",), ("zl",), ("zl", "y")):
        pieces.append(net.push(o_raw.at[unit_of(net.at, names)], o_whole.at[here], names))
    dk_ref[...] = jnp.zeros(dk_ref.shape, jnp.float32)
    dv_ref[...] = jnp.zeros(dv_ref.shape, jnp.float32)

    def attend(h, start, keys):
        at = pl.ds(pl.multiple_of(start, 128), 128)
        p = scores(h, at, start, 128, keys, q_ref, k_ref, fcol_ref, frow_ref, lens_ref)
        do = do_ref[h, at, :]
        dp = abt(do, v_ref[h, :keys, :])
        ds = p * (dp - jnp.sum(p * dp, axis=-1, keepdims=True))
        ds = ds.astype(jnp.bfloat16)
        dq_ref[h, at, :] = ab(ds, k_ref[h, :keys, :])
        dk_ref[h, :keys, :] += atb(ds, q_ref[h, at, :])
        dv_ref[h, :keys, :] += atb(p.astype(jnp.bfloat16), do)

    result.send_corner()
    result.send_y()
    for made in pieces:
        made.wait_recv()
    out.first()
    over_blocks(attend, 0, 3)
    result.pass_on()
    feed.pass_far_on(gfar_ref, 2, 4)
    over_blocks(attend, 3, 4)
    out.second(0)
    result.left_cores()
    out_own[...] = (mid_ref[...] + result.total()).astype(jnp.bfloat16)
    moved_out = move(net, [(out_own, out_ref)], sems)
    sums = unmixing(lens_ref, q_ref, k_ref, diff_ref, stat_ref, dq_ref, dk_ref, dv_ref, dproj_ref)

    result.left()
    total = Sum(net, part, core, near, corner)
    w = w_ref[...].reshape(width, -1)
    half(1 - net.at["core"], dproj_ref, w, abt, part)
    for names in (("zl", "y"), ("zl",), ("y",), ()):
        total.give(names)
    half(net.at["core"], dproj_ref, w, abt, part)
    total.send_corner()
    total.send_y()
    depth = width // 4

    def grad_attn(k, _):
        left = tall[:, pl.ds(pl.multiple_of(k * depth, depth), depth)]
        a_whole[k] = atb(left, dproj_ref[...]).astype(jnp.bfloat16).reshape(a_whole.shape[1:])
        return 0

    fetch[1].wait()
    lax.fori_loop(0, 4, grad_attn, 0)
    attn.first()
    total.pass_on()
    attn.second(0)
    for piece in range(4):
        gu_zh[2 * piece : 2 * piece + 2] = feed.total(piece).astype(jnp.bfloat16)
    given = exchange(net, gu_zh, gu_ref)
    attn.second(1)
    grad = swap_chunks(total.total())
    attn.second(2)
    value, inverse = normed(x_ref[...].astype(jnp.float32))
    back, gain = norm_grad(grad, gains_ref[0:1, :], value, inverse)
    gx_own[...] = (dmid_ref[...] + back).astype(jnp.bfloat16)
    attn.second(3)
    small[0] = jnp.concatenate(
        [gain, gain_two_ref[...], jnp.concatenate([sums, jnp.zeros((1, width - 128), jnp.float32)], axis=1)]
        + [jnp.zeros((5, width), jnp.float32)],
        axis=0,
    )
    first = net.push(small.at[0], small.at[1], ("x",))
    moved_gx = move(net, [(gx_own, gx_ref)], sems, 1)
    go_ref[...] = out.total(0)
    first.wait_recv()
    small[2] = small[0] + small[1]
    second = net.push(small.at[2], small.at[3], ("zh",))
    for piece in range(4):
        a_zh[2 * piece : 2 * piece + 2] = attn.total(piece).astype(jnp.bfloat16)
    given += exchange(net, a_zh, ga_ref)
    second.wait_recv()
    slots[rank] = small[2] + small[3]
    shared = [net.push(slots.at[rank], slots.at[rank], names) for names in PARTNERS[:7]]
    for made in shared + given:
        made.wait_recv()
    gain_ref[...] = jnp.sum(slots[:, 0:2, :], axis=0)
    bias_ref[...] = slots[:, 2:3, :128]
    moved_out()
    moved_gx()
    net.drain()


def finish(
    out_ref, gx_ref, gain_ref, bias_ref, ga_ref, go_ref, gu_ref, gdown_ref,
    out_out, gx_out, gain_out, bias_out, gq_out, gk_out, gv_out, gg_out, go_out, gh_out, gfg_out, gfu_out, gdown_out,
):
    for source, target in ((out_ref, out_out), (gain_ref, gain_out), (go_ref, go_out), (gdown_ref, gdown_out)):
        target[...] = source[...]
    gx_out[...] = gx_ref[...].astype(jnp.float32)
    size = gq_out.shape[1] // 8
    few = bias_out.shape[1] // 8
    block = gfg_out.shape[1] // 32
    for rank in range(8):
        at = slice_of(rank)
        for i, target in enumerate((gq_out, gg_out, gk_out, gv_out)):
            part = ga_ref[rank, :, i * size : (i + 1) * size]
            target[:, at * size : (at + 1) * size] = part.astype(jnp.float32)
        part = ga_ref[rank, :, 4 * size :].astype(jnp.float32)
        for i in range(2):
            to = (i * 8 + at) * few
            gh_out[:, to : to + few] = part[:, i * few : (i + 1) * few]
            bias_out[i : i + 1, at * few : (at + 1) * few] = bias_ref[rank, :, i * few : (i + 1) * few]
        for i, target in enumerate((gfg_out, gfu_out)):
            for unit in range(4):
                to = (unit // 2 * 16 + rank // 4 * 8 + unit % 2 * 4 + rank % 4) * block
                part = gu_ref[rank, :, (i * 4 + unit) * block : (i * 4 + unit + 1) * block]
                target[:, to : to + block] = part.astype(jnp.float32)


def squares(
    layer_input,
    cotangent,
    seq_lengths,
    gains,
    head_bias,
    w_query,
    w_key,
    w_value,
    w_gate,
    w_out,
    w_heads,
    w_ff_gate,
    w_ff_up,
    w_ff_down,
):
    rows, width = layer_input.shape
    heads = head_bias.shape[1]
    head_dim = width // heads
    ranks = 8
    group = rows * ranks
    mine = heads // ranks
    cols = mine * head_dim
    shard = w_query.shape[0]
    units = w_ff_gate.shape[1] // ranks
    low = jnp.bfloat16
    f32 = jnp.float32
    packs = (ranks, shard, 4 * cols + 128)
    feeds = (ranks, shard, 2 * units)
    lens_shape = (8, 128)
    packed, lengths, bias, cot_own, h_one_all, w_attn, proj, gu_own = call(
        kernel_a,
        1,
        (
            whole(layer_input.shape, low),
            whole(lens_shape, jnp.int32),
            whole((8, 128), f32),
            whole(cotangent.shape, low),
            whole((group, width), low),
            whole((4, *packs), low),
            whole((group, packs[2]), f32),
            whole(feeds, low),
        ),
        (
            layer_input, seq_lengths, gains, cotangent, head_bias,
            w_query, w_gate, w_key, w_value, w_heads, w_ff_gate, w_ff_up,
        ),
        48,
        [pltpu.VMEM(lens_shape, jnp.int32), pltpu.VMEM(packs, low), pltpu.VMEM(feeds, low)],
        local=3,
    )
    (
        q_all, k_all, v_all, diff, stat, fcol, frow, gate_sig, attn3, branch_in,
        w_o, w_gu, w_d, mid, h_two_all, cot_all,
    ) = call(
        kernel_b,
        2,
        (
            whole((mine, group, 128), low),
            whole((mine, group, 128), low),
            whole((mine, group, head_dim), low),
            whole((group, 2 * cols), f32),
            whole((group, 128), f32),
            whole((mine, group, 128), f32),
            whole((mine, 1, group), f32),
            whole((group, cols), f32),
            whole((mine, group, head_dim), f32),
            whole((group, cols), low),
            whole((4, shard, width), low),
            whole((4, *feeds), low),
            whole((4, *w_ff_down.shape), low),
            whole((rows, width), f32),
            whole((group, width), low),
            whole((group, width), low),
        ),
        (proj, lengths, bias, packed, cot_own, gains, w_out, gu_own, w_ff_down),
        64,
        [pltpu.VMEM((4, shard, width), low), *sum_scratch(rows, width)],
    )
    hidden, grad_mid, grad_branch, gain_two, grad_down, grad_gu, grad_far = call(
        kernel_c,
        3,
        (
            whole((group, units), low),
            whole((rows, width), f32),
            whole((group, width), low),
            whole((1, width), f32),
            whole((rows, width), f32),
            whole((4, *feeds), low),
            whole(feeds, low),
        ),
        (h_two_all, cot_all, w_gu, w_d, mid, gains),
        48,
        [
            pltpu.VMEM((group, 2 * units), low),
            pltpu.VMEM((4, rows, width), low),
            pltpu.VMEM((2, rows, width), low),
            pltpu.VMEM((rows, width), low),
            *sum_scratch(rows, width),
        ],
    )
    result, grad_input, gain_sums, bias_sums, grad_attn_w, grad_wout, grad_gu = call(
        kernel_d,
        4,
        (
            whole((rows, width), low),
            whole((rows, width), low),
            whole((2, width), f32),
            whole((ranks, 1, 128), f32),
            whole(packs, low),
            whole((shard, width), f32),
            whole(feeds, low),
        ),
        (
            grad_branch, w_o, branch_in, attn3, gate_sig, lengths, q_all, k_all, v_all, diff, stat,
            fcol, frow, w_attn, h_one_all, grad_mid, packed, gains, gain_two, grad_gu, grad_far,
            hidden, w_d, mid,
        ),
        96,
        [
            pltpu.VMEM((mine, group, head_dim), low),
            pltpu.VMEM((mine, group, 128), f32),
            pltpu.VMEM((mine, group, 128), f32),
            pltpu.VMEM((mine, group, head_dim), f32),
            pltpu.VMEM((group, packs[2]), low),
            *spread_scratch(feeds)[1:],
            *spread_scratch(packs),
            pltpu.VMEM((4, shard, width), low),
            *spread_scratch((shard, width)),
            pltpu.VMEM((4, 8, width), f32),
            pltpu.VMEM((ranks, 8, width), f32),
            pltpu.VMEM((group, width), low),
            pltpu.VMEM((rows, width), low),
            pltpu.VMEM((rows, width), low),
            *sum_scratch(rows, width),
            *sum_scratch(rows, width)[1:],
        ],
        4,
        (0, 14),
    )

    big = whole((shard, width), f32)
    outs = (
        whole((rows, width), low),
        whole((rows, width), f32),
        whole((2, width), f32),
        whole((2, heads), f32),
        big,
        big,
        big,
        big,
        big,
        whole((shard, 2 * heads), f32),
        whole(w_ff_gate.shape, f32),
        whole(w_ff_up.shape, f32),
        whole(w_ff_down.shape, f32),
    )
    args = (result, grad_input, gain_sums, bias_sums, grad_attn_w, grad_wout, grad_gu, grad_down)
    return pl.pallas_call(
        finish,
        out_shape=outs,
        in_specs=vmem(len(args)),
        out_specs=vmem(len(outs)),
        compiler_params=pltpu.CompilerParams(vmem_limit_bytes=60 * 2**20),
    )(*args)


def solution(mesh):
    if mesh.shape["dp"] == 4 and mesh.shape["ctx"] == 8:
        body, axes, group = squares, AXES, ("x", "core")
        mesh = Mesh(np.reshape(mesh.devices, (2, 2, 2, 2, 2)), AXES)
    else:
        body, axes, group = shards, ("dp", "ctx"), "dp"
    cut = P(axes, None)
    return jax.shard_map(
        body,
        mesh=mesh,
        in_specs=(cut, cut, P(group, None), P(), P()) + (cut,) * 9,
        out_specs=(cut, cut, P(), P()) + (cut,) * 9,
        check_vma=False,
    )
```

```python
import jax
import jax.numpy as jnp
import numpy as np
from jax import lax
from jax.experimental import pallas as pl
from jax.experimental.pallas import tpu as pltpu
from jax.sharding import Mesh
from jax.sharding import PartitionSpec as P

EPS = 1e-06


def passed_along(array, axis, by):
    size = lax.axis_size(axis)
    pairs = [(i, i + by) for i in range(size) if 0 <= i + by < size]
    return lax.ppermute(array, axis, pairs)


def entering(part, axis, combine, identity, reverse):
    count = lax.axis_size(axis)
    place = lax.axis_index(axis)
    ahead = count - 1 - place if reverse else place
    gathered = lax.all_gather(part, axis)
    state = jnp.zeros_like(part) + jnp.asarray(identity, part.dtype)

    def one(step, state):
        source = count - 1 - step if reverse else step
        return combine(state, lax.dynamic_index_in_dim(gathered, source, 0, False))

    return lax.fori_loop(0, ahead, one, state)


def fetch_attention(w_query, w_key, w_value, w_gate, w_out, w_heads):
    return (
        lax.all_gather(w_query, ("dp", "ctx"), axis=0, tiled=True),
        lax.all_gather(w_key, ("dp", "ctx"), axis=0, tiled=True),
        lax.all_gather(w_value, ("dp", "ctx"), axis=0, tiled=True),
        lax.all_gather(w_gate, ("dp", "ctx"), axis=0, tiled=True),
        lax.all_gather(w_out, ("dp", "ctx"), axis=0, tiled=True),
        lax.all_gather(w_heads, ("dp", "ctx"), axis=0, tiled=True),
    )


def fetch_feed(w_ff_gate, w_ff_up, w_ff_down):
    return (
        lax.all_gather(w_ff_gate, ("dp", "ctx"), axis=0, tiled=True),
        lax.all_gather(w_ff_up, ("dp", "ctx"), axis=0, tiled=True),
        lax.all_gather(w_ff_down, ("dp", "ctx"), axis=0, tiled=True),
    )


def add_arrays(earlier, later):
    return earlier + later


def norm_back(grad, normed, inverse):
    return inverse * (grad - normed * jnp.mean(grad * normed, axis=-1, keepdims=True))


def project(left, right):
    return jnp.dot(left, right, preferred_element_type=jnp.float32)


def weight_grad(left, right):
    return jnp.einsum("ra,rb->ab", left, right, preferred_element_type=jnp.float32)


def input_grad(grad, weight):
    return jnp.einsum("rb,ab->ra", grad, weight, preferred_element_type=jnp.float32)


def shards(
    layer_input,
    cotangent,
    seq_lengths,
    gains,
    head_bias,
    w_query,
    w_key,
    w_value,
    w_gate,
    w_out,
    w_heads,
    w_ff_gate,
    w_ff_up,
    w_ff_down,
):
    rows, width = layer_input.shape
    heads = head_bias.shape[1]
    head_dim = width // heads
    spans = lax.axis_size("ctx")
    group = rows * spans
    scale = head_dim ** (-0.5)
    here = lax.axis_index("ctx")
    local_pos = here * rows + jnp.arange(rows, dtype=jnp.int32)
    key_pos = jnp.arange(group, dtype=jnp.int32)
    first = seq_lengths[0, 0]
    second = first + seq_lengths[0, 1]
    local_seg = (local_pos >= first).astype(jnp.int32) + (local_pos >= second).astype(jnp.int32)
    key_seg = (key_pos >= first).astype(jnp.int32) + (key_pos >= second).astype(jnp.int32)
    starts = (local_pos == 0) | (local_pos == first) | (local_pos == second)
    keep = (1 - starts.astype(jnp.int32)).astype(jnp.float32)[:, None]
    allowed = (local_seg[:, None] == key_seg[None, :]) & (key_pos[None, :] <= local_pos[:, None])
    x_full = layer_input.astype(jnp.float32)
    inv_one = lax.rsqrt(jnp.mean(x_full * x_full, axis=-1, keepdims=True) + EPS)
    normed_one = x_full * inv_one
    h_one = (normed_one * gains[0]).astype(jnp.bfloat16)
    full_query, full_key, full_value, full_gate, full_out, full_heads = fetch_attention(
        w_query, w_key, w_value, w_gate, w_out, w_heads
    )
    query = project(h_one, full_query)
    key_raw = project(h_one, full_key)
    value_raw = project(h_one, full_value)
    gate_raw = project(h_one, full_gate)
    head_raw = project(h_one, full_heads)
    forget_logit = head_raw[:, :heads] + head_bias[0]
    shift_logit = head_raw[:, heads:] + head_bias[1]
    log_forget = jax.nn.log_sigmoid(forget_logit)
    mix_small = jax.nn.sigmoid(shift_logit)
    mix = jnp.repeat(mix_small, head_dim, axis=1)
    prev_row = passed_along(h_one[rows - 1 :], "ctx", 1)
    key_prev = jnp.concatenate([project(prev_row, full_key), key_raw[:-1]], 0) * keep
    value_prev = jnp.concatenate([project(prev_row, full_value), value_raw[:-1]], 0) * keep
    key_mix = mix * key_prev + (1.0 - mix) * key_raw
    value_mix = mix * value_prev + (1.0 - mix) * value_raw
    query4 = query.reshape(rows, heads, head_dim)
    query_inv = lax.rsqrt(jnp.mean(query4 * query4, axis=-1, keepdims=True) + EPS)
    query_norm = query4 * query_inv
    key4 = key_mix.reshape(rows, heads, head_dim)
    key_inv = lax.rsqrt(jnp.mean(key4 * key4, axis=-1, keepdims=True) + EPS)
    key_norm = key4 * key_inv
    q_low = query_norm.astype(jnp.bfloat16)
    k_low = key_norm.reshape(rows, width).astype(jnp.bfloat16)
    v_low = value_mix.astype(jnp.bfloat16)
    local_cum = jnp.cumsum(log_forget, axis=0)
    offset = entering(
        local_cum[rows - 1], "ctx", add_arrays, jnp.zeros((heads,), jnp.float32), False
    )
    decay = local_cum + offset
    gathered_k, gathered_v, all_decay = (
        lax.all_gather(k_low.astype(jnp.float32), "ctx", axis=0, tiled=True),
        lax.all_gather(v_low.astype(jnp.float32), "ctx", axis=0, tiled=True),
        lax.all_gather(decay, "ctx", axis=0, tiled=True),
    )
    all_keys = gathered_k.astype(jnp.bfloat16).reshape(group, heads, head_dim)
    all_values = gathered_v.astype(jnp.bfloat16).reshape(group, heads, head_dim)

    def scores_of(index, keys_whole, decay_whole):
        q_part = lax.dynamic_slice_in_dim(q_low, index * 4, 4, 1)
        k_part = lax.dynamic_slice_in_dim(keys_whole, index * 4, 4, 1)
        own = lax.dynamic_slice_in_dim(decay, index * 4, 4, 1)
        far = lax.dynamic_slice_in_dim(decay_whole, index * 4, 4, 1)
        raw = jnp.einsum("rhd,ghd->hrg", q_part, k_part, preferred_element_type=jnp.float32) * scale
        raw = raw + own.T[:, :, None] - far.T[:, None, :]
        return (jnp.where(allowed[None], raw, -1e30), q_part, k_part)

    group_count = heads // 4

    def forward_step(index, carry):
        mixed, log_total = carry
        scores, q_part, k_part = scores_of(index, all_keys, all_decay)
        v_part = lax.dynamic_slice_in_dim(all_values, index * 4, 4, 1)
        top = jnp.max(scores, axis=-1, keepdims=True)
        expd = jnp.exp(scores - top)
        total = jnp.sum(expd, axis=-1, keepdims=True)
        probs = (expd / total).astype(jnp.bfloat16)
        part = jnp.einsum("hrg,ghd->rhd", probs, v_part, preferred_element_type=jnp.float32)
        mixed = lax.dynamic_update_slice_in_dim(mixed, part, index * 4, 1)
        log_total = lax.dynamic_update_slice_in_dim(
            log_total, (top + jnp.log(total))[:, :, 0].T, index * 4, 1
        )
        return (mixed, log_total)

    attn4, log_total = lax.fori_loop(
        0,
        group_count,
        forward_step,
        (jnp.zeros((rows, heads, head_dim), jnp.float32), jnp.zeros((rows, heads), jnp.float32)),
    )
    attn = attn4.reshape(rows, width)
    gate_sig = jax.nn.sigmoid(gate_raw)
    branch_in = (gate_sig * attn).astype(jnp.bfloat16)
    mid = x_full + project(branch_in, full_out)
    inv_two = lax.rsqrt(jnp.mean(mid * mid, axis=-1, keepdims=True) + EPS)
    normed_two = mid * inv_two
    h_two = (normed_two * gains[1]).astype(jnp.bfloat16)
    full_ff_gate, full_ff_up, full_ff_down = fetch_feed(w_ff_gate, w_ff_up, w_ff_down)
    ff_gate = project(h_two, full_ff_gate)
    ff_up = project(h_two, full_ff_up)
    ff_sig = jax.nn.sigmoid(ff_gate)
    hidden = (ff_gate * ff_sig * ff_up).astype(jnp.bfloat16)
    result = (mid + project(hidden, full_ff_down)).astype(jnp.bfloat16)
    full_ff_gate, full_ff_up, full_ff_down = fetch_feed(w_ff_gate, w_ff_up, w_ff_down)
    full_query, full_key, full_value, full_gate, full_out, full_heads = fetch_attention(
        w_query, w_key, w_value, w_gate, w_out, w_heads
    )
    grad_out = cotangent.astype(jnp.float32)
    grad_down = weight_grad(hidden, cotangent)
    grad_hidden = input_grad(cotangent, full_ff_down)
    grad_gate_ff = (grad_hidden * ff_up * ff_sig * (1.0 + ff_gate * (1.0 - ff_sig))).astype(
        jnp.bfloat16
    )
    grad_up_ff = (grad_hidden * (ff_gate * ff_sig)).astype(jnp.bfloat16)
    ffn_grads = (
        lax.psum_scatter(
            weight_grad(h_two, grad_gate_ff), ("dp", "ctx"), scatter_dimension=0, tiled=True
        ),
        lax.psum_scatter(
            weight_grad(h_two, grad_up_ff), ("dp", "ctx"), scatter_dimension=0, tiled=True
        ),
        lax.psum_scatter(grad_down, ("dp", "ctx"), scatter_dimension=0, tiled=True),
    )
    grad_h_two = input_grad(grad_gate_ff, full_ff_gate) + input_grad(grad_up_ff, full_ff_up)
    gain_two = jnp.sum(grad_h_two * normed_two, axis=0)
    grad_mid = norm_back(grad_h_two * gains[1], normed_two, inv_two) + grad_out
    grad_branch = grad_mid.astype(jnp.bfloat16)
    grad_wout = weight_grad(branch_in, grad_branch)
    grad_branch_in = input_grad(grad_branch, full_out)
    grad_attn = (grad_branch_in * gate_sig).astype(jnp.bfloat16).reshape(rows, heads, head_dim)
    grad_gate = (grad_branch_in * attn * gate_sig * (1.0 - gate_sig)).astype(jnp.bfloat16)
    gathered_k, gathered_v, all_decay = (
        lax.all_gather(k_low.astype(jnp.float32), "ctx", axis=0, tiled=True),
        lax.all_gather(v_low.astype(jnp.float32), "ctx", axis=0, tiled=True),
        lax.all_gather(decay, "ctx", axis=0, tiled=True),
    )
    all_keys = gathered_k.astype(jnp.bfloat16).reshape(group, heads, head_dim)
    all_values = gathered_v.astype(jnp.bfloat16).reshape(group, heads, head_dim)

    def backward_step(index, carry):
        grad_q, grad_k, grad_v, grad_own, grad_far = carry
        scores, q_part, k_part = scores_of(index, all_keys, all_decay)
        v_part = lax.dynamic_slice_in_dim(all_values, index * 4, 4, 1)
        lse = lax.dynamic_slice_in_dim(log_total, index * 4, 4, 1).T[:, :, None]
        probs = jnp.exp(scores - lse)
        probs_low = probs.astype(jnp.bfloat16)
        grad_part = lax.dynamic_slice_in_dim(grad_attn, index * 4, 4, 1)
        grad_probs = jnp.einsum(
            "rhd,ghd->hrg", grad_part, v_part, preferred_element_type=jnp.float32
        )
        value_term = jnp.einsum(
            "hrg,rhd->ghd", probs_low, grad_part, preferred_element_type=jnp.float32
        )
        grad_scores = (
            probs * (grad_probs - jnp.sum(probs * grad_probs, axis=-1, keepdims=True))
        ).astype(jnp.bfloat16)
        query_term = (
            jnp.einsum("hrg,ghd->rhd", grad_scores, k_part, preferred_element_type=jnp.float32)
            * scale
        )
        key_term = (
            jnp.einsum("hrg,rhd->ghd", grad_scores, q_part, preferred_element_type=jnp.float32)
            * scale
        )
        scores_full = grad_scores.astype(jnp.float32)
        own_term = jnp.sum(scores_full, axis=-1).T
        far_term = -jnp.sum(scores_full, axis=1).T
        grad_q = lax.dynamic_update_slice_in_dim(grad_q, query_term, index * 4, 1)
        grad_k = lax.dynamic_update_slice_in_dim(grad_k, key_term, index * 4, 1)
        grad_v = lax.dynamic_update_slice_in_dim(grad_v, value_term, index * 4, 1)
        grad_own = lax.dynamic_update_slice_in_dim(grad_own, own_term, index * 4, 1)
        grad_far = lax.dynamic_update_slice_in_dim(grad_far, far_term, index * 4, 1)
        return (grad_q, grad_k, grad_v, grad_own, grad_far)

    grad_q, grad_k, grad_v, grad_own, grad_far = lax.fori_loop(
        0,
        group_count,
        backward_step,
        (
            jnp.zeros((rows, heads, head_dim), jnp.float32),
            jnp.zeros((group, heads, head_dim), jnp.float32),
            jnp.zeros((group, heads, head_dim), jnp.float32),
            jnp.zeros((rows, heads), jnp.float32),
            jnp.zeros((group, heads), jnp.float32),
        ),
    )
    grad_k_local, grad_v_local, grad_far_local = (
        lax.psum_scatter(grad_k, "ctx", scatter_dimension=0, tiled=True),
        lax.psum_scatter(grad_v, "ctx", scatter_dimension=0, tiled=True),
        lax.psum_scatter(grad_far, "ctx", scatter_dimension=0, tiled=True),
    )
    grad_decay = grad_own + grad_far_local
    local_rev = jnp.flip(jnp.cumsum(jnp.flip(grad_decay, 0), axis=0), 0)
    later = entering(
        jnp.sum(grad_decay, axis=0), "ctx", add_arrays, jnp.zeros((heads,), jnp.float32), True
    )
    grad_forget_logit = (local_rev + later) * jax.nn.sigmoid(-forget_logit)
    grad_query = norm_back(grad_q, query_norm, query_inv).reshape(rows, width)
    grad_key_mix = norm_back(grad_k_local, key_norm, key_inv).reshape(rows, width)
    grad_value_mix = grad_v_local.reshape(rows, width)
    grad_mix = jnp.sum(
        (grad_key_mix * (key_prev - key_raw) + grad_value_mix * (value_prev - value_raw)).reshape(
            rows, heads, head_dim
        ),
        axis=-1,
    )
    grad_shift_logit = grad_mix * mix_small * (1.0 - mix_small)
    carried_key = grad_key_mix * mix * keep
    carried_value = grad_value_mix * mix * keep
    from_next = passed_along(jnp.concatenate([carried_key[:1], carried_value[:1]], 0), "ctx", -1)
    grad_key_raw = (
        grad_key_mix * (1.0 - mix) + jnp.concatenate([carried_key[1:], from_next[:1]], 0)
    ).astype(jnp.bfloat16)
    grad_value_raw = (
        grad_value_mix * (1.0 - mix) + jnp.concatenate([carried_value[1:], from_next[1:]], 0)
    ).astype(jnp.bfloat16)
    grad_query_low = grad_query.astype(jnp.bfloat16)
    grad_head = jnp.concatenate([grad_forget_logit, grad_shift_logit], axis=1).astype(jnp.bfloat16)
    attn_grads = (
        lax.psum_scatter(
            weight_grad(h_one, grad_query_low), ("dp", "ctx"), scatter_dimension=0, tiled=True
        ),
        lax.psum_scatter(
            weight_grad(h_one, grad_key_raw), ("dp", "ctx"), scatter_dimension=0, tiled=True
        ),
        lax.psum_scatter(
            weight_grad(h_one, grad_value_raw), ("dp", "ctx"), scatter_dimension=0, tiled=True
        ),
        lax.psum_scatter(
            weight_grad(h_one, grad_gate), ("dp", "ctx"), scatter_dimension=0, tiled=True
        ),
        lax.psum_scatter(grad_wout, ("dp", "ctx"), scatter_dimension=0, tiled=True),
        lax.psum_scatter(
            weight_grad(h_one, grad_head), ("dp", "ctx"), scatter_dimension=0, tiled=True
        ),
    )
    grad_h_one = (
        input_grad(grad_query_low, full_query)
        + input_grad(grad_key_raw, full_key)
        + input_grad(grad_value_raw, full_value)
        + input_grad(grad_gate, full_gate)
        + input_grad(grad_head, full_heads)
    )
    gain_one = jnp.sum(grad_h_one * normed_one, axis=0)
    grad_input = norm_back(grad_h_one * gains[0], normed_one, inv_one) + grad_mid
    small = lax.psum(
        (
            jnp.stack([gain_one, gain_two]),
            jnp.stack([jnp.sum(grad_forget_logit, axis=0), jnp.sum(grad_shift_logit, axis=0)]),
        ),
        ("dp", "ctx"),
    )
    return (
        result,
        grad_input,
        small[0],
        small[1],
        attn_grads[0],
        attn_grads[1],
        attn_grads[2],
        attn_grads[3],
        attn_grads[4],
        attn_grads[5],
        ffn_grads[0],
        ffn_grads[1],
        ffn_grads[2],
    )


AXES = ("x", "core", "zh", "zl", "y")

def dot(left, right, dims):
    return lax.dot_general(left, right, (dims, ((), ())), preferred_element_type=jnp.float32)


def ab(left, right):
    return dot(left, right, ((1,), (0,)))


def abt(left, right):
    return dot(left, right, ((1,), (1,)))


def atb(left, right):
    return dot(left, right, ((0,), (0,)))


MESH = pl.DeviceIdType.MESH


class Net:
    def __init__(self, send, recv):
        self.send, self.recv, self.count, self.open = send, recv, 0, []
        self.at = {name: lax.axis_index(name) for name in AXES}

    def flip(self, names):
        return {name: 1 - self.at[name] for name in names}

    def greet(self):
        barrier = pltpu.get_barrier_semaphore()
        for names in PARTNERS:
            pl.semaphore_signal(barrier, 1, device_id=self.flip(names), device_id_type=MESH)
        moved = self.at["core"] != self.at["zh"]

        @pl.when(moved)
        def _():
            other = self.flip(("core", "zh"))
            pl.semaphore_signal(barrier, 1, device_id=other, device_id_type=MESH)
            pl.semaphore_wait(barrier, len(PARTNERS) + 1)

        @pl.when(jnp.logical_not(moved))
        def _():
            pl.semaphore_wait(barrier, len(PARTNERS))

    def copy(self, source, target, names):
        i = self.count
        self.count += 1
        return pltpu.make_async_remote_copy(
            source,
            target,
            self.send.at[i],
            self.recv.at[i],
            device_id=self.flip(names),
            device_id_type=MESH,
        )

    def push(self, source, target, names):
        made = self.copy(source, target, names)
        made.start()
        self.open.append(made)
        return made

    def left(self, copies):
        for made in copies:
            made.wait_send()
            self.open = [other for other in self.open if other is not made]

    def drain(self):
        for made in self.open:
            made.wait_send()


PARTNERS = (
    ("y",),
    ("zl",),
    ("zl", "y"),
    ("core",),
    ("core", "y"),
    ("core", "zl"),
    ("core", "zl", "y"),
    ("x",),
    ("zh",),
)


def rank_of(at):
    return (at["core"] * 2 + at["zl"]) * 2 + at["y"]


def flipped(at, names):
    return {name: 1 - at[name] if name in names else at[name] for name in at}


def unit_of(at, names):
    at = flipped(at, names)
    return at["zl"] * 2 + at["y"]


class Gather:
    def __init__(self, net, ref, rows):
        self.net, self.ref, self.rows = net, ref, rows

    def part(self, names, half=None):
        start = rank_of(flipped(self.net.at, names)) * self.rows
        size = self.rows
        if half is not None:
            size = self.rows // 2
            start = start + half * size
        return self.ref.at[pl.ds(pl.multiple_of(start, size), size)]

    def send(self, block, half, to):
        part = self.part(block, half)
        return self.net.push(part, part, to)

    def first(self):
        self.along = [self.send((), half, ("zl",)) for half in range(2)]
        self.near = self.send((), None, ("y",))
        self.cores = [self.send((), None, ("core",))]

    def second(self):
        self.corner = []
        for half in range(2):
            self.along[half].wait_recv()
            self.corner.append(self.send(("zl",), half, ("y",)))
        self.cores.append(self.send(("zl",), None, ("core",)))
        self.near.wait_recv()
        self.cores.append(self.send(("y",), None, ("core",)))

    def third(self):
        for made in self.corner:
            made.wait_recv()
        self.cores.append(self.send(("zl", "y"), None, ("core",)))

    def done(self):
        for made in self.cores:
            made.wait_recv()


class Spread:
    def __init__(self, net, ref, pieces):
        self.net, self.ref, self.pieces = net, ref, pieces
        self.size = ref.shape[1] // pieces
        self.unit = net.at["x"] * 2 + net.at["zh"]
        self.from_zh = net.at["x"] * 2 + 1 - net.at["zh"]

    def send(self, unit, piece, to):
        part = self.ref.at[unit, pl.ds(piece * self.size, self.size)]
        return self.net.push(part, part, to)

    def first(self, ahead):
        self.along, self.across, self.corner = [], [], []
        for piece in range(self.pieces):
            if piece < ahead:
                self.along.append(self.send(self.unit, piece, ("zh",)))
            self.across.append(self.send(self.unit, piece, ("x",)))

    def second(self, piece):
        self.along[piece].wait_recv()
        self.corner.append(self.send(self.from_zh, piece, ("x",)))
        if len(self.along) < self.pieces:
            self.push_next()

    def push_next(self):
        self.along.append(self.send(self.unit, len(self.along), ("zh",)))

    def wait_across(self):
        for made in self.across:
            made.wait_recv()

    def wait_corner(self):
        for made in self.corner:
            made.wait_recv()


def exchange(net, source, target):
    rank = rank_of(net.at)
    target[rank] = source[rank]
    made = []
    for names in PARTNERS[:7]:
        to = rank_of(flipped(net.at, names))
        made.append(net.push(source.at[to], target.at[rank], names))
    return made


def swap_chunks(value):
    size = value.shape[1] // 8
    order = (0, 2, 1, 3, 4, 6, 5, 7)
    return jnp.concatenate([value[:, i * size : (i + 1) * size] for i in order], axis=1)


def normed(value):
    inverse = lax.rsqrt(jnp.mean(value * value, axis=-1, keepdims=True) + EPS)
    return value * inverse, inverse


def slice_of(rank):
    return rank // 2 % 2 * 4 + rank // 4 * 2 + rank % 2


def pack_weights(wide, heads_ref, feeds, pack_ref, pack_gu_ref):
    size = wide[0].shape[1] // 8
    few = heads_ref.shape[1] // 16
    block = feeds[0].shape[1] // 32
    for rank in range(8):
        at = slice_of(rank)
        for i, ref in enumerate(wide):
            pack_ref[rank, :, i * size : (i + 1) * size] = ref[:, at * size : (at + 1) * size]
        pack_ref[rank, :, 4 * size :] = jnp.concatenate(
            [heads_ref[:, (i * 8 + at) * few : (i * 8 + at + 1) * few] for i in range(2)]
            + [jnp.zeros((heads_ref.shape[0], 128 - 2 * few), jnp.bfloat16)],
            axis=1,
        )
        for i, ref in enumerate(feeds):
            for unit in range(4):
                source = unit // 2 * 16 + rank // 4 * 8 + unit % 2 * 4 + rank % 4
                to = (i * 4 + unit) * block
                pack_gu_ref[rank, :, to : to + block] = ref[:, source * block : (source + 1) * block]


def whole(shape, dtype):
    return jax.ShapeDtypeStruct(shape, dtype)


def vmem(count):
    return [pl.BlockSpec(memory_space=pltpu.VMEM)] * count


def call(kernel, number, outs, args, copies, scratch=(), local=2, far=(), far_outs=()):
    return pl.pallas_call(
        kernel,
        out_shape=outs,
        in_specs=[
            pl.BlockSpec(memory_space=pl.ANY if i in far else pltpu.VMEM) for i in range(len(args))
        ],
        out_specs=[
            pl.BlockSpec(memory_space=pl.ANY if i in far_outs else pltpu.VMEM) for i in range(len(outs))
        ],
        scratch_shapes=[
            *scratch,
            pltpu.SemaphoreType.DMA((copies,)),
            pltpu.SemaphoreType.DMA((copies,)),
            pltpu.SemaphoreType.DMA((local,)),
        ],
        compiler_params=pltpu.CompilerParams(
            collective_id=number, has_side_effects=True, vmem_limit_bytes=60 * 2**20
        ),
    )(*args)


class Sum:
    def __init__(self, net, part, core, near, corner):
        self.net, self.part, self.core, self.near, self.corner = net, part, core, near, corner
        self.rows = part.shape[1]
        self.half = self.rows // 2
        self.given = {}

    def place(self, names):
        at = flipped(self.net.at, names)
        return at["zl"] * 2 + at["y"]

    def rank(self, names):
        return rank_of(flipped(self.net.at, names))

    def give(self, names):
        block = self.part.at[self.rank(("core", *names))]
        self.given[names] = self.net.push(block, self.core.at[self.place(names)], ("core",))

    def take(self, names):
        self.given[names].wait_recv()
        rank = self.rank(names)
        self.part[rank] = (
            self.part[rank].astype(jnp.float32) + self.core[self.place(names)].astype(jnp.float32)
        ).astype(jnp.bfloat16)

    def rows_of(self, names, half):
        return self.part.at[self.rank(names), pl.ds(half * self.half, self.half)]

    def send_corner(self):
        self.take(("zl", "y"))
        self.by_y = [
            self.net.push(self.rows_of(("zl", "y"), half), self.corner.at[half], ("y",))
            for half in range(2)
        ]

    def send_y(self):
        self.take(("y",))
        self.near_y = self.net.push(self.part.at[self.rank(("y",))], self.near.at[0], ("y",))

    def left_cores(self):
        self.net.left(self.given.values())

    def left(self):
        self.net.left((*self.by_y, self.near_y, *self.near_zl))

    def pass_on(self):
        self.take(("zl",))
        self.near_zl = []
        for half in range(2):
            self.by_y[half].wait_recv()
            rows = self.rows_of(("zl",), half)
            rows[...] = (
                rows[...].astype(jnp.float32) + self.corner[half].astype(jnp.float32)
            ).astype(jnp.bfloat16)
            to = self.near.at[1, pl.ds(half * self.half, self.half)]
            self.near_zl.append(self.net.push(rows, to, ("zl",)))

    def total(self):
        self.given[()].wait_recv()
        own = self.part[self.rank(())].astype(jnp.float32)
        own = own + self.core[self.place(())].astype(jnp.float32)
        for made in (self.near_y, *self.near_zl):
            made.wait_recv()
        return own + self.near[0].astype(jnp.float32) + self.near[1].astype(jnp.float32)


def sum_scratch(rows, width):
    return [
        pltpu.VMEM((8, rows, width), jnp.bfloat16),
        pltpu.VMEM((4, rows, width), jnp.bfloat16),
        pltpu.VMEM((2, rows, width), jnp.bfloat16),
        pltpu.VMEM((2, rows // 2, width), jnp.bfloat16),
    ]


def move(net, pairs, sems, start=0):
    moved = net.at["core"] != net.at["zh"]
    away = [net.copy(source, target, ("core", "zh")) for source, target in pairs]
    stay = [pltpu.make_async_copy(*pair, sems.at[start + i]) for i, pair in enumerate(pairs)]

    def each(act):
        @pl.when(moved)
        def _():
            for made in away:
                act(made)

        @pl.when(jnp.logical_not(moved))
        def _():
            for made in stay:
                act(made)

    each(lambda made: made.start())
    return lambda: each(lambda made: made.wait())


def lanes(columns, size):
    lane = lax.broadcasted_iota(jnp.int32, (size, 128), 1)
    out = jnp.zeros((size, 128), jnp.float32)
    for i, column in enumerate(columns):
        out = jnp.where(lane == i, column, out)
    return out


def triangle(size, upper):
    row = lax.broadcasted_iota(jnp.int32, (size, size), 0)
    col = lax.broadcasted_iota(jnp.int32, (size, size), 1)
    return jnp.where(row <= col if upper else row >= col, 1.0, 0.0)


def exact(left, right):
    return jnp.dot(
        left, right, precision=lax.Precision.HIGHEST, preferred_element_type=jnp.float32
    )


def spread_lanes(columns, size, wide):
    which = (lax.broadcasted_iota(jnp.int32, (size, wide), 1) // 64) % 3
    return jnp.where(which == 0, columns[0], jnp.where(which == 1, columns[1], columns[2]))


def bounds(lens_ref, first_row, size):
    place = first_row + lax.broadcasted_iota(jnp.int32, (size, 1), 0)
    first = lens_ref[0:1, 0:1]
    second = first + lens_ref[0:1, 1:2]
    low = jnp.where(place >= second, second, jnp.where(place >= first, first, 0))
    return place, low


def head_rows(value, h):
    return value[:, h * 64 : (h + 1) * 64]


def with_one(value, lane_at):
    size = value.shape[0]
    lane = lax.broadcasted_iota(jnp.int32, (size, 64), 1)
    return jnp.concatenate([value, jnp.where(lane == lane_at, 1.0, 0.0)], axis=1)


def mixing(proj_ref, lens_ref, bias_ref, q_ref, k_ref, v_ref, diff_ref, stat_ref, fcol_ref, frow_ref):
    size = 128
    lower = triangle(size, False)

    def one(i, carry):
        last, below = carry
        at = pl.ds(pl.multiple_of(i * size, size), size)
        block = proj_ref[at, :]
        kv = block[:, 384:768]
        logits = block[:, 768:896] + bias_ref[0:1, :]
        logf = jax.nn.log_sigmoid(logits)
        mix = jax.nn.sigmoid(logits)
        place, low = bounds(lens_ref, i * size, size)
        row = lax.broadcasted_iota(jnp.int32, (size, 384), 0)
        prev = jnp.where(row == 0, last, pltpu.roll(kv, 1, 0))
        prev = jnp.where(place == low, 0.0, prev)
        diff = prev - kv
        diff_ref[at, :] = diff
        mixed = kv + spread_lanes([mix[:, 3 + h : 4 + h] for h in range(3)], size, 384) * diff
        decay = exact(lower, logf) + below
        frows = decay.T
        stats = []
        for h in range(3):
            q = head_rows(block, h)
            inv = lax.rsqrt(jnp.mean(q * q, axis=-1, keepdims=True) + EPS)
            stats.append(inv)
            q_ref[h, at, :] = with_one(q * inv * 0.125, 0).astype(jnp.bfloat16)
            fcol_ref[h, at, :] = jnp.broadcast_to(decay[:, h : h + 1], (size, 128))
            frow_ref[h, :, at] = frows[h : h + 1, :]
        for h in range(3):
            k = head_rows(mixed, h)
            inv = lax.rsqrt(jnp.mean(k * k, axis=-1, keepdims=True) + EPS)
            stats.append(inv)
            k_ref[h, at, :] = with_one(k * inv, 1).astype(jnp.bfloat16)
            v_ref[h, at, :] = head_rows(mixed, 3 + h).astype(jnp.bfloat16)
        shut = jax.nn.sigmoid(-logits)
        stats += [shut[:, h : h + 1] for h in range(3)]
        stats += [mix[:, 3 + h : 4 + h] for h in range(3)]
        stat_ref[at, :] = lanes(stats, size)
        return kv[size - 1 :, :], decay[size - 1 :, :]

    lax.fori_loop(
        0,
        proj_ref.shape[0] // size,
        one,
        (jnp.zeros((1, 384), jnp.float32), jnp.zeros((1, 128), jnp.float32)),
    )


def scores(h, at, start, size, keys, q_ref, k_ref, fcol_ref, frow_ref, lens_ref):
    raw = abt(q_ref[h, at, :], k_ref[h, :keys, :])
    own = jnp.concatenate([fcol_ref[h, at, :]] * (keys // 128), axis=1)
    raw = raw + own - frow_ref[h, :, :keys]
    place, low = bounds(lens_ref, start, size)
    col = lax.broadcasted_iota(jnp.int32, (size, keys), 1)
    return jnp.where((col <= place) & (col >= low), jnp.exp(raw), 0.0)


def over_blocks(body, begin, end):
    for part in range(begin, end):

        def one(n, _, part=part):
            body(n // 2, part * 256 + n % 2 * 128, (part + 1) * 256)
            return 0

        lax.fori_loop(0, 6, one, 0)


def kernel_ab(
    x_ref, seq_ref, gains_ref, cot_ref, head_bias_ref, wq_ref, wg_ref, wk_ref, wv_ref, wh_ref, wfg_ref, wfu_ref,
    wo_ref, down_ref, xs_ref, lens_ref, mid_ref, *refs,
):
    far, refs = refs[:17], refs[17:]
    near_refs, refs = refs[:17], refs[17:]
    (
        h_ref, w_ref, q_ref, k_ref, v_ref, diff_ref, stat_ref, fcol_ref, frow_ref, gate_ref, attn_ref, a_ref,
        wo_all, gu_all, down_all, h2_ref, cot_all,
    ) = near_refs
    (
        lens_own, bias_ref, proj_ref, pack_ref, pack_gu_ref, spread_o,
        part, core, near, corner, send, recv, sems,
    ) = refs
    kept = []

    def keep(i):
        made = pltpu.make_async_copy(near_refs[i], far[i], sems.at[3 + i])
        made.start()
        kept.append(made)

    net = Net(send, recv)
    rows = x_ref.shape[0]
    rank = rank_of(net.at)
    lens_own[...] = jnp.zeros(lens_own.shape, jnp.int32)
    lens_own[0:1, 0:3] = seq_ref[...]
    pack_weights((wq_ref, wg_ref, wk_ref, wv_ref), wh_ref, (wfg_ref, wfu_ref), pack_ref, pack_gu_ref)
    few = head_bias_ref.shape[1] // 8
    bias = jnp.zeros((1, 128), jnp.float32)
    for at in range(8):
        own = jnp.concatenate(
            [head_bias_ref[i : i + 1, at * few : (at + 1) * few] for i in range(2)]
            + [jnp.zeros((1, 128 - 2 * few), jnp.float32)],
            axis=1,
        )
        bias = jnp.where(slice_of(rank) == at, own, bias)
    bias_ref[...] = jnp.broadcast_to(bias, bias_ref.shape)
    net.greet()
    moved = move(net, [(x_ref, xs_ref), (lens_own, lens_ref)], sems)
    spread = Spread(net, w_ref, 4)
    unit = spread.unit
    packs = exchange(net, pack_ref, w_ref.at[unit])

    moved()
    value, _inverse = normed(xs_ref[...].astype(jnp.float32))
    h_ref[pl.ds(pl.multiple_of(rank * rows, rows), rows)] = swap_chunks(
        (value * gains_ref[0:1, :]).astype(jnp.bfloat16)
    )
    gather = Gather(net, h_ref, rows)
    gather.first()
    for made in packs:
        made.wait_recv()
    spread.first(4)
    there = (net.at["zh"] * 2 + net.at["zl"]) * 2 + net.at["y"]
    there = pl.ds(pl.multiple_of(there * rows, rows), rows)
    moved_cot = move(net, [(cot_ref, cot_all.at[there])], sems, 2)
    out = Spread(net, spread_o, 1)
    spread_o[unit] = wo_ref[...]
    out.first(1)
    gather.second()
    spread.second(0)
    gather.third()
    spread.second(1)
    given = exchange(net, pack_gu_ref, gu_all.at[unit])
    depth = pack_ref.shape[0] * pack_ref.shape[1]
    tall = 2 * rows

    def multiply(which, fresh):
        def one(i, _):
            at = pl.ds(pl.multiple_of(i * tall, tall), tall)
            left = h_ref[at, pl.ds(pl.multiple_of(which * depth, 128), depth)]
            part = ab(left, w_ref[which].reshape(depth, -1))
            if fresh:
                proj_ref[at, :] = part
            else:
                proj_ref[at, :] += part
            return 0

        lax.fori_loop(0, h_ref.shape[0] // tall, one, 0)

    gather.done()
    keep(0)
    multiply(unit, True)
    spread.wait_across()
    multiply((1 - net.at["x"]) * 2 + net.at["zh"], False)
    spread.second(2)
    spread.second(3)
    multiply(spread.from_zh, False)
    spread.wait_corner()
    multiply((1 - net.at["x"]) * 2 + 1 - net.at["zh"], False)
    keep(1)
    group = proj_ref.shape[0]
    mine = pl.ds(pl.multiple_of(rank * rows, rows), rows)
    feed = Spread(net, gu_all, 4)
    down = Spread(net, down_all, 2)
    moved_cot()
    other = Gather(net, cot_all, rows)
    other.first()
    down_all[unit] = down_ref[...]
    for made in given:
        made.wait_recv()
    feed.first(2)
    down.first(0)
    mixing(proj_ref, lens_ref, bias_ref, q_ref, k_ref, v_ref, diff_ref, stat_ref, fcol_ref, frow_ref)
    for i in (2, 3, 4, 5, 6, 8):
        keep(i)
    out.second(0)
    other.second()

    def attend(h, start, keys):
        at = pl.ds(pl.multiple_of(start, 128), 128)
        e = scores(h, at, start, 128, keys, q_ref, k_ref, fcol_ref, frow_ref, lens_ref)
        total = jnp.sum(e, axis=-1, keepdims=True)
        inv = 1.0 / total
        fcol_ref[h, at, :] -= jnp.broadcast_to(jnp.log(total), (128, 128))
        attn_ref[h, at, :] = ab((e * inv).astype(jnp.bfloat16), v_ref[h, :keys, :])

    over_blocks(attend, 0, 2)
    other.third()
    out.wait_across()
    out.wait_corner()
    pieces = []
    wo_all[unit_of(net.at, ())] = spread_o[unit_of(net.at, ())]
    for names in (("y",), ("zl",), ("zl", "y")):
        pieces.append(net.push(spread_o.at[unit_of(net.at, names)], wo_all.at[unit_of(net.at, ())], names))
    feed.second(0)
    over_blocks(attend, 2, group // 256)
    feed.second(1)
    for h in range(3):
        gate = jax.nn.sigmoid(proj_ref[:, 192 + 64 * h : 256 + 64 * h])
        gate_ref[:, 64 * h : 64 * h + 64] = gate
        a_ref[:, 64 * h : 64 * h + 64] = (gate * attn_ref[h]).astype(jnp.bfloat16)
    for made in pieces:
        made.wait_recv()
    for i in (7, 9, 10, 11, 12):
        keep(i)

    total = Sum(net, part, core, near, corner)

    def project_block(names):
        to = rank_of(flipped(net.at, names))
        left = a_ref[pl.ds(pl.multiple_of(to * rows, rows), rows), :]
        part[to] = ab(left, wo_all[...].reshape(-1, wo_all.shape[2])).astype(jnp.bfloat16)

    for names in (("zl", "y"), ("zl",), ("y",), ()):
        project_block(("core", *names))
        total.give(names)
    project_block(("zl", "y"))
    total.send_corner()
    project_block(("zl",))
    project_block(("y",))
    total.send_y()
    project_block(())
    total.pass_on()
    feed.second(2)
    down.push_next()
    other.done()
    keep(16)
    mid = xs_ref[...].astype(jnp.float32) + total.total()
    mid_ref[...] = mid
    value, _inverse = normed(mid)
    h2_ref[mine] = swap_chunks((value * gains_ref[1:2, :]).astype(jnp.bfloat16))
    gather = Gather(net, h2_ref, rows)
    gather.first()
    feed.second(3)
    down.second(0)
    gather.second()
    feed.wait_across()
    feed.wait_corner()
    keep(13)
    gather.third()
    down.second(1)
    gather.done()
    keep(15)
    down.wait_across()
    down.wait_corner()
    keep(14)
    for made in kept:
        made.wait()
    net.drain()


class SpreadSum:
    def __init__(self, net, whole_ref, over_x, over_zh, pieces, relay=None):
        self.relay = relay
        self.net, self.whole, self.over_x, self.over_zh, self.pieces = net, whole_ref, over_x, over_zh, pieces
        self.size = whole_ref.shape[1] // pieces
        self.x, self.zh = net.at["x"], net.at["zh"]
        self.far, self.own, self.last = [], [], []

    def part(self, ref, at, piece):
        return ref.at[at, pl.ds(piece * self.size, self.size)]

    def send(self, zh, target, piece):
        source = self.part(self.whole, (1 - self.x) * 2 + zh, piece)
        return self.net.push(source, target, ("x",))

    def first(self):
        for zh, to in ((1 - self.zh, self.far), (self.zh, self.own)):
            for piece in range(self.pieces):
                to.append(self.send(zh, self.part(self.over_x, zh, piece), piece))

    def pass_far(self):
        for piece in range(self.pieces):
            to = self.over_x.at[pl.ds(piece * self.size, self.size)]
            self.own.append(self.send(self.zh, to, piece))

    def pass_far_on(self, far, begin, end):
        for piece in range(begin, end):
            self.pass_one(piece, far.at[pl.ds(piece * self.size, self.size)])

    def second(self, piece):
        self.far[piece].wait_recv()
        self.pass_one(piece, self.part(self.over_x, 1 - self.zh, piece))

    def pass_one(self, piece, came):
        here = self.part(self.whole, self.x * 2 + 1 - self.zh, piece)
        total = (here[...].astype(jnp.float32) + came[...].astype(jnp.float32)).astype(jnp.bfloat16)
        if self.relay is not None:
            here = self.relay.at[pl.ds(piece * self.size, self.size)]
        here[...] = total
        target = self.over_zh.at[pl.ds(piece * self.size, self.size)]
        self.last.append(self.net.push(here, target, ("zh",)))

    def total(self, piece):
        self.own[piece].wait_recv()
        self.last[piece].wait_recv()
        here = self.part(self.whole, self.x * 2 + self.zh, piece)
        if self.relay is None:
            came = self.part(self.over_x, self.zh, piece)
        else:
            came = self.over_x.at[pl.ds(piece * self.size, self.size)]
        last = self.over_zh.at[pl.ds(piece * self.size, self.size)]
        return (
            here[...].astype(jnp.float32) + came[...].astype(jnp.float32) + last[...].astype(jnp.float32)
        )


def norm_grad(grad, gain, value, inverse):
    scaled = grad * gain
    return (
        inverse * (scaled - value * jnp.mean(scaled * value, axis=-1, keepdims=True)),
        jnp.sum(grad * value, axis=0, keepdims=True),
    )


def kernel_c(
    h_ref, cot_ref, wgu_ref, wd_ref, mid_ref, gains_ref,
    hid_ref, dmid_ref, dao_ref, gain_ref, gdown_ref, ggu_ref, gfar_ref,
    dgu_ref, gd_ref, over_x, over_zh, part, core, near, corner, send, recv, sems,
):
    net = Net(send, recv)
    rank = rank_of(net.at)
    rows = mid_ref.shape[0]
    mine = pl.ds(pl.multiple_of(rank * rows, rows), rows)
    wide = hid_ref.shape[1]
    width = mid_ref.shape[1]
    four = 4 * rows
    net.greet()

    def half(which):
        at = pl.ds(pl.multiple_of(which * four, four), four)
        wgu = wgu_ref[...].reshape(width, 2 * wide)
        both = ab(h_ref[at, :], wgu)
        gate, up = both[:, :wide], both[:, wide:]
        sig = jax.nn.sigmoid(gate)
        act = gate * sig
        hid_ref[at, :] = (act * up).astype(jnp.bfloat16)
        grad = abt(cot_ref[at, :], wd_ref[...].reshape(wide, width))
        dgate = grad * up * sig * (1.0 + gate * (1.0 - sig))
        dgu = jnp.concatenate([dgate, grad * act], axis=1).astype(jnp.bfloat16)
        dgu_ref[at, :] = dgu
        back = abt(dgu, wgu).astype(jnp.bfloat16)
        for i in range(4):
            part[which * 4 + i] = back[i * rows : (i + 1) * rows]

    total = Sum(net, part, core, near, corner)
    half(1 - net.at["core"])
    for names in (("zl", "y"), ("zl",), ("y",), ()):
        total.give(names)
    half(net.at["core"])
    total.send_corner()
    total.send_y()
    down = SpreadSum(net, gd_ref, over_x, over_zh, 2)

    def grad_down(k, _):
        left = hid_ref[:, pl.ds(pl.multiple_of(k * rows, rows), rows)]
        gd_ref[k] = atb(left, cot_ref[...]).astype(jnp.bfloat16)
        return 0

    lax.fori_loop(0, 4, grad_down, 0)
    down.first()
    total.pass_on()
    depth = width // 4

    def grad_gu(k, _):
        left = h_ref[:, pl.ds(pl.multiple_of(k * depth, depth), depth)]
        ggu_ref[k] = atb(left, dgu_ref[...]).astype(jnp.bfloat16).reshape(ggu_ref.shape[1:])
        return 0

    lax.fori_loop(0, 4, grad_gu, 0)
    feed = SpreadSum(net, ggu_ref, None, None, 1)
    far = feed.send(1 - net.at["zh"], gfar_ref, 0)
    grad = swap_chunks(total.total())
    value, inverse = normed(mid_ref[...])
    back, gain = norm_grad(grad, gains_ref[1:2, :], value, inverse)
    gain_ref[...] = gain
    dmid = cot_ref[mine, :].astype(jnp.float32) + back
    dmid_ref[...] = dmid
    dao_ref[mine] = dmid.astype(jnp.bfloat16)
    gather = Gather(net, dao_ref, rows)
    gather.first()
    down.second(0)
    down.second(1)
    gather.second()
    gather.third()
    for piece in range(2):
        gdown_ref[pl.ds(piece * rows // 2, rows // 2)] = down.total(piece)
    gather.done()
    far.wait_recv()
    net.drain()


def spread_scratch(shape):
    return [
        pltpu.VMEM((4, *shape), jnp.bfloat16),
        pltpu.VMEM((2, *shape), jnp.bfloat16),
        pltpu.VMEM(shape, jnp.bfloat16),
    ]


def unmixing(
    lens_ref, q_ref, k_ref, diff_ref, stat_ref, dq_ref, dk_ref, dv_ref, dproj_ref
):
    size = 128
    count = diff_ref.shape[0] // size
    upper = triangle(size, True)

    def one(step, carry):
        after, above, sums = carry
        i = count - 1 - step
        at = pl.ds(pl.multiple_of(i * size, size), size)
        stat = stat_ref[at, :]
        decay, keys, values = [], [], []
        for h in range(3):
            dq, dk = dq_ref[h, at, :], dk_ref[h, at, :]
            decay.append(dq[:, 65:66] - dk[:, 64:65])
            grad = dq[:, :64] * 0.125
            unit = q_ref[h, at, :][:, :64].astype(jnp.float32) * 8.0
            grad = grad - unit * jnp.mean(grad * unit, axis=-1, keepdims=True)
            dproj_ref[at, 64 * h : 64 * h + 64] = (stat[:, h : h + 1] * grad).astype(jnp.bfloat16)
            grad = dk[:, :64]
            unit = k_ref[h, at, :][:, :64].astype(jnp.float32)
            grad = grad - unit * jnp.mean(grad * unit, axis=-1, keepdims=True)
            keys.append(stat[:, 3 + h : 4 + h] * grad)
            values.append(dv_ref[h, at, :])
        both = jnp.concatenate(keys + values, axis=1)
        prod = both * diff_ref[at, :]
        mix = [stat[:, 9 + h : 10 + h] for h in range(3)]
        mixes = spread_lanes(mix, size, 384)
        place, low = bounds(lens_ref, i * size, size)
        carried = jnp.where(place == low, 0.0, both * mixes)
        row = lax.broadcasted_iota(jnp.int32, (size, 384), 0)
        later = jnp.where(row == size - 1, after, pltpu.roll(carried, size - 1, 0))
        dproj_ref[at, 384:768] = (both * (1.0 - mixes) + later).astype(jnp.bfloat16)
        decay = lanes(decay, size)
        suffix = exact(upper, decay) + above
        small = []
        for h in range(3):
            small.append(suffix[:, h : h + 1] * stat[:, 6 + h : 7 + h])
        for h in range(3):
            grad = jnp.sum(head_rows(prod, h) + head_rows(prod, 3 + h), axis=-1, keepdims=True)
            small.append(grad * mix[h] * (1.0 - mix[h]))
        small = lanes(small, size)
        dproj_ref[at, 768:896] = small.astype(jnp.bfloat16)
        above = above + jnp.sum(decay, axis=0, keepdims=True)
        return carried[:1, :], above, sums + jnp.sum(small, axis=0, keepdims=True)

    none = jnp.zeros((1, 128), jnp.float32)
    carry = lax.fori_loop(0, count, one, (jnp.zeros((1, 384), jnp.float32), none, none))
    return carry[2]


def kernel_d(
    dao_ref, wo_ref, a_ref, attn_far, gate_far, lens_ref, q_far, k_far, v_far, diff_far, stat_far,
    fcol_far, frow_far, w_far, h_ref, dmid_far, x_far, gains_ref, gain_two_ref, ggu_ref, gfar_ref,
    hid_ref, wd_ref, mid_ref,
    out_ref, gx_ref, gain_ref, bias_ref, ga_ref, go_ref, gu_ref,
    do_ref, dq_ref, dk_ref, dv_ref, dproj_ref,
    gu_x, gu_zh, a_whole, a_x, a_zh, o_raw, o_whole, o_x, o_zh, small, slots, tall, gx_own, out_own,
    part, core, near, corner, core2, near2, corner2, *refs,
):
    *late, send, recv, sems = refs
    attn_ref, gate_ref, q_ref, k_ref, v_ref, fcol_ref, frow_ref, diff_ref, stat_ref, w_ref, dmid_ref, x_ref = late
    far = (attn_far, gate_far, q_far, k_far, v_far, fcol_far, frow_far, diff_far, stat_far, w_far, dmid_far, x_far)
    net = Net(send, recv)
    rank = rank_of(net.at)
    rows, width = mid_ref.shape
    group = a_ref.shape[0]
    mine = pl.ds(pl.multiple_of(rank * rows, rows), rows)
    fetch = [pltpu.make_async_copy(ref, tall, sems.at[2 + i]) for i, ref in enumerate((dao_ref, h_ref))]
    fetch[0].start()
    loads = [
        pltpu.make_async_copy(source, target, sems.at[4 + i])
        for i, (source, target) in enumerate(zip(far, late))
    ]
    for made in loads:
        made.start()
    net.greet()
    feed = SpreadSum(net, ggu_ref, gu_x.at[0], gu_zh, 4, gu_x.at[1])
    attn = SpreadSum(net, a_whole, a_x, a_zh, 4)
    out = SpreadSum(net, o_whole, o_x, o_zh, 1)

    wo = wo_ref[...].reshape(-1, width)
    four = 4 * rows

    def half(which, left_ref, right, multiply, to):
        def one(i, _):
            at = pl.multiple_of(which * four + i * 2 * rows, 2 * rows)
            back = multiply(left_ref[pl.ds(at, 2 * rows), :], right).astype(jnp.bfloat16)
            to[which * 4 + 2 * i] = back[:rows]
            to[which * 4 + 2 * i + 1] = back[rows:]
            return 0

        lax.fori_loop(0, 2, one, 0)

    result = Sum(net, part, core2, near2, corner2)
    wd = wd_ref[...].reshape(-1, width)
    feed.pass_far()
    feed.pass_far_on(gfar_ref, 0, 2)
    half(1 - net.at["core"], hid_ref, wd, ab, part)
    for names in (("zl", "y"), ("zl",), ("y",), ()):
        result.give(names)
    half(net.at["core"], hid_ref, wd, ab, part)
    fetch[0].wait()
    for made in loads[:2]:
        made.wait()
    da = abt(tall[...], wo)
    for h in range(3):
        sig = gate_ref[:, 64 * h : 64 * h + 64]
        grad = da[:, 64 * h : 64 * h + 64] * sig
        do_ref[h] = grad.astype(jnp.bfloat16)
        dproj_ref[:, 192 + 64 * h : 256 + 64 * h] = (grad * attn_ref[h] * (1.0 - sig)).astype(
            jnp.bfloat16
        )
    o_raw[...] = atb(a_ref[...], tall[...]).astype(jnp.bfloat16).reshape(o_raw.shape)
    fetch[1].start()
    here = unit_of(net.at, ())
    o_whole[here] = o_raw[here]
    pieces = []
    for names in (("y",), ("zl",), ("zl", "y")):
        pieces.append(net.push(o_raw.at[unit_of(net.at, names)], o_whole.at[here], names))
    dk_ref[...] = jnp.zeros(dk_ref.shape, jnp.float32)
    dv_ref[...] = jnp.zeros(dv_ref.shape, jnp.float32)

    def attend(h, start, keys):
        at = pl.ds(pl.multiple_of(start, 128), 128)
        p = scores(h, at, start, 128, keys, q_ref, k_ref, fcol_ref, frow_ref, lens_ref)
        do = do_ref[h, at, :]
        dp = abt(do, v_ref[h, :keys, :])
        ds = p * (dp - jnp.sum(p * dp, axis=-1, keepdims=True))
        ds = ds.astype(jnp.bfloat16)
        dq_ref[h, at, :] = ab(ds, k_ref[h, :keys, :])
        dk_ref[h, :keys, :] += atb(ds, q_ref[h, at, :])
        dv_ref[h, :keys, :] += atb(p.astype(jnp.bfloat16), do)

    result.send_corner()
    result.send_y()
    for made in pieces:
        made.wait_recv()
    out.first()
    for made in loads[2:]:
        made.wait()
    over_blocks(attend, 0, 3)
    result.pass_on()
    feed.pass_far_on(gfar_ref, 2, 4)
    over_blocks(attend, 3, 4)
    out.second(0)
    result.left_cores()
    out_own[...] = (mid_ref[...] + result.total()).astype(jnp.bfloat16)
    moved_out = move(net, [(out_own, out_ref)], sems)
    sums = unmixing(lens_ref, q_ref, k_ref, diff_ref, stat_ref, dq_ref, dk_ref, dv_ref, dproj_ref)

    result.left()
    total = Sum(net, part, core, near, corner)
    w = w_ref[...].reshape(width, -1)
    half(1 - net.at["core"], dproj_ref, w, abt, part)
    for names in (("zl", "y"), ("zl",), ("y",), ()):
        total.give(names)
    half(net.at["core"], dproj_ref, w, abt, part)
    total.send_corner()
    total.send_y()
    depth = width // 4

    def grad_attn(k, _):
        left = tall[:, pl.ds(pl.multiple_of(k * depth, depth), depth)]
        a_whole[k] = atb(left, dproj_ref[...]).astype(jnp.bfloat16).reshape(a_whole.shape[1:])
        return 0

    fetch[1].wait()
    lax.fori_loop(0, 4, grad_attn, 0)
    attn.first()
    total.pass_on()
    attn.second(0)
    for piece in range(4):
        gu_zh[2 * piece : 2 * piece + 2] = feed.total(piece).astype(jnp.bfloat16)
    given = exchange(net, gu_zh, gu_ref)
    attn.second(1)
    grad = swap_chunks(total.total())
    attn.second(2)
    value, inverse = normed(x_ref[...].astype(jnp.float32))
    back, gain = norm_grad(grad, gains_ref[0:1, :], value, inverse)
    gx_own[...] = (dmid_ref[...] + back).astype(jnp.bfloat16)
    attn.second(3)
    small[0] = jnp.concatenate(
        [gain, gain_two_ref[...], jnp.concatenate([sums, jnp.zeros((1, width - 128), jnp.float32)], axis=1)]
        + [jnp.zeros((5, width), jnp.float32)],
        axis=0,
    )
    first = net.push(small.at[0], small.at[1], ("x",))
    moved_gx = move(net, [(gx_own, gx_ref)], sems, 1)
    go_ref[...] = out.total(0)
    first.wait_recv()
    small[2] = small[0] + small[1]
    second = net.push(small.at[2], small.at[3], ("zh",))
    for piece in range(4):
        a_zh[2 * piece : 2 * piece + 2] = attn.total(piece).astype(jnp.bfloat16)
    given += exchange(net, a_zh, ga_ref)
    second.wait_recv()
    slots[rank] = small[2] + small[3]
    shared = [net.push(slots.at[rank], slots.at[rank], names) for names in PARTNERS[:7]]
    for made in shared + given:
        made.wait_recv()
    gain_ref[...] = jnp.sum(slots[:, 0:2, :], axis=0)
    bias_ref[...] = slots[:, 2:3, :128]
    moved_out()
    moved_gx()
    net.drain()


def finish(
    out_ref, gx_ref, gain_ref, bias_ref, ga_ref, go_ref, gu_ref, gdown_ref,
    out_out, gx_out, gain_out, bias_out, gq_out, gk_out, gv_out, gg_out, go_out, gh_out, gfg_out, gfu_out, gdown_out,
):
    for source, target in ((out_ref, out_out), (gain_ref, gain_out), (go_ref, go_out), (gdown_ref, gdown_out)):
        target[...] = source[...]
    gx_out[...] = gx_ref[...].astype(jnp.float32)
    size = gq_out.shape[1] // 8
    few = bias_out.shape[1] // 8
    block = gfg_out.shape[1] // 32
    for rank in range(8):
        at = slice_of(rank)
        for i, target in enumerate((gq_out, gg_out, gk_out, gv_out)):
            part = ga_ref[rank, :, i * size : (i + 1) * size]
            target[:, at * size : (at + 1) * size] = part.astype(jnp.float32)
        part = ga_ref[rank, :, 4 * size :].astype(jnp.float32)
        for i in range(2):
            to = (i * 8 + at) * few
            gh_out[:, to : to + few] = part[:, i * few : (i + 1) * few]
            bias_out[i : i + 1, at * few : (at + 1) * few] = bias_ref[rank, :, i * few : (i + 1) * few]
        for i, target in enumerate((gfg_out, gfu_out)):
            for unit in range(4):
                to = (unit // 2 * 16 + rank // 4 * 8 + unit % 2 * 4 + rank % 4) * block
                part = gu_ref[rank, :, (i * 4 + unit) * block : (i * 4 + unit + 1) * block]
                target[:, to : to + block] = part.astype(jnp.float32)


def squares(
    layer_input,
    cotangent,
    seq_lengths,
    gains,
    head_bias,
    w_query,
    w_key,
    w_value,
    w_gate,
    w_out,
    w_heads,
    w_ff_gate,
    w_ff_up,
    w_ff_down,
):
    rows, width = layer_input.shape
    heads = head_bias.shape[1]
    head_dim = width // heads
    ranks = 8
    group = rows * ranks
    mine = heads // ranks
    cols = mine * head_dim
    shard = w_query.shape[0]
    units = w_ff_gate.shape[1] // ranks
    low = jnp.bfloat16
    f32 = jnp.float32
    packs = (ranks, shard, 4 * cols + 128)
    feeds = (ranks, shard, 2 * units)
    lens_shape = (8, 128)
    kept = (
        whole((group, width), low),
        whole((4, *packs), low),
        whole((mine, group, 128), low),
        whole((mine, group, 128), low),
        whole((mine, group, head_dim), low),
        whole((group, 2 * cols), f32),
        whole((group, 128), f32),
        whole((mine, group, 128), f32),
        whole((mine, 1, group), f32),
        whole((group, cols), f32),
        whole((mine, group, head_dim), f32),
        whole((group, cols), low),
        whole((4, shard, width), low),
        whole((4, *feeds), low),
        whole((4, *w_ff_down.shape), low),
        whole((group, width), low),
        whole((group, width), low),
    )
    (
        packed, lengths, mid,
        h_one_all, w_attn, q_all, k_all, v_all, diff, stat, fcol, frow, gate_sig, attn3, branch_in,
        w_o, w_gu, w_d, h_two_all, cot_all,
    ) = call(
        kernel_ab,
        1,
        (
            whole(layer_input.shape, low),
            whole(lens_shape, jnp.int32),
            whole((rows, width), f32),
            *kept,
        ),
        (
            layer_input, seq_lengths, gains, cotangent, head_bias,
            w_query, w_gate, w_key, w_value, w_heads, w_ff_gate, w_ff_up, w_out, w_ff_down,
        ),
        112,
        [
            *(pltpu.VMEM(leaf.shape, leaf.dtype) for leaf in kept),
            pltpu.VMEM(lens_shape, jnp.int32),
            pltpu.VMEM((8, 128), f32),
            pltpu.VMEM((group, packs[2]), f32),
            pltpu.VMEM(packs, low),
            pltpu.VMEM(feeds, low),
            pltpu.VMEM((4, shard, width), low),
            *sum_scratch(rows, width),
        ],
        local=3 + len(kept),
        far_outs=range(3, 3 + len(kept)),
    )
    hidden, grad_mid, grad_branch, gain_two, grad_down, grad_gu, grad_far = call(
        kernel_c,
        3,
        (
            whole((group, units), low),
            whole((rows, width), f32),
            whole((group, width), low),
            whole((1, width), f32),
            whole((rows, width), f32),
            whole((4, *feeds), low),
            whole(feeds, low),
        ),
        (h_two_all, cot_all, w_gu, w_d, mid, gains),
        48,
        [
            pltpu.VMEM((group, 2 * units), low),
            pltpu.VMEM((4, rows, width), low),
            pltpu.VMEM((2, rows, width), low),
            pltpu.VMEM((rows, width), low),
            *sum_scratch(rows, width),
        ],
    )
    result, grad_input, gain_sums, bias_sums, grad_attn_w, grad_wout, grad_gu = call(
        kernel_d,
        4,
        (
            whole((rows, width), low),
            whole((rows, width), low),
            whole((2, width), f32),
            whole((ranks, 1, 128), f32),
            whole(packs, low),
            whole((shard, width), f32),
            whole(feeds, low),
        ),
        (
            grad_branch, w_o, branch_in, attn3, gate_sig, lengths, q_all, k_all, v_all, diff, stat,
            fcol, frow, w_attn, h_one_all, grad_mid, packed, gains, gain_two, grad_gu, grad_far,
            hidden, w_d, mid,
        ),
        96,
        [
            pltpu.VMEM((mine, group, head_dim), low),
            pltpu.VMEM((mine, group, 128), f32),
            pltpu.VMEM((mine, group, 128), f32),
            pltpu.VMEM((mine, group, head_dim), f32),
            pltpu.VMEM((group, packs[2]), low),
            *spread_scratch(feeds)[1:],
            *spread_scratch(packs),
            pltpu.VMEM((4, shard, width), low),
            *spread_scratch((shard, width)),
            pltpu.VMEM((4, 8, width), f32),
            pltpu.VMEM((ranks, 8, width), f32),
            pltpu.VMEM((group, width), low),
            pltpu.VMEM((rows, width), low),
            pltpu.VMEM((rows, width), low),
            *sum_scratch(rows, width),
            *sum_scratch(rows, width)[1:],
            *(pltpu.VMEM(leaf.shape, leaf.dtype) for leaf in (attn3, gate_sig, q_all, k_all, v_all, fcol, frow, diff, stat, w_attn, grad_mid, packed)),
        ],
        16,
        (0, 14, 3, 4, 6, 7, 8, 11, 12, 9, 10, 13, 15, 16),
    )

    big = whole((shard, width), f32)
    outs = (
        whole((rows, width), low),
        whole((rows, width), f32),
        whole((2, width), f32),
        whole((2, heads), f32),
        big,
        big,
        big,
        big,
        big,
        whole((shard, 2 * heads), f32),
        whole(w_ff_gate.shape, f32),
        whole(w_ff_up.shape, f32),
        whole(w_ff_down.shape, f32),
    )
    args = (result, grad_input, gain_sums, bias_sums, grad_attn_w, grad_wout, grad_gu, grad_down)
    return pl.pallas_call(
        finish,
        out_shape=outs,
        in_specs=vmem(len(args)),
        out_specs=vmem(len(outs)),
        compiler_params=pltpu.CompilerParams(vmem_limit_bytes=60 * 2**20),
    )(*args)


def solution(mesh):
    if mesh.shape["dp"] == 4 and mesh.shape["ctx"] == 8:
        body, axes, group = squares, AXES, ("x", "core")
        mesh = Mesh(np.reshape(mesh.devices, (2, 2, 2, 2, 2)), AXES)
    else:
        body, axes, group = shards, ("dp", "ctx"), "dp"
    cut = P(axes, None)
    return jax.shard_map(
        body,
        mesh=mesh,
        in_specs=(cut, cut, P(group, None), P(), P()) + (cut,) * 9,
        out_specs=(cut, cut, P(), P()) + (cut,) * 9,
        check_vma=False,
    )
```

```python
import jax
import jax.numpy as jnp
import numpy as np
from jax import lax
from jax.experimental import pallas as pl
from jax.experimental.pallas import tpu as pltpu
from jax.sharding import Mesh
from jax.sharding import PartitionSpec as P

EPS = 1e-06


def passed_along(array, axis, by):
    size = lax.axis_size(axis)
    pairs = [(i, i + by) for i in range(size) if 0 <= i + by < size]
    return lax.ppermute(array, axis, pairs)


def entering(part, axis, combine, identity, reverse):
    count = lax.axis_size(axis)
    place = lax.axis_index(axis)
    ahead = count - 1 - place if reverse else place
    gathered = lax.all_gather(part, axis)
    state = jnp.zeros_like(part) + jnp.asarray(identity, part.dtype)

    def one(step, state):
        source = count - 1 - step if reverse else step
        return combine(state, lax.dynamic_index_in_dim(gathered, source, 0, False))

    return lax.fori_loop(0, ahead, one, state)


def fetch_attention(w_query, w_key, w_value, w_gate, w_out, w_heads):
    return (
        lax.all_gather(w_query, ("dp", "ctx"), axis=0, tiled=True),
        lax.all_gather(w_key, ("dp", "ctx"), axis=0, tiled=True),
        lax.all_gather(w_value, ("dp", "ctx"), axis=0, tiled=True),
        lax.all_gather(w_gate, ("dp", "ctx"), axis=0, tiled=True),
        lax.all_gather(w_out, ("dp", "ctx"), axis=0, tiled=True),
        lax.all_gather(w_heads, ("dp", "ctx"), axis=0, tiled=True),
    )


def fetch_feed(w_ff_gate, w_ff_up, w_ff_down):
    return (
        lax.all_gather(w_ff_gate, ("dp", "ctx"), axis=0, tiled=True),
        lax.all_gather(w_ff_up, ("dp", "ctx"), axis=0, tiled=True),
        lax.all_gather(w_ff_down, ("dp", "ctx"), axis=0, tiled=True),
    )


def add_arrays(earlier, later):
    return earlier + later


def norm_back(grad, normed, inverse):
    return inverse * (grad - normed * jnp.mean(grad * normed, axis=-1, keepdims=True))


def project(left, right):
    return jnp.dot(left, right, preferred_element_type=jnp.float32)


def weight_grad(left, right):
    return jnp.einsum("ra,rb->ab", left, right, preferred_element_type=jnp.float32)


def input_grad(grad, weight):
    return jnp.einsum("rb,ab->ra", grad, weight, preferred_element_type=jnp.float32)


def shards(
    layer_input,
    cotangent,
    seq_lengths,
    gains,
    head_bias,
    w_query,
    w_key,
    w_value,
    w_gate,
    w_out,
    w_heads,
    w_ff_gate,
    w_ff_up,
    w_ff_down,
):
    rows, width = layer_input.shape
    heads = head_bias.shape[1]
    head_dim = width // heads
    spans = lax.axis_size("ctx")
    group = rows * spans
    scale = head_dim ** (-0.5)
    here = lax.axis_index("ctx")
    local_pos = here * rows + jnp.arange(rows, dtype=jnp.int32)
    key_pos = jnp.arange(group, dtype=jnp.int32)
    first = seq_lengths[0, 0]
    second = first + seq_lengths[0, 1]
    local_seg = (local_pos >= first).astype(jnp.int32) + (local_pos >= second).astype(jnp.int32)
    key_seg = (key_pos >= first).astype(jnp.int32) + (key_pos >= second).astype(jnp.int32)
    starts = (local_pos == 0) | (local_pos == first) | (local_pos == second)
    keep = (1 - starts.astype(jnp.int32)).astype(jnp.float32)[:, None]
    allowed = (local_seg[:, None] == key_seg[None, :]) & (key_pos[None, :] <= local_pos[:, None])
    x_full = layer_input.astype(jnp.float32)
    inv_one = lax.rsqrt(jnp.mean(x_full * x_full, axis=-1, keepdims=True) + EPS)
    normed_one = x_full * inv_one
    h_one = (normed_one * gains[0]).astype(jnp.bfloat16)
    full_query, full_key, full_value, full_gate, full_out, full_heads = fetch_attention(
        w_query, w_key, w_value, w_gate, w_out, w_heads
    )
    query = project(h_one, full_query)
    key_raw = project(h_one, full_key)
    value_raw = project(h_one, full_value)
    gate_raw = project(h_one, full_gate)
    head_raw = project(h_one, full_heads)
    forget_logit = head_raw[:, :heads] + head_bias[0]
    shift_logit = head_raw[:, heads:] + head_bias[1]
    log_forget = jax.nn.log_sigmoid(forget_logit)
    mix_small = jax.nn.sigmoid(shift_logit)
    mix = jnp.repeat(mix_small, head_dim, axis=1)
    prev_row = passed_along(h_one[rows - 1 :], "ctx", 1)
    key_prev = jnp.concatenate([project(prev_row, full_key), key_raw[:-1]], 0) * keep
    value_prev = jnp.concatenate([project(prev_row, full_value), value_raw[:-1]], 0) * keep
    key_mix = mix * key_prev + (1.0 - mix) * key_raw
    value_mix = mix * value_prev + (1.0 - mix) * value_raw
    query4 = query.reshape(rows, heads, head_dim)
    query_inv = lax.rsqrt(jnp.mean(query4 * query4, axis=-1, keepdims=True) + EPS)
    query_norm = query4 * query_inv
    key4 = key_mix.reshape(rows, heads, head_dim)
    key_inv = lax.rsqrt(jnp.mean(key4 * key4, axis=-1, keepdims=True) + EPS)
    key_norm = key4 * key_inv
    q_low = query_norm.astype(jnp.bfloat16)
    k_low = key_norm.reshape(rows, width).astype(jnp.bfloat16)
    v_low = value_mix.astype(jnp.bfloat16)
    local_cum = jnp.cumsum(log_forget, axis=0)
    offset = entering(
        local_cum[rows - 1], "ctx", add_arrays, jnp.zeros((heads,), jnp.float32), False
    )
    decay = local_cum + offset
    gathered_k, gathered_v, all_decay = (
        lax.all_gather(k_low.astype(jnp.float32), "ctx", axis=0, tiled=True),
        lax.all_gather(v_low.astype(jnp.float32), "ctx", axis=0, tiled=True),
        lax.all_gather(decay, "ctx", axis=0, tiled=True),
    )
    all_keys = gathered_k.astype(jnp.bfloat16).reshape(group, heads, head_dim)
    all_values = gathered_v.astype(jnp.bfloat16).reshape(group, heads, head_dim)

    def scores_of(index, keys_whole, decay_whole):
        q_part = lax.dynamic_slice_in_dim(q_low, index * 4, 4, 1)
        k_part = lax.dynamic_slice_in_dim(keys_whole, index * 4, 4, 1)
        own = lax.dynamic_slice_in_dim(decay, index * 4, 4, 1)
        far = lax.dynamic_slice_in_dim(decay_whole, index * 4, 4, 1)
        raw = jnp.einsum("rhd,ghd->hrg", q_part, k_part, preferred_element_type=jnp.float32) * scale
        raw = raw + own.T[:, :, None] - far.T[:, None, :]
        return (jnp.where(allowed[None], raw, -1e30), q_part, k_part)

    group_count = heads // 4

    def forward_step(index, carry):
        mixed, log_total = carry
        scores, q_part, k_part = scores_of(index, all_keys, all_decay)
        v_part = lax.dynamic_slice_in_dim(all_values, index * 4, 4, 1)
        top = jnp.max(scores, axis=-1, keepdims=True)
        expd = jnp.exp(scores - top)
        total = jnp.sum(expd, axis=-1, keepdims=True)
        probs = (expd / total).astype(jnp.bfloat16)
        part = jnp.einsum("hrg,ghd->rhd", probs, v_part, preferred_element_type=jnp.float32)
        mixed = lax.dynamic_update_slice_in_dim(mixed, part, index * 4, 1)
        log_total = lax.dynamic_update_slice_in_dim(
            log_total, (top + jnp.log(total))[:, :, 0].T, index * 4, 1
        )
        return (mixed, log_total)

    attn4, log_total = lax.fori_loop(
        0,
        group_count,
        forward_step,
        (jnp.zeros((rows, heads, head_dim), jnp.float32), jnp.zeros((rows, heads), jnp.float32)),
    )
    attn = attn4.reshape(rows, width)
    gate_sig = jax.nn.sigmoid(gate_raw)
    branch_in = (gate_sig * attn).astype(jnp.bfloat16)
    mid = x_full + project(branch_in, full_out)
    inv_two = lax.rsqrt(jnp.mean(mid * mid, axis=-1, keepdims=True) + EPS)
    normed_two = mid * inv_two
    h_two = (normed_two * gains[1]).astype(jnp.bfloat16)
    full_ff_gate, full_ff_up, full_ff_down = fetch_feed(w_ff_gate, w_ff_up, w_ff_down)
    ff_gate = project(h_two, full_ff_gate)
    ff_up = project(h_two, full_ff_up)
    ff_sig = jax.nn.sigmoid(ff_gate)
    hidden = (ff_gate * ff_sig * ff_up).astype(jnp.bfloat16)
    result = (mid + project(hidden, full_ff_down)).astype(jnp.bfloat16)
    full_ff_gate, full_ff_up, full_ff_down = fetch_feed(w_ff_gate, w_ff_up, w_ff_down)
    full_query, full_key, full_value, full_gate, full_out, full_heads = fetch_attention(
        w_query, w_key, w_value, w_gate, w_out, w_heads
    )
    grad_out = cotangent.astype(jnp.float32)
    grad_down = weight_grad(hidden, cotangent)
    grad_hidden = input_grad(cotangent, full_ff_down)
    grad_gate_ff = (grad_hidden * ff_up * ff_sig * (1.0 + ff_gate * (1.0 - ff_sig))).astype(
        jnp.bfloat16
    )
    grad_up_ff = (grad_hidden * (ff_gate * ff_sig)).astype(jnp.bfloat16)
    ffn_grads = (
        lax.psum_scatter(
            weight_grad(h_two, grad_gate_ff), ("dp", "ctx"), scatter_dimension=0, tiled=True
        ),
        lax.psum_scatter(
            weight_grad(h_two, grad_up_ff), ("dp", "ctx"), scatter_dimension=0, tiled=True
        ),
        lax.psum_scatter(grad_down, ("dp", "ctx"), scatter_dimension=0, tiled=True),
    )
    grad_h_two = input_grad(grad_gate_ff, full_ff_gate) + input_grad(grad_up_ff, full_ff_up)
    gain_two = jnp.sum(grad_h_two * normed_two, axis=0)
    grad_mid = norm_back(grad_h_two * gains[1], normed_two, inv_two) + grad_out
    grad_branch = grad_mid.astype(jnp.bfloat16)
    grad_wout = weight_grad(branch_in, grad_branch)
    grad_branch_in = input_grad(grad_branch, full_out)
    grad_attn = (grad_branch_in * gate_sig).astype(jnp.bfloat16).reshape(rows, heads, head_dim)
    grad_gate = (grad_branch_in * attn * gate_sig * (1.0 - gate_sig)).astype(jnp.bfloat16)
    gathered_k, gathered_v, all_decay = (
        lax.all_gather(k_low.astype(jnp.float32), "ctx", axis=0, tiled=True),
        lax.all_gather(v_low.astype(jnp.float32), "ctx", axis=0, tiled=True),
        lax.all_gather(decay, "ctx", axis=0, tiled=True),
    )
    all_keys = gathered_k.astype(jnp.bfloat16).reshape(group, heads, head_dim)
    all_values = gathered_v.astype(jnp.bfloat16).reshape(group, heads, head_dim)

    def backward_step(index, carry):
        grad_q, grad_k, grad_v, grad_own, grad_far = carry
        scores, q_part, k_part = scores_of(index, all_keys, all_decay)
        v_part = lax.dynamic_slice_in_dim(all_values, index * 4, 4, 1)
        lse = lax.dynamic_slice_in_dim(log_total, index * 4, 4, 1).T[:, :, None]
        probs = jnp.exp(scores - lse)
        probs_low = probs.astype(jnp.bfloat16)
        grad_part = lax.dynamic_slice_in_dim(grad_attn, index * 4, 4, 1)
        grad_probs = jnp.einsum(
            "rhd,ghd->hrg", grad_part, v_part, preferred_element_type=jnp.float32
        )
        value_term = jnp.einsum(
            "hrg,rhd->ghd", probs_low, grad_part, preferred_element_type=jnp.float32
        )
        grad_scores = (
            probs * (grad_probs - jnp.sum(probs * grad_probs, axis=-1, keepdims=True))
        ).astype(jnp.bfloat16)
        query_term = (
            jnp.einsum("hrg,ghd->rhd", grad_scores, k_part, preferred_element_type=jnp.float32)
            * scale
        )
        key_term = (
            jnp.einsum("hrg,rhd->ghd", grad_scores, q_part, preferred_element_type=jnp.float32)
            * scale
        )
        scores_full = grad_scores.astype(jnp.float32)
        own_term = jnp.sum(scores_full, axis=-1).T
        far_term = -jnp.sum(scores_full, axis=1).T
        grad_q = lax.dynamic_update_slice_in_dim(grad_q, query_term, index * 4, 1)
        grad_k = lax.dynamic_update_slice_in_dim(grad_k, key_term, index * 4, 1)
        grad_v = lax.dynamic_update_slice_in_dim(grad_v, value_term, index * 4, 1)
        grad_own = lax.dynamic_update_slice_in_dim(grad_own, own_term, index * 4, 1)
        grad_far = lax.dynamic_update_slice_in_dim(grad_far, far_term, index * 4, 1)
        return (grad_q, grad_k, grad_v, grad_own, grad_far)

    grad_q, grad_k, grad_v, grad_own, grad_far = lax.fori_loop(
        0,
        group_count,
        backward_step,
        (
            jnp.zeros((rows, heads, head_dim), jnp.float32),
            jnp.zeros((group, heads, head_dim), jnp.float32),
            jnp.zeros((group, heads, head_dim), jnp.float32),
            jnp.zeros((rows, heads), jnp.float32),
            jnp.zeros((group, heads), jnp.float32),
        ),
    )
    grad_k_local, grad_v_local, grad_far_local = (
        lax.psum_scatter(grad_k, "ctx", scatter_dimension=0, tiled=True),
        lax.psum_scatter(grad_v, "ctx", scatter_dimension=0, tiled=True),
        lax.psum_scatter(grad_far, "ctx", scatter_dimension=0, tiled=True),
    )
    grad_decay = grad_own + grad_far_local
    local_rev = jnp.flip(jnp.cumsum(jnp.flip(grad_decay, 0), axis=0), 0)
    later = entering(
        jnp.sum(grad_decay, axis=0), "ctx", add_arrays, jnp.zeros((heads,), jnp.float32), True
    )
    grad_forget_logit = (local_rev + later) * jax.nn.sigmoid(-forget_logit)
    grad_query = norm_back(grad_q, query_norm, query_inv).reshape(rows, width)
    grad_key_mix = norm_back(grad_k_local, key_norm, key_inv).reshape(rows, width)
    grad_value_mix = grad_v_local.reshape(rows, width)
    grad_mix = jnp.sum(
        (grad_key_mix * (key_prev - key_raw) + grad_value_mix * (value_prev - value_raw)).reshape(
            rows, heads, head_dim
        ),
        axis=-1,
    )
    grad_shift_logit = grad_mix * mix_small * (1.0 - mix_small)
    carried_key = grad_key_mix * mix * keep
    carried_value = grad_value_mix * mix * keep
    from_next = passed_along(jnp.concatenate([carried_key[:1], carried_value[:1]], 0), "ctx", -1)
    grad_key_raw = (
        grad_key_mix * (1.0 - mix) + jnp.concatenate([carried_key[1:], from_next[:1]], 0)
    ).astype(jnp.bfloat16)
    grad_value_raw = (
        grad_value_mix * (1.0 - mix) + jnp.concatenate([carried_value[1:], from_next[1:]], 0)
    ).astype(jnp.bfloat16)
    grad_query_low = grad_query.astype(jnp.bfloat16)
    grad_head = jnp.concatenate([grad_forget_logit, grad_shift_logit], axis=1).astype(jnp.bfloat16)
    attn_grads = (
        lax.psum_scatter(
            weight_grad(h_one, grad_query_low), ("dp", "ctx"), scatter_dimension=0, tiled=True
        ),
        lax.psum_scatter(
            weight_grad(h_one, grad_key_raw), ("dp", "ctx"), scatter_dimension=0, tiled=True
        ),
        lax.psum_scatter(
            weight_grad(h_one, grad_value_raw), ("dp", "ctx"), scatter_dimension=0, tiled=True
        ),
        lax.psum_scatter(
            weight_grad(h_one, grad_gate), ("dp", "ctx"), scatter_dimension=0, tiled=True
        ),
        lax.psum_scatter(grad_wout, ("dp", "ctx"), scatter_dimension=0, tiled=True),
        lax.psum_scatter(
            weight_grad(h_one, grad_head), ("dp", "ctx"), scatter_dimension=0, tiled=True
        ),
    )
    grad_h_one = (
        input_grad(grad_query_low, full_query)
        + input_grad(grad_key_raw, full_key)
        + input_grad(grad_value_raw, full_value)
        + input_grad(grad_gate, full_gate)
        + input_grad(grad_head, full_heads)
    )
    gain_one = jnp.sum(grad_h_one * normed_one, axis=0)
    grad_input = norm_back(grad_h_one * gains[0], normed_one, inv_one) + grad_mid
    small = lax.psum(
        (
            jnp.stack([gain_one, gain_two]),
            jnp.stack([jnp.sum(grad_forget_logit, axis=0), jnp.sum(grad_shift_logit, axis=0)]),
        ),
        ("dp", "ctx"),
    )
    return (
        result,
        grad_input,
        small[0],
        small[1],
        attn_grads[0],
        attn_grads[1],
        attn_grads[2],
        attn_grads[3],
        attn_grads[4],
        attn_grads[5],
        ffn_grads[0],
        ffn_grads[1],
        ffn_grads[2],
    )


AXES = ("x", "core", "zh", "zl", "y")

def dot(left, right, dims):
    return lax.dot_general(left, right, (dims, ((), ())), preferred_element_type=jnp.float32)


def ab(left, right):
    return dot(left, right, ((1,), (0,)))


def abt(left, right):
    return dot(left, right, ((1,), (1,)))


def atb(left, right):
    return dot(left, right, ((0,), (0,)))


MESH = pl.DeviceIdType.MESH


class Net:
    def __init__(self, send, recv):
        self.send, self.recv, self.count, self.open = send, recv, 0, []
        self.at = {name: lax.axis_index(name) for name in AXES}

    def flip(self, names):
        return {name: 1 - self.at[name] for name in names}

    def greet(self):
        barrier = pltpu.get_barrier_semaphore()
        for names in PARTNERS:
            pl.semaphore_signal(barrier, 1, device_id=self.flip(names), device_id_type=MESH)
        moved = self.at["core"] != self.at["zh"]

        @pl.when(moved)
        def _():
            other = self.flip(("core", "zh"))
            pl.semaphore_signal(barrier, 1, device_id=other, device_id_type=MESH)
            pl.semaphore_wait(barrier, len(PARTNERS) + 1)

        @pl.when(jnp.logical_not(moved))
        def _():
            pl.semaphore_wait(barrier, len(PARTNERS))

    def copy(self, source, target, names):
        i = self.count
        self.count += 1
        return pltpu.make_async_remote_copy(
            source,
            target,
            self.send.at[i],
            self.recv.at[i],
            device_id=self.flip(names),
            device_id_type=MESH,
        )

    def push(self, source, target, names):
        made = self.copy(source, target, names)
        made.start()
        self.open.append(made)
        return made

    def left(self, copies):
        for made in copies:
            made.wait_send()
            self.open = [other for other in self.open if other is not made]

    def drain(self):
        for made in self.open:
            made.wait_send()


PARTNERS = (
    ("y",),
    ("zl",),
    ("zl", "y"),
    ("core",),
    ("core", "y"),
    ("core", "zl"),
    ("core", "zl", "y"),
    ("x",),
    ("zh",),
)


def rank_of(at):
    return (at["core"] * 2 + at["zl"]) * 2 + at["y"]


def flipped(at, names):
    return {name: 1 - at[name] if name in names else at[name] for name in at}


def unit_of(at, names):
    at = flipped(at, names)
    return at["zl"] * 2 + at["y"]


class Gather:
    def __init__(self, net, ref, rows):
        self.net, self.ref, self.rows = net, ref, rows

    def part(self, names, half=None):
        start = rank_of(flipped(self.net.at, names)) * self.rows
        size = self.rows
        if half is not None:
            size = self.rows // 2
            start = start + half * size
        return self.ref.at[pl.ds(pl.multiple_of(start, size), size)]

    def send(self, block, half, to):
        part = self.part(block, half)
        return self.net.push(part, part, to)

    def first(self):
        self.along = [self.send((), half, ("zl",)) for half in range(2)]
        self.near = self.send((), None, ("y",))
        self.cores = [self.send((), None, ("core",))]

    def second(self):
        self.corner = []
        for half in range(2):
            self.along[half].wait_recv()
            self.corner.append(self.send(("zl",), half, ("y",)))
        self.cores.append(self.send(("zl",), None, ("core",)))
        self.near.wait_recv()
        self.cores.append(self.send(("y",), None, ("core",)))

    def third(self):
        for made in self.corner:
            made.wait_recv()
        self.cores.append(self.send(("zl", "y"), None, ("core",)))

    def done(self):
        for made in self.cores:
            made.wait_recv()


QUARTERS = (("core", "zl"), ("zl",), ("core",), ())


def quarter(net, piece):
    at = flipped(net.at, QUARTERS[piece])
    return (at["core"] * 2 + at["zl"]) * 2


class Spread:
    def __init__(self, net, ref, pieces):
        self.net, self.ref, self.pieces = net, ref, pieces
        self.size = ref.shape[1] // pieces
        self.unit = net.at["x"] * 2 + net.at["zh"]
        self.from_zh = net.at["x"] * 2 + 1 - net.at["zh"]

    def send(self, unit, piece, to):
        part = self.ref.at[unit, pl.ds(piece * self.size, self.size)]
        return self.net.push(part, part, to)

    def first(self, ahead):
        self.along, self.across, self.corner = [], [], []
        for piece in range(self.pieces):
            if piece < ahead:
                self.along.append(self.send(self.unit, piece, ("zh",)))
            self.across.append(self.send(self.unit, piece, ("x",)))

    def second(self, piece):
        self.along[piece].wait_recv()
        self.corner.append(self.send(self.from_zh, piece, ("x",)))
        if len(self.along) < self.pieces:
            self.push_next()

    def push_next(self):
        self.along.append(self.send(self.unit, len(self.along), ("zh",)))

    def wait_across(self):
        for made in self.across:
            made.wait_recv()

    def wait_corner(self):
        for made in self.corner:
            made.wait_recv()


def exchange(net, source, target):
    rank = rank_of(net.at)
    target[rank] = source[rank]
    made = []
    for names in PARTNERS[:7]:
        to = rank_of(flipped(net.at, names))
        made.append(net.push(source.at[to], target.at[rank], names))
    return made


def swap_chunks(value):
    size = value.shape[1] // 8
    order = (0, 2, 1, 3, 4, 6, 5, 7)
    return jnp.concatenate([value[:, i * size : (i + 1) * size] for i in order], axis=1)


def normed(value):
    inverse = lax.rsqrt(jnp.mean(value * value, axis=-1, keepdims=True) + EPS)
    return value * inverse, inverse


def slice_of(rank):
    return rank // 2 % 2 * 4 + rank // 4 * 2 + rank % 2


def pack_attention(wide, heads_ref, pack_ref):
    size = wide[0].shape[1] // 8
    few = heads_ref.shape[1] // 16
    for rank in range(8):
        at = slice_of(rank)
        for i, ref in enumerate(wide):
            pack_ref[rank, :, i * size : (i + 1) * size] = ref[:, at * size : (at + 1) * size]
        pack_ref[rank, :, 4 * size :] = jnp.concatenate(
            [heads_ref[:, (i * 8 + at) * few : (i * 8 + at + 1) * few] for i in range(2)]
            + [jnp.zeros((heads_ref.shape[0], 128 - 2 * few), jnp.bfloat16)],
            axis=1,
        )


def pack_feeds(feeds, pack_gu_ref):
    block = feeds[0].shape[1] // 32
    for rank in range(8):
        for i, ref in enumerate(feeds):
            for unit in range(4):
                source = unit // 2 * 16 + rank // 4 * 8 + unit % 2 * 4 + rank % 4
                to = (i * 4 + unit) * block
                pack_gu_ref[rank, :, to : to + block] = ref[:, source * block : (source + 1) * block]


def whole(shape, dtype):
    return jax.ShapeDtypeStruct(shape, dtype)


def vmem(count):
    return [pl.BlockSpec(memory_space=pltpu.VMEM)] * count


def call(kernel, number, outs, args, copies, scratch=(), local=2, far=(), far_outs=()):
    return pl.pallas_call(
        kernel,
        out_shape=outs,
        in_specs=[
            pl.BlockSpec(memory_space=pl.ANY if i in far else pltpu.VMEM) for i in range(len(args))
        ],
        out_specs=[
            pl.BlockSpec(memory_space=pl.ANY if i in far_outs else pltpu.VMEM) for i in range(len(outs))
        ],
        scratch_shapes=[
            *scratch,
            pltpu.SemaphoreType.DMA((copies,)),
            pltpu.SemaphoreType.DMA((copies,)),
            pltpu.SemaphoreType.DMA((local,)),
        ],
        compiler_params=pltpu.CompilerParams(
            collective_id=number, has_side_effects=True, vmem_limit_bytes=60 * 2**20
        ),
    )(*args)


class Sum:
    def __init__(self, net, part, core, near, corner):
        self.net, self.part, self.core, self.near, self.corner = net, part, core, near, corner
        self.rows = part.shape[1]
        self.half = self.rows // 2
        self.given = {}

    def place(self, names):
        at = flipped(self.net.at, names)
        return at["zl"] * 2 + at["y"]

    def rank(self, names):
        return rank_of(flipped(self.net.at, names))

    def give(self, names):
        block = self.part.at[self.rank(("core", *names))]
        self.given[names] = self.net.push(block, self.core.at[self.place(names)], ("core",))

    def take(self, names):
        self.given[names].wait_recv()
        rank = self.rank(names)
        self.part[rank] = (
            self.part[rank].astype(jnp.float32) + self.core[self.place(names)].astype(jnp.float32)
        ).astype(jnp.bfloat16)

    def rows_of(self, names, half):
        return self.part.at[self.rank(names), pl.ds(half * self.half, self.half)]

    def send_corner(self):
        self.take(("zl", "y"))
        self.by_y = [
            self.net.push(self.rows_of(("zl", "y"), half), self.corner.at[half], ("y",))
            for half in range(2)
        ]

    def send_y(self):
        self.take(("y",))
        self.near_y = self.net.push(self.part.at[self.rank(("y",))], self.near.at[0], ("y",))

    def left_cores(self):
        self.net.left(self.given.values())

    def left(self):
        self.net.left((*self.by_y, self.near_y, *self.near_zl))

    def pass_on(self):
        self.take(("zl",))
        self.near_zl = []
        for half in range(2):
            self.by_y[half].wait_recv()
            rows = self.rows_of(("zl",), half)
            rows[...] = (
                rows[...].astype(jnp.float32) + self.corner[half].astype(jnp.float32)
            ).astype(jnp.bfloat16)
            to = self.near.at[1, pl.ds(half * self.half, self.half)]
            self.near_zl.append(self.net.push(rows, to, ("zl",)))

    def total(self):
        self.given[()].wait_recv()
        own = self.part[self.rank(())].astype(jnp.float32)
        own = own + self.core[self.place(())].astype(jnp.float32)
        for made in (self.near_y, *self.near_zl):
            made.wait_recv()
        return own + self.near[0].astype(jnp.float32) + self.near[1].astype(jnp.float32)


def sum_scratch(rows, width):
    return [
        pltpu.VMEM((8, rows, width), jnp.bfloat16),
        pltpu.VMEM((4, rows, width), jnp.bfloat16),
        pltpu.VMEM((2, rows, width), jnp.bfloat16),
        pltpu.VMEM((2, rows // 2, width), jnp.bfloat16),
    ]


def move(net, pairs, sems, start=0):
    moved = net.at["core"] != net.at["zh"]
    away = [net.copy(source, target, ("core", "zh")) for source, target in pairs]
    stay = [pltpu.make_async_copy(*pair, sems.at[start + i]) for i, pair in enumerate(pairs)]

    def each(act):
        @pl.when(moved)
        def _():
            for made in away:
                act(made)

        @pl.when(jnp.logical_not(moved))
        def _():
            for made in stay:
                act(made)

    each(lambda made: made.start())
    return lambda: each(lambda made: made.wait())


def lanes(columns, size):
    lane = lax.broadcasted_iota(jnp.int32, (size, 128), 1)
    out = jnp.zeros((size, 128), jnp.float32)
    for i, column in enumerate(columns):
        out = jnp.where(lane == i, column, out)
    return out


def triangle(size, upper):
    row = lax.broadcasted_iota(jnp.int32, (size, size), 0)
    col = lax.broadcasted_iota(jnp.int32, (size, size), 1)
    return jnp.where(row <= col if upper else row >= col, 1.0, 0.0)


def exact(left, right):
    return jnp.dot(
        left, right, precision=lax.Precision.HIGHEST, preferred_element_type=jnp.float32
    )


def spread_lanes(columns, size, wide):
    which = (lax.broadcasted_iota(jnp.int32, (size, wide), 1) // 64) % 3
    return jnp.where(which == 0, columns[0], jnp.where(which == 1, columns[1], columns[2]))


def bounds(lens_ref, first_row, size):
    place = first_row + lax.broadcasted_iota(jnp.int32, (size, 1), 0)
    first = lens_ref[0:1, 0:1]
    second = first + lens_ref[0:1, 1:2]
    low = jnp.where(place >= second, second, jnp.where(place >= first, first, 0))
    return place, low


def head_rows(value, h):
    return value[:, h * 64 : (h + 1) * 64]


def with_one(value, lane_at):
    size = value.shape[0]
    lane = lax.broadcasted_iota(jnp.int32, (size, 64), 1)
    return jnp.concatenate([value, jnp.where(lane == lane_at, 1.0, 0.0)], axis=1)


def mixing(proj_ref, lens_ref, bias_ref, q_ref, k_ref, v_ref, diff_ref, stat_ref, fcol_ref, frow_ref):
    size = 128
    lower = triangle(size, False)

    def one(i, carry):
        last, below = carry
        at = pl.ds(pl.multiple_of(i * size, size), size)
        block = proj_ref[at, :]
        kv = block[:, 384:768]
        logits = block[:, 768:896] + bias_ref[0:1, :]
        logf = jax.nn.log_sigmoid(logits)
        mix = jax.nn.sigmoid(logits)
        place, low = bounds(lens_ref, i * size, size)
        row = lax.broadcasted_iota(jnp.int32, (size, 384), 0)
        prev = jnp.where(row == 0, last, pltpu.roll(kv, 1, 0))
        prev = jnp.where(place == low, 0.0, prev)
        diff = prev - kv
        diff_ref[at, :] = diff
        mixed = kv + spread_lanes([mix[:, 3 + h : 4 + h] for h in range(3)], size, 384) * diff
        decay = exact(lower, logf) + below
        frows = decay.T
        stats = []
        for h in range(3):
            q = head_rows(block, h)
            inv = lax.rsqrt(jnp.mean(q * q, axis=-1, keepdims=True) + EPS)
            stats.append(inv)
            q_ref[h, at, :] = with_one(q * inv * 0.125, 0).astype(jnp.bfloat16)
            fcol_ref[h, at, :] = jnp.broadcast_to(decay[:, h : h + 1], (size, 128))
            frow_ref[h, :, at] = frows[h : h + 1, :]
        for h in range(3):
            k = head_rows(mixed, h)
            inv = lax.rsqrt(jnp.mean(k * k, axis=-1, keepdims=True) + EPS)
            stats.append(inv)
            k_ref[h, at, :] = with_one(k * inv, 1).astype(jnp.bfloat16)
            v_ref[h, at, :] = head_rows(mixed, 3 + h).astype(jnp.bfloat16)
        shut = jax.nn.sigmoid(-logits)
        stats += [shut[:, h : h + 1] for h in range(3)]
        stats += [mix[:, 3 + h : 4 + h] for h in range(3)]
        stat_ref[at, :] = lanes(stats, size)
        return kv[size - 1 :, :], decay[size - 1 :, :]

    lax.fori_loop(
        0,
        proj_ref.shape[0] // size,
        one,
        (jnp.zeros((1, 384), jnp.float32), jnp.zeros((1, 128), jnp.float32)),
    )


def scores(h, at, start, size, keys, q_ref, k_ref, fcol_ref, frow_ref, lens_ref):
    raw = abt(q_ref[h, at, :], k_ref[h, :keys, :])
    own = jnp.concatenate([fcol_ref[h, at, :]] * (keys // 128), axis=1)
    raw = raw + own - frow_ref[h, :, :keys]
    place, low = bounds(lens_ref, start, size)
    col = lax.broadcasted_iota(jnp.int32, (size, keys), 1)
    return jnp.where((col <= place) & (col >= low), jnp.exp(raw), 0.0)


def over_blocks(body, begin, end):
    for part in range(begin, end):

        def one(n, _, part=part):
            body(n // 2, part * 256 + n % 2 * 128, (part + 1) * 256)
            return 0

        lax.fori_loop(0, 6, one, 0)


def kernel_ab(
    x_ref, seq_ref, gains_ref, cot_ref, head_bias_ref, wq_ref, wg_ref, wk_ref, wv_ref, wh_ref, wfg_ref, wfu_ref,
    wo_ref, down_ref, xs_ref, lens_ref, mid_ref, *refs,
):
    far, refs = refs[:17], refs[17:]
    near_refs, refs = refs[:17], refs[17:]
    (
        h_ref, w_ref, q_ref, k_ref, v_ref, diff_ref, stat_ref, fcol_ref, frow_ref, gate_ref, attn_ref, a_ref,
        wo_all, gu_all, down_all, h2_ref, cot_all,
    ) = near_refs
    (
        lens_own, bias_ref, proj_ref, pack_ref, pack_gu_ref, spread_o,
        part, core, near, corner, send, recv, sems,
    ) = refs
    kept = []

    def keep(i):
        made = pltpu.make_async_copy(near_refs[i], far[i], sems.at[3 + i])
        made.start()
        kept.append(made)

    net = Net(send, recv)
    rows = x_ref.shape[0]
    rank = rank_of(net.at)
    lens_own[...] = jnp.zeros(lens_own.shape, jnp.int32)
    lens_own[0:1, 0:3] = seq_ref[...]
    net.greet()
    moved = move(net, [(x_ref, xs_ref), (lens_own, lens_ref)], sems)
    pack_attention((wq_ref, wg_ref, wk_ref, wv_ref), wh_ref, pack_ref)
    few = head_bias_ref.shape[1] // 8
    bias = jnp.zeros((1, 128), jnp.float32)
    for at in range(8):
        own = jnp.concatenate(
            [head_bias_ref[i : i + 1, at * few : (at + 1) * few] for i in range(2)]
            + [jnp.zeros((1, 128 - 2 * few), jnp.float32)],
            axis=1,
        )
        bias = jnp.where(slice_of(rank) == at, own, bias)
    bias_ref[...] = jnp.broadcast_to(bias, bias_ref.shape)
    spread = Spread(net, w_ref, 4)
    unit = spread.unit
    packs = exchange(net, pack_ref, w_ref.at[unit])
    pack_feeds((wfg_ref, wfu_ref), pack_gu_ref)

    moved()
    value, _inverse = normed(xs_ref[...].astype(jnp.float32))
    h_ref[pl.ds(pl.multiple_of(rank * rows, rows), rows)] = swap_chunks(
        (value * gains_ref[0:1, :]).astype(jnp.bfloat16)
    )
    gather = Gather(net, h_ref, rows)
    gather.first()
    for made in packs:
        made.wait_recv()
    spread.first(4)
    there = (net.at["zh"] * 2 + net.at["zl"]) * 2 + net.at["y"]
    there = pl.ds(pl.multiple_of(there * rows, rows), rows)
    moved_cot = move(net, [(cot_ref, cot_all.at[there])], sems, 2)
    out = Spread(net, spread_o, 1)
    spread_o[unit] = wo_ref[...]
    out.first(1)
    gather.second()
    spread.second(0)
    gather.third()
    spread.second(1)
    given = exchange(net, pack_gu_ref, gu_all.at[unit])
    depth = pack_ref.shape[0] * pack_ref.shape[1]
    tall = 2 * rows

    def multiply(which, fresh):
        def one(i, _):
            at = pl.ds(pl.multiple_of(i * tall, tall), tall)
            left = h_ref[at, pl.ds(pl.multiple_of(which * depth, 128), depth)]
            part = ab(left, w_ref[which].reshape(depth, -1))
            if fresh:
                proj_ref[at, :] = part
            else:
                proj_ref[at, :] += part
            return 0

        lax.fori_loop(0, h_ref.shape[0] // tall, one, 0)

    gather.done()
    keep(0)
    multiply(unit, True)
    spread.wait_across()
    multiply((1 - net.at["x"]) * 2 + net.at["zh"], False)
    spread.second(2)
    spread.second(3)
    multiply(spread.from_zh, False)
    spread.wait_corner()
    multiply((1 - net.at["x"]) * 2 + 1 - net.at["zh"], False)
    keep(1)
    group = proj_ref.shape[0]
    mine = pl.ds(pl.multiple_of(rank * rows, rows), rows)
    feed = Spread(net, gu_all, 4)
    down = Spread(net, down_all, 2)
    moved_cot()
    other = Gather(net, cot_all, rows)
    other.first()
    down_all[unit] = down_ref[...]
    for made in given:
        made.wait_recv()
    feed.first(2)
    down.first(0)
    mixing(proj_ref, lens_ref, bias_ref, q_ref, k_ref, v_ref, diff_ref, stat_ref, fcol_ref, frow_ref)
    for i in (2, 3, 4, 5, 6, 8):
        keep(i)
    out.second(0)
    other.second()

    def attend(h, start, keys):
        at = pl.ds(pl.multiple_of(start, 128), 128)
        e = scores(h, at, start, 128, keys, q_ref, k_ref, fcol_ref, frow_ref, lens_ref)
        total = jnp.sum(e, axis=-1, keepdims=True)
        inv = 1.0 / total
        fcol_ref[h, at, :] -= jnp.broadcast_to(jnp.log(total), (128, 128))
        attn_ref[h, at, :] = ab((e * inv).astype(jnp.bfloat16), v_ref[h, :keys, :])

    over_blocks(attend, 0, 2)
    other.third()
    out.wait_across()
    out.wait_corner()
    pieces = []
    wo_all[unit_of(net.at, ())] = spread_o[unit_of(net.at, ())]
    for names in (("y",), ("zl",), ("zl", "y")):
        pieces.append(net.push(spread_o.at[unit_of(net.at, names)], wo_all.at[unit_of(net.at, ())], names))
    feed.second(0)
    over_blocks(attend, 2, group // 256)
    feed.second(1)
    for h in range(3):
        gate = jax.nn.sigmoid(proj_ref[:, 192 + 64 * h : 256 + 64 * h])
        gate_ref[:, 64 * h : 64 * h + 64] = gate
        a_ref[:, 64 * h : 64 * h + 64] = (gate * attn_ref[h]).astype(jnp.bfloat16)
    for made in pieces:
        made.wait_recv()
    for i in (7, 9, 10, 11, 12):
        keep(i)

    total = Sum(net, part, core, near, corner)

    def project_block(names):
        to = rank_of(flipped(net.at, names))
        left = a_ref[pl.ds(pl.multiple_of(to * rows, rows), rows), :]
        part[to] = ab(left, wo_all[...].reshape(-1, wo_all.shape[2])).astype(jnp.bfloat16)

    for names in (("zl", "y"), ("zl",), ("y",), ()):
        project_block(("core", *names))
        total.give(names)
    project_block(("zl", "y"))
    total.send_corner()
    project_block(("zl",))
    project_block(("y",))
    total.send_y()
    project_block(())
    total.pass_on()
    feed.second(2)
    down.push_next()
    other.done()
    keep(16)
    mid = xs_ref[...].astype(jnp.float32) + total.total()
    mid_ref[...] = mid
    value, _inverse = normed(mid)
    h2_ref[mine] = swap_chunks((value * gains_ref[1:2, :]).astype(jnp.bfloat16))
    gather = Gather(net, h2_ref, rows)
    gather.first()
    feed.second(3)
    down.second(0)
    gather.second()
    feed.wait_across()
    feed.wait_corner()
    keep(13)
    gather.third()
    down.second(1)
    gather.done()
    keep(15)
    down.wait_across()
    down.wait_corner()
    keep(14)
    for made in kept:
        made.wait()
    net.drain()


class SpreadSum:
    def __init__(self, net, whole_ref, over_x, over_zh, pieces, relay=None, by_rank=False):
        self.relay, self.by_rank = relay, by_rank
        self.net, self.whole, self.over_x, self.over_zh, self.pieces = net, whole_ref, over_x, over_zh, pieces
        self.size = whole_ref.shape[1] // pieces
        self.x, self.zh = net.at["x"], net.at["zh"]
        self.far, self.own, self.last = [], [], []

    def rows(self, piece):
        return pl.ds(quarter(self.net, piece) if self.by_rank else piece * self.size, self.size)

    def part(self, ref, at, piece):
        return ref.at[at, self.rows(piece)]

    def send(self, zh, target, piece):
        source = self.part(self.whole, (1 - self.x) * 2 + zh, piece)
        return self.net.push(source, target, ("x",))

    def first_far(self):
        for piece in range(self.pieces):
            zh = 1 - self.zh
            self.far.append(self.send(zh, self.part(self.over_x, zh, piece), piece))

    def first_own(self):
        for piece in range(self.pieces):
            self.own.append(self.send(self.zh, self.part(self.over_x, self.zh, piece), piece))

    def first(self):
        self.first_far()
        self.first_own()

    def pass_far(self):
        for piece in range(self.pieces):
            to = self.over_x.at[self.rows(piece)]
            self.own.append(self.send(self.zh, to, piece))

    def pass_far_on(self, far, begin, end):
        for piece in range(begin, end):
            self.pass_one(piece, far.at[self.rows(piece)])

    def hand_out(self, target):
        made = []
        rank = rank_of(self.net.at)
        for piece, names in enumerate(QUARTERS):
            self.over_zh[self.rows(piece)] = self.total(piece).astype(jnp.bfloat16)
            for more in (names, (*names, "y")):
                if more:
                    to = self.over_zh.at[rank_of(flipped(self.net.at, more))]
                    made.append(self.net.push(to, target.at[rank], more))
                else:
                    target[rank] = self.over_zh[rank]
        return made

    def second(self, piece):
        self.far[piece].wait_recv()
        self.pass_one(piece, self.part(self.over_x, 1 - self.zh, piece))

    def pass_one(self, piece, came):
        here = self.part(self.whole, self.x * 2 + 1 - self.zh, piece)
        total = (here[...].astype(jnp.float32) + came[...].astype(jnp.float32)).astype(jnp.bfloat16)
        if self.relay is not None:
            here = self.relay.at[self.rows(piece)]
        here[...] = total
        target = self.over_zh.at[self.rows(piece)]
        self.last.append(self.net.push(here, target, ("zh",)))

    def total(self, piece):
        self.own[piece].wait_recv()
        self.last[piece].wait_recv()
        here = self.part(self.whole, self.x * 2 + self.zh, piece)
        if self.relay is None:
            came = self.part(self.over_x, self.zh, piece)
        else:
            came = self.over_x.at[self.rows(piece)]
        last = self.over_zh.at[self.rows(piece)]
        return (
            here[...].astype(jnp.float32) + came[...].astype(jnp.float32) + last[...].astype(jnp.float32)
        )


def norm_grad(grad, gain, value, inverse):
    scaled = grad * gain
    return (
        inverse * (scaled - value * jnp.mean(scaled * value, axis=-1, keepdims=True)),
        jnp.sum(grad * value, axis=0, keepdims=True),
    )


def kernel_c(
    h_ref, cot_ref, wgu_ref, wd_ref, mid_ref, gains_ref,
    hid_ref, dmid_ref, dao_ref, gain_ref, gdown_ref, ggu_ref, gfar_ref,
    dgu_ref, gd_ref, over_x, over_zh, part, core, near, corner, send, recv, sems,
):
    net = Net(send, recv)
    rank = rank_of(net.at)
    rows = mid_ref.shape[0]
    mine = pl.ds(pl.multiple_of(rank * rows, rows), rows)
    wide = hid_ref.shape[1]
    width = mid_ref.shape[1]
    four = 4 * rows
    net.greet()

    def half(which):
        at = pl.ds(pl.multiple_of(which * four, four), four)
        wgu = wgu_ref[...].reshape(width, 2 * wide)
        both = ab(h_ref[at, :], wgu)
        gate, up = both[:, :wide], both[:, wide:]
        sig = jax.nn.sigmoid(gate)
        act = gate * sig
        hid_ref[at, :] = (act * up).astype(jnp.bfloat16)
        grad = abt(cot_ref[at, :], wd_ref[...].reshape(wide, width))
        dgate = grad * up * sig * (1.0 + gate * (1.0 - sig))
        dgu = jnp.concatenate([dgate, grad * act], axis=1).astype(jnp.bfloat16)
        dgu_ref[at, :] = dgu
        back = abt(dgu, wgu).astype(jnp.bfloat16)
        for i in range(4):
            part[which * 4 + i] = back[i * rows : (i + 1) * rows]

    total = Sum(net, part, core, near, corner)
    half(1 - net.at["core"])
    for names in (("zl", "y"), ("zl",), ("y",), ()):
        total.give(names)
    half(net.at["core"])
    total.send_corner()
    total.send_y()
    down = SpreadSum(net, gd_ref, over_x, over_zh, 2)

    def grad_down(k, _):
        left = hid_ref[:, pl.ds(pl.multiple_of(k * rows, rows), rows)]
        gd_ref[k] = atb(left, cot_ref[...]).astype(jnp.bfloat16)
        return 0

    lax.fori_loop(0, 4, grad_down, 0)
    down.first()
    total.pass_on()
    depth = width // 4

    def grad_gu(k, _):
        left = h_ref[:, pl.ds(pl.multiple_of(k * depth, depth), depth)]
        ggu_ref[k] = atb(left, dgu_ref[...]).astype(jnp.bfloat16).reshape(ggu_ref.shape[1:])
        return 0

    lax.fori_loop(0, 4, grad_gu, 0)
    feed = SpreadSum(net, ggu_ref, None, None, 1)
    far = feed.send(1 - net.at["zh"], gfar_ref, 0)
    grad = swap_chunks(total.total())
    value, inverse = normed(mid_ref[...])
    back, gain = norm_grad(grad, gains_ref[1:2, :], value, inverse)
    gain_ref[...] = gain
    dmid = cot_ref[mine, :].astype(jnp.float32) + back
    dmid_ref[...] = dmid
    dao_ref[mine] = dmid.astype(jnp.bfloat16)
    gather = Gather(net, dao_ref, rows)
    gather.first()
    down.second(0)
    down.second(1)
    gather.second()
    gather.third()
    for piece in range(2):
        gdown_ref[pl.ds(piece * rows // 2, rows // 2)] = down.total(piece)
    gather.done()
    far.wait_recv()
    net.drain()


def spread_scratch(shape):
    return [
        pltpu.VMEM((4, *shape), jnp.bfloat16),
        pltpu.VMEM((2, *shape), jnp.bfloat16),
        pltpu.VMEM(shape, jnp.bfloat16),
    ]


def unmixing(
    lens_ref, q_ref, k_ref, diff_ref, stat_ref, dq_ref, dk_ref, dv_ref, dproj_ref
):
    size = 128
    count = diff_ref.shape[0] // size
    upper = triangle(size, True)

    def one(step, carry):
        after, above, sums = carry
        i = count - 1 - step
        at = pl.ds(pl.multiple_of(i * size, size), size)
        stat = stat_ref[at, :]
        decay, keys, values = [], [], []
        for h in range(3):
            dq, dk = dq_ref[h, at, :], dk_ref[h, at, :]
            decay.append(dq[:, 65:66] - dk[:, 64:65])
            grad = dq[:, :64] * 0.125
            unit = q_ref[h, at, :][:, :64].astype(jnp.float32) * 8.0
            grad = grad - unit * jnp.mean(grad * unit, axis=-1, keepdims=True)
            dproj_ref[at, 64 * h : 64 * h + 64] = (stat[:, h : h + 1] * grad).astype(jnp.bfloat16)
            grad = dk[:, :64]
            unit = k_ref[h, at, :][:, :64].astype(jnp.float32)
            grad = grad - unit * jnp.mean(grad * unit, axis=-1, keepdims=True)
            keys.append(stat[:, 3 + h : 4 + h] * grad)
            values.append(dv_ref[h, at, :])
        both = jnp.concatenate(keys + values, axis=1)
        prod = both * diff_ref[at, :]
        mix = [stat[:, 9 + h : 10 + h] for h in range(3)]
        mixes = spread_lanes(mix, size, 384)
        place, low = bounds(lens_ref, i * size, size)
        carried = jnp.where(place == low, 0.0, both * mixes)
        row = lax.broadcasted_iota(jnp.int32, (size, 384), 0)
        later = jnp.where(row == size - 1, after, pltpu.roll(carried, size - 1, 0))
        dproj_ref[at, 384:768] = (both * (1.0 - mixes) + later).astype(jnp.bfloat16)
        decay = lanes(decay, size)
        suffix = exact(upper, decay) + above
        small = []
        for h in range(3):
            small.append(suffix[:, h : h + 1] * stat[:, 6 + h : 7 + h])
        for h in range(3):
            grad = jnp.sum(head_rows(prod, h) + head_rows(prod, 3 + h), axis=-1, keepdims=True)
            small.append(grad * mix[h] * (1.0 - mix[h]))
        small = lanes(small, size)
        dproj_ref[at, 768:896] = small.astype(jnp.bfloat16)
        above = above + jnp.sum(decay, axis=0, keepdims=True)
        return carried[:1, :], above, sums + jnp.sum(small, axis=0, keepdims=True)

    none = jnp.zeros((1, 128), jnp.float32)
    carry = lax.fori_loop(0, count, one, (jnp.zeros((1, 384), jnp.float32), none, none))
    return carry[2]


def kernel_d(
    dao_ref, wo_ref, a_ref, attn_far, gate_far, lens_ref, q_far, k_far, v_far, diff_far, stat_far,
    fcol_far, frow_far, w_far, h_ref, dmid_far, x_far, gains_ref, gain_two_ref, ggu_ref, gfar_ref,
    hid_ref, wd_ref, mid_ref,
    out_ref, gx_ref, gain_ref, bias_ref, ga_ref, go_ref, gu_ref,
    do_ref, dq_ref, dk_ref, dv_ref, dproj_ref,
    gu_x, gu_zh, a_whole, a_x, a_zh, o_raw, o_whole, o_x, o_zh, small, slots, tall, gx_own, out_own,
    part, core, near, corner, core2, near2, corner2, *refs,
):
    *late, send, recv, sems = refs
    attn_ref, gate_ref, q_ref, k_ref, v_ref, fcol_ref, frow_ref, diff_ref, stat_ref, w_ref, dmid_ref, x_ref = late
    far = (attn_far, gate_far, q_far, k_far, v_far, fcol_far, frow_far, diff_far, stat_far, w_far, dmid_far, x_far)
    net = Net(send, recv)
    rank = rank_of(net.at)
    rows, width = mid_ref.shape
    group = a_ref.shape[0]
    mine = pl.ds(pl.multiple_of(rank * rows, rows), rows)
    fetch = [pltpu.make_async_copy(ref, tall, sems.at[2 + i]) for i, ref in enumerate((dao_ref, h_ref))]
    fetch[0].start()
    loads = [
        pltpu.make_async_copy(source, target, sems.at[4 + i])
        for i, (source, target) in enumerate(zip(far, late))
    ]
    for made in loads:
        made.start()
    net.greet()
    feed = SpreadSum(net, ggu_ref, gu_x.at[0], gu_zh, 4, gu_x.at[1], True)
    attn = SpreadSum(net, a_whole, a_x, a_zh, 4, None, True)
    out = SpreadSum(net, o_whole, o_x, o_zh, 1)

    wo = wo_ref[...].reshape(-1, width)
    four = 4 * rows

    def half(which, left_ref, right, multiply, to):
        def one(i, _):
            at = pl.multiple_of(which * four + i * 2 * rows, 2 * rows)
            back = multiply(left_ref[pl.ds(at, 2 * rows), :], right).astype(jnp.bfloat16)
            to[which * 4 + 2 * i] = back[:rows]
            to[which * 4 + 2 * i + 1] = back[rows:]
            return 0

        lax.fori_loop(0, 2, one, 0)

    result = Sum(net, part, core2, near2, corner2)
    wd = wd_ref[...].reshape(-1, width)
    feed.pass_far()
    feed.pass_far_on(gfar_ref, 0, 2)
    half(1 - net.at["core"], hid_ref, wd, ab, part)
    for names in (("zl", "y"), ("zl",), ("y",), ()):
        result.give(names)
    half(net.at["core"], hid_ref, wd, ab, part)
    fetch[0].wait()
    for made in loads[:2]:
        made.wait()
    da = abt(tall[...], wo)
    for h in range(3):
        sig = gate_ref[:, 64 * h : 64 * h + 64]
        grad = da[:, 64 * h : 64 * h + 64] * sig
        do_ref[h] = grad.astype(jnp.bfloat16)
        dproj_ref[:, 192 + 64 * h : 256 + 64 * h] = (grad * attn_ref[h] * (1.0 - sig)).astype(
            jnp.bfloat16
        )
    o_raw[...] = atb(a_ref[...], tall[...]).astype(jnp.bfloat16).reshape(o_raw.shape)
    fetch[1].start()
    here = unit_of(net.at, ())
    o_whole[here] = o_raw[here]
    pieces = []
    for names in (("y",), ("zl",), ("zl", "y")):
        pieces.append(net.push(o_raw.at[unit_of(net.at, names)], o_whole.at[here], names))
    dk_ref[...] = jnp.zeros(dk_ref.shape, jnp.float32)
    dv_ref[...] = jnp.zeros(dv_ref.shape, jnp.float32)

    def attend(h, start, keys):
        at = pl.ds(pl.multiple_of(start, 128), 128)
        p = scores(h, at, start, 128, keys, q_ref, k_ref, fcol_ref, frow_ref, lens_ref)
        do = do_ref[h, at, :]
        dp = abt(do, v_ref[h, :keys, :])
        ds = p * (dp - jnp.sum(p * dp, axis=-1, keepdims=True))
        ds = ds.astype(jnp.bfloat16)
        dq_ref[h, at, :] = ab(ds, k_ref[h, :keys, :])
        dk_ref[h, :keys, :] += atb(ds, q_ref[h, at, :])
        dv_ref[h, :keys, :] += atb(p.astype(jnp.bfloat16), do)

    result.send_corner()
    result.send_y()
    for made in pieces:
        made.wait_recv()
    out.first()
    for made in loads[2:]:
        made.wait()
    over_blocks(attend, 0, 3)
    result.pass_on()
    feed.pass_far_on(gfar_ref, 2, 4)
    over_blocks(attend, 3, 4)
    out.second(0)
    sums = unmixing(lens_ref, q_ref, k_ref, diff_ref, stat_ref, dq_ref, dk_ref, dv_ref, dproj_ref)

    result.left_cores()
    out_own[...] = (mid_ref[...] + result.total()).astype(jnp.bfloat16)
    moved_out = move(net, [(out_own, out_ref)], sems)
    result.left()
    total = Sum(net, part, core, near, corner)
    w = w_ref[...].reshape(width, -1)
    half(1 - net.at["core"], dproj_ref, w, abt, part)
    for names in (("zl", "y"), ("zl",), ("y",), ()):
        total.give(names)
    half(net.at["core"], dproj_ref, w, abt, part)
    total.send_corner()
    total.send_y()
    depth = width // 4

    def grad_attn(k, _):
        left = tall[:, pl.ds(pl.multiple_of(k * depth, depth), depth)]
        a_whole[k] = atb(left, dproj_ref[...]).astype(jnp.bfloat16).reshape(a_whole.shape[1:])
        return 0

    fetch[1].wait()
    lax.fori_loop(0, 4, grad_attn, 0)
    attn.first_far()
    total.pass_on()
    attn.second(0)
    given = feed.hand_out(gu_ref)
    attn.second(1)
    grad = swap_chunks(total.total())
    attn.second(2)
    value, inverse = normed(x_ref[...].astype(jnp.float32))
    back, gain = norm_grad(grad, gains_ref[0:1, :], value, inverse)
    small[0] = jnp.concatenate(
        [gain, gain_two_ref[...], jnp.concatenate([sums, jnp.zeros((1, width - 128), jnp.float32)], axis=1)]
        + [jnp.zeros((5, width), jnp.float32)],
        axis=0,
    )
    first = net.push(small.at[0], small.at[1], ("x",))
    attn.first_own()
    gx_own[...] = (dmid_ref[...] + back).astype(jnp.bfloat16)
    go_ref[...] = out.total(0)
    first.wait_recv()
    small[2] = small[0] + small[1]
    second = net.push(small.at[2], small.at[3], ("zh",))
    attn.second(3)
    second.wait_recv()
    slots[rank] = small[2] + small[3]
    shared = [net.push(slots.at[rank], slots.at[rank], names) for names in PARTNERS[:7]]
    moved_gx = move(net, [(gx_own, gx_ref)], sems, 1)
    given += attn.hand_out(ga_ref)
    for made in shared + given:
        made.wait_recv()
    gain_ref[...] = jnp.sum(slots[:, 0:2, :], axis=0)
    bias_ref[...] = slots[:, 2:3, :128]
    moved_out()
    moved_gx()
    net.drain()


def finish(
    out_ref, gx_ref, gain_ref, bias_ref, ga_ref, go_ref, gu_ref, gdown_ref,
    out_out, gx_out, gain_out, bias_out, gq_out, gk_out, gv_out, gg_out, go_out, gh_out, gfg_out, gfu_out, gdown_out,
):
    for source, target in ((out_ref, out_out), (gain_ref, gain_out), (go_ref, go_out), (gdown_ref, gdown_out)):
        target[...] = source[...]
    gx_out[...] = gx_ref[...].astype(jnp.float32)
    size = gq_out.shape[1] // 8
    few = bias_out.shape[1] // 8
    block = gfg_out.shape[1] // 32
    for rank in range(8):
        at = slice_of(rank)
        for i, target in enumerate((gq_out, gg_out, gk_out, gv_out)):
            part = ga_ref[rank, :, i * size : (i + 1) * size]
            target[:, at * size : (at + 1) * size] = part.astype(jnp.float32)
        part = ga_ref[rank, :, 4 * size :].astype(jnp.float32)
        for i in range(2):
            to = (i * 8 + at) * few
            gh_out[:, to : to + few] = part[:, i * few : (i + 1) * few]
            bias_out[i : i + 1, at * few : (at + 1) * few] = bias_ref[rank, :, i * few : (i + 1) * few]
        for i, target in enumerate((gfg_out, gfu_out)):
            for unit in range(4):
                to = (unit // 2 * 16 + rank // 4 * 8 + unit % 2 * 4 + rank % 4) * block
                part = gu_ref[rank, :, (i * 4 + unit) * block : (i * 4 + unit + 1) * block]
                target[:, to : to + block] = part.astype(jnp.float32)


def squares(
    layer_input,
    cotangent,
    seq_lengths,
    gains,
    head_bias,
    w_query,
    w_key,
    w_value,
    w_gate,
    w_out,
    w_heads,
    w_ff_gate,
    w_ff_up,
    w_ff_down,
):
    rows, width = layer_input.shape
    heads = head_bias.shape[1]
    head_dim = width // heads
    ranks = 8
    group = rows * ranks
    mine = heads // ranks
    cols = mine * head_dim
    shard = w_query.shape[0]
    units = w_ff_gate.shape[1] // ranks
    low = jnp.bfloat16
    f32 = jnp.float32
    packs = (ranks, shard, 4 * cols + 128)
    feeds = (ranks, shard, 2 * units)
    lens_shape = (8, 128)
    kept = (
        whole((group, width), low),
        whole((4, *packs), low),
        whole((mine, group, 128), low),
        whole((mine, group, 128), low),
        whole((mine, group, head_dim), low),
        whole((group, 2 * cols), f32),
        whole((group, 128), f32),
        whole((mine, group, 128), f32),
        whole((mine, 1, group), f32),
        whole((group, cols), f32),
        whole((mine, group, head_dim), f32),
        whole((group, cols), low),
        whole((4, shard, width), low),
        whole((4, *feeds), low),
        whole((4, *w_ff_down.shape), low),
        whole((group, width), low),
        whole((group, width), low),
    )
    (
        packed, lengths, mid,
        h_one_all, w_attn, q_all, k_all, v_all, diff, stat, fcol, frow, gate_sig, attn3, branch_in,
        w_o, w_gu, w_d, h_two_all, cot_all,
    ) = call(
        kernel_ab,
        1,
        (
            whole(layer_input.shape, low),
            whole(lens_shape, jnp.int32),
            whole((rows, width), f32),
            *kept,
        ),
        (
            layer_input, seq_lengths, gains, cotangent, head_bias,
            w_query, w_gate, w_key, w_value, w_heads, w_ff_gate, w_ff_up, w_out, w_ff_down,
        ),
        112,
        [
            *(pltpu.VMEM(leaf.shape, leaf.dtype) for leaf in kept),
            pltpu.VMEM(lens_shape, jnp.int32),
            pltpu.VMEM((8, 128), f32),
            pltpu.VMEM((group, packs[2]), f32),
            pltpu.VMEM(packs, low),
            pltpu.VMEM(feeds, low),
            pltpu.VMEM((4, shard, width), low),
            *sum_scratch(rows, width),
        ],
        local=3 + len(kept),
        far_outs=range(3, 3 + len(kept)),
    )
    hidden, grad_mid, grad_branch, gain_two, grad_down, grad_gu, grad_far = call(
        kernel_c,
        3,
        (
            whole((group, units), low),
            whole((rows, width), f32),
            whole((group, width), low),
            whole((1, width), f32),
            whole((rows, width), f32),
            whole((4, *feeds), low),
            whole(feeds, low),
        ),
        (h_two_all, cot_all, w_gu, w_d, mid, gains),
        48,
        [
            pltpu.VMEM((group, 2 * units), low),
            pltpu.VMEM((4, rows, width), low),
            pltpu.VMEM((2, rows, width), low),
            pltpu.VMEM((rows, width), low),
            *sum_scratch(rows, width),
        ],
    )
    result, grad_input, gain_sums, bias_sums, grad_attn_w, grad_wout, grad_gu = call(
        kernel_d,
        4,
        (
            whole((rows, width), low),
            whole((rows, width), low),
            whole((2, width), f32),
            whole((ranks, 1, 128), f32),
            whole(packs, low),
            whole((shard, width), f32),
            whole(feeds, low),
        ),
        (
            grad_branch, w_o, branch_in, attn3, gate_sig, lengths, q_all, k_all, v_all, diff, stat,
            fcol, frow, w_attn, h_one_all, grad_mid, packed, gains, gain_two, grad_gu, grad_far,
            hidden, w_d, mid,
        ),
        96,
        [
            pltpu.VMEM((mine, group, head_dim), low),
            pltpu.VMEM((mine, group, 128), f32),
            pltpu.VMEM((mine, group, 128), f32),
            pltpu.VMEM((mine, group, head_dim), f32),
            pltpu.VMEM((group, packs[2]), low),
            *spread_scratch(feeds)[1:],
            *spread_scratch(packs),
            pltpu.VMEM((4, shard, width), low),
            *spread_scratch((shard, width)),
            pltpu.VMEM((4, 8, width), f32),
            pltpu.VMEM((ranks, 8, width), f32),
            pltpu.VMEM((group, width), low),
            pltpu.VMEM((rows, width), low),
            pltpu.VMEM((rows, width), low),
            *sum_scratch(rows, width),
            *sum_scratch(rows, width)[1:],
            *(pltpu.VMEM(leaf.shape, leaf.dtype) for leaf in (attn3, gate_sig, q_all, k_all, v_all, fcol, frow, diff, stat, w_attn, grad_mid, packed)),
        ],
        16,
        (0, 14, 3, 4, 6, 7, 8, 11, 12, 9, 10, 13, 15, 16),
    )

    big = whole((shard, width), f32)
    outs = (
        whole((rows, width), low),
        whole((rows, width), f32),
        whole((2, width), f32),
        whole((2, heads), f32),
        big,
        big,
        big,
        big,
        big,
        whole((shard, 2 * heads), f32),
        whole(w_ff_gate.shape, f32),
        whole(w_ff_up.shape, f32),
        whole(w_ff_down.shape, f32),
    )
    args = (result, grad_input, gain_sums, bias_sums, grad_attn_w, grad_wout, grad_gu, grad_down)
    return pl.pallas_call(
        finish,
        out_shape=outs,
        in_specs=vmem(len(args)),
        out_specs=vmem(len(outs)),
        compiler_params=pltpu.CompilerParams(vmem_limit_bytes=60 * 2**20),
    )(*args)


def solution(mesh):
    if mesh.shape["dp"] == 4 and mesh.shape["ctx"] == 8:
        body, axes, group = squares, AXES, ("x", "core")
        mesh = Mesh(np.reshape(mesh.devices, (2, 2, 2, 2, 2)), AXES)
    else:
        body, axes, group = shards, ("dp", "ctx"), "dp"
    cut = P(axes, None)
    return jax.shard_map(
        body,
        mesh=mesh,
        in_specs=(cut, cut, P(group, None), P(), P()) + (cut,) * 9,
        out_specs=(cut, cut, P(), P()) + (cut,) * 9,
        check_vma=False,
    )
```

```python
import jax
import jax.numpy as jnp
import numpy as np
from jax import lax
from jax.experimental import pallas as pl
from jax.experimental.pallas import tpu as pltpu
from jax.sharding import Mesh
from jax.sharding import PartitionSpec as P

EPS = 1e-06


def passed_along(array, axis, by):
    size = lax.axis_size(axis)
    pairs = [(i, i + by) for i in range(size) if 0 <= i + by < size]
    return lax.ppermute(array, axis, pairs)


def entering(part, axis, combine, identity, reverse):
    count = lax.axis_size(axis)
    place = lax.axis_index(axis)
    ahead = count - 1 - place if reverse else place
    gathered = lax.all_gather(part, axis)
    state = jnp.zeros_like(part) + jnp.asarray(identity, part.dtype)

    def one(step, state):
        source = count - 1 - step if reverse else step
        return combine(state, lax.dynamic_index_in_dim(gathered, source, 0, False))

    return lax.fori_loop(0, ahead, one, state)


def fetch_attention(w_query, w_key, w_value, w_gate, w_out, w_heads):
    return (
        lax.all_gather(w_query, ("dp", "ctx"), axis=0, tiled=True),
        lax.all_gather(w_key, ("dp", "ctx"), axis=0, tiled=True),
        lax.all_gather(w_value, ("dp", "ctx"), axis=0, tiled=True),
        lax.all_gather(w_gate, ("dp", "ctx"), axis=0, tiled=True),
        lax.all_gather(w_out, ("dp", "ctx"), axis=0, tiled=True),
        lax.all_gather(w_heads, ("dp", "ctx"), axis=0, tiled=True),
    )


def fetch_feed(w_ff_gate, w_ff_up, w_ff_down):
    return (
        lax.all_gather(w_ff_gate, ("dp", "ctx"), axis=0, tiled=True),
        lax.all_gather(w_ff_up, ("dp", "ctx"), axis=0, tiled=True),
        lax.all_gather(w_ff_down, ("dp", "ctx"), axis=0, tiled=True),
    )


def add_arrays(earlier, later):
    return earlier + later


def norm_back(grad, normed, inverse):
    return inverse * (grad - normed * jnp.mean(grad * normed, axis=-1, keepdims=True))


def project(left, right):
    return jnp.dot(left, right, preferred_element_type=jnp.float32)


def weight_grad(left, right):
    return jnp.einsum("ra,rb->ab", left, right, preferred_element_type=jnp.float32)


def input_grad(grad, weight):
    return jnp.einsum("rb,ab->ra", grad, weight, preferred_element_type=jnp.float32)


def shards(
    layer_input,
    cotangent,
    seq_lengths,
    gains,
    head_bias,
    w_query,
    w_key,
    w_value,
    w_gate,
    w_out,
    w_heads,
    w_ff_gate,
    w_ff_up,
    w_ff_down,
):
    rows, width = layer_input.shape
    heads = head_bias.shape[1]
    head_dim = width // heads
    spans = lax.axis_size("ctx")
    group = rows * spans
    scale = head_dim ** (-0.5)
    here = lax.axis_index("ctx")
    local_pos = here * rows + jnp.arange(rows, dtype=jnp.int32)
    key_pos = jnp.arange(group, dtype=jnp.int32)
    first = seq_lengths[0, 0]
    second = first + seq_lengths[0, 1]
    local_seg = (local_pos >= first).astype(jnp.int32) + (local_pos >= second).astype(jnp.int32)
    key_seg = (key_pos >= first).astype(jnp.int32) + (key_pos >= second).astype(jnp.int32)
    starts = (local_pos == 0) | (local_pos == first) | (local_pos == second)
    keep = (1 - starts.astype(jnp.int32)).astype(jnp.float32)[:, None]
    allowed = (local_seg[:, None] == key_seg[None, :]) & (key_pos[None, :] <= local_pos[:, None])
    x_full = layer_input.astype(jnp.float32)
    inv_one = lax.rsqrt(jnp.mean(x_full * x_full, axis=-1, keepdims=True) + EPS)
    normed_one = x_full * inv_one
    h_one = (normed_one * gains[0]).astype(jnp.bfloat16)
    full_query, full_key, full_value, full_gate, full_out, full_heads = fetch_attention(
        w_query, w_key, w_value, w_gate, w_out, w_heads
    )
    query = project(h_one, full_query)
    key_raw = project(h_one, full_key)
    value_raw = project(h_one, full_value)
    gate_raw = project(h_one, full_gate)
    head_raw = project(h_one, full_heads)
    forget_logit = head_raw[:, :heads] + head_bias[0]
    shift_logit = head_raw[:, heads:] + head_bias[1]
    log_forget = jax.nn.log_sigmoid(forget_logit)
    mix_small = jax.nn.sigmoid(shift_logit)
    mix = jnp.repeat(mix_small, head_dim, axis=1)
    prev_row = passed_along(h_one[rows - 1 :], "ctx", 1)
    key_prev = jnp.concatenate([project(prev_row, full_key), key_raw[:-1]], 0) * keep
    value_prev = jnp.concatenate([project(prev_row, full_value), value_raw[:-1]], 0) * keep
    key_mix = mix * key_prev + (1.0 - mix) * key_raw
    value_mix = mix * value_prev + (1.0 - mix) * value_raw
    query4 = query.reshape(rows, heads, head_dim)
    query_inv = lax.rsqrt(jnp.mean(query4 * query4, axis=-1, keepdims=True) + EPS)
    query_norm = query4 * query_inv
    key4 = key_mix.reshape(rows, heads, head_dim)
    key_inv = lax.rsqrt(jnp.mean(key4 * key4, axis=-1, keepdims=True) + EPS)
    key_norm = key4 * key_inv
    q_low = query_norm.astype(jnp.bfloat16)
    k_low = key_norm.reshape(rows, width).astype(jnp.bfloat16)
    v_low = value_mix.astype(jnp.bfloat16)
    local_cum = jnp.cumsum(log_forget, axis=0)
    offset = entering(
        local_cum[rows - 1], "ctx", add_arrays, jnp.zeros((heads,), jnp.float32), False
    )
    decay = local_cum + offset
    gathered_k, gathered_v, all_decay = (
        lax.all_gather(k_low.astype(jnp.float32), "ctx", axis=0, tiled=True),
        lax.all_gather(v_low.astype(jnp.float32), "ctx", axis=0, tiled=True),
        lax.all_gather(decay, "ctx", axis=0, tiled=True),
    )
    all_keys = gathered_k.astype(jnp.bfloat16).reshape(group, heads, head_dim)
    all_values = gathered_v.astype(jnp.bfloat16).reshape(group, heads, head_dim)

    def scores_of(index, keys_whole, decay_whole):
        q_part = lax.dynamic_slice_in_dim(q_low, index * 4, 4, 1)
        k_part = lax.dynamic_slice_in_dim(keys_whole, index * 4, 4, 1)
        own = lax.dynamic_slice_in_dim(decay, index * 4, 4, 1)
        far = lax.dynamic_slice_in_dim(decay_whole, index * 4, 4, 1)
        raw = jnp.einsum("rhd,ghd->hrg", q_part, k_part, preferred_element_type=jnp.float32) * scale
        raw = raw + own.T[:, :, None] - far.T[:, None, :]
        return (jnp.where(allowed[None], raw, -1e30), q_part, k_part)

    group_count = heads // 4

    def forward_step(index, carry):
        mixed, log_total = carry
        scores, q_part, k_part = scores_of(index, all_keys, all_decay)
        v_part = lax.dynamic_slice_in_dim(all_values, index * 4, 4, 1)
        top = jnp.max(scores, axis=-1, keepdims=True)
        expd = jnp.exp(scores - top)
        total = jnp.sum(expd, axis=-1, keepdims=True)
        probs = (expd / total).astype(jnp.bfloat16)
        part = jnp.einsum("hrg,ghd->rhd", probs, v_part, preferred_element_type=jnp.float32)
        mixed = lax.dynamic_update_slice_in_dim(mixed, part, index * 4, 1)
        log_total = lax.dynamic_update_slice_in_dim(
            log_total, (top + jnp.log(total))[:, :, 0].T, index * 4, 1
        )
        return (mixed, log_total)

    attn4, log_total = lax.fori_loop(
        0,
        group_count,
        forward_step,
        (jnp.zeros((rows, heads, head_dim), jnp.float32), jnp.zeros((rows, heads), jnp.float32)),
    )
    attn = attn4.reshape(rows, width)
    gate_sig = jax.nn.sigmoid(gate_raw)
    branch_in = (gate_sig * attn).astype(jnp.bfloat16)
    mid = x_full + project(branch_in, full_out)
    inv_two = lax.rsqrt(jnp.mean(mid * mid, axis=-1, keepdims=True) + EPS)
    normed_two = mid * inv_two
    h_two = (normed_two * gains[1]).astype(jnp.bfloat16)
    full_ff_gate, full_ff_up, full_ff_down = fetch_feed(w_ff_gate, w_ff_up, w_ff_down)
    ff_gate = project(h_two, full_ff_gate)
    ff_up = project(h_two, full_ff_up)
    ff_sig = jax.nn.sigmoid(ff_gate)
    hidden = (ff_gate * ff_sig * ff_up).astype(jnp.bfloat16)
    result = (mid + project(hidden, full_ff_down)).astype(jnp.bfloat16)
    full_ff_gate, full_ff_up, full_ff_down = fetch_feed(w_ff_gate, w_ff_up, w_ff_down)
    full_query, full_key, full_value, full_gate, full_out, full_heads = fetch_attention(
        w_query, w_key, w_value, w_gate, w_out, w_heads
    )
    grad_out = cotangent.astype(jnp.float32)
    grad_down = weight_grad(hidden, cotangent)
    grad_hidden = input_grad(cotangent, full_ff_down)
    grad_gate_ff = (grad_hidden * ff_up * ff_sig * (1.0 + ff_gate * (1.0 - ff_sig))).astype(
        jnp.bfloat16
    )
    grad_up_ff = (grad_hidden * (ff_gate * ff_sig)).astype(jnp.bfloat16)
    ffn_grads = (
        lax.psum_scatter(
            weight_grad(h_two, grad_gate_ff), ("dp", "ctx"), scatter_dimension=0, tiled=True
        ),
        lax.psum_scatter(
            weight_grad(h_two, grad_up_ff), ("dp", "ctx"), scatter_dimension=0, tiled=True
        ),
        lax.psum_scatter(grad_down, ("dp", "ctx"), scatter_dimension=0, tiled=True),
    )
    grad_h_two = input_grad(grad_gate_ff, full_ff_gate) + input_grad(grad_up_ff, full_ff_up)
    gain_two = jnp.sum(grad_h_two * normed_two, axis=0)
    grad_mid = norm_back(grad_h_two * gains[1], normed_two, inv_two) + grad_out
    grad_branch = grad_mid.astype(jnp.bfloat16)
    grad_wout = weight_grad(branch_in, grad_branch)
    grad_branch_in = input_grad(grad_branch, full_out)
    grad_attn = (grad_branch_in * gate_sig).astype(jnp.bfloat16).reshape(rows, heads, head_dim)
    grad_gate = (grad_branch_in * attn * gate_sig * (1.0 - gate_sig)).astype(jnp.bfloat16)
    gathered_k, gathered_v, all_decay = (
        lax.all_gather(k_low.astype(jnp.float32), "ctx", axis=0, tiled=True),
        lax.all_gather(v_low.astype(jnp.float32), "ctx", axis=0, tiled=True),
        lax.all_gather(decay, "ctx", axis=0, tiled=True),
    )
    all_keys = gathered_k.astype(jnp.bfloat16).reshape(group, heads, head_dim)
    all_values = gathered_v.astype(jnp.bfloat16).reshape(group, heads, head_dim)

    def backward_step(index, carry):
        grad_q, grad_k, grad_v, grad_own, grad_far = carry
        scores, q_part, k_part = scores_of(index, all_keys, all_decay)
        v_part = lax.dynamic_slice_in_dim(all_values, index * 4, 4, 1)
        lse = lax.dynamic_slice_in_dim(log_total, index * 4, 4, 1).T[:, :, None]
        probs = jnp.exp(scores - lse)
        probs_low = probs.astype(jnp.bfloat16)
        grad_part = lax.dynamic_slice_in_dim(grad_attn, index * 4, 4, 1)
        grad_probs = jnp.einsum(
            "rhd,ghd->hrg", grad_part, v_part, preferred_element_type=jnp.float32
        )
        value_term = jnp.einsum(
            "hrg,rhd->ghd", probs_low, grad_part, preferred_element_type=jnp.float32
        )
        grad_scores = (
            probs * (grad_probs - jnp.sum(probs * grad_probs, axis=-1, keepdims=True))
        ).astype(jnp.bfloat16)
        query_term = (
            jnp.einsum("hrg,ghd->rhd", grad_scores, k_part, preferred_element_type=jnp.float32)
            * scale
        )
        key_term = (
            jnp.einsum("hrg,rhd->ghd", grad_scores, q_part, preferred_element_type=jnp.float32)
            * scale
        )
        scores_full = grad_scores.astype(jnp.float32)
        own_term = jnp.sum(scores_full, axis=-1).T
        far_term = -jnp.sum(scores_full, axis=1).T
        grad_q = lax.dynamic_update_slice_in_dim(grad_q, query_term, index * 4, 1)
        grad_k = lax.dynamic_update_slice_in_dim(grad_k, key_term, index * 4, 1)
        grad_v = lax.dynamic_update_slice_in_dim(grad_v, value_term, index * 4, 1)
        grad_own = lax.dynamic_update_slice_in_dim(grad_own, own_term, index * 4, 1)
        grad_far = lax.dynamic_update_slice_in_dim(grad_far, far_term, index * 4, 1)
        return (grad_q, grad_k, grad_v, grad_own, grad_far)

    grad_q, grad_k, grad_v, grad_own, grad_far = lax.fori_loop(
        0,
        group_count,
        backward_step,
        (
            jnp.zeros((rows, heads, head_dim), jnp.float32),
            jnp.zeros((group, heads, head_dim), jnp.float32),
            jnp.zeros((group, heads, head_dim), jnp.float32),
            jnp.zeros((rows, heads), jnp.float32),
            jnp.zeros((group, heads), jnp.float32),
        ),
    )
    grad_k_local, grad_v_local, grad_far_local = (
        lax.psum_scatter(grad_k, "ctx", scatter_dimension=0, tiled=True),
        lax.psum_scatter(grad_v, "ctx", scatter_dimension=0, tiled=True),
        lax.psum_scatter(grad_far, "ctx", scatter_dimension=0, tiled=True),
    )
    grad_decay = grad_own + grad_far_local
    local_rev = jnp.flip(jnp.cumsum(jnp.flip(grad_decay, 0), axis=0), 0)
    later = entering(
        jnp.sum(grad_decay, axis=0), "ctx", add_arrays, jnp.zeros((heads,), jnp.float32), True
    )
    grad_forget_logit = (local_rev + later) * jax.nn.sigmoid(-forget_logit)
    grad_query = norm_back(grad_q, query_norm, query_inv).reshape(rows, width)
    grad_key_mix = norm_back(grad_k_local, key_norm, key_inv).reshape(rows, width)
    grad_value_mix = grad_v_local.reshape(rows, width)
    grad_mix = jnp.sum(
        (grad_key_mix * (key_prev - key_raw) + grad_value_mix * (value_prev - value_raw)).reshape(
            rows, heads, head_dim
        ),
        axis=-1,
    )
    grad_shift_logit = grad_mix * mix_small * (1.0 - mix_small)
    carried_key = grad_key_mix * mix * keep
    carried_value = grad_value_mix * mix * keep
    from_next = passed_along(jnp.concatenate([carried_key[:1], carried_value[:1]], 0), "ctx", -1)
    grad_key_raw = (
        grad_key_mix * (1.0 - mix) + jnp.concatenate([carried_key[1:], from_next[:1]], 0)
    ).astype(jnp.bfloat16)
    grad_value_raw = (
        grad_value_mix * (1.0 - mix) + jnp.concatenate([carried_value[1:], from_next[1:]], 0)
    ).astype(jnp.bfloat16)
    grad_query_low = grad_query.astype(jnp.bfloat16)
    grad_head = jnp.concatenate([grad_forget_logit, grad_shift_logit], axis=1).astype(jnp.bfloat16)
    attn_grads = (
        lax.psum_scatter(
            weight_grad(h_one, grad_query_low), ("dp", "ctx"), scatter_dimension=0, tiled=True
        ),
        lax.psum_scatter(
            weight_grad(h_one, grad_key_raw), ("dp", "ctx"), scatter_dimension=0, tiled=True
        ),
        lax.psum_scatter(
            weight_grad(h_one, grad_value_raw), ("dp", "ctx"), scatter_dimension=0, tiled=True
        ),
        lax.psum_scatter(
            weight_grad(h_one, grad_gate), ("dp", "ctx"), scatter_dimension=0, tiled=True
        ),
        lax.psum_scatter(grad_wout, ("dp", "ctx"), scatter_dimension=0, tiled=True),
        lax.psum_scatter(
            weight_grad(h_one, grad_head), ("dp", "ctx"), scatter_dimension=0, tiled=True
        ),
    )
    grad_h_one = (
        input_grad(grad_query_low, full_query)
        + input_grad(grad_key_raw, full_key)
        + input_grad(grad_value_raw, full_value)
        + input_grad(grad_gate, full_gate)
        + input_grad(grad_head, full_heads)
    )
    gain_one = jnp.sum(grad_h_one * normed_one, axis=0)
    grad_input = norm_back(grad_h_one * gains[0], normed_one, inv_one) + grad_mid
    small = lax.psum(
        (
            jnp.stack([gain_one, gain_two]),
            jnp.stack([jnp.sum(grad_forget_logit, axis=0), jnp.sum(grad_shift_logit, axis=0)]),
        ),
        ("dp", "ctx"),
    )
    return (
        result,
        grad_input,
        small[0],
        small[1],
        attn_grads[0],
        attn_grads[1],
        attn_grads[2],
        attn_grads[3],
        attn_grads[4],
        attn_grads[5],
        ffn_grads[0],
        ffn_grads[1],
        ffn_grads[2],
    )


AXES = ("x", "core", "zh", "zl", "y")

def dot(left, right, dims):
    return lax.dot_general(left, right, (dims, ((), ())), preferred_element_type=jnp.float32)


def ab(left, right):
    return dot(left, right, ((1,), (0,)))


def abt(left, right):
    return dot(left, right, ((1,), (1,)))


def atb(left, right):
    return dot(left, right, ((0,), (0,)))


MESH = pl.DeviceIdType.MESH


class Net:
    def __init__(self, send, recv):
        self.send, self.recv, self.count, self.open = send, recv, 0, []
        self.at = {name: lax.axis_index(name) for name in AXES}

    def flip(self, names):
        return {name: 1 - self.at[name] for name in names}

    def greet(self):
        barrier = pltpu.get_barrier_semaphore()
        for names in PARTNERS:
            pl.semaphore_signal(barrier, 1, device_id=self.flip(names), device_id_type=MESH)
        moved = self.at["core"] != self.at["zh"]

        @pl.when(moved)
        def _():
            other = self.flip(("core", "zh"))
            pl.semaphore_signal(barrier, 1, device_id=other, device_id_type=MESH)
            pl.semaphore_wait(barrier, len(PARTNERS) + 1)

        @pl.when(jnp.logical_not(moved))
        def _():
            pl.semaphore_wait(barrier, len(PARTNERS))

    def copy(self, source, target, names):
        i = self.count
        self.count += 1
        return pltpu.make_async_remote_copy(
            source,
            target,
            self.send.at[i],
            self.recv.at[i],
            device_id=self.flip(names),
            device_id_type=MESH,
        )

    def push(self, source, target, names):
        made = self.copy(source, target, names)
        made.start()
        self.open.append(made)
        return made

    def left(self, copies):
        for made in copies:
            made.wait_send()
            self.open = [other for other in self.open if other is not made]

    def drain(self):
        for made in self.open:
            made.wait_send()


PARTNERS = (
    ("y",),
    ("zl",),
    ("zl", "y"),
    ("core",),
    ("core", "y"),
    ("core", "zl"),
    ("core", "zl", "y"),
    ("x",),
    ("zh",),
)


def rank_of(at):
    return (at["core"] * 2 + at["zl"]) * 2 + at["y"]


def flipped(at, names):
    return {name: 1 - at[name] if name in names else at[name] for name in at}


def unit_of(at, names):
    at = flipped(at, names)
    return at["zl"] * 2 + at["y"]


class Gather:
    def __init__(self, net, ref, rows):
        self.net, self.ref, self.rows = net, ref, rows

    def part(self, names, half=None):
        start = rank_of(flipped(self.net.at, names)) * self.rows
        size = self.rows
        if half is not None:
            size = self.rows // 2
            start = start + half * size
        return self.ref.at[pl.ds(pl.multiple_of(start, size), size)]

    def send(self, block, half, to):
        part = self.part(block, half)
        return self.net.push(part, part, to)

    def first(self):
        self.along = [self.send((), half, ("zl",)) for half in range(2)]
        self.near = self.send((), None, ("y",))
        self.cores = [self.send((), None, ("core",))]

    def second(self):
        self.corner = []
        for half in range(2):
            self.along[half].wait_recv()
            self.corner.append(self.send(("zl",), half, ("y",)))
        self.cores.append(self.send(("zl",), None, ("core",)))
        self.near.wait_recv()
        self.cores.append(self.send(("y",), None, ("core",)))

    def third(self):
        for made in self.corner:
            made.wait_recv()
        self.cores.append(self.send(("zl", "y"), None, ("core",)))

    def done(self):
        for made in self.cores:
            made.wait_recv()


QUARTERS = (("core", "zl"), ("zl",), ("core",), ())


def quarter(net, piece):
    at = flipped(net.at, QUARTERS[piece])
    return (at["core"] * 2 + at["zl"]) * 2


class Spread:
    def __init__(self, net, ref, pieces):
        self.net, self.ref, self.pieces = net, ref, pieces
        self.size = ref.shape[1] // pieces
        self.unit = net.at["x"] * 2 + net.at["zh"]
        self.from_zh = net.at["x"] * 2 + 1 - net.at["zh"]

    def send(self, unit, piece, to):
        part = self.ref.at[unit, pl.ds(piece * self.size, self.size)]
        return self.net.push(part, part, to)

    def first(self, ahead):
        self.along, self.across, self.corner = [], [], []
        for piece in range(self.pieces):
            if piece < ahead:
                self.along.append(self.send(self.unit, piece, ("zh",)))
            self.across.append(self.send(self.unit, piece, ("x",)))

    def second(self, piece):
        self.along[piece].wait_recv()
        self.corner.append(self.send(self.from_zh, piece, ("x",)))
        if len(self.along) < self.pieces:
            self.push_next()

    def push_next(self):
        self.along.append(self.send(self.unit, len(self.along), ("zh",)))

    def wait_across(self):
        for made in self.across:
            made.wait_recv()

    def wait_corner(self):
        for made in self.corner:
            made.wait_recv()


def exchange(net, source, target):
    rank = rank_of(net.at)
    target[rank] = source[rank]
    made = []
    for names in PARTNERS[:7]:
        to = rank_of(flipped(net.at, names))
        made.append(net.push(source.at[to], target.at[rank], names))
    return made


def swap_chunks(value):
    size = value.shape[1] // 8
    order = (0, 2, 1, 3, 4, 6, 5, 7)
    return jnp.concatenate([value[:, i * size : (i + 1) * size] for i in order], axis=1)


def normed(value):
    inverse = lax.rsqrt(jnp.mean(value * value, axis=-1, keepdims=True) + EPS)
    return value * inverse, inverse


def slice_of(rank):
    return rank // 2 % 2 * 4 + rank // 4 * 2 + rank % 2


def pack_attention(wide, heads_ref, pack_ref):
    size = wide[0].shape[1] // 8
    few = heads_ref.shape[1] // 16
    for rank in range(8):
        at = slice_of(rank)
        for i, ref in enumerate(wide):
            pack_ref[rank, :, i * size : (i + 1) * size] = ref[:, at * size : (at + 1) * size]
        pack_ref[rank, :, 4 * size :] = jnp.concatenate(
            [heads_ref[:, (i * 8 + at) * few : (i * 8 + at + 1) * few] for i in range(2)]
            + [jnp.zeros((heads_ref.shape[0], 128 - 2 * few), jnp.bfloat16)],
            axis=1,
        )


def pack_feeds(feeds, pack_gu_ref):
    block = feeds[0].shape[1] // 32
    for rank in range(8):
        for i, ref in enumerate(feeds):
            for unit in range(4):
                source = unit // 2 * 16 + rank // 4 * 8 + unit % 2 * 4 + rank % 4
                to = (i * 4 + unit) * block
                pack_gu_ref[rank, :, to : to + block] = ref[:, source * block : (source + 1) * block]


def whole(shape, dtype):
    return jax.ShapeDtypeStruct(shape, dtype)


def vmem(count):
    return [pl.BlockSpec(memory_space=pltpu.VMEM)] * count


def call(kernel, number, outs, args, copies, scratch=(), local=2, far=(), far_outs=()):
    return pl.pallas_call(
        kernel,
        out_shape=outs,
        in_specs=[
            pl.BlockSpec(memory_space=pl.ANY if i in far else pltpu.VMEM) for i in range(len(args))
        ],
        out_specs=[
            pl.BlockSpec(memory_space=pl.ANY if i in far_outs else pltpu.VMEM) for i in range(len(outs))
        ],
        scratch_shapes=[
            *scratch,
            pltpu.SemaphoreType.DMA((copies,)),
            pltpu.SemaphoreType.DMA((copies,)),
            pltpu.SemaphoreType.DMA((local,)),
        ],
        compiler_params=pltpu.CompilerParams(
            collective_id=number, has_side_effects=True, vmem_limit_bytes=60 * 2**20
        ),
    )(*args)


class Sum:
    def __init__(self, net, part, core, near, corner):
        self.net, self.part, self.core, self.near, self.corner = net, part, core, near, corner
        self.rows = part.shape[1]
        self.half = self.rows // 2
        self.given = {}

    def place(self, names):
        at = flipped(self.net.at, names)
        return at["zl"] * 2 + at["y"]

    def rank(self, names):
        return rank_of(flipped(self.net.at, names))

    def give(self, names):
        block = self.part.at[self.rank(("core", *names))]
        self.given[names] = self.net.push(block, self.core.at[self.place(names)], ("core",))

    def take(self, names):
        self.given[names].wait_recv()
        rank = self.rank(names)
        self.part[rank] = (
            self.part[rank].astype(jnp.float32) + self.core[self.place(names)].astype(jnp.float32)
        ).astype(jnp.bfloat16)

    def rows_of(self, names, half):
        return self.part.at[self.rank(names), pl.ds(half * self.half, self.half)]

    def send_corner(self):
        self.take(("zl", "y"))
        self.by_y = [
            self.net.push(self.rows_of(("zl", "y"), half), self.corner.at[half], ("y",))
            for half in range(2)
        ]

    def send_y(self):
        self.take(("y",))
        self.near_y = self.net.push(self.part.at[self.rank(("y",))], self.near.at[0], ("y",))

    def left_cores(self):
        self.net.left(self.given.values())

    def left(self):
        self.net.left((*self.by_y, self.near_y, *self.near_zl))

    def pass_on(self):
        self.take(("zl",))
        self.near_zl = []
        for half in range(2):
            self.by_y[half].wait_recv()
            rows = self.rows_of(("zl",), half)
            rows[...] = (
                rows[...].astype(jnp.float32) + self.corner[half].astype(jnp.float32)
            ).astype(jnp.bfloat16)
            to = self.near.at[1, pl.ds(half * self.half, self.half)]
            self.near_zl.append(self.net.push(rows, to, ("zl",)))

    def total(self):
        self.given[()].wait_recv()
        own = self.part[self.rank(())].astype(jnp.float32)
        own = own + self.core[self.place(())].astype(jnp.float32)
        for made in (self.near_y, *self.near_zl):
            made.wait_recv()
        return own + self.near[0].astype(jnp.float32) + self.near[1].astype(jnp.float32)


def sum_scratch(rows, width):
    return [
        pltpu.VMEM((8, rows, width), jnp.bfloat16),
        pltpu.VMEM((4, rows, width), jnp.bfloat16),
        pltpu.VMEM((2, rows, width), jnp.bfloat16),
        pltpu.VMEM((2, rows // 2, width), jnp.bfloat16),
    ]


def move(net, pairs, sems, start=0):
    moved = net.at["core"] != net.at["zh"]
    away = [net.copy(source, target, ("core", "zh")) for source, target in pairs]
    stay = [pltpu.make_async_copy(*pair, sems.at[start + i]) for i, pair in enumerate(pairs)]

    def each(act):
        @pl.when(moved)
        def _():
            for made in away:
                act(made)

        @pl.when(jnp.logical_not(moved))
        def _():
            for made in stay:
                act(made)

    each(lambda made: made.start())
    return lambda: each(lambda made: made.wait())


def lanes(columns, size):
    lane = lax.broadcasted_iota(jnp.int32, (size, 128), 1)
    out = jnp.zeros((size, 128), jnp.float32)
    for i, column in enumerate(columns):
        out = jnp.where(lane == i, column, out)
    return out


def triangle(size, upper):
    row = lax.broadcasted_iota(jnp.int32, (size, size), 0)
    col = lax.broadcasted_iota(jnp.int32, (size, size), 1)
    return jnp.where(row <= col if upper else row >= col, 1.0, 0.0)


def exact(left, right):
    return jnp.dot(
        left, right, precision=lax.Precision.HIGHEST, preferred_element_type=jnp.float32
    )


def spread_lanes(columns, size, wide):
    which = (lax.broadcasted_iota(jnp.int32, (size, wide), 1) // 64) % 3
    return jnp.where(which == 0, columns[0], jnp.where(which == 1, columns[1], columns[2]))


def bounds(lens_ref, first_row, size):
    place = first_row + lax.broadcasted_iota(jnp.int32, (size, 1), 0)
    first = lens_ref[0:1, 0:1]
    second = first + lens_ref[0:1, 1:2]
    low = jnp.where(place >= second, second, jnp.where(place >= first, first, 0))
    return place, low


def head_rows(value, h):
    return value[:, h * 64 : (h + 1) * 64]


def with_one(value, lane_at):
    size = value.shape[0]
    lane = lax.broadcasted_iota(jnp.int32, (size, 64), 1)
    return jnp.concatenate([value, jnp.where(lane == lane_at, 1.0, 0.0)], axis=1)


def mixing(proj_ref, lens_ref, bias_ref, q_ref, k_ref, v_ref, diff_ref, stat_ref, fcol_ref, frow_ref):
    size = 128
    lower = triangle(size, False)

    def one(i, carry):
        last, below = carry
        at = pl.ds(pl.multiple_of(i * size, size), size)
        block = proj_ref[at, :]
        kv = block[:, 384:768]
        logits = block[:, 768:896] + bias_ref[0:1, :]
        logf = jax.nn.log_sigmoid(logits)
        mix = jax.nn.sigmoid(logits)
        place, low = bounds(lens_ref, i * size, size)
        row = lax.broadcasted_iota(jnp.int32, (size, 384), 0)
        prev = jnp.where(row == 0, last, pltpu.roll(kv, 1, 0))
        prev = jnp.where(place == low, 0.0, prev)
        diff = prev - kv
        diff_ref[at, :] = diff
        mixed = kv + spread_lanes([mix[:, 3 + h : 4 + h] for h in range(3)], size, 384) * diff
        decay = exact(lower, logf) + below
        frows = decay.T
        stats = []
        for h in range(3):
            q = head_rows(block, h)
            inv = lax.rsqrt(jnp.mean(q * q, axis=-1, keepdims=True) + EPS)
            stats.append(inv)
            q_ref[h, at, :] = with_one(q * inv * 0.125, 0).astype(jnp.bfloat16)
            fcol_ref[h, at, :] = jnp.broadcast_to(decay[:, h : h + 1], (size, 128))
            frow_ref[h, :, at] = frows[h : h + 1, :]
        for h in range(3):
            k = head_rows(mixed, h)
            inv = lax.rsqrt(jnp.mean(k * k, axis=-1, keepdims=True) + EPS)
            stats.append(inv)
            k_ref[h, at, :] = with_one(k * inv, 1).astype(jnp.bfloat16)
            v_ref[h, at, :] = head_rows(mixed, 3 + h).astype(jnp.bfloat16)
        shut = jax.nn.sigmoid(-logits)
        stats += [shut[:, h : h + 1] for h in range(3)]
        stats += [mix[:, 3 + h : 4 + h] for h in range(3)]
        stat_ref[at, :] = lanes(stats, size)
        return kv[size - 1 :, :], decay[size - 1 :, :]

    lax.fori_loop(
        0,
        proj_ref.shape[0] // size,
        one,
        (jnp.zeros((1, 384), jnp.float32), jnp.zeros((1, 128), jnp.float32)),
    )


def scores(h, at, start, size, keys, q_ref, k_ref, fcol_ref, frow_ref, lens_ref):
    raw = abt(q_ref[h, at, :], k_ref[h, :keys, :])
    own = jnp.concatenate([fcol_ref[h, at, :]] * (keys // 128), axis=1)
    raw = raw + own - frow_ref[h, :, :keys]
    place, low = bounds(lens_ref, start, size)
    col = lax.broadcasted_iota(jnp.int32, (size, keys), 1)
    return jnp.where((col <= place) & (col >= low), jnp.exp(raw), 0.0)


def over_blocks(body, begin, end):
    for part in range(begin, end):

        def one(n, _, part=part):
            body(n // 2, part * 256 + n % 2 * 128, (part + 1) * 256)
            return 0

        lax.fori_loop(0, 6, one, 0)


def kernel_ab(
    x_ref, seq_ref, gains_ref, cot_ref, head_bias_ref, wq_ref, wg_ref, wk_ref, wv_ref, wh_ref, wfg_ref, wfu_ref,
    wo_ref, down_ref, xs_ref, lens_ref, mid_ref, *refs,
):
    far, refs = refs[:17], refs[17:]
    near_refs, refs = refs[:17], refs[17:]
    (
        h_ref, w_ref, q_ref, k_ref, v_ref, diff_ref, stat_ref, fcol_ref, frow_ref, gate_ref, attn_ref, a_ref,
        wo_all, gu_all, down_all, h2_ref, cot_all,
    ) = near_refs
    (
        lens_own, bias_ref, proj_ref, pack_ref, pack_gu_ref, spread_o,
        part, core, near, corner, send, recv, sems,
    ) = refs
    kept = []

    def keep(i):
        made = pltpu.make_async_copy(near_refs[i], far[i], sems.at[3 + i])
        made.start()
        kept.append(made)

    net = Net(send, recv)
    rows = x_ref.shape[0]
    rank = rank_of(net.at)
    lens_own[...] = jnp.zeros(lens_own.shape, jnp.int32)
    lens_own[0:1, 0:3] = seq_ref[...]
    net.greet()
    moved = move(net, [(x_ref, xs_ref), (lens_own, lens_ref)], sems)
    pack_attention((wq_ref, wg_ref, wk_ref, wv_ref), wh_ref, pack_ref)
    few = head_bias_ref.shape[1] // 8
    bias = jnp.zeros((1, 128), jnp.float32)
    for at in range(8):
        own = jnp.concatenate(
            [head_bias_ref[i : i + 1, at * few : (at + 1) * few] for i in range(2)]
            + [jnp.zeros((1, 128 - 2 * few), jnp.float32)],
            axis=1,
        )
        bias = jnp.where(slice_of(rank) == at, own, bias)
    bias_ref[...] = jnp.broadcast_to(bias, bias_ref.shape)
    spread = Spread(net, w_ref, 4)
    unit = spread.unit
    packs = exchange(net, pack_ref, w_ref.at[unit])
    pack_feeds((wfg_ref, wfu_ref), pack_gu_ref)

    moved()
    value, _inverse = normed(xs_ref[...].astype(jnp.float32))
    h_ref[pl.ds(pl.multiple_of(rank * rows, rows), rows)] = swap_chunks(
        (value * gains_ref[0:1, :]).astype(jnp.bfloat16)
    )
    gather = Gather(net, h_ref, rows)
    gather.first()
    for made in packs:
        made.wait_recv()
    spread.first(4)
    there = (net.at["zh"] * 2 + net.at["zl"]) * 2 + net.at["y"]
    there = pl.ds(pl.multiple_of(there * rows, rows), rows)
    moved_cot = move(net, [(cot_ref, cot_all.at[there])], sems, 2)
    out = Spread(net, spread_o, 1)
    spread_o[unit] = wo_ref[...]
    out.first(1)
    gather.second()
    spread.second(0)
    gather.third()
    spread.second(1)
    given = exchange(net, pack_gu_ref, gu_all.at[unit])
    depth = pack_ref.shape[0] * pack_ref.shape[1]
    tall = 2 * rows

    def multiply(which, fresh):
        def one(i, _):
            at = pl.ds(pl.multiple_of(i * tall, tall), tall)
            left = h_ref[at, pl.ds(pl.multiple_of(which * depth, 128), depth)]
            part = ab(left, w_ref[which].reshape(depth, -1))
            if fresh:
                proj_ref[at, :] = part
            else:
                proj_ref[at, :] += part
            return 0

        lax.fori_loop(0, h_ref.shape[0] // tall, one, 0)

    gather.done()
    keep(0)
    multiply(unit, True)
    spread.wait_across()
    multiply((1 - net.at["x"]) * 2 + net.at["zh"], False)
    spread.second(2)
    spread.second(3)
    multiply(spread.from_zh, False)
    spread.wait_corner()
    multiply((1 - net.at["x"]) * 2 + 1 - net.at["zh"], False)
    keep(1)
    group = proj_ref.shape[0]
    mine = pl.ds(pl.multiple_of(rank * rows, rows), rows)
    feed = Spread(net, gu_all, 4)
    down = Spread(net, down_all, 2)
    moved_cot()
    other = Gather(net, cot_all, rows)
    other.first()
    down_all[unit] = down_ref[...]
    for made in given:
        made.wait_recv()
    feed.first(2)
    down.first(0)
    mixing(proj_ref, lens_ref, bias_ref, q_ref, k_ref, v_ref, diff_ref, stat_ref, fcol_ref, frow_ref)
    for i in (2, 3, 4, 5, 6, 8):
        keep(i)
    out.second(0)
    other.second()

    def attend(h, start, keys):
        at = pl.ds(pl.multiple_of(start, 128), 128)
        e = scores(h, at, start, 128, keys, q_ref, k_ref, fcol_ref, frow_ref, lens_ref)
        total = jnp.sum(e, axis=-1, keepdims=True)
        inv = 1.0 / total
        fcol_ref[h, at, :] -= jnp.broadcast_to(jnp.log(total), (128, 128))
        attn_ref[h, at, :] = ab((e * inv).astype(jnp.bfloat16), v_ref[h, :keys, :])

    over_blocks(attend, 0, 2)
    other.third()
    out.wait_across()
    out.wait_corner()
    pieces = []
    wo_all[unit_of(net.at, ())] = spread_o[unit_of(net.at, ())]
    for names in (("y",), ("zl",), ("zl", "y")):
        pieces.append(net.push(spread_o.at[unit_of(net.at, names)], wo_all.at[unit_of(net.at, ())], names))
    feed.second(0)
    over_blocks(attend, 2, group // 256)
    feed.second(1)
    for h in range(3):
        gate = jax.nn.sigmoid(proj_ref[:, 192 + 64 * h : 256 + 64 * h])
        gate_ref[:, 64 * h : 64 * h + 64] = gate
        a_ref[:, 64 * h : 64 * h + 64] = (gate * attn_ref[h]).astype(jnp.bfloat16)
    for made in pieces:
        made.wait_recv()
    for i in (7, 9, 10, 11, 12):
        keep(i)

    total = Sum(net, part, core, near, corner)

    def project_block(names):
        to = rank_of(flipped(net.at, names))
        left = a_ref[pl.ds(pl.multiple_of(to * rows, rows), rows), :]
        part[to] = ab(left, wo_all[...].reshape(-1, wo_all.shape[2])).astype(jnp.bfloat16)

    for names in (("zl", "y"), ("zl",), ("y",), ()):
        project_block(("core", *names))
        total.give(names)
    project_block(("zl", "y"))
    total.send_corner()
    project_block(("zl",))
    project_block(("y",))
    total.send_y()
    project_block(())
    total.pass_on()
    feed.second(2)
    down.push_next()
    other.done()
    keep(16)
    mid = xs_ref[...].astype(jnp.float32) + total.total()
    mid_ref[...] = mid
    value, _inverse = normed(mid)
    h2_ref[mine] = swap_chunks((value * gains_ref[1:2, :]).astype(jnp.bfloat16))
    gather = Gather(net, h2_ref, rows)
    gather.first()
    feed.second(3)
    down.second(0)
    gather.second()
    feed.wait_across()
    feed.wait_corner()
    keep(13)
    gather.third()
    down.second(1)
    gather.done()
    keep(15)
    down.wait_across()
    down.wait_corner()
    keep(14)
    for made in kept:
        made.wait()
    net.drain()


class SpreadSum:
    def __init__(self, net, whole_ref, over_x, over_zh, pieces, relay=None, by_rank=False):
        self.relay, self.by_rank = relay, by_rank
        self.net, self.whole, self.over_x, self.over_zh, self.pieces = net, whole_ref, over_x, over_zh, pieces
        self.size = whole_ref.shape[1] // pieces
        self.x, self.zh = net.at["x"], net.at["zh"]
        self.far, self.own, self.last = [], [], []

    def rows(self, piece):
        return pl.ds(quarter(self.net, piece) if self.by_rank else piece * self.size, self.size)

    def part(self, ref, at, piece):
        return ref.at[at, self.rows(piece)]

    def send(self, zh, target, piece):
        source = self.part(self.whole, (1 - self.x) * 2 + zh, piece)
        return self.net.push(source, target, ("x",))

    def first_far(self):
        for piece in range(self.pieces):
            zh = 1 - self.zh
            self.far.append(self.send(zh, self.part(self.over_x, zh, piece), piece))

    def first_own(self):
        for piece in range(self.pieces):
            self.own.append(self.send(self.zh, self.part(self.over_x, self.zh, piece), piece))

    def first(self):
        self.first_far()
        self.first_own()

    def pass_far(self):
        for piece in range(self.pieces):
            to = self.over_x.at[self.rows(piece)]
            self.own.append(self.send(self.zh, to, piece))

    def pass_far_on(self, far, begin, end):
        for piece in range(begin, end):
            self.pass_one(piece, far.at[self.rows(piece)])

    def hand_out(self, target):
        made = []
        rank = rank_of(self.net.at)
        for piece, names in enumerate(QUARTERS):
            self.over_zh[self.rows(piece)] = self.total(piece).astype(jnp.bfloat16)
            for more in (names, (*names, "y")):
                if more:
                    to = self.over_zh.at[rank_of(flipped(self.net.at, more))]
                    made.append(self.net.push(to, target.at[rank], more))
                else:
                    target[rank] = self.over_zh[rank]
        return made

    def second(self, piece):
        self.far[piece].wait_recv()
        self.pass_one(piece, self.part(self.over_x, 1 - self.zh, piece))

    def pass_one(self, piece, came):
        here = self.part(self.whole, self.x * 2 + 1 - self.zh, piece)
        total = (here[...].astype(jnp.float32) + came[...].astype(jnp.float32)).astype(jnp.bfloat16)
        if self.relay is not None:
            here = self.relay.at[self.rows(piece)]
        here[...] = total
        target = self.over_zh.at[self.rows(piece)]
        self.last.append(self.net.push(here, target, ("zh",)))

    def total(self, piece):
        self.own[piece].wait_recv()
        self.last[piece].wait_recv()
        here = self.part(self.whole, self.x * 2 + self.zh, piece)
        if self.relay is None:
            came = self.part(self.over_x, self.zh, piece)
        else:
            came = self.over_x.at[self.rows(piece)]
        last = self.over_zh.at[self.rows(piece)]
        return (
            here[...].astype(jnp.float32) + came[...].astype(jnp.float32) + last[...].astype(jnp.float32)
        )


def norm_grad(grad, gain, value, inverse):
    scaled = grad * gain
    return (
        inverse * (scaled - value * jnp.mean(scaled * value, axis=-1, keepdims=True)),
        jnp.sum(grad * value, axis=0, keepdims=True),
    )


def kernel_c(
    h_far, cot_far, wgu_far, wd_far, mid_far, gains_ref,
    hid_ref, dmid_ref, dao_ref, gain_ref, gdown_ref, ggu_ref, gfar_ref,
    dgu_ref, gd_ref, over_x, over_zh, part, core, near, corner,
    h_ref, wgu_ref, cot_ref, wd_ref, mid_ref, send, recv, sems,
):
    net = Net(send, recv)
    rank = rank_of(net.at)
    rows = mid_ref.shape[0]
    mine = pl.ds(pl.multiple_of(rank * rows, rows), rows)
    wide = hid_ref.shape[1]
    width = mid_ref.shape[1]
    four = 4 * rows
    loads = [
        pltpu.make_async_copy(source, target, sems.at[i])
        for i, (source, target) in enumerate(
            ((h_far, h_ref), (wgu_far, wgu_ref), (cot_far, cot_ref), (wd_far, wd_ref), (mid_far, mid_ref))
        )
    ]
    for made in loads:
        made.start()
    net.greet()
    for made in loads:
        made.wait()

    def half(which):
        at = pl.ds(pl.multiple_of(which * four, four), four)
        wgu = wgu_ref[...].reshape(width, 2 * wide)
        both = ab(h_ref[at, :], wgu)
        gate, up = both[:, :wide], both[:, wide:]
        sig = jax.nn.sigmoid(gate)
        act = gate * sig
        hid_ref[at, :] = (act * up).astype(jnp.bfloat16)
        grad = abt(cot_ref[at, :], wd_ref[...].reshape(wide, width))
        dgate = grad * up * sig * (1.0 + gate * (1.0 - sig))
        dgu = jnp.concatenate([dgate, grad * act], axis=1).astype(jnp.bfloat16)
        dgu_ref[at, :] = dgu
        back = abt(dgu, wgu).astype(jnp.bfloat16)
        for i in range(4):
            part[which * 4 + i] = back[i * rows : (i + 1) * rows]

    total = Sum(net, part, core, near, corner)
    half(1 - net.at["core"])
    for names in (("zl", "y"), ("zl",), ("y",), ()):
        total.give(names)
    half(net.at["core"])
    total.send_corner()
    total.send_y()
    down = SpreadSum(net, gd_ref, over_x, over_zh, 2)

    def grad_down(k, _):
        left = hid_ref[:, pl.ds(pl.multiple_of(k * rows, rows), rows)]
        gd_ref[k] = atb(left, cot_ref[...]).astype(jnp.bfloat16)
        return 0

    lax.fori_loop(0, 4, grad_down, 0)
    down.first()
    total.pass_on()
    depth = width // 4

    def grad_gu(k, _):
        left = h_ref[:, pl.ds(pl.multiple_of(k * depth, depth), depth)]
        ggu_ref[k] = atb(left, dgu_ref[...]).astype(jnp.bfloat16).reshape(ggu_ref.shape[1:])
        return 0

    lax.fori_loop(0, 4, grad_gu, 0)
    feed = SpreadSum(net, ggu_ref, None, None, 1)
    far = feed.send(1 - net.at["zh"], gfar_ref, 0)
    grad = swap_chunks(total.total())
    value, inverse = normed(mid_ref[...])
    back, gain = norm_grad(grad, gains_ref[1:2, :], value, inverse)
    gain_ref[...] = gain
    dmid = cot_ref[mine, :].astype(jnp.float32) + back
    dmid_ref[...] = dmid
    dao_ref[mine] = dmid.astype(jnp.bfloat16)
    gather = Gather(net, dao_ref, rows)
    gather.first()
    down.second(0)
    down.second(1)
    gather.second()
    gather.third()
    for piece in range(2):
        gdown_ref[pl.ds(piece * rows // 2, rows // 2)] = down.total(piece)
    gather.done()
    far.wait_recv()
    net.drain()


def spread_scratch(shape):
    return [
        pltpu.VMEM((4, *shape), jnp.bfloat16),
        pltpu.VMEM((2, *shape), jnp.bfloat16),
        pltpu.VMEM(shape, jnp.bfloat16),
    ]


def unmixing(
    lens_ref, q_ref, k_ref, diff_ref, stat_ref, dq_ref, dk_ref, dv_ref, dproj_ref
):
    size = 128
    count = diff_ref.shape[0] // size
    upper = triangle(size, True)

    def one(step, carry):
        after, above, sums = carry
        i = count - 1 - step
        at = pl.ds(pl.multiple_of(i * size, size), size)
        stat = stat_ref[at, :]
        decay, keys, values = [], [], []
        for h in range(3):
            dq, dk = dq_ref[h, at, :], dk_ref[h, at, :]
            decay.append(dq[:, 65:66] - dk[:, 64:65])
            grad = dq[:, :64] * 0.125
            unit = q_ref[h, at, :][:, :64].astype(jnp.float32) * 8.0
            grad = grad - unit * jnp.mean(grad * unit, axis=-1, keepdims=True)
            dproj_ref[at, 64 * h : 64 * h + 64] = (stat[:, h : h + 1] * grad).astype(jnp.bfloat16)
            grad = dk[:, :64]
            unit = k_ref[h, at, :][:, :64].astype(jnp.float32)
            grad = grad - unit * jnp.mean(grad * unit, axis=-1, keepdims=True)
            keys.append(stat[:, 3 + h : 4 + h] * grad)
            values.append(dv_ref[h, at, :])
        both = jnp.concatenate(keys + values, axis=1)
        prod = both * diff_ref[at, :]
        mix = [stat[:, 9 + h : 10 + h] for h in range(3)]
        mixes = spread_lanes(mix, size, 384)
        place, low = bounds(lens_ref, i * size, size)
        carried = jnp.where(place == low, 0.0, both * mixes)
        row = lax.broadcasted_iota(jnp.int32, (size, 384), 0)
        later = jnp.where(row == size - 1, after, pltpu.roll(carried, size - 1, 0))
        dproj_ref[at, 384:768] = (both * (1.0 - mixes) + later).astype(jnp.bfloat16)
        decay = lanes(decay, size)
        suffix = exact(upper, decay) + above
        small = []
        for h in range(3):
            small.append(suffix[:, h : h + 1] * stat[:, 6 + h : 7 + h])
        for h in range(3):
            grad = jnp.sum(head_rows(prod, h) + head_rows(prod, 3 + h), axis=-1, keepdims=True)
            small.append(grad * mix[h] * (1.0 - mix[h]))
        small = lanes(small, size)
        dproj_ref[at, 768:896] = small.astype(jnp.bfloat16)
        above = above + jnp.sum(decay, axis=0, keepdims=True)
        return carried[:1, :], above, sums + jnp.sum(small, axis=0, keepdims=True)

    none = jnp.zeros((1, 128), jnp.float32)
    carry = lax.fori_loop(0, count, one, (jnp.zeros((1, 384), jnp.float32), none, none))
    return carry[2]


def kernel_d(
    dao_ref, wo_far, a_far, attn_far, gate_far, lens_ref, q_far, k_far, v_far, diff_far, stat_far,
    fcol_far, frow_far, w_far, h_ref, dmid_far, x_far, gains_ref, gain_two_ref, ggu_far, gfar_far,
    hid_far, wd_far, mid_far,
    out_ref, gx_ref, gain_ref, bias_ref, ga_ref, go_ref, gu_ref,
    do_ref, dq_ref, dk_ref, dv_ref, dproj_ref,
    gu_x, gu_zh, a_whole, a_x, a_zh, o_raw, o_whole, o_x, o_zh, small, slots, tall, gx_own, out_own,
    part, core, near, corner, core2, near2, corner2, *refs,
):
    *late, send, recv, sems = refs
    ggu_ref, gfar_ref, hid_ref, wd_ref, wo_ref, a_ref, mid_ref, attn_ref, gate_ref, q_ref, k_ref, v_ref, \
        fcol_ref, frow_ref, diff_ref, stat_ref, w_ref, dmid_ref, x_ref = late
    far = (
        ggu_far, gfar_far, hid_far, wd_far, wo_far, a_far, mid_far, attn_far, gate_far, q_far, k_far, v_far,
        fcol_far, frow_far, diff_far, stat_far, w_far, dmid_far, x_far,
    )
    net = Net(send, recv)
    rank = rank_of(net.at)
    rows, width = mid_ref.shape
    group = a_ref.shape[0]
    mine = pl.ds(pl.multiple_of(rank * rows, rows), rows)
    fetch = [pltpu.make_async_copy(ref, tall, sems.at[2 + i]) for i, ref in enumerate((dao_ref, h_ref))]
    loads = [
        pltpu.make_async_copy(source, target, sems.at[4 + i])
        for i, (source, target) in enumerate(zip(far, late))
    ]
    for made in (*loads[:4], fetch[0], *loads[4:]):
        made.start()
    net.greet()
    for made in loads[:4]:
        made.wait()
    feed = SpreadSum(net, ggu_ref, gu_x.at[0], gu_zh, 4, gu_x.at[1], True)
    attn = SpreadSum(net, a_whole, a_x, a_zh, 4, None, True)
    out = SpreadSum(net, o_whole, o_x, o_zh, 1)

    four = 4 * rows

    def half(which, left_ref, right, multiply, to):
        def one(i, _):
            at = pl.multiple_of(which * four + i * 2 * rows, 2 * rows)
            back = multiply(left_ref[pl.ds(at, 2 * rows), :], right).astype(jnp.bfloat16)
            to[which * 4 + 2 * i] = back[:rows]
            to[which * 4 + 2 * i + 1] = back[rows:]
            return 0

        lax.fori_loop(0, 2, one, 0)

    result = Sum(net, part, core2, near2, corner2)
    wd = wd_ref[...].reshape(-1, width)
    feed.pass_far()
    feed.pass_far_on(gfar_ref, 0, 2)
    half(1 - net.at["core"], hid_ref, wd, ab, part)
    for names in (("zl", "y"), ("zl",), ("y",), ()):
        result.give(names)
    half(net.at["core"], hid_ref, wd, ab, part)
    fetch[0].wait()
    for made in loads[4:9]:
        made.wait()
    da = abt(tall[...], wo_ref[...].reshape(-1, width))
    for h in range(3):
        sig = gate_ref[:, 64 * h : 64 * h + 64]
        grad = da[:, 64 * h : 64 * h + 64] * sig
        do_ref[h] = grad.astype(jnp.bfloat16)
        dproj_ref[:, 192 + 64 * h : 256 + 64 * h] = (grad * attn_ref[h] * (1.0 - sig)).astype(
            jnp.bfloat16
        )
    o_raw[...] = atb(a_ref[...], tall[...]).astype(jnp.bfloat16).reshape(o_raw.shape)
    fetch[1].start()
    here = unit_of(net.at, ())
    o_whole[here] = o_raw[here]
    pieces = []
    for names in (("y",), ("zl",), ("zl", "y")):
        pieces.append(net.push(o_raw.at[unit_of(net.at, names)], o_whole.at[here], names))
    dk_ref[...] = jnp.zeros(dk_ref.shape, jnp.float32)
    dv_ref[...] = jnp.zeros(dv_ref.shape, jnp.float32)

    def attend(h, start, keys):
        at = pl.ds(pl.multiple_of(start, 128), 128)
        p = scores(h, at, start, 128, keys, q_ref, k_ref, fcol_ref, frow_ref, lens_ref)
        do = do_ref[h, at, :]
        dp = abt(do, v_ref[h, :keys, :])
        ds = p * (dp - jnp.sum(p * dp, axis=-1, keepdims=True))
        ds = ds.astype(jnp.bfloat16)
        dq_ref[h, at, :] = ab(ds, k_ref[h, :keys, :])
        dk_ref[h, :keys, :] += atb(ds, q_ref[h, at, :])
        dv_ref[h, :keys, :] += atb(p.astype(jnp.bfloat16), do)

    result.send_corner()
    result.send_y()
    for made in pieces:
        made.wait_recv()
    out.first()
    for made in loads[9:]:
        made.wait()
    over_blocks(attend, 0, 3)
    result.pass_on()
    feed.pass_far_on(gfar_ref, 2, 4)
    over_blocks(attend, 3, 4)
    out.second(0)
    sums = unmixing(lens_ref, q_ref, k_ref, diff_ref, stat_ref, dq_ref, dk_ref, dv_ref, dproj_ref)

    result.left_cores()
    out_own[...] = (mid_ref[...] + result.total()).astype(jnp.bfloat16)
    moved_out = move(net, [(out_own, out_ref)], sems)
    result.left()
    total = Sum(net, part, core, near, corner)
    w = w_ref[...].reshape(width, -1)
    half(1 - net.at["core"], dproj_ref, w, abt, part)
    for names in (("zl", "y"), ("zl",), ("y",), ()):
        total.give(names)
    half(net.at["core"], dproj_ref, w, abt, part)
    total.send_corner()
    total.send_y()
    depth = width // 4

    def grad_attn(k, _):
        left = tall[:, pl.ds(pl.multiple_of(k * depth, depth), depth)]
        a_whole[k] = atb(left, dproj_ref[...]).astype(jnp.bfloat16).reshape(a_whole.shape[1:])
        return 0

    fetch[1].wait()
    lax.fori_loop(0, 4, grad_attn, 0)
    attn.first_far()
    total.pass_on()
    attn.second(0)
    given = feed.hand_out(gu_ref)
    attn.second(1)
    grad = swap_chunks(total.total())
    attn.second(2)
    value, inverse = normed(x_ref[...].astype(jnp.float32))
    back, gain = norm_grad(grad, gains_ref[0:1, :], value, inverse)
    small[0] = jnp.concatenate(
        [gain, gain_two_ref[...], jnp.concatenate([sums, jnp.zeros((1, width - 128), jnp.float32)], axis=1)]
        + [jnp.zeros((5, width), jnp.float32)],
        axis=0,
    )
    first = net.push(small.at[0], small.at[1], ("x",))
    attn.first_own()
    gx_own[...] = (dmid_ref[...] + back).astype(jnp.bfloat16)
    go_ref[...] = out.total(0)
    first.wait_recv()
    small[2] = small[0] + small[1]
    second = net.push(small.at[2], small.at[3], ("zh",))
    attn.second(3)
    second.wait_recv()
    slots[rank] = small[2] + small[3]
    shared = [net.push(slots.at[rank], slots.at[rank], names) for names in PARTNERS[:7]]
    moved_gx = move(net, [(gx_own, gx_ref)], sems, 1)
    given += attn.hand_out(ga_ref)
    for made in shared + given:
        made.wait_recv()
    gain_ref[...] = jnp.sum(slots[:, 0:2, :], axis=0)
    bias_ref[...] = slots[:, 2:3, :128]
    moved_out()
    moved_gx()
    net.drain()


def finish(
    out_ref, gx_ref, gain_ref, bias_ref, ga_ref, go_ref, gu_ref, gdown_ref,
    out_out, gx_out, gain_out, bias_out, gq_out, gk_out, gv_out, gg_out, go_out, gh_out, gfg_out, gfu_out, gdown_out,
):
    for source, target in ((out_ref, out_out), (gain_ref, gain_out), (go_ref, go_out), (gdown_ref, gdown_out)):
        target[...] = source[...]
    gx_out[...] = gx_ref[...].astype(jnp.float32)
    size = gq_out.shape[1] // 8
    few = bias_out.shape[1] // 8
    block = gfg_out.shape[1] // 32
    for rank in range(8):
        at = slice_of(rank)
        for i, target in enumerate((gq_out, gg_out, gk_out, gv_out)):
            part = ga_ref[rank, :, i * size : (i + 1) * size]
            target[:, at * size : (at + 1) * size] = part.astype(jnp.float32)
        part = ga_ref[rank, :, 4 * size :].astype(jnp.float32)
        for i in range(2):
            to = (i * 8 + at) * few
            gh_out[:, to : to + few] = part[:, i * few : (i + 1) * few]
            bias_out[i : i + 1, at * few : (at + 1) * few] = bias_ref[rank, :, i * few : (i + 1) * few]
        for i, target in enumerate((gfg_out, gfu_out)):
            for unit in range(4):
                to = (unit // 2 * 16 + rank // 4 * 8 + unit % 2 * 4 + rank % 4) * block
                part = gu_ref[rank, :, (i * 4 + unit) * block : (i * 4 + unit + 1) * block]
                target[:, to : to + block] = part.astype(jnp.float32)


def squares(
    layer_input,
    cotangent,
    seq_lengths,
    gains,
    head_bias,
    w_query,
    w_key,
    w_value,
    w_gate,
    w_out,
    w_heads,
    w_ff_gate,
    w_ff_up,
    w_ff_down,
):
    rows, width = layer_input.shape
    heads = head_bias.shape[1]
    head_dim = width // heads
    ranks = 8
    group = rows * ranks
    mine = heads // ranks
    cols = mine * head_dim
    shard = w_query.shape[0]
    units = w_ff_gate.shape[1] // ranks
    low = jnp.bfloat16
    f32 = jnp.float32
    packs = (ranks, shard, 4 * cols + 128)
    feeds = (ranks, shard, 2 * units)
    lens_shape = (8, 128)
    kept = (
        whole((group, width), low),
        whole((4, *packs), low),
        whole((mine, group, 128), low),
        whole((mine, group, 128), low),
        whole((mine, group, head_dim), low),
        whole((group, 2 * cols), f32),
        whole((group, 128), f32),
        whole((mine, group, 128), f32),
        whole((mine, 1, group), f32),
        whole((group, cols), f32),
        whole((mine, group, head_dim), f32),
        whole((group, cols), low),
        whole((4, shard, width), low),
        whole((4, *feeds), low),
        whole((4, *w_ff_down.shape), low),
        whole((group, width), low),
        whole((group, width), low),
    )
    (
        packed, lengths, mid,
        h_one_all, w_attn, q_all, k_all, v_all, diff, stat, fcol, frow, gate_sig, attn3, branch_in,
        w_o, w_gu, w_d, h_two_all, cot_all,
    ) = call(
        kernel_ab,
        1,
        (
            whole(layer_input.shape, low),
            whole(lens_shape, jnp.int32),
            whole((rows, width), f32),
            *kept,
        ),
        (
            layer_input, seq_lengths, gains, cotangent, head_bias,
            w_query, w_gate, w_key, w_value, w_heads, w_ff_gate, w_ff_up, w_out, w_ff_down,
        ),
        112,
        [
            *(pltpu.VMEM(leaf.shape, leaf.dtype) for leaf in kept),
            pltpu.VMEM(lens_shape, jnp.int32),
            pltpu.VMEM((8, 128), f32),
            pltpu.VMEM((group, packs[2]), f32),
            pltpu.VMEM(packs, low),
            pltpu.VMEM(feeds, low),
            pltpu.VMEM((4, shard, width), low),
            *sum_scratch(rows, width),
        ],
        local=3 + len(kept),
        far_outs=range(3, 3 + len(kept)),
    )
    hidden, grad_mid, grad_branch, gain_two, grad_down, grad_gu, grad_far = call(
        kernel_c,
        3,
        (
            whole((group, units), low),
            whole((rows, width), f32),
            whole((group, width), low),
            whole((1, width), f32),
            whole((rows, width), f32),
            whole((4, *feeds), low),
            whole(feeds, low),
        ),
        (h_two_all, cot_all, w_gu, w_d, mid, gains),
        48,
        [
            pltpu.VMEM((group, 2 * units), low),
            pltpu.VMEM((4, rows, width), low),
            pltpu.VMEM((2, rows, width), low),
            pltpu.VMEM((rows, width), low),
            *sum_scratch(rows, width),
            *(pltpu.VMEM(leaf.shape, leaf.dtype) for leaf in (h_two_all, w_gu, cot_all, w_d, mid)),
        ],
        5,
        range(5),
    )
    result, grad_input, gain_sums, bias_sums, grad_attn_w, grad_wout, grad_gu = call(
        kernel_d,
        4,
        (
            whole((rows, width), low),
            whole((rows, width), low),
            whole((2, width), f32),
            whole((ranks, 1, 128), f32),
            whole(packs, low),
            whole((shard, width), f32),
            whole(feeds, low),
        ),
        (
            grad_branch, w_o, branch_in, attn3, gate_sig, lengths, q_all, k_all, v_all, diff, stat,
            fcol, frow, w_attn, h_one_all, grad_mid, packed, gains, gain_two, grad_gu, grad_far,
            hidden, w_d, mid,
        ),
        96,
        [
            pltpu.VMEM((mine, group, head_dim), low),
            pltpu.VMEM((mine, group, 128), f32),
            pltpu.VMEM((mine, group, 128), f32),
            pltpu.VMEM((mine, group, head_dim), f32),
            pltpu.VMEM((group, packs[2]), low),
            *spread_scratch(feeds)[1:],
            *spread_scratch(packs),
            pltpu.VMEM((4, shard, width), low),
            *spread_scratch((shard, width)),
            pltpu.VMEM((4, 8, width), f32),
            pltpu.VMEM((ranks, 8, width), f32),
            pltpu.VMEM((group, width), low),
            pltpu.VMEM((rows, width), low),
            pltpu.VMEM((rows, width), low),
            *sum_scratch(rows, width),
            *sum_scratch(rows, width)[1:],
            *(pltpu.VMEM(leaf.shape, leaf.dtype) for leaf in (grad_gu, grad_far, hidden, w_d, w_o, branch_in, mid, attn3, gate_sig, q_all, k_all, v_all, fcol, frow, diff, stat, w_attn, grad_mid, packed)),
        ],
        24,
        (0, 14, 19, 20, 21, 22, 1, 2, 23, 3, 4, 6, 7, 8, 11, 12, 9, 10, 13, 15, 16),
    )

    big = whole((shard, width), f32)
    outs = (
        whole((rows, width), low),
        whole((rows, width), f32),
        whole((2, width), f32),
        whole((2, heads), f32),
        big,
        big,
        big,
        big,
        big,
        whole((shard, 2 * heads), f32),
        whole(w_ff_gate.shape, f32),
        whole(w_ff_up.shape, f32),
        whole(w_ff_down.shape, f32),
    )
    args = (result, grad_input, gain_sums, bias_sums, grad_attn_w, grad_wout, grad_gu, grad_down)
    return pl.pallas_call(
        finish,
        out_shape=outs,
        in_specs=vmem(len(args)),
        out_specs=vmem(len(outs)),
        compiler_params=pltpu.CompilerParams(vmem_limit_bytes=60 * 2**20),
    )(*args)


def solution(mesh):
    if mesh.shape["dp"] == 4 and mesh.shape["ctx"] == 8:
        body, axes, group = squares, AXES, ("x", "core")
        mesh = Mesh(np.reshape(mesh.devices, (2, 2, 2, 2, 2)), AXES)
    else:
        body, axes, group = shards, ("dp", "ctx"), "dp"
    cut = P(axes, None)
    return jax.shard_map(
        body,
        mesh=mesh,
        in_specs=(cut, cut, P(group, None), P(), P()) + (cut,) * 9,
        out_specs=(cut, cut, P(), P()) + (cut,) * 9,
        check_vma=False,
    )
```

```python
import jax
import jax.numpy as jnp
import numpy as np
from jax import lax
from jax.experimental import pallas as pl
from jax.experimental.pallas import tpu as pltpu
from jax.sharding import Mesh
from jax.sharding import PartitionSpec as P

EPS = 1e-06


def passed_along(array, axis, by):
    size = lax.axis_size(axis)
    pairs = [(i, i + by) for i in range(size) if 0 <= i + by < size]
    return lax.ppermute(array, axis, pairs)


def entering(part, axis, combine, identity, reverse):
    count = lax.axis_size(axis)
    place = lax.axis_index(axis)
    ahead = count - 1 - place if reverse else place
    gathered = lax.all_gather(part, axis)
    state = jnp.zeros_like(part) + jnp.asarray(identity, part.dtype)

    def one(step, state):
        source = count - 1 - step if reverse else step
        return combine(state, lax.dynamic_index_in_dim(gathered, source, 0, False))

    return lax.fori_loop(0, ahead, one, state)


def fetch_attention(w_query, w_key, w_value, w_gate, w_out, w_heads):
    return (
        lax.all_gather(w_query, ("dp", "ctx"), axis=0, tiled=True),
        lax.all_gather(w_key, ("dp", "ctx"), axis=0, tiled=True),
        lax.all_gather(w_value, ("dp", "ctx"), axis=0, tiled=True),
        lax.all_gather(w_gate, ("dp", "ctx"), axis=0, tiled=True),
        lax.all_gather(w_out, ("dp", "ctx"), axis=0, tiled=True),
        lax.all_gather(w_heads, ("dp", "ctx"), axis=0, tiled=True),
    )


def fetch_feed(w_ff_gate, w_ff_up, w_ff_down):
    return (
        lax.all_gather(w_ff_gate, ("dp", "ctx"), axis=0, tiled=True),
        lax.all_gather(w_ff_up, ("dp", "ctx"), axis=0, tiled=True),
        lax.all_gather(w_ff_down, ("dp", "ctx"), axis=0, tiled=True),
    )


def add_arrays(earlier, later):
    return earlier + later


def norm_back(grad, normed, inverse):
    return inverse * (grad - normed * jnp.mean(grad * normed, axis=-1, keepdims=True))


def project(left, right):
    return jnp.dot(left, right, preferred_element_type=jnp.float32)


def weight_grad(left, right):
    return jnp.einsum("ra,rb->ab", left, right, preferred_element_type=jnp.float32)


def input_grad(grad, weight):
    return jnp.einsum("rb,ab->ra", grad, weight, preferred_element_type=jnp.float32)


def shards(
    layer_input,
    cotangent,
    seq_lengths,
    gains,
    head_bias,
    w_query,
    w_key,
    w_value,
    w_gate,
    w_out,
    w_heads,
    w_ff_gate,
    w_ff_up,
    w_ff_down,
):
    rows, width = layer_input.shape
    heads = head_bias.shape[1]
    head_dim = width // heads
    spans = lax.axis_size("ctx")
    group = rows * spans
    scale = head_dim ** (-0.5)
    here = lax.axis_index("ctx")
    local_pos = here * rows + jnp.arange(rows, dtype=jnp.int32)
    key_pos = jnp.arange(group, dtype=jnp.int32)
    first = seq_lengths[0, 0]
    second = first + seq_lengths[0, 1]
    local_seg = (local_pos >= first).astype(jnp.int32) + (local_pos >= second).astype(jnp.int32)
    key_seg = (key_pos >= first).astype(jnp.int32) + (key_pos >= second).astype(jnp.int32)
    starts = (local_pos == 0) | (local_pos == first) | (local_pos == second)
    keep = (1 - starts.astype(jnp.int32)).astype(jnp.float32)[:, None]
    allowed = (local_seg[:, None] == key_seg[None, :]) & (key_pos[None, :] <= local_pos[:, None])
    x_full = layer_input.astype(jnp.float32)
    inv_one = lax.rsqrt(jnp.mean(x_full * x_full, axis=-1, keepdims=True) + EPS)
    normed_one = x_full * inv_one
    h_one = (normed_one * gains[0]).astype(jnp.bfloat16)
    full_query, full_key, full_value, full_gate, full_out, full_heads = fetch_attention(
        w_query, w_key, w_value, w_gate, w_out, w_heads
    )
    query = project(h_one, full_query)
    key_raw = project(h_one, full_key)
    value_raw = project(h_one, full_value)
    gate_raw = project(h_one, full_gate)
    head_raw = project(h_one, full_heads)
    forget_logit = head_raw[:, :heads] + head_bias[0]
    shift_logit = head_raw[:, heads:] + head_bias[1]
    log_forget = jax.nn.log_sigmoid(forget_logit)
    mix_small = jax.nn.sigmoid(shift_logit)
    mix = jnp.repeat(mix_small, head_dim, axis=1)
    prev_row = passed_along(h_one[rows - 1 :], "ctx", 1)
    key_prev = jnp.concatenate([project(prev_row, full_key), key_raw[:-1]], 0) * keep
    value_prev = jnp.concatenate([project(prev_row, full_value), value_raw[:-1]], 0) * keep
    key_mix = mix * key_prev + (1.0 - mix) * key_raw
    value_mix = mix * value_prev + (1.0 - mix) * value_raw
    query4 = query.reshape(rows, heads, head_dim)
    query_inv = lax.rsqrt(jnp.mean(query4 * query4, axis=-1, keepdims=True) + EPS)
    query_norm = query4 * query_inv
    key4 = key_mix.reshape(rows, heads, head_dim)
    key_inv = lax.rsqrt(jnp.mean(key4 * key4, axis=-1, keepdims=True) + EPS)
    key_norm = key4 * key_inv
    q_low = query_norm.astype(jnp.bfloat16)
    k_low = key_norm.reshape(rows, width).astype(jnp.bfloat16)
    v_low = value_mix.astype(jnp.bfloat16)
    local_cum = jnp.cumsum(log_forget, axis=0)
    offset = entering(
        local_cum[rows - 1], "ctx", add_arrays, jnp.zeros((heads,), jnp.float32), False
    )
    decay = local_cum + offset
    gathered_k, gathered_v, all_decay = (
        lax.all_gather(k_low.astype(jnp.float32), "ctx", axis=0, tiled=True),
        lax.all_gather(v_low.astype(jnp.float32), "ctx", axis=0, tiled=True),
        lax.all_gather(decay, "ctx", axis=0, tiled=True),
    )
    all_keys = gathered_k.astype(jnp.bfloat16).reshape(group, heads, head_dim)
    all_values = gathered_v.astype(jnp.bfloat16).reshape(group, heads, head_dim)

    def scores_of(index, keys_whole, decay_whole):
        q_part = lax.dynamic_slice_in_dim(q_low, index * 4, 4, 1)
        k_part = lax.dynamic_slice_in_dim(keys_whole, index * 4, 4, 1)
        own = lax.dynamic_slice_in_dim(decay, index * 4, 4, 1)
        far = lax.dynamic_slice_in_dim(decay_whole, index * 4, 4, 1)
        raw = jnp.einsum("rhd,ghd->hrg", q_part, k_part, preferred_element_type=jnp.float32) * scale
        raw = raw + own.T[:, :, None] - far.T[:, None, :]
        return (jnp.where(allowed[None], raw, -1e30), q_part, k_part)

    group_count = heads // 4

    def forward_step(index, carry):
        mixed, log_total = carry
        scores, q_part, k_part = scores_of(index, all_keys, all_decay)
        v_part = lax.dynamic_slice_in_dim(all_values, index * 4, 4, 1)
        top = jnp.max(scores, axis=-1, keepdims=True)
        expd = jnp.exp(scores - top)
        total = jnp.sum(expd, axis=-1, keepdims=True)
        probs = (expd / total).astype(jnp.bfloat16)
        part = jnp.einsum("hrg,ghd->rhd", probs, v_part, preferred_element_type=jnp.float32)
        mixed = lax.dynamic_update_slice_in_dim(mixed, part, index * 4, 1)
        log_total = lax.dynamic_update_slice_in_dim(
            log_total, (top + jnp.log(total))[:, :, 0].T, index * 4, 1
        )
        return (mixed, log_total)

    attn4, log_total = lax.fori_loop(
        0,
        group_count,
        forward_step,
        (jnp.zeros((rows, heads, head_dim), jnp.float32), jnp.zeros((rows, heads), jnp.float32)),
    )
    attn = attn4.reshape(rows, width)
    gate_sig = jax.nn.sigmoid(gate_raw)
    branch_in = (gate_sig * attn).astype(jnp.bfloat16)
    mid = x_full + project(branch_in, full_out)
    inv_two = lax.rsqrt(jnp.mean(mid * mid, axis=-1, keepdims=True) + EPS)
    normed_two = mid * inv_two
    h_two = (normed_two * gains[1]).astype(jnp.bfloat16)
    full_ff_gate, full_ff_up, full_ff_down = fetch_feed(w_ff_gate, w_ff_up, w_ff_down)
    ff_gate = project(h_two, full_ff_gate)
    ff_up = project(h_two, full_ff_up)
    ff_sig = jax.nn.sigmoid(ff_gate)
    hidden = (ff_gate * ff_sig * ff_up).astype(jnp.bfloat16)
    result = (mid + project(hidden, full_ff_down)).astype(jnp.bfloat16)
    full_ff_gate, full_ff_up, full_ff_down = fetch_feed(w_ff_gate, w_ff_up, w_ff_down)
    full_query, full_key, full_value, full_gate, full_out, full_heads = fetch_attention(
        w_query, w_key, w_value, w_gate, w_out, w_heads
    )
    grad_out = cotangent.astype(jnp.float32)
    grad_down = weight_grad(hidden, cotangent)
    grad_hidden = input_grad(cotangent, full_ff_down)
    grad_gate_ff = (grad_hidden * ff_up * ff_sig * (1.0 + ff_gate * (1.0 - ff_sig))).astype(
        jnp.bfloat16
    )
    grad_up_ff = (grad_hidden * (ff_gate * ff_sig)).astype(jnp.bfloat16)
    ffn_grads = (
        lax.psum_scatter(
            weight_grad(h_two, grad_gate_ff), ("dp", "ctx"), scatter_dimension=0, tiled=True
        ),
        lax.psum_scatter(
            weight_grad(h_two, grad_up_ff), ("dp", "ctx"), scatter_dimension=0, tiled=True
        ),
        lax.psum_scatter(grad_down, ("dp", "ctx"), scatter_dimension=0, tiled=True),
    )
    grad_h_two = input_grad(grad_gate_ff, full_ff_gate) + input_grad(grad_up_ff, full_ff_up)
    gain_two = jnp.sum(grad_h_two * normed_two, axis=0)
    grad_mid = norm_back(grad_h_two * gains[1], normed_two, inv_two) + grad_out
    grad_branch = grad_mid.astype(jnp.bfloat16)
    grad_wout = weight_grad(branch_in, grad_branch)
    grad_branch_in = input_grad(grad_branch, full_out)
    grad_attn = (grad_branch_in * gate_sig).astype(jnp.bfloat16).reshape(rows, heads, head_dim)
    grad_gate = (grad_branch_in * attn * gate_sig * (1.0 - gate_sig)).astype(jnp.bfloat16)
    gathered_k, gathered_v, all_decay = (
        lax.all_gather(k_low.astype(jnp.float32), "ctx", axis=0, tiled=True),
        lax.all_gather(v_low.astype(jnp.float32), "ctx", axis=0, tiled=True),
        lax.all_gather(decay, "ctx", axis=0, tiled=True),
    )
    all_keys = gathered_k.astype(jnp.bfloat16).reshape(group, heads, head_dim)
    all_values = gathered_v.astype(jnp.bfloat16).reshape(group, heads, head_dim)

    def backward_step(index, carry):
        grad_q, grad_k, grad_v, grad_own, grad_far = carry
        scores, q_part, k_part = scores_of(index, all_keys, all_decay)
        v_part = lax.dynamic_slice_in_dim(all_values, index * 4, 4, 1)
        lse = lax.dynamic_slice_in_dim(log_total, index * 4, 4, 1).T[:, :, None]
        probs = jnp.exp(scores - lse)
        probs_low = probs.astype(jnp.bfloat16)
        grad_part = lax.dynamic_slice_in_dim(grad_attn, index * 4, 4, 1)
        grad_probs = jnp.einsum(
            "rhd,ghd->hrg", grad_part, v_part, preferred_element_type=jnp.float32
        )
        value_term = jnp.einsum(
            "hrg,rhd->ghd", probs_low, grad_part, preferred_element_type=jnp.float32
        )
        grad_scores = (
            probs * (grad_probs - jnp.sum(probs * grad_probs, axis=-1, keepdims=True))
        ).astype(jnp.bfloat16)
        query_term = (
            jnp.einsum("hrg,ghd->rhd", grad_scores, k_part, preferred_element_type=jnp.float32)
            * scale
        )
        key_term = (
            jnp.einsum("hrg,rhd->ghd", grad_scores, q_part, preferred_element_type=jnp.float32)
            * scale
        )
        scores_full = grad_scores.astype(jnp.float32)
        own_term = jnp.sum(scores_full, axis=-1).T
        far_term = -jnp.sum(scores_full, axis=1).T
        grad_q = lax.dynamic_update_slice_in_dim(grad_q, query_term, index * 4, 1)
        grad_k = lax.dynamic_update_slice_in_dim(grad_k, key_term, index * 4, 1)
        grad_v = lax.dynamic_update_slice_in_dim(grad_v, value_term, index * 4, 1)
        grad_own = lax.dynamic_update_slice_in_dim(grad_own, own_term, index * 4, 1)
        grad_far = lax.dynamic_update_slice_in_dim(grad_far, far_term, index * 4, 1)
        return (grad_q, grad_k, grad_v, grad_own, grad_far)

    grad_q, grad_k, grad_v, grad_own, grad_far = lax.fori_loop(
        0,
        group_count,
        backward_step,
        (
            jnp.zeros((rows, heads, head_dim), jnp.float32),
            jnp.zeros((group, heads, head_dim), jnp.float32),
            jnp.zeros((group, heads, head_dim), jnp.float32),
            jnp.zeros((rows, heads), jnp.float32),
            jnp.zeros((group, heads), jnp.float32),
        ),
    )
    grad_k_local, grad_v_local, grad_far_local = (
        lax.psum_scatter(grad_k, "ctx", scatter_dimension=0, tiled=True),
        lax.psum_scatter(grad_v, "ctx", scatter_dimension=0, tiled=True),
        lax.psum_scatter(grad_far, "ctx", scatter_dimension=0, tiled=True),
    )
    grad_decay = grad_own + grad_far_local
    local_rev = jnp.flip(jnp.cumsum(jnp.flip(grad_decay, 0), axis=0), 0)
    later = entering(
        jnp.sum(grad_decay, axis=0), "ctx", add_arrays, jnp.zeros((heads,), jnp.float32), True
    )
    grad_forget_logit = (local_rev + later) * jax.nn.sigmoid(-forget_logit)
    grad_query = norm_back(grad_q, query_norm, query_inv).reshape(rows, width)
    grad_key_mix = norm_back(grad_k_local, key_norm, key_inv).reshape(rows, width)
    grad_value_mix = grad_v_local.reshape(rows, width)
    grad_mix = jnp.sum(
        (grad_key_mix * (key_prev - key_raw) + grad_value_mix * (value_prev - value_raw)).reshape(
            rows, heads, head_dim
        ),
        axis=-1,
    )
    grad_shift_logit = grad_mix * mix_small * (1.0 - mix_small)
    carried_key = grad_key_mix * mix * keep
    carried_value = grad_value_mix * mix * keep
    from_next = passed_along(jnp.concatenate([carried_key[:1], carried_value[:1]], 0), "ctx", -1)
    grad_key_raw = (
        grad_key_mix * (1.0 - mix) + jnp.concatenate([carried_key[1:], from_next[:1]], 0)
    ).astype(jnp.bfloat16)
    grad_value_raw = (
        grad_value_mix * (1.0 - mix) + jnp.concatenate([carried_value[1:], from_next[1:]], 0)
    ).astype(jnp.bfloat16)
    grad_query_low = grad_query.astype(jnp.bfloat16)
    grad_head = jnp.concatenate([grad_forget_logit, grad_shift_logit], axis=1).astype(jnp.bfloat16)
    attn_grads = (
        lax.psum_scatter(
            weight_grad(h_one, grad_query_low), ("dp", "ctx"), scatter_dimension=0, tiled=True
        ),
        lax.psum_scatter(
            weight_grad(h_one, grad_key_raw), ("dp", "ctx"), scatter_dimension=0, tiled=True
        ),
        lax.psum_scatter(
            weight_grad(h_one, grad_value_raw), ("dp", "ctx"), scatter_dimension=0, tiled=True
        ),
        lax.psum_scatter(
            weight_grad(h_one, grad_gate), ("dp", "ctx"), scatter_dimension=0, tiled=True
        ),
        lax.psum_scatter(grad_wout, ("dp", "ctx"), scatter_dimension=0, tiled=True),
        lax.psum_scatter(
            weight_grad(h_one, grad_head), ("dp", "ctx"), scatter_dimension=0, tiled=True
        ),
    )
    grad_h_one = (
        input_grad(grad_query_low, full_query)
        + input_grad(grad_key_raw, full_key)
        + input_grad(grad_value_raw, full_value)
        + input_grad(grad_gate, full_gate)
        + input_grad(grad_head, full_heads)
    )
    gain_one = jnp.sum(grad_h_one * normed_one, axis=0)
    grad_input = norm_back(grad_h_one * gains[0], normed_one, inv_one) + grad_mid
    small = lax.psum(
        (
            jnp.stack([gain_one, gain_two]),
            jnp.stack([jnp.sum(grad_forget_logit, axis=0), jnp.sum(grad_shift_logit, axis=0)]),
        ),
        ("dp", "ctx"),
    )
    return (
        result,
        grad_input,
        small[0],
        small[1],
        attn_grads[0],
        attn_grads[1],
        attn_grads[2],
        attn_grads[3],
        attn_grads[4],
        attn_grads[5],
        ffn_grads[0],
        ffn_grads[1],
        ffn_grads[2],
    )


AXES = ("x", "core", "zh", "zl", "y")

def dot(left, right, dims):
    return lax.dot_general(left, right, (dims, ((), ())), preferred_element_type=jnp.float32)


def ab(left, right):
    return dot(left, right, ((1,), (0,)))


def abt(left, right):
    return dot(left, right, ((1,), (1,)))


def atb(left, right):
    return dot(left, right, ((0,), (0,)))


MESH = pl.DeviceIdType.MESH


class Net:
    def __init__(self, send, recv):
        self.send, self.recv, self.count, self.open = send, recv, 0, []
        self.at = {name: lax.axis_index(name) for name in AXES}

    def flip(self, names):
        return {name: 1 - self.at[name] for name in names}

    def greet(self):
        barrier = pltpu.get_barrier_semaphore()
        for names in PARTNERS:
            pl.semaphore_signal(barrier, 1, device_id=self.flip(names), device_id_type=MESH)
        moved = self.at["core"] != self.at["zh"]

        @pl.when(moved)
        def _():
            other = self.flip(("core", "zh"))
            pl.semaphore_signal(barrier, 1, device_id=other, device_id_type=MESH)
            pl.semaphore_wait(barrier, len(PARTNERS) + 1)

        @pl.when(jnp.logical_not(moved))
        def _():
            pl.semaphore_wait(barrier, len(PARTNERS))

    def copy(self, source, target, names):
        i = self.count
        self.count += 1
        return pltpu.make_async_remote_copy(
            source,
            target,
            self.send.at[i],
            self.recv.at[i],
            device_id=self.flip(names),
            device_id_type=MESH,
        )

    def push(self, source, target, names):
        made = self.copy(source, target, names)
        made.start()
        self.open.append(made)
        return made

    def left(self, copies):
        for made in copies:
            made.wait_send()
            self.open = [other for other in self.open if other is not made]

    def drain(self):
        for made in self.open:
            made.wait_send()


PARTNERS = (
    ("y",),
    ("zl",),
    ("zl", "y"),
    ("core",),
    ("core", "y"),
    ("core", "zl"),
    ("core", "zl", "y"),
    ("x",),
    ("zh",),
)


def rank_of(at):
    return (at["core"] * 2 + at["zl"]) * 2 + at["y"]


def flipped(at, names):
    return {name: 1 - at[name] if name in names else at[name] for name in at}


def unit_of(at, names):
    at = flipped(at, names)
    return at["zl"] * 2 + at["y"]


class Gather:
    def __init__(self, net, ref, rows):
        self.net, self.ref, self.rows = net, ref, rows

    def part(self, names, half=None):
        start = rank_of(flipped(self.net.at, names)) * self.rows
        size = self.rows
        if half is not None:
            size = self.rows // 2
            start = start + half * size
        return self.ref.at[pl.ds(pl.multiple_of(start, size), size)]

    def send(self, block, half, to):
        part = self.part(block, half)
        return self.net.push(part, part, to)

    def first(self):
        self.along = [self.send((), half, ("zl",)) for half in range(2)]
        self.near = self.send((), None, ("y",))
        self.cores = [self.send((), None, ("core",))]

    def second(self):
        self.corner = []
        for half in range(2):
            self.along[half].wait_recv()
            self.corner.append(self.send(("zl",), half, ("y",)))
        self.cores.append(self.send(("zl",), None, ("core",)))
        self.near.wait_recv()
        self.cores.append(self.send(("y",), None, ("core",)))

    def third(self):
        for made in self.corner:
            made.wait_recv()
        self.cores.append(self.send(("zl", "y"), None, ("core",)))

    def done(self):
        for made in self.cores:
            made.wait_recv()


QUARTERS = (("core", "zl"), ("zl",), ("core",), ())


def quarter(net, piece):
    at = flipped(net.at, QUARTERS[piece])
    return (at["core"] * 2 + at["zl"]) * 2


class Spread:
    def __init__(self, net, ref, pieces):
        self.net, self.ref, self.pieces = net, ref, pieces
        self.size = ref.shape[1] // pieces
        self.unit = net.at["x"] * 2 + net.at["zh"]
        self.from_zh = net.at["x"] * 2 + 1 - net.at["zh"]

    def send(self, unit, piece, to):
        part = self.ref.at[unit, pl.ds(piece * self.size, self.size)]
        return self.net.push(part, part, to)

    def first(self, ahead):
        self.along, self.across, self.corner = [], [], []
        for piece in range(self.pieces):
            if piece < ahead:
                self.along.append(self.send(self.unit, piece, ("zh",)))
            self.across.append(self.send(self.unit, piece, ("x",)))

    def second(self, piece):
        self.along[piece].wait_recv()
        self.corner.append(self.send(self.from_zh, piece, ("x",)))
        if len(self.along) < self.pieces:
            self.push_next()

    def push_next(self):
        self.along.append(self.send(self.unit, len(self.along), ("zh",)))

    def wait_across(self):
        for made in self.across:
            made.wait_recv()

    def wait_corner(self):
        for made in self.corner:
            made.wait_recv()


def exchange(net, source, target):
    rank = rank_of(net.at)
    target[rank] = source[rank]
    made = []
    for names in PARTNERS[:7]:
        to = rank_of(flipped(net.at, names))
        made.append(net.push(source.at[to], target.at[rank], names))
    return made


def swap_chunks(value):
    size = value.shape[1] // 8
    order = (0, 2, 1, 3, 4, 6, 5, 7)
    return jnp.concatenate([value[:, i * size : (i + 1) * size] for i in order], axis=1)


def normed(value):
    inverse = lax.rsqrt(jnp.mean(value * value, axis=-1, keepdims=True) + EPS)
    return value * inverse, inverse


def slice_of(rank):
    return rank // 2 % 2 * 4 + rank // 4 * 2 + rank % 2


def pack_attention(wide, heads_ref, pack_ref):
    size = wide[0].shape[1] // 8
    few = heads_ref.shape[1] // 16
    for rank in range(8):
        at = slice_of(rank)
        for i, ref in enumerate(wide):
            pack_ref[rank, :, i * size : (i + 1) * size] = ref[:, at * size : (at + 1) * size]
        pack_ref[rank, :, 4 * size :] = jnp.concatenate(
            [heads_ref[:, (i * 8 + at) * few : (i * 8 + at + 1) * few] for i in range(2)]
            + [jnp.zeros((heads_ref.shape[0], 128 - 2 * few), jnp.bfloat16)],
            axis=1,
        )


def pack_feeds(feeds, pack_gu_ref):
    block = feeds[0].shape[1] // 32
    for rank in range(8):
        for i, ref in enumerate(feeds):
            for unit in range(4):
                source = unit // 2 * 16 + rank // 4 * 8 + unit % 2 * 4 + rank % 4
                to = (i * 4 + unit) * block
                pack_gu_ref[rank, :, to : to + block] = ref[:, source * block : (source + 1) * block]


def whole(shape, dtype):
    return jax.ShapeDtypeStruct(shape, dtype)


def vmem(count):
    return [pl.BlockSpec(memory_space=pltpu.VMEM)] * count


def call(kernel, number, outs, args, copies, scratch=(), local=2, far=(), far_outs=()):
    return pl.pallas_call(
        kernel,
        out_shape=outs,
        in_specs=[
            pl.BlockSpec(memory_space=pl.ANY if i in far else pltpu.VMEM) for i in range(len(args))
        ],
        out_specs=[
            pl.BlockSpec(memory_space=pl.ANY if i in far_outs else pltpu.VMEM) for i in range(len(outs))
        ],
        scratch_shapes=[
            *scratch,
            pltpu.SemaphoreType.DMA((copies,)),
            pltpu.SemaphoreType.DMA((copies,)),
            pltpu.SemaphoreType.DMA((local,)),
        ],
        compiler_params=pltpu.CompilerParams(
            collective_id=number, has_side_effects=True, vmem_limit_bytes=60 * 2**20
        ),
    )(*args)


class Sum:
    def __init__(self, net, part, core, near, corner):
        self.net, self.part, self.core, self.near, self.corner = net, part, core, near, corner
        self.rows = part.shape[1]
        self.half = self.rows // 2
        self.given = {}

    def place(self, names):
        at = flipped(self.net.at, names)
        return at["zl"] * 2 + at["y"]

    def rank(self, names):
        return rank_of(flipped(self.net.at, names))

    def give(self, names):
        block = self.part.at[self.rank(("core", *names))]
        self.given[names] = self.net.push(block, self.core.at[self.place(names)], ("core",))

    def take(self, names):
        self.given[names].wait_recv()
        rank = self.rank(names)
        self.part[rank] = (
            self.part[rank].astype(jnp.float32) + self.core[self.place(names)].astype(jnp.float32)
        ).astype(jnp.bfloat16)

    def rows_of(self, names, half):
        return self.part.at[self.rank(names), pl.ds(half * self.half, self.half)]

    def send_corner(self):
        self.take(("zl", "y"))
        self.by_y = [
            self.net.push(self.rows_of(("zl", "y"), half), self.corner.at[half], ("y",))
            for half in range(2)
        ]

    def send_y(self):
        self.take(("y",))
        self.near_y = self.net.push(self.part.at[self.rank(("y",))], self.near.at[0], ("y",))

    def left_cores(self):
        self.net.left(self.given.values())

    def left(self):
        self.net.left((*self.by_y, self.near_y, *self.near_zl))

    def pass_on(self):
        self.take(("zl",))
        self.near_zl = []
        for half in range(2):
            self.by_y[half].wait_recv()
            rows = self.rows_of(("zl",), half)
            rows[...] = (
                rows[...].astype(jnp.float32) + self.corner[half].astype(jnp.float32)
            ).astype(jnp.bfloat16)
            to = self.near.at[1, pl.ds(half * self.half, self.half)]
            self.near_zl.append(self.net.push(rows, to, ("zl",)))

    def total(self):
        self.given[()].wait_recv()
        own = self.part[self.rank(())].astype(jnp.float32)
        own = own + self.core[self.place(())].astype(jnp.float32)
        for made in (self.near_y, *self.near_zl):
            made.wait_recv()
        return own + self.near[0].astype(jnp.float32) + self.near[1].astype(jnp.float32)


def sum_scratch(rows, width):
    return [
        pltpu.VMEM((8, rows, width), jnp.bfloat16),
        pltpu.VMEM((4, rows, width), jnp.bfloat16),
        pltpu.VMEM((2, rows, width), jnp.bfloat16),
        pltpu.VMEM((2, rows // 2, width), jnp.bfloat16),
    ]


def move(net, pairs, sems, start=0):
    moved = net.at["core"] != net.at["zh"]
    away = [net.copy(source, target, ("core", "zh")) for source, target in pairs]
    stay = [pltpu.make_async_copy(*pair, sems.at[start + i]) for i, pair in enumerate(pairs)]

    def each(act):
        @pl.when(moved)
        def _():
            for made in away:
                act(made)

        @pl.when(jnp.logical_not(moved))
        def _():
            for made in stay:
                act(made)

    each(lambda made: made.start())
    return lambda: each(lambda made: made.wait())


def lanes(columns, size):
    lane = lax.broadcasted_iota(jnp.int32, (size, 128), 1)
    out = jnp.zeros((size, 128), jnp.float32)
    for i, column in enumerate(columns):
        out = jnp.where(lane == i, column, out)
    return out


def triangle(size, upper):
    row = lax.broadcasted_iota(jnp.int32, (size, size), 0)
    col = lax.broadcasted_iota(jnp.int32, (size, size), 1)
    return jnp.where(row <= col if upper else row >= col, 1.0, 0.0)


def exact(left, right):
    return jnp.dot(
        left, right, precision=lax.Precision.HIGHEST, preferred_element_type=jnp.float32
    )


def spread_lanes(columns, size, wide):
    which = (lax.broadcasted_iota(jnp.int32, (size, wide), 1) // 64) % 3
    return jnp.where(which == 0, columns[0], jnp.where(which == 1, columns[1], columns[2]))


def bounds(lens_ref, first_row, size):
    place = first_row + lax.broadcasted_iota(jnp.int32, (size, 1), 0)
    first = lens_ref[0:1, 0:1]
    second = first + lens_ref[0:1, 1:2]
    low = jnp.where(place >= second, second, jnp.where(place >= first, first, 0))
    return place, low


def head_rows(value, h):
    return value[:, h * 64 : (h + 1) * 64]


def with_one(value, lane_at):
    size = value.shape[0]
    lane = lax.broadcasted_iota(jnp.int32, (size, 64), 1)
    return jnp.concatenate([value, jnp.where(lane == lane_at, 1.0, 0.0)], axis=1)


def mixing(proj_ref, lens_ref, bias_ref, q_ref, k_ref, v_ref, diff_ref, stat_ref, fcol_ref, frow_ref):
    size = 128
    lower = triangle(size, False)

    def one(i, carry):
        last, below = carry
        at = pl.ds(pl.multiple_of(i * size, size), size)
        block = proj_ref[at, :]
        kv = block[:, 384:768]
        logits = block[:, 768:896] + bias_ref[0:1, :]
        logf = jax.nn.log_sigmoid(logits)
        mix = jax.nn.sigmoid(logits)
        place, low = bounds(lens_ref, i * size, size)
        row = lax.broadcasted_iota(jnp.int32, (size, 384), 0)
        prev = jnp.where(row == 0, last, pltpu.roll(kv, 1, 0))
        prev = jnp.where(place == low, 0.0, prev)
        diff = prev - kv
        diff_ref[at, :] = diff
        mixed = kv + spread_lanes([mix[:, 3 + h : 4 + h] for h in range(3)], size, 384) * diff
        decay = exact(lower, logf) + below
        frows = decay.T
        stats = []
        for h in range(3):
            q = head_rows(block, h)
            inv = lax.rsqrt(jnp.mean(q * q, axis=-1, keepdims=True) + EPS)
            stats.append(inv)
            q_ref[h, at, :] = with_one(q * inv * 0.125, 0).astype(jnp.bfloat16)
            fcol_ref[h, at, :] = jnp.broadcast_to(decay[:, h : h + 1], (size, 128))
            frow_ref[h, :, at] = frows[h : h + 1, :]
        for h in range(3):
            k = head_rows(mixed, h)
            inv = lax.rsqrt(jnp.mean(k * k, axis=-1, keepdims=True) + EPS)
            stats.append(inv)
            k_ref[h, at, :] = with_one(k * inv, 1).astype(jnp.bfloat16)
            v_ref[h, at, :] = head_rows(mixed, 3 + h).astype(jnp.bfloat16)
        shut = jax.nn.sigmoid(-logits)
        stats += [shut[:, h : h + 1] for h in range(3)]
        stats += [mix[:, 3 + h : 4 + h] for h in range(3)]
        stat_ref[at, :] = lanes(stats, size)
        return kv[size - 1 :, :], decay[size - 1 :, :]

    lax.fori_loop(
        0,
        proj_ref.shape[0] // size,
        one,
        (jnp.zeros((1, 384), jnp.float32), jnp.zeros((1, 128), jnp.float32)),
    )


def scores(h, at, start, size, keys, q_ref, k_ref, fcol_ref, frow_ref, lens_ref):
    raw = abt(q_ref[h, at, :], k_ref[h, :keys, :])
    own = jnp.concatenate([fcol_ref[h, at, :]] * (keys // 128), axis=1)
    raw = raw + own - frow_ref[h, :, :keys]
    place, low = bounds(lens_ref, start, size)
    col = lax.broadcasted_iota(jnp.int32, (size, keys), 1)
    return jnp.where((col <= place) & (col >= low), jnp.exp(raw), 0.0)


def over_blocks(body, begin, end):
    for part in range(begin, end):

        def one(n, _, part=part):
            body(n // 2, part * 256 + n % 2 * 128, (part + 1) * 256)
            return 0

        lax.fori_loop(0, 6, one, 0)


def kernel_ab(
    x_ref, seq_ref, gains_ref, cot_ref, head_bias_ref, wq_ref, wg_ref, wk_ref, wv_ref, wh_ref, wfg_far, wfu_far,
    wo_far, down_far, xs_ref, lens_ref, mid_ref, *refs,
):
    far, refs = refs[:17], refs[17:]
    near_refs, refs = refs[:17], refs[17:]
    (
        h_ref, w_ref, q_ref, k_ref, v_ref, diff_ref, stat_ref, fcol_ref, frow_ref, gate_ref, attn_ref, a_ref,
        wo_all, gu_all, down_all, h2_ref, cot_all,
    ) = near_refs
    (
        lens_own, bias_ref, proj_ref, pack_ref, pack_gu_ref, spread_o,
        part, core, near, corner, wfg_ref, wfu_ref, wo_ref, down_ref, send, recv, sems,
    ) = refs
    loads = [
        pltpu.make_async_copy(source, target, sems.at[20 + i])
        for i, (source, target) in enumerate(
            ((wfg_far, wfg_ref), (wfu_far, wfu_ref), (wo_far, wo_ref), (down_far, down_ref))
        )
    ]
    for made in loads:
        made.start()
    kept = []

    def keep(i):
        made = pltpu.make_async_copy(near_refs[i], far[i], sems.at[3 + i])
        made.start()
        kept.append(made)

    net = Net(send, recv)
    rows = x_ref.shape[0]
    rank = rank_of(net.at)
    lens_own[...] = jnp.zeros(lens_own.shape, jnp.int32)
    lens_own[0:1, 0:3] = seq_ref[...]
    net.greet()
    moved = move(net, [(x_ref, xs_ref), (lens_own, lens_ref)], sems)
    pack_attention((wq_ref, wg_ref, wk_ref, wv_ref), wh_ref, pack_ref)
    few = head_bias_ref.shape[1] // 8
    bias = jnp.zeros((1, 128), jnp.float32)
    for at in range(8):
        own = jnp.concatenate(
            [head_bias_ref[i : i + 1, at * few : (at + 1) * few] for i in range(2)]
            + [jnp.zeros((1, 128 - 2 * few), jnp.float32)],
            axis=1,
        )
        bias = jnp.where(slice_of(rank) == at, own, bias)
    bias_ref[...] = jnp.broadcast_to(bias, bias_ref.shape)
    spread = Spread(net, w_ref, 4)
    unit = spread.unit
    packs = exchange(net, pack_ref, w_ref.at[unit])
    for made in loads:
        made.wait()
    pack_feeds((wfg_ref, wfu_ref), pack_gu_ref)

    moved()
    value, _inverse = normed(xs_ref[...].astype(jnp.float32))
    h_ref[pl.ds(pl.multiple_of(rank * rows, rows), rows)] = swap_chunks(
        (value * gains_ref[0:1, :]).astype(jnp.bfloat16)
    )
    gather = Gather(net, h_ref, rows)
    gather.first()
    for made in packs:
        made.wait_recv()
    spread.first(4)
    there = (net.at["zh"] * 2 + net.at["zl"]) * 2 + net.at["y"]
    there = pl.ds(pl.multiple_of(there * rows, rows), rows)
    moved_cot = move(net, [(cot_ref, cot_all.at[there])], sems, 2)
    out = Spread(net, spread_o, 1)
    spread_o[unit] = wo_ref[...]
    out.first(1)
    gather.second()
    spread.second(0)
    gather.third()
    spread.second(1)
    given = exchange(net, pack_gu_ref, gu_all.at[unit])
    depth = pack_ref.shape[0] * pack_ref.shape[1]
    tall = 2 * rows

    def multiply(which, fresh):
        def one(i, _):
            at = pl.ds(pl.multiple_of(i * tall, tall), tall)
            left = h_ref[at, pl.ds(pl.multiple_of(which * depth, 128), depth)]
            part = ab(left, w_ref[which].reshape(depth, -1))
            if fresh:
                proj_ref[at, :] = part
            else:
                proj_ref[at, :] += part
            return 0

        lax.fori_loop(0, h_ref.shape[0] // tall, one, 0)

    gather.done()
    keep(0)
    multiply(unit, True)
    spread.wait_across()
    multiply((1 - net.at["x"]) * 2 + net.at["zh"], False)
    spread.second(2)
    spread.second(3)
    multiply(spread.from_zh, False)
    spread.wait_corner()
    multiply((1 - net.at["x"]) * 2 + 1 - net.at["zh"], False)
    keep(1)
    group = proj_ref.shape[0]
    mine = pl.ds(pl.multiple_of(rank * rows, rows), rows)
    feed = Spread(net, gu_all, 4)
    down = Spread(net, down_all, 2)
    moved_cot()
    other = Gather(net, cot_all, rows)
    other.first()
    down_all[unit] = down_ref[...]
    for made in given:
        made.wait_recv()
    feed.first(2)
    down.first(0)
    mixing(proj_ref, lens_ref, bias_ref, q_ref, k_ref, v_ref, diff_ref, stat_ref, fcol_ref, frow_ref)
    for i in (2, 3, 4, 5, 6, 8):
        keep(i)
    out.second(0)
    other.second()

    def attend(h, start, keys):
        at = pl.ds(pl.multiple_of(start, 128), 128)
        e = scores(h, at, start, 128, keys, q_ref, k_ref, fcol_ref, frow_ref, lens_ref)
        total = jnp.sum(e, axis=-1, keepdims=True)
        inv = 1.0 / total
        fcol_ref[h, at, :] -= jnp.broadcast_to(jnp.log(total), (128, 128))
        attn_ref[h, at, :] = ab((e * inv).astype(jnp.bfloat16), v_ref[h, :keys, :])

    over_blocks(attend, 0, 2)
    other.third()
    out.wait_across()
    out.wait_corner()
    pieces = []
    wo_all[unit_of(net.at, ())] = spread_o[unit_of(net.at, ())]
    for names in (("y",), ("zl",), ("zl", "y")):
        pieces.append(net.push(spread_o.at[unit_of(net.at, names)], wo_all.at[unit_of(net.at, ())], names))
    feed.second(0)
    over_blocks(attend, 2, group // 256)
    feed.second(1)
    for h in range(3):
        gate = jax.nn.sigmoid(proj_ref[:, 192 + 64 * h : 256 + 64 * h])
        gate_ref[:, 64 * h : 64 * h + 64] = gate
        a_ref[:, 64 * h : 64 * h + 64] = (gate * attn_ref[h]).astype(jnp.bfloat16)
    for made in pieces:
        made.wait_recv()
    for i in (7, 9, 10, 11, 12):
        keep(i)

    total = Sum(net, part, core, near, corner)

    def project_block(names):
        to = rank_of(flipped(net.at, names))
        left = a_ref[pl.ds(pl.multiple_of(to * rows, rows), rows), :]
        part[to] = ab(left, wo_all[...].reshape(-1, wo_all.shape[2])).astype(jnp.bfloat16)

    for names in (("zl", "y"), ("zl",), ("y",), ()):
        project_block(("core", *names))
        total.give(names)
    project_block(("zl", "y"))
    total.send_corner()
    project_block(("zl",))
    project_block(("y",))
    total.send_y()
    project_block(())
    total.pass_on()
    feed.second(2)
    down.push_next()
    other.done()
    keep(16)
    mid = xs_ref[...].astype(jnp.float32) + total.total()
    mid_ref[...] = mid
    value, _inverse = normed(mid)
    h2_ref[mine] = swap_chunks((value * gains_ref[1:2, :]).astype(jnp.bfloat16))
    gather = Gather(net, h2_ref, rows)
    gather.first()
    feed.second(3)
    down.second(0)
    gather.second()
    feed.wait_across()
    feed.wait_corner()
    keep(13)
    gather.third()
    down.second(1)
    gather.done()
    keep(15)
    down.wait_across()
    down.wait_corner()
    keep(14)
    for made in kept:
        made.wait()
    net.drain()


class SpreadSum:
    def __init__(self, net, whole_ref, over_x, over_zh, pieces, relay=None, by_rank=False):
        self.relay, self.by_rank = relay, by_rank
        self.net, self.whole, self.over_x, self.over_zh, self.pieces = net, whole_ref, over_x, over_zh, pieces
        self.size = whole_ref.shape[1] // pieces
        self.x, self.zh = net.at["x"], net.at["zh"]
        self.far, self.own, self.last = [], [], []

    def rows(self, piece):
        return pl.ds(quarter(self.net, piece) if self.by_rank else piece * self.size, self.size)

    def part(self, ref, at, piece):
        return ref.at[at, self.rows(piece)]

    def send(self, zh, target, piece):
        source = self.part(self.whole, (1 - self.x) * 2 + zh, piece)
        return self.net.push(source, target, ("x",))

    def first_far(self):
        for piece in range(self.pieces):
            zh = 1 - self.zh
            self.far.append(self.send(zh, self.part(self.over_x, zh, piece), piece))

    def first_own(self):
        for piece in range(self.pieces):
            self.own.append(self.send(self.zh, self.part(self.over_x, self.zh, piece), piece))

    def first(self):
        self.first_far()
        self.first_own()

    def pass_far(self):
        for piece in range(self.pieces):
            to = self.over_x.at[self.rows(piece)]
            self.own.append(self.send(self.zh, to, piece))

    def pass_far_on(self, far, begin, end):
        for piece in range(begin, end):
            self.pass_one(piece, far.at[self.rows(piece)])

    def hand_out(self, target):
        made = []
        rank = rank_of(self.net.at)
        for piece, names in enumerate(QUARTERS):
            self.over_zh[self.rows(piece)] = self.total(piece).astype(jnp.bfloat16)
            for more in (names, (*names, "y")):
                if more:
                    to = self.over_zh.at[rank_of(flipped(self.net.at, more))]
                    made.append(self.net.push(to, target.at[rank], more))
                else:
                    target[rank] = self.over_zh[rank]
        return made

    def second(self, piece):
        self.far[piece].wait_recv()
        self.pass_one(piece, self.part(self.over_x, 1 - self.zh, piece))

    def pass_one(self, piece, came):
        here = self.part(self.whole, self.x * 2 + 1 - self.zh, piece)
        total = (here[...].astype(jnp.float32) + came[...].astype(jnp.float32)).astype(jnp.bfloat16)
        if self.relay is not None:
            here = self.relay.at[self.rows(piece)]
        here[...] = total
        target = self.over_zh.at[self.rows(piece)]
        self.last.append(self.net.push(here, target, ("zh",)))

    def total(self, piece):
        self.own[piece].wait_recv()
        self.last[piece].wait_recv()
        here = self.part(self.whole, self.x * 2 + self.zh, piece)
        if self.relay is None:
            came = self.part(self.over_x, self.zh, piece)
        else:
            came = self.over_x.at[self.rows(piece)]
        last = self.over_zh.at[self.rows(piece)]
        return (
            here[...].astype(jnp.float32) + came[...].astype(jnp.float32) + last[...].astype(jnp.float32)
        )


def norm_grad(grad, gain, value, inverse):
    scaled = grad * gain
    return (
        inverse * (scaled - value * jnp.mean(scaled * value, axis=-1, keepdims=True)),
        jnp.sum(grad * value, axis=0, keepdims=True),
    )


def kernel_c(
    h_far, cot_far, wgu_far, wd_far, mid_far, gains_ref,
    hid_far, dmid_ref, dao_ref, gain_ref, gdown_ref, ggu_far, gfar_ref,
    dgu_ref, gd_ref, over_x, over_zh, part, core, near, corner,
    h_ref, wgu_ref, cot_ref, wd_ref, mid_ref, hid_ref, ggu_ref, send, recv, sems,
):
    net = Net(send, recv)
    rank = rank_of(net.at)
    rows = mid_ref.shape[0]
    mine = pl.ds(pl.multiple_of(rank * rows, rows), rows)
    wide = hid_ref.shape[1]
    width = mid_ref.shape[1]
    four = 4 * rows
    loads = [
        pltpu.make_async_copy(source, target, sems.at[i])
        for i, (source, target) in enumerate(
            ((h_far, h_ref), (wgu_far, wgu_ref), (cot_far, cot_ref), (wd_far, wd_ref), (mid_far, mid_ref))
        )
    ]
    for made in loads:
        made.start()
    net.greet()
    for made in loads:
        made.wait()

    def half(which):
        at = pl.ds(pl.multiple_of(which * four, four), four)
        wgu = wgu_ref[...].reshape(width, 2 * wide)
        both = ab(h_ref[at, :], wgu)
        gate, up = both[:, :wide], both[:, wide:]
        sig = jax.nn.sigmoid(gate)
        act = gate * sig
        hid_ref[at, :] = (act * up).astype(jnp.bfloat16)
        grad = abt(cot_ref[at, :], wd_ref[...].reshape(wide, width))
        dgate = grad * up * sig * (1.0 + gate * (1.0 - sig))
        dgu = jnp.concatenate([dgate, grad * act], axis=1).astype(jnp.bfloat16)
        dgu_ref[at, :] = dgu
        back = abt(dgu, wgu).astype(jnp.bfloat16)
        for i in range(4):
            part[which * 4 + i] = back[i * rows : (i + 1) * rows]

    total = Sum(net, part, core, near, corner)
    half(1 - net.at["core"])
    for names in (("zl", "y"), ("zl",), ("y",), ()):
        total.give(names)
    half(net.at["core"])
    total.send_corner()
    total.send_y()
    down = SpreadSum(net, gd_ref, over_x, over_zh, 2)

    def grad_down(k, _):
        left = hid_ref[:, pl.ds(pl.multiple_of(k * rows, rows), rows)]
        gd_ref[k] = atb(left, cot_ref[...]).astype(jnp.bfloat16)
        return 0

    lax.fori_loop(0, 4, grad_down, 0)
    down.first()
    total.pass_on()
    depth = width // 4

    def grad_gu(k, _):
        left = h_ref[:, pl.ds(pl.multiple_of(k * depth, depth), depth)]
        ggu_ref[k] = atb(left, dgu_ref[...]).astype(jnp.bfloat16).reshape(ggu_ref.shape[1:])
        return 0

    lax.fori_loop(0, 4, grad_gu, 0)
    kept = [
        pltpu.make_async_copy(hid_ref, hid_far, sems.at[5]),
        pltpu.make_async_copy(ggu_ref, ggu_far, sems.at[6]),
    ]
    for made in kept:
        made.start()
    feed = SpreadSum(net, ggu_ref, None, None, 1)
    far = feed.send(1 - net.at["zh"], gfar_ref, 0)
    grad = swap_chunks(total.total())
    value, inverse = normed(mid_ref[...])
    back, gain = norm_grad(grad, gains_ref[1:2, :], value, inverse)
    gain_ref[...] = gain
    dmid = cot_ref[mine, :].astype(jnp.float32) + back
    dmid_ref[...] = dmid
    dao_ref[mine] = dmid.astype(jnp.bfloat16)
    gather = Gather(net, dao_ref, rows)
    gather.first()
    down.second(0)
    down.second(1)
    gather.second()
    gather.third()
    for piece in range(2):
        gdown_ref[pl.ds(piece * rows // 2, rows // 2)] = down.total(piece)
    gather.done()
    far.wait_recv()
    for made in kept:
        made.wait()
    net.drain()


def spread_scratch(shape):
    return [
        pltpu.VMEM((4, *shape), jnp.bfloat16),
        pltpu.VMEM((2, *shape), jnp.bfloat16),
        pltpu.VMEM(shape, jnp.bfloat16),
    ]


def unmixing(
    lens_ref, q_ref, k_ref, diff_ref, stat_ref, dq_ref, dk_ref, dv_ref, dproj_ref
):
    size = 128
    count = diff_ref.shape[0] // size
    upper = triangle(size, True)

    def one(step, carry):
        after, above, sums = carry
        i = count - 1 - step
        at = pl.ds(pl.multiple_of(i * size, size), size)
        stat = stat_ref[at, :]
        decay, keys, values = [], [], []
        for h in range(3):
            dq, dk = dq_ref[h, at, :], dk_ref[h, at, :]
            decay.append(dq[:, 65:66] - dk[:, 64:65])
            grad = dq[:, :64] * 0.125
            unit = q_ref[h, at, :][:, :64].astype(jnp.float32) * 8.0
            grad = grad - unit * jnp.mean(grad * unit, axis=-1, keepdims=True)
            dproj_ref[at, 64 * h : 64 * h + 64] = (stat[:, h : h + 1] * grad).astype(jnp.bfloat16)
            grad = dk[:, :64]
            unit = k_ref[h, at, :][:, :64].astype(jnp.float32)
            grad = grad - unit * jnp.mean(grad * unit, axis=-1, keepdims=True)
            keys.append(stat[:, 3 + h : 4 + h] * grad)
            values.append(dv_ref[h, at, :])
        both = jnp.concatenate(keys + values, axis=1)
        prod = both * diff_ref[at, :]
        mix = [stat[:, 9 + h : 10 + h] for h in range(3)]
        mixes = spread_lanes(mix, size, 384)
        place, low = bounds(lens_ref, i * size, size)
        carried = jnp.where(place == low, 0.0, both * mixes)
        row = lax.broadcasted_iota(jnp.int32, (size, 384), 0)
        later = jnp.where(row == size - 1, after, pltpu.roll(carried, size - 1, 0))
        dproj_ref[at, 384:768] = (both * (1.0 - mixes) + later).astype(jnp.bfloat16)
        decay = lanes(decay, size)
        suffix = exact(upper, decay) + above
        small = []
        for h in range(3):
            small.append(suffix[:, h : h + 1] * stat[:, 6 + h : 7 + h])
        for h in range(3):
            grad = jnp.sum(head_rows(prod, h) + head_rows(prod, 3 + h), axis=-1, keepdims=True)
            small.append(grad * mix[h] * (1.0 - mix[h]))
        small = lanes(small, size)
        dproj_ref[at, 768:896] = small.astype(jnp.bfloat16)
        above = above + jnp.sum(decay, axis=0, keepdims=True)
        return carried[:1, :], above, sums + jnp.sum(small, axis=0, keepdims=True)

    none = jnp.zeros((1, 128), jnp.float32)
    carry = lax.fori_loop(0, count, one, (jnp.zeros((1, 384), jnp.float32), none, none))
    return carry[2]


def kernel_d(
    dao_ref, wo_far, a_far, attn_far, gate_far, lens_ref, q_far, k_far, v_far, diff_far, stat_far,
    fcol_far, frow_far, w_far, h_ref, dmid_far, x_far, gains_ref, gain_two_ref, ggu_far, gfar_far,
    hid_far, wd_far, mid_far,
    out_ref, gx_ref, gain_ref, bias_ref, ga_ref, go_ref, gu_ref,
    do_ref, dq_ref, dk_ref, dv_ref, dproj_ref,
    gu_x, gu_zh, a_whole, a_x, a_zh, o_raw, o_whole, o_x, o_zh, small, slots, tall, gx_own, out_own,
    part, core, near, corner, core2, near2, corner2, *refs,
):
    *late, send, recv, sems = refs
    ggu_ref, gfar_ref, hid_ref, wd_ref, wo_ref, a_ref, mid_ref, attn_ref, gate_ref, q_ref, k_ref, v_ref, \
        fcol_ref, frow_ref, diff_ref, stat_ref, w_ref, dmid_ref, x_ref = late
    far = (
        ggu_far, gfar_far, hid_far, wd_far, wo_far, a_far, mid_far, attn_far, gate_far, q_far, k_far, v_far,
        fcol_far, frow_far, diff_far, stat_far, w_far, dmid_far, x_far,
    )
    net = Net(send, recv)
    rank = rank_of(net.at)
    rows, width = mid_ref.shape
    group = a_ref.shape[0]
    mine = pl.ds(pl.multiple_of(rank * rows, rows), rows)
    fetch = [pltpu.make_async_copy(ref, tall, sems.at[2 + i]) for i, ref in enumerate((dao_ref, h_ref))]
    loads = [
        pltpu.make_async_copy(source, target, sems.at[4 + i])
        for i, (source, target) in enumerate(zip(far, late))
    ]
    for made in (*loads[:4], fetch[0], *loads[4:]):
        made.start()
    net.greet()
    for made in loads[:4]:
        made.wait()
    feed = SpreadSum(net, ggu_ref, gu_x.at[0], gu_zh, 4, gu_x.at[1], True)
    attn = SpreadSum(net, a_whole, a_x, a_zh, 4, None, True)
    out = SpreadSum(net, o_whole, o_x, o_zh, 1)

    four = 4 * rows

    def half(which, left_ref, right, multiply, to):
        def one(i, _):
            at = pl.multiple_of(which * four + i * 2 * rows, 2 * rows)
            back = multiply(left_ref[pl.ds(at, 2 * rows), :], right).astype(jnp.bfloat16)
            to[which * 4 + 2 * i] = back[:rows]
            to[which * 4 + 2 * i + 1] = back[rows:]
            return 0

        lax.fori_loop(0, 2, one, 0)

    result = Sum(net, part, core2, near2, corner2)
    wd = wd_ref[...].reshape(-1, width)
    feed.pass_far()
    feed.pass_far_on(gfar_ref, 0, 2)
    half(1 - net.at["core"], hid_ref, wd, ab, part)
    for names in (("zl", "y"), ("zl",), ("y",), ()):
        result.give(names)
    half(net.at["core"], hid_ref, wd, ab, part)
    fetch[0].wait()
    for made in loads[4:9]:
        made.wait()
    da = abt(tall[...], wo_ref[...].reshape(-1, width))
    for h in range(3):
        sig = gate_ref[:, 64 * h : 64 * h + 64]
        grad = da[:, 64 * h : 64 * h + 64] * sig
        do_ref[h] = grad.astype(jnp.bfloat16)
        dproj_ref[:, 192 + 64 * h : 256 + 64 * h] = (grad * attn_ref[h] * (1.0 - sig)).astype(
            jnp.bfloat16
        )
    o_raw[...] = atb(a_ref[...], tall[...]).astype(jnp.bfloat16).reshape(o_raw.shape)
    fetch[1].start()
    here = unit_of(net.at, ())
    o_whole[here] = o_raw[here]
    pieces = []
    for names in (("y",), ("zl",), ("zl", "y")):
        pieces.append(net.push(o_raw.at[unit_of(net.at, names)], o_whole.at[here], names))
    dk_ref[...] = jnp.zeros(dk_ref.shape, jnp.float32)
    dv_ref[...] = jnp.zeros(dv_ref.shape, jnp.float32)

    def attend(h, start, keys):
        at = pl.ds(pl.multiple_of(start, 128), 128)
        p = scores(h, at, start, 128, keys, q_ref, k_ref, fcol_ref, frow_ref, lens_ref)
        do = do_ref[h, at, :]
        dp = abt(do, v_ref[h, :keys, :])
        ds = p * (dp - jnp.sum(p * dp, axis=-1, keepdims=True))
        ds = ds.astype(jnp.bfloat16)
        dq_ref[h, at, :] = ab(ds, k_ref[h, :keys, :])
        dk_ref[h, :keys, :] += atb(ds, q_ref[h, at, :])
        dv_ref[h, :keys, :] += atb(p.astype(jnp.bfloat16), do)

    result.send_corner()
    result.send_y()
    for made in pieces:
        made.wait_recv()
    out.first()
    for made in loads[9:]:
        made.wait()
    over_blocks(attend, 0, 3)
    result.pass_on()
    feed.pass_far_on(gfar_ref, 2, 4)
    over_blocks(attend, 3, 4)
    out.second(0)
    sums = unmixing(lens_ref, q_ref, k_ref, diff_ref, stat_ref, dq_ref, dk_ref, dv_ref, dproj_ref)

    result.left_cores()
    out_own[...] = (mid_ref[...] + result.total()).astype(jnp.bfloat16)
    moved_out = move(net, [(out_own, out_ref)], sems)
    result.left()
    total = Sum(net, part, core, near, corner)
    w = w_ref[...].reshape(width, -1)
    half(1 - net.at["core"], dproj_ref, w, abt, part)
    for names in (("zl", "y"), ("zl",), ("y",), ()):
        total.give(names)
    half(net.at["core"], dproj_ref, w, abt, part)
    total.send_corner()
    total.send_y()
    depth = width // 4

    def grad_attn(k, _):
        left = tall[:, pl.ds(pl.multiple_of(k * depth, depth), depth)]
        a_whole[k] = atb(left, dproj_ref[...]).astype(jnp.bfloat16).reshape(a_whole.shape[1:])
        return 0

    fetch[1].wait()
    lax.fori_loop(0, 4, grad_attn, 0)
    attn.first_far()
    total.pass_on()
    attn.second(0)
    given = feed.hand_out(gu_ref)
    attn.second(1)
    grad = swap_chunks(total.total())
    attn.second(2)
    value, inverse = normed(x_ref[...].astype(jnp.float32))
    back, gain = norm_grad(grad, gains_ref[0:1, :], value, inverse)
    small[0] = jnp.concatenate(
        [gain, gain_two_ref[...], jnp.concatenate([sums, jnp.zeros((1, width - 128), jnp.float32)], axis=1)]
        + [jnp.zeros((5, width), jnp.float32)],
        axis=0,
    )
    first = net.push(small.at[0], small.at[1], ("x",))
    attn.first_own()
    gx_own[...] = (dmid_ref[...] + back).astype(jnp.bfloat16)
    go_ref[...] = out.total(0)
    first.wait_recv()
    small[2] = small[0] + small[1]
    second = net.push(small.at[2], small.at[3], ("zh",))
    attn.second(3)
    second.wait_recv()
    slots[rank] = small[2] + small[3]
    shared = [net.push(slots.at[rank], slots.at[rank], names) for names in PARTNERS[:7]]
    moved_gx = move(net, [(gx_own, gx_ref)], sems, 1)
    given += attn.hand_out(ga_ref)
    for made in shared + given:
        made.wait_recv()
    gain_ref[...] = jnp.sum(slots[:, 0:2, :], axis=0)
    bias_ref[...] = slots[:, 2:3, :128]
    moved_out()
    moved_gx()
    net.drain()


def finish(
    out_ref, gx_ref, gain_ref, bias_ref, ga_ref, go_ref, gu_ref, gdown_ref,
    out_out, gx_out, gain_out, bias_out, gq_out, gk_out, gv_out, gg_out, go_out, gh_out, gfg_out, gfu_out, gdown_out,
):
    for source, target in ((out_ref, out_out), (gain_ref, gain_out), (go_ref, go_out), (gdown_ref, gdown_out)):
        target[...] = source[...]
    gx_out[...] = gx_ref[...].astype(jnp.float32)
    size = gq_out.shape[1] // 8
    few = bias_out.shape[1] // 8
    block = gfg_out.shape[1] // 32
    for rank in range(8):
        at = slice_of(rank)
        for i, target in enumerate((gq_out, gg_out, gk_out, gv_out)):
            part = ga_ref[rank, :, i * size : (i + 1) * size]
            target[:, at * size : (at + 1) * size] = part.astype(jnp.float32)
        part = ga_ref[rank, :, 4 * size :].astype(jnp.float32)
        for i in range(2):
            to = (i * 8 + at) * few
            gh_out[:, to : to + few] = part[:, i * few : (i + 1) * few]
            bias_out[i : i + 1, at * few : (at + 1) * few] = bias_ref[rank, :, i * few : (i + 1) * few]
        for i, target in enumerate((gfg_out, gfu_out)):
            for unit in range(4):
                to = (unit // 2 * 16 + rank // 4 * 8 + unit % 2 * 4 + rank % 4) * block
                part = gu_ref[rank, :, (i * 4 + unit) * block : (i * 4 + unit + 1) * block]
                target[:, to : to + block] = part.astype(jnp.float32)


def squares(
    layer_input,
    cotangent,
    seq_lengths,
    gains,
    head_bias,
    w_query,
    w_key,
    w_value,
    w_gate,
    w_out,
    w_heads,
    w_ff_gate,
    w_ff_up,
    w_ff_down,
):
    rows, width = layer_input.shape
    heads = head_bias.shape[1]
    head_dim = width // heads
    ranks = 8
    group = rows * ranks
    mine = heads // ranks
    cols = mine * head_dim
    shard = w_query.shape[0]
    units = w_ff_gate.shape[1] // ranks
    low = jnp.bfloat16
    f32 = jnp.float32
    packs = (ranks, shard, 4 * cols + 128)
    feeds = (ranks, shard, 2 * units)
    lens_shape = (8, 128)
    kept = (
        whole((group, width), low),
        whole((4, *packs), low),
        whole((mine, group, 128), low),
        whole((mine, group, 128), low),
        whole((mine, group, head_dim), low),
        whole((group, 2 * cols), f32),
        whole((group, 128), f32),
        whole((mine, group, 128), f32),
        whole((mine, 1, group), f32),
        whole((group, cols), f32),
        whole((mine, group, head_dim), f32),
        whole((group, cols), low),
        whole((4, shard, width), low),
        whole((4, *feeds), low),
        whole((4, *w_ff_down.shape), low),
        whole((group, width), low),
        whole((group, width), low),
    )
    (
        packed, lengths, mid,
        h_one_all, w_attn, q_all, k_all, v_all, diff, stat, fcol, frow, gate_sig, attn3, branch_in,
        w_o, w_gu, w_d, h_two_all, cot_all,
    ) = call(
        kernel_ab,
        1,
        (
            whole(layer_input.shape, low),
            whole(lens_shape, jnp.int32),
            whole((rows, width), f32),
            *kept,
        ),
        (
            layer_input, seq_lengths, gains, cotangent, head_bias,
            w_query, w_gate, w_key, w_value, w_heads, w_ff_gate, w_ff_up, w_out, w_ff_down,
        ),
        112,
        [
            *(pltpu.VMEM(leaf.shape, leaf.dtype) for leaf in kept),
            pltpu.VMEM(lens_shape, jnp.int32),
            pltpu.VMEM((8, 128), f32),
            pltpu.VMEM((group, packs[2]), f32),
            pltpu.VMEM(packs, low),
            pltpu.VMEM(feeds, low),
            pltpu.VMEM((4, shard, width), low),
            *sum_scratch(rows, width),
            *(pltpu.VMEM(leaf.shape, low) for leaf in (w_ff_gate, w_ff_up, w_out, w_ff_down)),
        ],
        local=7 + len(kept),
        far=range(10, 14),
        far_outs=range(3, 3 + len(kept)),
    )
    hidden, grad_mid, grad_branch, gain_two, grad_down, grad_gu, grad_far = call(
        kernel_c,
        3,
        (
            whole((group, units), low),
            whole((rows, width), f32),
            whole((group, width), low),
            whole((1, width), f32),
            whole((rows, width), f32),
            whole((4, *feeds), low),
            whole(feeds, low),
        ),
        (h_two_all, cot_all, w_gu, w_d, mid, gains),
        48,
        [
            pltpu.VMEM((group, 2 * units), low),
            pltpu.VMEM((4, rows, width), low),
            pltpu.VMEM((2, rows, width), low),
            pltpu.VMEM((rows, width), low),
            *sum_scratch(rows, width),
            *(pltpu.VMEM(leaf.shape, leaf.dtype) for leaf in (h_two_all, w_gu, cot_all, w_d, mid)),
            pltpu.VMEM((group, units), low),
            pltpu.VMEM((4, *feeds), low),
        ],
        7,
        range(5),
        (0, 5),
    )
    result, grad_input, gain_sums, bias_sums, grad_attn_w, grad_wout, grad_gu = call(
        kernel_d,
        4,
        (
            whole((rows, width), low),
            whole((rows, width), low),
            whole((2, width), f32),
            whole((ranks, 1, 128), f32),
            whole(packs, low),
            whole((shard, width), f32),
            whole(feeds, low),
        ),
        (
            grad_branch, w_o, branch_in, attn3, gate_sig, lengths, q_all, k_all, v_all, diff, stat,
            fcol, frow, w_attn, h_one_all, grad_mid, packed, gains, gain_two, grad_gu, grad_far,
            hidden, w_d, mid,
        ),
        96,
        [
            pltpu.VMEM((mine, group, head_dim), low),
            pltpu.VMEM((mine, group, 128), f32),
            pltpu.VMEM((mine, group, 128), f32),
            pltpu.VMEM((mine, group, head_dim), f32),
            pltpu.VMEM((group, packs[2]), low),
            *spread_scratch(feeds)[1:],
            *spread_scratch(packs),
            pltpu.VMEM((4, shard, width), low),
            *spread_scratch((shard, width)),
            pltpu.VMEM((4, 8, width), f32),
            pltpu.VMEM((ranks, 8, width), f32),
            pltpu.VMEM((group, width), low),
            pltpu.VMEM((rows, width), low),
            pltpu.VMEM((rows, width), low),
            *sum_scratch(rows, width),
            *sum_scratch(rows, width)[1:],
            *(pltpu.VMEM(leaf.shape, leaf.dtype) for leaf in (grad_gu, grad_far, hidden, w_d, w_o, branch_in, mid, attn3, gate_sig, q_all, k_all, v_all, fcol, frow, diff, stat, w_attn, grad_mid, packed)),
        ],
        24,
        (0, 14, 19, 20, 21, 22, 1, 2, 23, 3, 4, 6, 7, 8, 11, 12, 9, 10, 13, 15, 16),
    )

    big = whole((shard, width), f32)
    outs = (
        whole((rows, width), low),
        whole((rows, width), f32),
        whole((2, width), f32),
        whole((2, heads), f32),
        big,
        big,
        big,
        big,
        big,
        whole((shard, 2 * heads), f32),
        whole(w_ff_gate.shape, f32),
        whole(w_ff_up.shape, f32),
        whole(w_ff_down.shape, f32),
    )
    args = (result, grad_input, gain_sums, bias_sums, grad_attn_w, grad_wout, grad_gu, grad_down)
    return pl.pallas_call(
        finish,
        out_shape=outs,
        in_specs=vmem(len(args)),
        out_specs=vmem(len(outs)),
        compiler_params=pltpu.CompilerParams(vmem_limit_bytes=60 * 2**20),
    )(*args)


def solution(mesh):
    if mesh.shape["dp"] == 4 and mesh.shape["ctx"] == 8:
        body, axes, group = squares, AXES, ("x", "core")
        mesh = Mesh(np.reshape(mesh.devices, (2, 2, 2, 2, 2)), AXES)
    else:
        body, axes, group = shards, ("dp", "ctx"), "dp"
    cut = P(axes, None)
    return jax.shard_map(
        body,
        mesh=mesh,
        in_specs=(cut, cut, P(group, None), P(), P()) + (cut,) * 9,
        out_specs=(cut, cut, P(), P()) + (cut,) * 9,
        check_vma=False,
    )
```
